32 devices in a mesh: dp: 16 (over z, x, core), mp: 2 (over y).
Axes of the slice: x: 2, y: 2, z: 4, core: 2. Of those that a mesh axis runs over, the one named last changes fastest.
Arguments:
- tokens: bfloat16 [32, 788, 768], P(('dp', 'mp')), may hold values from -6 to 6
- cotangent: float32 [32, 788, 768], P(('dp', 'mp')), as said below
- rel_index: int32 [197, 197], replicated, may hold values from 0 to 731
- attn_owner: int32 [144], replicated, may hold values from 0 to 159, as said below
- mlp_owner: int32 [144], replicated, may hold values from 0 to 143, as said below
- attn_state: float32 [160, 7, 128, 128], P(('dp', 'mp')), as said below
- mlp_state: float32 [2, 144, 7, 128, 128], P('mp', 'dp'), as said below
- vec_param: float32 [10, 768], replicated
- vec_moments: float32 [2, 10, 768], replicated
- rel_table: float32 [12, 732], replicated, may hold values from -3 to 3
- rel_table_moments: float32 [2, 12, 732], replicated
- up_bias: float32 [3072], replicated, may hold values from -1 to 1
- up_bias_moments: float32 [2, 3072], replicated
Outputs:
- output: bfloat16 [32, 788, 768], P(('dp', 'mp'))
- input_grad: float32 [32, 788, 768], P(('dp', 'mp'))
- attn_update: float32 [160, 5, 128, 128], P(('dp', 'mp'))
- attn_copy: bfloat16 [160, 128, 128], P(('dp', 'mp'))
- mlp_update: float32 [2, 144, 5, 128, 128], P('mp', 'dp')
- mlp_copy: bfloat16 [2, 144, 128, 128], P('mp', 'dp')
- vector_update: float32 [4, 10, 768], replicated
- table_update: float32 [4, 12, 732], replicated
- up_bias_update: float32 [4, 3072], replicated
The draws below stay inside these ranges and needn't reach their ends.
Inputs may be any that keep to these rules, and one draw needn't show every extreme that they name: `cotangent`: independent normal entries with deviation (25216)^-0.5. `attn_owner`: distinct slots, one for each attention tile; slots that no tile names stay empty. `mlp_owner`: distinct slots, one for each feed-forward tile of a part, the same list for every part; slots that no tile names stay empty. `attn_state`: channels 3 and 4 are symmetric positive definite, channels 5 and 6 orthogonal. `mlp_state`: channels 3 and 4 are symmetric positive definite, channels 5 and 6 orthogonal.
All inputs are finite; a program needn't handle non-finite values.
Results may differ from the reference program's by a relative error of at most 0.028.
Values may be sent and summed in bfloat16 or wider, within the bound.
A program may use at most 192 MiB of HBM per device.

```python
import math
from functools import partial
import jax
import jax.numpy as jnp
from jax import lax

D = 768
H = 12
HD = 64
FF = 3072
NREL = 732
NPOS = 197
IMGS = 4
LEN = 788
B = 128
NV = 10
STEP = 5
SEQS = 32
NB_A = 144
SLOTS_A = 160
NB_M = 144
SLOTS_M = 144
N_MP = 2


beta_one = 0.9


beta_two = 0.95


beta_stat = 0.95


def draw_cotangent(key, part):
    key = jax.random.fold_in(key, 61)
    values = jax.random.truncated_normal(key, -6.0, 6.0, (SEQS, LEN, D))
    return (values * (1.0 / math.sqrt(SEQS * LEN))).astype(jnp.float32)


def owner_slots(key, block_total, slot_total):
    first_key, second_key = jax.random.split(key)
    interior = jax.random.permutation(first_key, jnp.arange(1, slot_total - 1, dtype=jnp.int32))
    chosen = jnp.concatenate([jnp.array([0, slot_total - 1], dtype=jnp.int32), interior[:block_total - 2]])
    return jax.random.permutation(second_key, chosen)


def draw_attn_owner(key, part):
    return owner_slots(jax.random.fold_in(key, 11), NB_A, SLOTS_A)


def draw_mlp_owner(key, part):
    return owner_slots(jax.random.fold_in(key, 12), NB_M, SLOTS_M)


def slot_blocks(owner_list, slot_total):
    marked = jnp.zeros((slot_total,), jnp.int32).at[owner_list].set(jnp.arange(owner_list.shape[0], dtype=jnp.int32) + 1)
    return jnp.maximum(marked - 1, 0)


def stat_matrix(key, slot_count):
    diag_key, off_key = jax.random.split(key)
    diagonal = jax.random.uniform(diag_key, (slot_count, B), minval=1.2, maxval=1.6)
    off_diagonal = jax.random.uniform(off_key, (slot_count, B, B), minval=-0.9 / B, maxval=0.9 / B)
    off_diagonal = 0.5 * (off_diagonal + jnp.swapaxes(off_diagonal, 1, 2))
    identity = jnp.eye(B, dtype=jnp.float32)
    return off_diagonal * (1.0 - identity) + identity * diagonal[:, :, None]


def reflector(key, slot_count):
    dir_key, sign_key = jax.random.split(key)
    direction = jax.random.normal(dir_key, (slot_count, B))
    direction = direction * jax.lax.rsqrt(jnp.sum(direction * direction, axis=1, keepdims=True))
    sign_flip = jnp.where(jax.random.bernoulli(sign_key, 0.5, (slot_count, B)), 1.0, -1.0)
    identity = jnp.eye(B, dtype=jnp.float32)
    return sign_flip[:, :, None] * (identity[None] - 2.0 * direction[:, :, None] * direction[:, None, :])


def block_states(key, grad_scale, weight_std):
    subkeys = jax.random.split(key, 7)
    slot_count = grad_scale.shape[0]
    scale_cube = grad_scale[:, None, None]
    array_shape = (slot_count, B, B)
    weight = jax.random.normal(subkeys[0], array_shape) * weight_std[:, None, None]
    first_moment = (1.0 - beta_one) / beta_one * scale_cube * jax.random.normal(subkeys[1], array_shape)
    second_moment = (1.0 - beta_two) / beta_two * scale_cube * scale_cube * jnp.exp(jax.random.uniform(subkeys[2], array_shape, minval=0.0, maxval=math.log(4.0)))
    stat_scale = 2.0 * (1.0 - beta_stat) / beta_stat * B * scale_cube * scale_cube
    left_stat = stat_matrix(subkeys[3], slot_count) * stat_scale
    right_stat = stat_matrix(subkeys[4], slot_count) * stat_scale
    left_basis = reflector(subkeys[5], slot_count)
    right_basis = reflector(subkeys[6], slot_count)
    return jnp.stack([weight, first_moment, second_moment, left_stat, right_stat, left_basis, right_basis], axis=1).astype(jnp.float32)


def draw_attn_state(key, part):
    owner_list = draw_attn_owner(key, part)
    block_kind = slot_blocks(owner_list, SLOTS_A) // (NB_A // 4)
    qkv_scale = 9.0 / math.sqrt(NPOS)
    out_scale = 2.7 * math.sqrt(1.0 / NPOS + 0.03)
    grad_table = jnp.array([qkv_scale, qkv_scale, qkv_scale, out_scale], jnp.float32)
    std_table = jnp.array([D ** (-0.5), D ** (-0.5), D ** (-0.5), (D // 16) ** (-0.5)], jnp.float32)
    return block_states(jax.random.fold_in(key, 21), grad_table[block_kind], std_table[block_kind])


def draw_mlp_state(key, part):
    owner_list = draw_mlp_owner(key, part)
    block_kind = (slot_blocks(owner_list, SLOTS_M) >= NB_M // 2).astype(jnp.int32)
    grad_table = jnp.array([0.3, 0.6], jnp.float32)
    std_table = jnp.array([D ** (-0.5), FF ** (-0.5)], jnp.float32)
    return jnp.stack([block_states(jax.random.fold_in(key, 31 + part_idx), grad_table[block_kind], std_table[block_kind]) for part_idx in range(N_MP)])


def draw_vec_param(key, part):
    low_end = jnp.array([0.7, -0.2, -0.3, -0.3, -0.2, 1.5, 0.7, -0.2, -0.2, 0.5], jnp.float32)
    high_end = jnp.array([1.3, 0.2, 0.3, 0.3, 0.2, 3.0, 1.3, 0.2, 0.2, 1.5], jnp.float32)
    uniform_draw = jax.random.uniform(jax.random.fold_in(key, 41), (NV, D))
    return low_end[:, None] + (high_end - low_end)[:, None] * uniform_draw


def adam_moments(key, grad_scale):
    first_key, second_key = jax.random.split(key)
    first_moment = (1.0 - beta_one) / beta_one * grad_scale * jax.random.normal(first_key, grad_scale.shape)
    second_moment = (1.0 - beta_two) / beta_two * grad_scale * grad_scale * jnp.exp(jax.random.uniform(second_key, grad_scale.shape, minval=0.0, maxval=math.log(4.0)))
    return jnp.stack([first_moment, second_moment]).astype(jnp.float32)


def draw_vec_moments(key, part):
    norm_one = 15.0 / math.sqrt(NPOS)
    head_scale = 9.0 / math.sqrt(NPOS)
    gamma_one = 4.8 * math.sqrt(1.0 / NPOS + 0.03)
    row_scale = jnp.array([norm_one, norm_one, head_scale, head_scale, 2.7, gamma_one, 0.6, 0.6, 1.0, 1.0], jnp.float32)
    return adam_moments(jax.random.fold_in(key, 51), jnp.broadcast_to(row_scale[:, None], (NV, D)))


def draw_rel_table_moments(key, part):
    table_scale = 9.0 * math.sqrt(HD * IMGS / (NREL * LEN))
    return adam_moments(jax.random.fold_in(key, 52), jnp.full((H, NREL), table_scale, jnp.float32))


def draw_up_bias_moments(key, part):
    return adam_moments(jax.random.fold_in(key, 53), jnp.full((FF,), 0.3, jnp.float32))


def with_ends(values, own_key, least, top_value):
    spot = [jax.random.randint(jax.random.fold_in(own_key, axis), (), 0, length) for axis, length in enumerate(values.shape)]
    main_axis = values.shape.index(max(values.shape))
    next_to = spot[:main_axis] + [(spot[main_axis] + 1) % values.shape[main_axis]] + spot[main_axis + 1:]
    return values.at[tuple(spot)].set(least).at[tuple(next_to)].set(top_value)


def block_levels(stream_key, extent, cuts, low, top_value):
    factor_of, own = 1.0, jax.random.fold_in(stream_key, 6)
    for dim, blocks in cuts:
        steps = jnp.exp(jax.random.uniform(jax.random.fold_in(own, dim), (blocks,), jnp.float32, low / len(cuts), top_value / len(cuts)))
        factor_of = factor_of * jnp.repeat(steps, extent[dim] // blocks).reshape([-1 if axis == dim else 1 for axis in range(len(extent))])
    return factor_of


def noise(key, extent, width, bound, cuts=(), kind=jnp.bfloat16):
    values = jax.random.normal(key, extent, jnp.float32) * width
    if len(cuts) > 0:
        values = block_levels(key, extent, cuts, -0.22, 0.18) * values
    return jnp.clip(values, min=-bound, max=bound).astype(kind)


def setup_inputs(seed: int = 0) -> dict:
    streams_of = jax.random.split(jax.random.key(seed), 14)
    return {
        "tokens": noise(streams_of[0], (SEQS, LEN, D), 1.0, 6.0, ((0, 32),)),
        "cotangent": draw_cotangent(jax.random.fold_in(streams_of[13], 71), 0),
        "rel_index": with_ends(jax.random.randint(streams_of[2], (NPOS, NPOS), 0, NREL), jax.random.fold_in(streams_of[2], 1), 0, NREL - 1).astype(jnp.int32),
        "attn_owner": draw_attn_owner(jax.random.fold_in(streams_of[13], 71), 0),
        "mlp_owner": draw_mlp_owner(jax.random.fold_in(streams_of[13], 71), 0),
        "attn_state": draw_attn_state(jax.random.fold_in(streams_of[13], 71), 0),
        "mlp_state": draw_mlp_state(jax.random.fold_in(streams_of[13], 71), 0),
        "vec_param": draw_vec_param(jax.random.fold_in(streams_of[13], 71), 0),
        "vec_moments": draw_vec_moments(jax.random.fold_in(streams_of[13], 71), 0),
        "rel_table": noise(streams_of[9], (H, NREL), 0.5, 3.0, (), jnp.float32),
        "rel_table_moments": draw_rel_table_moments(jax.random.fold_in(streams_of[13], 71), 0),
        "up_bias": noise(streams_of[11], (FF,), 0.2, 1.0, (), jnp.float32),
        "up_bias_moments": draw_up_bias_moments(jax.random.fold_in(streams_of[13], 71), 0),
    }


precise = lax.Precision.HIGHEST
ln_eps = 1e-06
beta_one = 0.9
beta_two = 0.95
beta_stat = 0.95
adam_eps = 1e-08
matrix_rate = 0.05
vector_rate = 0.2
decay_rate = 0.05

@jax.custom_vjp
def low(v):
    return lax.optimization_barrier(v.astype(jnp.bfloat16)).astype(jnp.float32)

@jax.custom_vjp
def low_back(v):
    return v

def low_keep(v):
    return (low(v), None)

def low_pass(kept, grad):
    return (grad,)

def back_keep(v):
    return (v, None)

def back_low(kept, grad):
    return (low(grad),)
low.defvjp(low_keep, low_pass)
low_back.defvjp(back_keep, back_low)

def matmul(left, right):
    return jnp.dot(left.astype(jnp.float32), right.astype(jnp.float32), precision=precise, preferred_element_type=jnp.float32)

def layer_norm(values, gain_row, shift_row):
    centered = values - lax.optimization_barrier(jnp.mean(values, axis=-1, keepdims=True))
    variance = lax.optimization_barrier(jnp.mean(centered * centered, axis=-1, keepdims=True))
    return centered * lax.rsqrt(variance + ln_eps) * gain_row + shift_row

def positions(segment_ids):
    row_ids = jnp.arange(segment_ids.shape[0], dtype=jnp.int32)
    same_label = segment_ids[:, None] == segment_ids[None, :]
    first_row = lax.optimization_barrier(jnp.min(jnp.where(same_label, row_ids[None, :], jnp.int32(segment_ids.shape[0])), axis=1)).astype(jnp.int32)
    return row_ids - first_row

def split_heads(matrix):
    return matrix.reshape(matrix.shape[0], H, HD).transpose(1, 0, 2)

def forward(tokens_f, attn_w, up_w, down_w, vec_param, rel_table, up_bias, segments, rel_index):
    score_scale = HD ** (-0.5)
    normed_one = low(layer_norm(tokens_f, vec_param[0], vec_param[1]))
    queries = low(low_back(matmul(normed_one, attn_w[0]) + vec_param[2]))
    keys_all = low(low_back(matmul(normed_one, attn_w[1])))
    values_all = low(low_back(matmul(normed_one, attn_w[2]) + vec_param[3]))

    def one_sequence(members):
        q_seq, k_seq, v_seq, seg_ids = members
        position = positions(seg_ids)
        same_image = seg_ids[:, None] == seg_ids[None, :]
        bias_all = rel_table[:, rel_index[position[:, None], position[None, :]]]
        q_heads = split_heads(q_seq)
        k_heads = split_heads(k_seq)
        v_heads = split_heads(v_seq)
        scores = low_back(jnp.einsum('hid,hjd->hij', q_heads, k_heads, precision=precise) * score_scale + bias_all)
        attn_probs = jax.nn.softmax(jnp.where(same_image[None], scores, -1e+30), axis=-1)
        mixed_heads = jnp.einsum('hij,hjd->hid', low(attn_probs), v_heads, precision=precise)
        return mixed_heads.transpose(1, 0, 2).reshape(seg_ids.shape[0], H * HD)
    mixed_all = lax.map(jax.checkpoint(one_sequence), (queries, keys_all, values_all, segments))
    attended = low(low_back(mixed_all))
    branch = low_back(matmul(attended, attn_w[3]) + vec_param[4])
    middle = tokens_f + vec_param[5] * branch
    normed_two = low(layer_norm(middle, vec_param[6], vec_param[7]))
    part_width = FF // N_MP
    hidden = jnp.concatenate([matmul(low_back(normed_two), up_w[:, part_idx * part_width:(part_idx + 1) * part_width]) for part_idx in range(N_MP)], axis=-1)
    hidden = low_back(hidden + up_bias)
    activated = low(jax.nn.gelu(hidden, approximate=False))
    summed = vec_param[8]
    for part_idx in range(N_MP):
        summed = summed + low(matmul(activated[..., part_idx * part_width:(part_idx + 1) * part_width], down_w[part_idx * part_width:(part_idx + 1) * part_width]))
    summed = low_back(summed)
    return middle + vec_param[9] * summed

def cholesky_orth(product):
    gram = jnp.einsum('sji,sjk->sik', product, product, precision=precise)
    factor = jnp.linalg.cholesky(gram)
    solved = jax.vmap(partial(jax.scipy.linalg.solve_triangular, lower=True))(factor, jnp.swapaxes(product, 1, 2))
    return jnp.swapaxes(solved, 1, 2)

def soap_update(grads, state, step_number):
    weight = state[:, 0]
    first_moment = state[:, 1]
    second_moment = state[:, 2]
    left_stat = state[:, 3]
    right_stat = state[:, 4]
    left_basis = state[:, 5]
    right_basis = state[:, 6]
    new_left = beta_stat * left_stat + (1.0 - beta_stat) * jnp.einsum('sij,skj->sik', grads, grads, precision=precise)
    new_right = beta_stat * right_stat + (1.0 - beta_stat) * jnp.einsum('sji,sjk->sik', grads, grads, precision=precise)
    left_orth = cholesky_orth(jnp.einsum('sij,sjk->sik', new_left, left_basis, precision=precise))
    right_orth = cholesky_orth(jnp.einsum('sij,sjk->sik', new_right, right_basis, precision=precise))
    half_turn = jnp.einsum('sji,sjk->sik', left_orth, grads, precision=precise)
    rotated = jnp.einsum('sij,sjk->sik', half_turn, right_orth, precision=precise)
    new_first = beta_one * first_moment + (1.0 - beta_one) * rotated
    new_second = beta_two * second_moment + (1.0 - beta_two) * rotated * rotated
    fix_one = 1.0 - beta_one ** step_number
    fix_two = 1.0 - beta_two ** step_number
    normalized = new_first / fix_one / (jnp.sqrt(new_second / fix_two) + adam_eps)
    back_half = jnp.einsum('sij,sjk->sik', left_orth, normalized, precision=precise)
    update = jnp.einsum('sij,skj->sik', back_half, right_orth, precision=precise)
    new_weight = weight - matrix_rate * (update + decay_rate * weight)
    return jnp.stack([new_weight, new_first, new_second, left_orth, right_orth], axis=1)

def adam_vector(grads, param, moments, step_number):
    new_first = beta_one * moments[0] + (1.0 - beta_one) * grads
    new_second = beta_two * moments[1] + (1.0 - beta_two) * grads * grads
    fix_one = 1.0 - beta_one ** step_number
    fix_two = 1.0 - beta_two ** step_number
    new_param = param - vector_rate * (new_first / fix_one) / (jnp.sqrt(new_second / fix_two) + adam_eps)
    return jnp.stack([grads, new_param, new_first, new_second])

def reference(tokens, cotangent, rel_index, attn_owner, mlp_owner, attn_state, mlp_state, vec_param, vec_moments, rel_table, rel_table_moments, up_bias, up_bias_moments):
    tile_count = D // B
    segments = jnp.broadcast_to((jnp.arange(LEN, dtype=jnp.int32) // NPOS)[None, :], (tokens.shape[0], LEN)).astype(jnp.int32)
    attn_blocks = low(attn_state[attn_owner, 0])
    attn_w = attn_blocks.reshape(4, tile_count, tile_count, B, B).transpose(0, 1, 3, 2, 4).reshape(4, D, D)
    part_width = FF // N_MP
    local_tiles = part_width // B
    half_blocks = tile_count * local_tiles
    up_list = []
    down_list = []
    for part_idx in range(N_MP):
        blocks_here = low(mlp_state[part_idx][mlp_owner, 0])
        up_list.append(blocks_here[:half_blocks].reshape(tile_count, local_tiles, B, B).transpose(0, 2, 1, 3).reshape(D, part_width))
        down_list.append(blocks_here[half_blocks:].reshape(local_tiles, tile_count, B, B).transpose(0, 2, 1, 3).reshape(part_width, D))
    up_w = jnp.concatenate(up_list, axis=1)
    down_w = jnp.concatenate(down_list, axis=0)
    tokens_f = tokens.astype(jnp.float32)
    forward_fixed = partial(forward, segments=segments, rel_index=rel_index)
    result, pullback = jax.vjp(forward_fixed, tokens_f, attn_w, up_w, down_w, vec_param, rel_table, up_bias)
    grad_tokens, grad_attn, grad_up, grad_down, grad_vec, grad_table, grad_bias = pullback(cotangent.astype(jnp.float32))
    attn_tiles = grad_attn.reshape(4, tile_count, B, tile_count, B).transpose(0, 1, 3, 2, 4).reshape(-1, B, B)
    attn_slots = jnp.zeros((attn_state.shape[0], B, B), jnp.float32).at[attn_owner].set(attn_tiles)
    attn_update = soap_update(attn_slots, attn_state, STEP)
    mlp_list = []
    for part_idx in range(N_MP):
        up_part = grad_up[:, part_idx * part_width:(part_idx + 1) * part_width].reshape(tile_count, B, local_tiles, B).transpose(0, 2, 1, 3).reshape(-1, B, B)
        down_part = grad_down[part_idx * part_width:(part_idx + 1) * part_width].reshape(local_tiles, B, tile_count, B).transpose(0, 2, 1, 3).reshape(-1, B, B)
        slots_here = jnp.zeros((mlp_state.shape[1], B, B), jnp.float32).at[mlp_owner].set(jnp.concatenate([up_part, down_part], axis=0))
        mlp_list.append(soap_update(slots_here, mlp_state[part_idx], STEP))
    mlp_update = jnp.stack(mlp_list)
    return (result.astype(jnp.bfloat16), grad_tokens, attn_update, attn_update[:, 0].astype(jnp.bfloat16), mlp_update, mlp_update[:, :, 0].astype(jnp.bfloat16), adam_vector(grad_vec, vec_param, vec_moments, STEP), adam_vector(grad_table, rel_table, rel_table_moments, STEP), adam_vector(grad_bias, up_bias, up_bias_moments, STEP))
```

```python
from functools import partial
import math

import jax
import jax.numpy as jnp
from jax import lax
from jax.experimental import pallas as pl
from jax.experimental.pallas import tpu as pltpu
from jax.sharding import PartitionSpec as P

D = 768
H = 12
HD = 64
FF = 3072
NPOS = 197
NP = 208
NL = 256
B = 128
STEP = 5
T = D // B

f32 = jnp.float32
bf16 = jnp.bfloat16

ln_eps = 1e-06
beta_one = 0.9
beta_two = 0.95
beta_stat = 0.95
adam_eps = 1e-08
matrix_rate = 0.05
vector_rate = 0.2
decay_rate = 0.05

VMEM = pl.BlockSpec(memory_space=pltpu.VMEM)
SMEM = pl.BlockSpec(memory_space=pltpu.SMEM)
ANY = pl.BlockSpec(memory_space=pl.ANY)
LIMIT = 60 << 20


def shape(dims, kind):
    return jax.ShapeDtypeStruct(dims, kind)


def dot_nn(x, y):
    return lax.dot_general(x, y, (((1,), (0,)), ((), ())), preferred_element_type=f32)


def dot_nt(x, y):
    return lax.dot_general(x, y, (((1,), (1,)), ((), ())), preferred_element_type=f32)


def dot_tn(x, y):
    return lax.dot_general(x, y, (((0,), (0,)), ((), ())), preferred_element_type=f32)


def norm_parts(values):
    centered = values - jnp.mean(values, axis=-1, keepdims=True)
    inv_std = lax.rsqrt(jnp.mean(centered * centered, axis=-1, keepdims=True) + ln_eps)
    return (centered * inv_std, inv_std)


def norm_back(grad_normed, scaled, inv_std, gain_row):
    tangent = grad_normed * gain_row
    return inv_std * (
        tangent
        - jnp.mean(tangent, axis=-1, keepdims=True)
        - scaled * jnp.mean(tangent * scaled, axis=-1, keepdims=True)
    )


def lookup_kernel(idx_ref, table_ref, out_ref, spread):
    chunks = table_ref.shape[1] // B
    for h in range(H):
        for c in range(chunks):
            spread[h, c] = jnp.broadcast_to(table_ref[h : h + 1, c * B : (c + 1) * B], (8, B))

    @pl.loop(0, NP // 8)
    def _(jt):
        rows = pl.ds(pl.multiple_of(jt * 8, 8), 8)
        real = jt * 8 + lax.broadcasted_iota(jnp.int32, (8, B), 0) < NPOS
        for half in range(NL // B):
            lanes = slice(half * B, (half + 1) * B)
            idx = idx_ref[rows, lanes]
            low = jnp.bitwise_and(idx, B - 1)
            high = jnp.right_shift(idx, 7)
            for h in range(H):
                acc = jnp.take_along_axis(spread[h, 0], low, axis=1, mode="promise_in_bounds")
                for c in range(1, chunks):
                    part = jnp.take_along_axis(spread[h, c], low, axis=1, mode="promise_in_bounds")
                    acc = jnp.where(high == c, part, acc)
                out_ref[h, rows, lanes] = jnp.where(real, acc, -1e30)


def table_lookup(idx_t, table_pad):
    return pl.pallas_call(
        lookup_kernel,
        in_specs=[VMEM, VMEM],
        out_specs=VMEM,
        out_shape=shape((H, NP, NL), f32),
        scratch_shapes=[pltpu.VMEM((H, table_pad.shape[1] // B, 8, B), f32)],
        compiler_params=pltpu.CompilerParams(vmem_limit_bytes=LIMIT),
        name="table_lookup",
    )(idx_t, table_pad)


def accumulate_kernel(grid_ref, idx_ref, out_ref):
    chunks = out_ref.shape[0]
    out_ref[...] = jnp.zeros_like(out_ref)
    lo_rows = lax.broadcasted_iota(jnp.int32, (B, NL), 0)

    @pl.loop(0, NPOS)
    def _(j):
        values = grid_ref[:, j, :]
        values = jnp.concatenate([values, jnp.zeros((4, NL), f32)], axis=0)
        idx = idx_ref[pl.ds(j, 1), :]
        low = jnp.bitwise_and(idx, B - 1)
        high = jnp.right_shift(idx, 7)
        onehot = jnp.where(lo_rows == low, 1.0, 0.0).astype(bf16)
        first = values.astype(bf16)
        second = (values - first.astype(f32)).astype(bf16)
        rows = []
        for c in range(chunks):
            rows.append(jnp.where(high == c, values, 0.0))
        stacked = jnp.concatenate(rows, axis=0)
        first = stacked.astype(bf16)
        second = (stacked - first.astype(f32)).astype(bf16)
        got = dot_nt(jnp.concatenate([first, second], axis=0), onehot)
        for c in range(chunks):
            base = c * 16
            out_ref[c] += got[base : base + 16] + got[chunks * 16 + base : chunks * 16 + base + 16]


def table_accumulate(grid_t, idx_t, chunks):
    return pl.pallas_call(
        accumulate_kernel,
        in_specs=[VMEM, VMEM],
        out_specs=VMEM,
        out_shape=shape((chunks, 16, B), f32),
        compiler_params=pltpu.CompilerParams(vmem_limit_bytes=LIMIT),
        name="table_accumulate",
    )(grid_t, idx_t)


def attn_tile(weights, b):
    m = b // (T * T)
    r = lax.rem(b // T, T)
    c = lax.rem(b, T)
    return weights.at[
        m, pl.ds(pl.multiple_of(r * B, B), B), pl.ds(pl.multiple_of(c * B, B), B)
    ]


def pad_rows(x):
    return jnp.concatenate([x, jnp.zeros((NL - NP, x.shape[1]), x.dtype)], axis=0)


def forward_kernel(
    own, tok, slots, vec, bias, w, q, k, v, att, lse, mid, bra, n2, n1, sem
):
    imgs = q.shape[0]

    @pl.loop(0, own.shape[0])
    def _(b):
        pltpu.make_async_copy(slots.at[own[b]], attn_tile(w, b), sem).start()

    for img in range(imgs):
        x, _ = norm_parts(tok[img].astype(f32))
        n1[img * NP : (img + 1) * NP] = (x * vec[0:1] + vec[1:2]).astype(bf16)
    pltpu.make_async_copy(w, w, sem).wait()

    for m, (out, row, scale) in enumerate(((q, 2, HD**-0.5), (k, None, 1.0), (v, 3, 1.0))):
        for n in range(D // NL):
            lanes = slice(n * NL, (n + 1) * NL)
            part = dot_nn(n1[...], w[m, :, lanes])
            if row is not None:
                part = part + vec[row : row + 1, lanes]
            part = part.astype(bf16)
            if scale != 1.0:
                part = part * jnp.asarray(scale, bf16)
            for img in range(imgs):
                out[img, :, lanes] = part[img * NP : (img + 1) * NP]

    @pl.loop(0, imgs)
    def _(img):
        side = lax.broadcasted_iota(jnp.int32, (1, B), 1) // HD
        for pair in range(H // 2):
            lanes = slice(pair * B, (pair + 1) * B)
            k_pair = k[img, :, lanes]
            q_pair = pad_rows(q[img, :, lanes])
            v_turn = v[img, :, lanes].astype(f32).T.astype(bf16)
            mixed = []
            for sub in range(2):
                h = pair * 2 + sub
                q_one = jnp.where(side == sub, q_pair, jnp.zeros_like(q_pair))
                s = dot_nt(k_pair, q_one) + bias[h]
                top = jnp.max(s, axis=0, keepdims=True)
                e = jnp.exp(s - top)
                total = jnp.sum(e, axis=0, keepdims=True)
                o = dot_nn(v_turn[sub * HD : (sub + 1) * HD], e.astype(bf16))
                mixed.append(o * (1.0 / total))
                lse[img, h : h + 1] = top + jnp.log(total)
            both = jnp.concatenate(mixed, axis=0).T
            att[img, :, lanes] = both[:NP].astype(bf16)

    @pl.loop(0, imgs)
    def _(img):
        branch = dot_nn(att[img], w[3]) + vec[4:5]
        bra[img] = branch
        middle = tok[img].astype(f32) + vec[5:6] * branch
        mid[img] = middle
        x, _ = norm_parts(middle)
        n2[img] = (x * vec[6:7] + vec[7:8]).astype(bf16)


def forward_attention(tok, slots, own, vec, bias):
    imgs = tok.shape[0]
    big = shape((imgs, NP, D), bf16)
    wide = shape((imgs, NP, D), f32)
    return pl.pallas_call(
        forward_kernel,
        in_specs=[SMEM, VMEM, ANY, VMEM, VMEM],
        out_specs=[VMEM] * 9,
        out_shape=[
            shape((4, D, D), bf16),
            big,
            big,
            big,
            big,
            shape((imgs, H, NL), f32),
            wide,
            wide,
            big,
        ],
        scratch_shapes=[pltpu.VMEM((imgs * NP, D), bf16), pltpu.SemaphoreType.DMA(())],
        compiler_params=pltpu.CompilerParams(vmem_limit_bytes=LIMIT),
        name="forward_attention",
    )(own, tok, slots, vec, bias)


CH = 512


def mlp_kernel(
    parts,
    each,
    own,
    mid,
    bra,
    n2,
    cot,
    slots,
    vec,
    upb,
    out,
    gmid,
    gbra,
    sums,
    bgrad,
    tiles_out,
    w1,
    w2,
    gs,
    act,
    gh,
    summed,
    gn2,
    tiles,
    sem_in,
    sem_out,
):
    imgs = mid.shape[0]
    rows = imgs * NP
    chunks = FF // CH
    per = CH // B
    half = own.shape[0] // 2
    total = parts * half
    local = half // T

    def place(slot, p):
        return (slot // each) * (parts * each) + p * each + lax.rem(slot, each)

    @pl.loop(0, total)
    def _(b):
        p = b // half
        rest = lax.rem(b, half)
        r = rest // local
        c = p * local + lax.rem(rest, local)
        pltpu.make_async_copy(
            slots.at[place(own[rest], p)],
            w1.at[
                c // per,
                pl.ds(pl.multiple_of(r * B, B), B),
                pl.ds(pl.multiple_of(lax.rem(c, per) * B, B), B),
            ],
            sem_in,
        ).start()
        r2 = p * local + rest // T
        c2 = lax.rem(rest, T)
        pltpu.make_async_copy(
            slots.at[place(own[half + rest], p)],
            w2.at[pl.ds(pl.multiple_of(r2 * B, B), B), pl.ds(pl.multiple_of(c2 * B, B), B)],
            sem_in,
        ).start()

    for img in range(imgs):
        gs[img * NP : (img + 1) * NP] = (vec[9:10] * cot[img]).astype(bf16)
    summed[...] = jnp.zeros_like(summed)
    gn2[...] = jnp.zeros_like(gn2)
    pltpu.make_async_copy(w1, w1, sem_in).wait()
    pltpu.make_async_copy(w2, w2, sem_in).wait()

    @pl.loop(0, chunks)
    def _(c):
        span = pl.ds(pl.multiple_of(c * CH, CH), CH)
        bias_sum = jnp.zeros((1, CH), f32)
        for rb in range(imgs // 2):
            block = slice(rb * 2 * NP, (rb + 1) * 2 * NP)
            hid = dot_nn(n2[block], w1[c]) + upb[:, span]
            back = dot_nt(gs[block], w2[span])
            phi = 0.5 * (1.0 + lax.erf(hid * (1.0 / math.sqrt(2.0))))
            density = jnp.exp(-0.5 * hid * hid) * (1.0 / math.sqrt(2.0 * math.pi))
            a = (hid * phi).astype(bf16)
            g = (back * (phi + hid * density)).astype(bf16)
            act[block] = a
            gh[block] = g
            bias_sum = bias_sum + jnp.sum(g.astype(f32), axis=0, keepdims=True)
            summed[block] += dot_nn(a, w2[span])
            gn2[block] += dot_nt(g, w1[c])
        bgrad[:, span] = bias_sum
        up_grad = dot_tn(n2[...], gh[...])
        down_grad = dot_tn(act[...], gs[...])
        for r in range(T):
            for cc in range(per):
                tiles[c, r * per + cc] = up_grad[
                    r * B : (r + 1) * B, cc * B : (cc + 1) * B
                ].astype(bf16)
        for r in range(per):
            for cc in range(T):
                tiles[c, T * per + r * T + cc] = down_grad[
                    r * B : (r + 1) * B, cc * B : (cc + 1) * B
                ].astype(bf16)

        @pl.loop(0, T * per)
        def _(t):
            r = t // per
            g = c * per + lax.rem(t, per)
            p = g // local
            b = r * local + lax.rem(g, local)
            pltpu.make_async_copy(
                tiles.at[c, t], tiles_out.at[place(own[b], p)], sem_out
            ).start()
            g2 = c * per + t // T
            p2 = g2 // local
            b2 = half + lax.rem(g2, local) * T + lax.rem(t, T)
            pltpu.make_async_copy(
                tiles.at[c, T * per + t], tiles_out.at[place(own[b2], p2)], sem_out
            ).start()

    s4 = jnp.zeros((1, D), f32)
    s5 = jnp.zeros((1, D), f32)
    s6 = jnp.zeros((1, D), f32)
    s7 = jnp.zeros((1, D), f32)
    s8 = jnp.zeros((1, D), f32)
    s9 = jnp.zeros((1, D), f32)
    for img in range(imgs):
        block = slice(img * NP, (img + 1) * NP)
        up = cot[img]
        middle = mid[img]
        sm = summed[block] + vec[8:9]
        out[img] = (middle + vec[9:10] * sm).astype(bf16)
        s9 += jnp.sum(up * sm, axis=0, keepdims=True)
        s8 += jnp.sum(gs[block].astype(f32), axis=0, keepdims=True)
        x, inv = norm_parts(middle)
        gn = gn2[block]
        s6 += jnp.sum(gn * x, axis=0, keepdims=True)
        s7 += jnp.sum(gn, axis=0, keepdims=True)
        gm = up + norm_back(gn, x, inv, vec[6:7])
        gmid[img] = gm
        gb = (vec[5:6] * gm).astype(bf16)
        gbra[img] = gb
        s4 += jnp.sum(gb.astype(f32), axis=0, keepdims=True)
        s5 += jnp.sum(gm * bra[img], axis=0, keepdims=True)
    sums[...] = jnp.concatenate([s4, s5, s6, s7, s8, s9, s9, s9], axis=0)
    pltpu.make_async_copy(tiles, tiles, sem_out).wait()


def feed_forward(mid, bra, n2, cot, slots, own, vec, up_bias, parts, each):
    imgs = mid.shape[0]
    rows = imgs * NP
    chunks = FF // CH
    per = CH // B
    return pl.pallas_call(
        partial(mlp_kernel, parts, each),
        in_specs=[SMEM, VMEM, VMEM, VMEM, VMEM, ANY, VMEM, VMEM],
        out_specs=[VMEM] * 5 + [ANY],
        out_shape=[
            shape((imgs, NP, D), bf16),
            shape((imgs, NP, D), f32),
            shape((imgs, NP, D), bf16),
            shape((8, D), f32),
            shape((1, FF), f32),
            shape(slots.shape, bf16),
        ],
        scratch_shapes=[
            pltpu.VMEM((chunks, D, CH), bf16),
            pltpu.VMEM((FF, D), bf16),
            pltpu.VMEM((rows, D), bf16),
            pltpu.VMEM((rows, CH), bf16),
            pltpu.VMEM((rows, CH), bf16),
            pltpu.VMEM((rows, D), f32),
            pltpu.VMEM((rows, D), f32),
            pltpu.VMEM((chunks, 2 * T * per, B, B), bf16),
            pltpu.SemaphoreType.DMA(()),
            pltpu.SemaphoreType.DMA(()),
        ],
        compiler_params=pltpu.CompilerParams(vmem_limit_bytes=LIMIT),
        name="feed_forward",
    )(own, mid, bra, n2.reshape(rows, D), cot, slots, vec, up_bias)


def backward_kernel(
    own,
    tok,
    w,
    q,
    k,
    v,
    att,
    lse,
    bias,
    gmid,
    gbra,
    vec,
    gin,
    grid,
    sums,
    tiles_out,
    n1,
    gatt,
    gqkv,
    tiles,
    sem,
):
    imgs = q.shape[0]
    for img in range(imgs):
        x, _ = norm_parts(tok[img].astype(f32))
        n1[img * NP : (img + 1) * NP] = (x * vec[0:1] + vec[1:2]).astype(bf16)
    for n in range(D // NL):
        lanes = slice(n * NL, (n + 1) * NL)
        got = dot_nt(gbra[...], w[3, lanes, :]).astype(bf16)
        for img in range(imgs):
            gatt[img, :, lanes] = got[img * NP : (img + 1) * NP]
    grid[...] = jnp.zeros_like(grid)

    @pl.loop(0, imgs)
    def _(img):
        side = lax.broadcasted_iota(jnp.int32, (1, B), 1) // HD
        here = pl.ds(pl.multiple_of(img * NP, 16), NP)
        for pair in range(H // 2):
            lanes = slice(pair * B, (pair + 1) * B)
            k_pair = k[img, :, lanes]
            v_pair = v[img, :, lanes]
            q_pair = pad_rows(q[img, :, lanes])
            g_pair = pad_rows(gatt[img, :, lanes])
            k_turn = k_pair.astype(f32).T.astype(bf16)
            gq = []
            gk = jnp.zeros((NP, B), f32)
            gv = jnp.zeros((NP, B), f32)
            for sub in range(2):
                h = pair * 2 + sub
                q_one = jnp.where(side == sub, q_pair, jnp.zeros_like(q_pair))
                g_one = jnp.where(side == sub, g_pair, jnp.zeros_like(g_pair))
                s = dot_nt(k_pair, q_one) + bias[h]
                p = jnp.exp(s - lse[img, h : h + 1])
                dp = dot_nt(v_pair, g_one)
                gv = gv + dot_nn(p.astype(bf16), g_one)
                inner = jnp.sum(p * dp, axis=0, keepdims=True)
                ds = (p * (dp - inner)).astype(bf16)
                gk = gk + dot_nn(ds, q_one)
                gq.append(dot_nn(k_turn[sub * HD : (sub + 1) * HD], ds))
                grid[h] += ds.astype(f32)
            turned = jnp.concatenate(gq, axis=0).T
            gqkv[here, lanes] = (turned[:NP] * HD**-0.5).astype(bf16)
            gqkv[here, D + pair * B : D + (pair + 1) * B] = gk.astype(bf16)
            gqkv[here, 2 * D + pair * B : 2 * D + (pair + 1) * B] = gv.astype(bf16)

    def put(m, n, grad):
        for r in range(T):
            for cc in range(NL // B):
                tiles[m * T * T + r * T + n * (NL // B) + cc] = grad[
                    r * B : (r + 1) * B, cc * B : (cc + 1) * B
                ].astype(bf16)

    for n in range(D // NL):
        lanes = slice(n * NL, (n + 1) * NL)
        put(3, n, dot_tn(att[...], gbra[:, lanes]))
    for m in range(3):
        for n in range(D // NL):
            put(m, n, dot_tn(n1[...], gqkv[:, m * D + n * NL : m * D + (n + 1) * NL]))

    @pl.loop(0, own.shape[0])
    def _(b):
        pltpu.make_async_copy(tiles.at[b], tiles_out.at[own[b]], sem).start()

    s0 = jnp.zeros((1, D), f32)
    s1 = jnp.zeros((1, D), f32)
    s2 = jnp.zeros((1, D), f32)
    s3 = jnp.zeros((1, D), f32)
    for img in range(imgs):
        here = slice(img * NP, (img + 1) * NP)
        gq = gqkv[here, 0:D]
        gk = gqkv[here, D : 2 * D]
        gv = gqkv[here, 2 * D : 3 * D]
        gn = dot_nt(gq, w[0]) + dot_nt(gk, w[1]) + dot_nt(gv, w[2])
        x, inv = norm_parts(tok[img].astype(f32))
        s0 += jnp.sum(gn * x, axis=0, keepdims=True)
        s1 += jnp.sum(gn, axis=0, keepdims=True)
        s2 += jnp.sum(gq.astype(f32), axis=0, keepdims=True)
        s3 += jnp.sum(gv.astype(f32), axis=0, keepdims=True)
        gin[img] = gmid[img] + norm_back(gn, x, inv, vec[0:1])
    sums[...] = jnp.concatenate([s0, s1, s2, s3, s3, s3, s3, s3], axis=0)
    pltpu.make_async_copy(tiles, tiles, sem).wait()


def backward_attention(tok, w, q, k, v, att, lse, bias, gmid, gbra, own, vec, slot_total):
    imgs = tok.shape[0]
    rows = imgs * NP
    return pl.pallas_call(
        backward_kernel,
        in_specs=[SMEM] + [VMEM] * 11,
        out_specs=[VMEM] * 3 + [ANY],
        out_shape=[
            shape((imgs, NP, D), f32),
            shape((H, NP, NL), f32),
            shape((8, D), f32),
            shape((slot_total, B, B), bf16),
        ],
        scratch_shapes=[
            pltpu.VMEM((rows, D), bf16),
            pltpu.VMEM((imgs, NP, D), bf16),
            pltpu.VMEM((rows, 3 * D), bf16),
            pltpu.VMEM((4 * T * T, B, B), bf16),
            pltpu.SemaphoreType.DMA(()),
        ],
        compiler_params=pltpu.CompilerParams(vmem_limit_bytes=LIMIT),
        name="backward_attention",
    )(
        own,
        tok,
        w,
        q,
        k,
        v,
        att.reshape(rows, D),
        lse,
        bias,
        gmid,
        gbra.reshape(rows, D),
        vec,
    )


NB = 16


def split_two(x):
    first = x.astype(bf16)
    return first, (x - first.astype(f32)).astype(bf16)


def wide_dot(x, y, dims):
    xa, xb = split_two(x)
    ya, yb = split_two(y)
    xs = jnp.concatenate([xa, xa, xb], axis=dims[0])
    ys = jnp.concatenate([ya, yb, ya], axis=dims[1])
    return lax.dot_general(
        xs, ys, (((dims[0],), (dims[1],)), ((), ())), preferred_element_type=f32
    )


def orth_turned(mats):
    count = len(mats)
    tails = []
    for a in mats:
        turned = a.T
        tails.append(jnp.concatenate([wide_dot(turned, turned, (1, 1)), turned], axis=1))
    rows = lax.broadcasted_iota(jnp.int32, (NB, 1), 0)
    eye = lax.broadcasted_iota(jnp.int32, (NB, NB), 0) == lax.broadcasted_iota(
        jnp.int32, (NB, NB), 1
    )
    outs = [[] for _ in range(count)]
    for p in range(B // NB):
        base = p * NB
        strips = [t[:NB] for t in tails]
        for kk in range(NB):
            at = base + kk
            for m in range(count):
                s = strips[m]
                pivot_row = jnp.broadcast_to(s[kk : kk + 1, :], (NB, 2 * B))
                factor = s[:, at : at + 1] * (1.0 / s[kk : kk + 1, at : at + 1])
                strips[m] = s - jnp.where(rows > kk, factor, 0.0) * pivot_row
        for m in range(count):
            s = strips[m]
            diag = jnp.sum(jnp.where(eye, s[:, base : base + NB], 0.0), axis=1, keepdims=True)
            u = s * lax.rsqrt(diag)
            outs[m].append(u[:, B:])
            if base + NB < B:
                tails[m] = tails[m][NB:] - wide_dot(u[:, base + NB : B], u, (0, 0))
    return [jnp.concatenate(o, axis=0) for o in outs]


def soap_kernel(live, grads, state, update, copy):
    count = grads.shape[0]
    mats = []
    first_slot = pl.program_id(0) * count
    gs = []
    for i in range(count):
        g = jnp.where(live[first_slot + i] > 0, grads[i].astype(f32), 0.0)
        gs.append(g)
        left = beta_stat * state[i, 3] + (1.0 - beta_stat) * wide_dot(g, g, (1, 1))
        right = beta_stat * state[i, 4] + (1.0 - beta_stat) * wide_dot(g, g, (0, 0))
        mats.append(wide_dot(left, state[i, 5], (1, 0)))
        mats.append(wide_dot(right, state[i, 6], (1, 0)))
    turned = orth_turned(mats)
    fix_one = 1.0 - beta_one**STEP
    fix_two = 1.0 - beta_two**STEP
    for i in range(count):
        tl, tr = turned[2 * i], turned[2 * i + 1]
        rotated = wide_dot(wide_dot(tl, gs[i], (1, 0)), tr, (1, 1))
        new_first = beta_one * state[i, 1] + (1.0 - beta_one) * rotated
        new_second = beta_two * state[i, 2] + (1.0 - beta_two) * rotated * rotated
        normalized = new_first / fix_one / (jnp.sqrt(new_second / fix_two) + adam_eps)
        step = wide_dot(wide_dot(tl, normalized, (0, 0)), tr, (1, 0))
        weight = state[i, 0]
        weight = weight - matrix_rate * (step + decay_rate * weight)
        update[i, 0] = weight
        update[i, 1] = new_first
        update[i, 2] = new_second
        update[i, 3] = tl.T
        update[i, 4] = tr.T
        copy[i] = weight.astype(bf16)


def soap_update(grads, state, live):
    slots = grads.shape[0]
    count = max(c for c in range(1, 10) if slots % c == 0)
    return pl.pallas_call(
        soap_kernel,
        grid_spec=pltpu.PrefetchScalarGridSpec(
            num_scalar_prefetch=1,
            grid=(slots // count,),
            in_specs=[
                pl.BlockSpec((count, B, B), lambda i, s: (i, 0, 0)),
                pl.BlockSpec((count, 7, B, B), lambda i, s: (i, 0, 0, 0)),
            ],
            out_specs=[
                pl.BlockSpec((count, 5, B, B), lambda i, s: (i, 0, 0, 0)),
                pl.BlockSpec((count, B, B), lambda i, s: (i, 0, 0)),
            ],
        ),
        out_shape=[shape((slots, 5, B, B), f32), shape((slots, B, B), bf16)],
        compiler_params=pltpu.CompilerParams(vmem_limit_bytes=LIMIT),
        name="soap",
    )(live, grads, state)


def adam_vector(grads, param, moments, step_number):
    new_first = beta_one * moments[0] + (1.0 - beta_one) * grads
    new_second = beta_two * moments[1] + (1.0 - beta_two) * grads * grads
    fix_one = 1.0 - beta_one**step_number
    fix_two = 1.0 - beta_two**step_number
    new_param = param - vector_rate * (new_first / fix_one) / (
        jnp.sqrt(new_second / fix_two) + adam_eps
    )
    return jnp.stack([grads, new_param, new_first, new_second])


def body(
    tokens,
    cotangent,
    rel_index,
    attn_owner,
    mlp_owner,
    attn_state,
    mlp_state,
    vec_param,
    vec_moments,
    rel_table,
    rel_table_moments,
    up_bias,
    up_bias_moments,
):
    both = ("dp", "mp")
    parts = lax.axis_size("mp")
    rank = lax.axis_index("dp") * parts + lax.axis_index("mp")
    imgs = tokens.shape[1] // NPOS
    attn_local = attn_state.shape[0]
    mlp_local = mlp_state.shape[1]
    attn_total = attn_local * lax.axis_size("dp") * parts

    attn_slots = lax.all_gather(attn_state[:, 0].astype(bf16), both, axis=0, tiled=True)
    mlp_slots = lax.all_gather(mlp_state[0, :, 0].astype(bf16), both, axis=0, tiled=True)

    wide_total = -(-rel_table.shape[1] // B) * B
    idx_t = jnp.pad(rel_index.T, ((0, NP - NPOS), (0, NL - NPOS)))
    table_pad = jnp.pad(rel_table, ((0, 0), (0, wide_total - rel_table.shape[1])))
    bias = table_lookup(idx_t, table_pad)

    def padded(x):
        return jnp.pad(x.reshape(imgs, NPOS, D), ((0, 0), (0, NP - NPOS), (0, 0)))

    def unpadded(x):
        return x[:, :NPOS].reshape(1, imgs * NPOS, D)

    tok = padded(tokens)
    cot = padded(cotangent)
    w, q, k, v, att, lse, mid, bra, n2 = forward_attention(
        tok, attn_slots, attn_owner, vec_param, bias
    )
    out, gmid, gbra, mlp_sums, bias_grad, mlp_grads = feed_forward(
        mid, bra, n2, cot, mlp_slots, mlp_owner, vec_param, up_bias[None], parts, mlp_local
    )
    mlp_mine = lax.psum_scatter(mlp_grads, both, scatter_dimension=0, tiled=True)
    gin, grid, attn_sums, attn_grads = backward_attention(
        tok, w, q, k, v, att, lse, bias, gmid, gbra, attn_owner, vec_param, attn_total
    )
    attn_mine = lax.psum_scatter(attn_grads, both, scatter_dimension=0, tiled=True)
    table_grad = table_accumulate(grid, idx_t, wide_total // B)
    table_grad = table_grad.transpose(1, 0, 2).reshape(16, wide_total)[:H, : rel_table.shape[1]]

    vector_grad = jnp.concatenate([attn_sums[:4], mlp_sums[:6]], axis=0)
    vector_total, table_total, bias_total = lax.psum(
        (vector_grad, table_grad, bias_grad[0]), both
    )

    def live(owner, first, count):
        mine = first + jnp.arange(count, dtype=jnp.int32)
        return jnp.any(owner[None, :] == mine[:, None], axis=1).astype(jnp.int32)

    mlp_result, mlp_copy = soap_update(
        mlp_mine,
        mlp_state[0],
        live(mlp_owner, lax.axis_index("dp") * mlp_local, mlp_local),
    )
    attn_result, attn_copy = soap_update(
        attn_mine, attn_state, live(attn_owner, rank * attn_local, attn_local)
    )
    return (
        unpadded(out),
        unpadded(gin),
        attn_result,
        attn_copy,
        mlp_result[None],
        mlp_copy[None],
        adam_vector(vector_total, vec_param, vec_moments, STEP),
        adam_vector(table_total, rel_table, rel_table_moments, STEP),
        adam_vector(bias_total, up_bias, up_bias_moments, STEP),
    )


def solution(mesh):
    placed = (
        P(("dp", "mp"), None, None),
        P(("dp", "mp"), None, None),
        P(),
        P(),
        P(),
        P(("dp", "mp"), None, None, None),
        P("mp", "dp", None, None, None),
        P(),
        P(),
        P(),
        P(),
        P(),
        P(),
    )
    return jax.shard_map(
        body,
        mesh=mesh,
        in_specs=placed,
        out_specs=(
            P(("dp", "mp"), None, None),
            P(("dp", "mp"), None, None),
            P(("dp", "mp"), None, None, None),
            P(("dp", "mp"), None, None),
            P("mp", "dp", None, None, None),
            P("mp", "dp", None, None),
            P(),
            P(),
            P(),
        ),
        check_vma=False,
    )
```

```python
from functools import partial
import math

import jax
import jax.numpy as jnp
from jax import lax
from jax.experimental import pallas as pl
from jax.experimental.pallas import tpu as pltpu
from jax.sharding import PartitionSpec as P

D = 768
H = 12
HD = 64
FF = 3072
NPOS = 197
NP = 208
NL = 256
B = 128
STEP = 5
T = D // B

f32 = jnp.float32
bf16 = jnp.bfloat16

ln_eps = 1e-06
beta_one = 0.9
beta_two = 0.95
beta_stat = 0.95
adam_eps = 1e-08
matrix_rate = 0.05
vector_rate = 0.2
decay_rate = 0.05

VMEM = pl.BlockSpec(memory_space=pltpu.VMEM)
SMEM = pl.BlockSpec(memory_space=pltpu.SMEM)
ANY = pl.BlockSpec(memory_space=pl.ANY)
LIMIT = 60 << 20


def shape(dims, kind):
    return jax.ShapeDtypeStruct(dims, kind)


def dot_nn(x, y):
    return lax.dot_general(x, y, (((1,), (0,)), ((), ())), preferred_element_type=f32)


def dot_nt(x, y):
    return lax.dot_general(x, y, (((1,), (1,)), ((), ())), preferred_element_type=f32)


def dot_tn(x, y):
    return lax.dot_general(x, y, (((0,), (0,)), ((), ())), preferred_element_type=f32)


def norm_parts(values):
    centered = values - jnp.mean(values, axis=-1, keepdims=True)
    inv_std = lax.rsqrt(jnp.mean(centered * centered, axis=-1, keepdims=True) + ln_eps)
    return (centered * inv_std, inv_std)


def norm_back(grad_normed, scaled, inv_std, gain_row):
    tangent = grad_normed * gain_row
    return inv_std * (
        tangent
        - jnp.mean(tangent, axis=-1, keepdims=True)
        - scaled * jnp.mean(tangent * scaled, axis=-1, keepdims=True)
    )


MESH = pl.DeviceIdType.MESH
COPIES = 35


def own_kernels(dp_total, parts):
    return dp_total == 16 and parts == 2


class Place:
    def __init__(self):
        dp = lax.axis_index("dp")
        self.y = lax.axis_index("mp")
        self.z = dp // 4
        self.x = lax.rem(dp // 2, 2)
        self.c = lax.rem(dp, 2)

    def rank(self, d=0, dx=0, dc=0, dy=0):
        z = lax.rem(self.z + d + 4, 4)
        x = 1 - self.x if dx else self.x
        c = 1 - self.c if dc else self.c
        y = 1 - self.y if dy else self.y
        return ((z * 2 + x) * 2 + c) * 2 + y

    def device(self, d=0, dx=0, dc=0, dy=0):
        z = lax.rem(self.z + d + 4, 4)
        x = 1 - self.x if dx else self.x
        c = 1 - self.c if dc else self.c
        y = 1 - self.y if dy else self.y
        return ((z * 2 + x) * 2 + c, y)

    def greet(self):
        barrier = pltpu.get_barrier_semaphore()
        for d, dx, dc, dy in PARTNERS:
            pl.semaphore_signal(
                barrier, inc=1, device_id=self.device(d, dx, dc, dy), device_id_type=MESH
            )
        pl.semaphore_wait(barrier, len(PARTNERS))


PARTNERS = ((1, 0, 0, 0), (2, 0, 0, 0), (3, 0, 0, 0), (0, 1, 0, 0), (0, 0, 1, 0), (0, 0, 0, 1))


class Copies:
    def __init__(self, place, send, recv):
        self.place = place
        self.send = send
        self.recv = recv
        self.made = {}

    def start(self, key, src, dst, **to):
        i = len(self.made)
        copy = pltpu.make_async_remote_copy(
            src_ref=src,
            dst_ref=dst,
            send_sem=self.send.at[i],
            recv_sem=self.recv.at[i],
            device_id=self.place.device(**to),
            device_id_type=MESH,
        )
        copy.start()
        self.made[key] = copy

    def arrived(self, key):
        self.made[key].wait_recv()

    def sent(self):
        for copy in self.made.values():
            copy.wait_send()


class Gather(Copies):
    def __init__(self, place, own, full, n, send, recv, local):
        super().__init__(place, send, recv)
        self.own = own
        self.full = full
        self.n = n
        self.half = n // 2
        self.local = pltpu.make_async_copy(own, self.at(), local)

    def at(self, d=0, dx=0, dc=0, dy=0, lo=0, hi=None):
        hi = self.n if hi is None else hi
        return self.full.at[pl.ds(self.place.rank(d, dx, dc, dy) * self.n + lo, hi - lo)]

    def spread(self, d):
        src = self.own if d == 0 else self.at(d=-d)
        dst = self.at(d=-d)
        self.start(("x", d), src, dst, dx=1)
        self.start(("y", d), src, dst, dy=1)
        self.start(("c", d, 0, 0), src, dst, dc=1)

    def along(self, d):
        self.start(("z", d), self.own, self.at(), d=d)

    def share(self, d, dx, dy):
        ref = self.at(d=-d, dx=dx, dy=dy)
        self.start(("c", d, dx, dy), ref, ref, dc=1)

    def corner(self, d):
        ref = self.at(d=-d, dy=1, lo=self.half)
        self.start(("xd", d), ref, ref, dx=1)
        ref = self.at(d=-d, dx=1, hi=self.half)
        self.start(("yd", d), ref, ref, dy=1)

    def sides(self, d):
        self.arrived(("x", d))
        self.share(d, 1, 0)
        self.arrived(("y", d))
        self.share(d, 0, 1)

    def cornered(self, d):
        self.arrived(("xd", d))
        self.arrived(("yd", d))
        self.share(d, 1, 1)

    def step(self, i):
        if i == 0:
            self.local.start()
            self.along(1)
            self.spread(0)
        elif i == 1:
            self.arrived(("z", 1))
            self.along(3)
            self.spread(1)
            self.sides(0)
        elif i == 2:
            self.arrived(("z", 3))
            self.along(2)
            self.spread(3)
            self.sides(1)
            self.corner(0)
        elif i == 3:
            self.corner(1)
            self.sides(3)
        elif i == 4:
            self.arrived(("z", 2))
            self.spread(2)
            self.cornered(0)
            self.corner(3)
            self.cornered(1)
        elif i == 5:
            self.sides(2)
            self.corner(2)
            self.cornered(3)
        else:
            self.cornered(2)
            for d in range(4):
                for dx in range(2):
                    for dy in range(2):
                        self.arrived(("c", d, dx, dy))
            self.local.wait()
            self.sent()


GATHER_STEPS = 7


class Scatter(Copies):
    def __init__(self, place, full, n, acc, peer, side, corner, along, send, recv):
        super().__init__(place, send, recv)
        self.full = full
        self.n = n
        self.half = n // 2
        self.acc = acc
        self.peer = peer
        self.side = side
        self.cor = corner
        self.col = along

    def block(self, d, dx, dc, dy):
        return pl.ds(self.place.rank(d, dx, dc, dy) * self.n, self.n)

    def core(self, d):
        for dx in range(2):
            for dy in range(2):
                self.start(
                    ("c", d, dx, dy),
                    self.full.at[self.block(d, dx, 1, dy)],
                    self.peer.at[d, dx, dy],
                    dc=1,
                )

    def pair(self, d, dx, dy):
        self.arrived(("c", d, dx, dy))
        n = self.n

        @pl.loop(0, n)
        def _(i):
            mine = self.full[self.place.rank(d, dx, 0, dy) * n + i].astype(f32)
            self.acc[d, dx, dy, i] = (mine + self.peer[d, dx, dy, i].astype(f32)).astype(bf16)

    def add(self, d, dx, dy, other, lo, hi):
        @pl.loop(lo, hi)
        def _(i):
            total = self.acc[d, dx, dy, i].astype(f32) + other[i - lo].astype(f32)
            self.acc[d, dx, dy, i] = total.astype(bf16)

    def corner(self, d):
        self.pair(d, 1, 1)
        h, n = self.half, self.n
        self.start(("xd", d), self.acc.at[d, 1, 1, pl.ds(0, h)], self.cor.at[d, pl.ds(0, h)], dx=1)
        self.start(
            ("yd", d), self.acc.at[d, 1, 1, pl.ds(h, n - h)], self.cor.at[d, pl.ds(h, n - h)], dy=1
        )
        self.pair(d, 1, 0)
        self.pair(d, 0, 1)
        self.pair(d, 0, 0)

    def sides(self, d):
        h, n = self.half, self.n
        self.arrived(("yd", d))
        self.add(d, 1, 0, self.cor.at[d, pl.ds(h, n - h)], h, n)
        self.start(("x", d), self.acc.at[d, 1, 0], self.side.at[d, 0], dx=1)
        self.arrived(("xd", d))
        self.add(d, 0, 1, self.cor.at[d, pl.ds(0, h)], 0, h)
        self.start(("y", d), self.acc.at[d, 0, 1], self.side.at[d, 1], dy=1)

    def along(self, d):
        self.arrived(("x", d))
        self.arrived(("y", d))

        @pl.loop(0, self.n)
        def _(i):
            total = (
                self.acc[d, 0, 0, i].astype(f32)
                + self.side[d, 0, i].astype(f32)
                + self.side[d, 1, i].astype(f32)
            )
            self.acc[d, 0, 0, i] = total.astype(bf16)

        if d > 0:
            self.start(("z", d), self.acc.at[d, 0, 0], self.col.at[d - 1], d=d)

    def step(self, i, out=None):
        if i == 0:
            for d in (2, 3, 0, 1):
                self.core(d)
            self.corner(2)
            self.corner(3)
        elif i == 1:
            self.sides(2)
            self.corner(0)
        elif i == 2:
            self.along(2)
            self.corner(1)
            self.sides(3)
        elif i == 3:
            self.along(3)
            self.sides(1)
        elif i == 4:
            self.along(1)
            self.sides(0)
        else:
            self.along(0)
            for d in (1, 2, 3):
                self.arrived(("z", d))

            @pl.loop(0, self.n)
            def _(i):
                out[i] = (
                    (self.acc[0, 0, 0, i].astype(f32) + self.col[0, i].astype(f32))
                    + self.col[1, i].astype(f32)
                ) + self.col[2, i].astype(f32)

            self.sent()


SCATTER_STEPS = 6


def scatter_scratch(n):
    return [
        pltpu.VMEM((4, 2, 2, n, B, B), bf16),
        pltpu.VMEM((4, 2, 2, n, B, B), bf16),
        pltpu.VMEM((4, 2, n, B, B), bf16),
        pltpu.VMEM((4, n, B, B), bf16),
        pltpu.VMEM((3, n, B, B), bf16),
        pltpu.SemaphoreType.DMA((COPIES,)),
        pltpu.SemaphoreType.DMA((COPIES,)),
    ]


def gather_kernel(n, own, full, send, recv, local):
    place = Place()
    place.greet()
    moves = Gather(place, own, full, n, send, recv, local)
    for i in range(GATHER_STEPS):
        moves.step(i)


def gather_blocks(own, cid):
    n = own.shape[0]
    return pl.pallas_call(
        partial(gather_kernel, n),
        in_specs=[VMEM],
        out_specs=VMEM,
        out_shape=shape((32 * n, B, B), bf16),
        scratch_shapes=[
            pltpu.SemaphoreType.DMA((COPIES,)),
            pltpu.SemaphoreType.DMA((COPIES,)),
            pltpu.SemaphoreType.DMA(()),
        ],
        compiler_params=pltpu.CompilerParams(
            collective_id=cid, has_side_effects=True, vmem_limit_bytes=LIMIT
        ),
        name=f"gather{cid}",
    )(own)


def scatter_kernel(n, full, out, acc, peer, side, corner, along, send, recv):
    place = Place()
    place.greet()
    moves = Scatter(place, full, n, acc, peer, side, corner, along, send, recv)
    for i in range(SCATTER_STEPS):
        moves.step(i, out)


def scatter_blocks(full, cid):
    n = full.shape[0] // 32
    return pl.pallas_call(
        partial(scatter_kernel, n),
        in_specs=[VMEM],
        out_specs=VMEM,
        out_shape=shape((n, B, B), f32),
        scratch_shapes=scatter_scratch(n),
        compiler_params=pltpu.CompilerParams(
            collective_id=cid, has_side_effects=True, vmem_limit_bytes=LIMIT
        ),
        name=f"scatter{cid}",
    )(full)


def lookup_kernel(idx_ref, table_ref, out_ref, spread):
    chunks = table_ref.shape[1] // B
    for h in range(H):
        for c in range(chunks):
            spread[h, c] = jnp.broadcast_to(table_ref[h : h + 1, c * B : (c + 1) * B], (8, B))

    @pl.loop(0, NP // 8)
    def _(jt):
        rows = pl.ds(pl.multiple_of(jt * 8, 8), 8)
        real = jt * 8 + lax.broadcasted_iota(jnp.int32, (8, B), 0) < NPOS
        for half in range(NL // B):
            lanes = slice(half * B, (half + 1) * B)
            idx = idx_ref[rows, lanes]
            low = jnp.bitwise_and(idx, B - 1)
            high = jnp.right_shift(idx, 7)
            for h in range(H):
                acc = jnp.take_along_axis(spread[h, 0], low, axis=1, mode="promise_in_bounds")
                for c in range(1, chunks):
                    part = jnp.take_along_axis(spread[h, c], low, axis=1, mode="promise_in_bounds")
                    acc = jnp.where(high == c, part, acc)
                out_ref[h, rows, lanes] = jnp.where(real, acc, -1e30)


def table_lookup(idx_t, table_pad):
    return pl.pallas_call(
        lookup_kernel,
        in_specs=[VMEM, VMEM],
        out_specs=VMEM,
        out_shape=shape((H, NP, NL), f32),
        scratch_shapes=[pltpu.VMEM((H, table_pad.shape[1] // B, 8, B), f32)],
        compiler_params=pltpu.CompilerParams(vmem_limit_bytes=LIMIT),
        name="table_lookup",
    )(idx_t, table_pad)


def accumulate_kernel(grid_ref, idx_ref, out_ref):
    chunks = out_ref.shape[0]
    out_ref[...] = jnp.zeros_like(out_ref)
    lo_rows = lax.broadcasted_iota(jnp.int32, (B, NL), 0)

    @pl.loop(0, NPOS)
    def _(j):
        values = grid_ref[:, j, :]
        values = jnp.concatenate([values, jnp.zeros((4, NL), f32)], axis=0)
        idx = idx_ref[pl.ds(j, 1), :]
        low = jnp.bitwise_and(idx, B - 1)
        high = jnp.right_shift(idx, 7)
        onehot = jnp.where(lo_rows == low, 1.0, 0.0).astype(bf16)
        first = values.astype(bf16)
        second = (values - first.astype(f32)).astype(bf16)
        rows = []
        for c in range(chunks):
            rows.append(jnp.where(high == c, values, 0.0))
        stacked = jnp.concatenate(rows, axis=0)
        first = stacked.astype(bf16)
        second = (stacked - first.astype(f32)).astype(bf16)
        got = dot_nt(jnp.concatenate([first, second], axis=0), onehot)
        for c in range(chunks):
            base = c * 16
            out_ref[c] += got[base : base + 16] + got[chunks * 16 + base : chunks * 16 + base + 16]


def table_accumulate(grid_t, idx_t, chunks):
    return pl.pallas_call(
        accumulate_kernel,
        in_specs=[VMEM, VMEM],
        out_specs=VMEM,
        out_shape=shape((chunks, 16, B), f32),
        compiler_params=pltpu.CompilerParams(vmem_limit_bytes=LIMIT),
        name="table_accumulate",
    )(grid_t, idx_t)


def attn_tile(weights, b):
    m = b // (T * T)
    r = lax.rem(b // T, T)
    c = lax.rem(b, T)
    return weights.at[
        m, pl.ds(pl.multiple_of(r * B, B), B), pl.ds(pl.multiple_of(c * B, B), B)
    ]


def pad_rows(x):
    return jnp.concatenate([x, jnp.zeros((NL - NP, x.shape[1]), x.dtype)], axis=0)


def forward_kernel(
    own, tok, slots, vec, bias, w, q, k, v, att, lse, mid, bra, n2, n1, sem
):
    imgs = q.shape[0]

    @pl.loop(0, own.shape[0])
    def _(b):
        pltpu.make_async_copy(slots.at[own[b]], attn_tile(w, b), sem).start()

    for img in range(imgs):
        x, _ = norm_parts(tok[img].astype(f32))
        n1[img * NP : (img + 1) * NP] = (x * vec[0:1] + vec[1:2]).astype(bf16)
    pltpu.make_async_copy(w, w, sem).wait()

    for m, (out, row, scale) in enumerate(((q, 2, HD**-0.5), (k, None, 1.0), (v, 3, 1.0))):
        for n in range(D // NL):
            lanes = slice(n * NL, (n + 1) * NL)
            part = dot_nn(n1[...], w[m, :, lanes])
            if row is not None:
                part = part + vec[row : row + 1, lanes]
            part = part.astype(bf16)
            if scale != 1.0:
                part = part * jnp.asarray(scale, bf16)
            for img in range(imgs):
                out[img, :, lanes] = part[img * NP : (img + 1) * NP]

    @pl.loop(0, imgs)
    def _(img):
        side = lax.broadcasted_iota(jnp.int32, (1, B), 1) // HD
        for pair in range(H // 2):
            lanes = slice(pair * B, (pair + 1) * B)
            k_pair = k[img, :, lanes]
            q_pair = pad_rows(q[img, :, lanes])
            v_turn = v[img, :, lanes].astype(f32).T.astype(bf16)
            mixed = []
            for sub in range(2):
                h = pair * 2 + sub
                q_one = jnp.where(side == sub, q_pair, jnp.zeros_like(q_pair))
                s = dot_nt(k_pair, q_one) + bias[h]
                top = jnp.max(s, axis=0, keepdims=True)
                e = jnp.exp(s - top)
                total = jnp.sum(e, axis=0, keepdims=True)
                o = dot_nn(v_turn[sub * HD : (sub + 1) * HD], e.astype(bf16))
                mixed.append(o * (1.0 / total))
                lse[img, h : h + 1] = top + jnp.log(total)
            both = jnp.concatenate(mixed, axis=0).T
            att[img, :, lanes] = both[:NP].astype(bf16)

    @pl.loop(0, imgs)
    def _(img):
        branch = dot_nn(att[img], w[3]) + vec[4:5]
        bra[img] = branch
        middle = tok[img].astype(f32) + vec[5:6] * branch
        mid[img] = middle
        x, _ = norm_parts(middle)
        n2[img] = (x * vec[6:7] + vec[7:8]).astype(bf16)


def forward_attention(tok, slots, own, vec, bias):
    imgs = tok.shape[0]
    big = shape((imgs, NP, D), bf16)
    wide = shape((imgs, NP, D), f32)
    return pl.pallas_call(
        forward_kernel,
        in_specs=[SMEM, VMEM, ANY, VMEM, VMEM],
        out_specs=[VMEM] * 9,
        out_shape=[
            shape((4, D, D), bf16),
            big,
            big,
            big,
            big,
            shape((imgs, H, NL), f32),
            wide,
            wide,
            big,
        ],
        scratch_shapes=[pltpu.VMEM((imgs * NP, D), bf16), pltpu.SemaphoreType.DMA(())],
        compiler_params=pltpu.CompilerParams(vmem_limit_bytes=LIMIT),
        name="forward_attention",
    )(own, tok, slots, vec, bias)


CH = 512


def mlp_kernel(
    parts,
    each,
    own,
    mid,
    bra,
    n2,
    cot,
    slots,
    vec,
    upb,
    out,
    gmid,
    gbra,
    sums,
    bgrad,
    tiles_out,
    w1,
    w2,
    gs,
    act,
    gh,
    summed,
    gn2,
    tiles,
    sem_in,
    sem_out,
):
    imgs = mid.shape[0]
    rows = imgs * NP
    chunks = FF // CH
    per = CH // B
    half = own.shape[0] // 2
    total = parts * half
    local = half // T

    def place(slot, p):
        return (slot // each) * (parts * each) + p * each + lax.rem(slot, each)

    @pl.loop(0, total)
    def _(b):
        p = b // half
        rest = lax.rem(b, half)
        r = rest // local
        c = p * local + lax.rem(rest, local)
        pltpu.make_async_copy(
            slots.at[place(own[rest], p)],
            w1.at[
                c // per,
                pl.ds(pl.multiple_of(r * B, B), B),
                pl.ds(pl.multiple_of(lax.rem(c, per) * B, B), B),
            ],
            sem_in,
        ).start()
        r2 = p * local + rest // T
        c2 = lax.rem(rest, T)
        pltpu.make_async_copy(
            slots.at[place(own[half + rest], p)],
            w2.at[pl.ds(pl.multiple_of(r2 * B, B), B), pl.ds(pl.multiple_of(c2 * B, B), B)],
            sem_in,
        ).start()

    for img in range(imgs):
        gs[img * NP : (img + 1) * NP] = (vec[9:10] * cot[img]).astype(bf16)
    summed[...] = jnp.zeros_like(summed)
    gn2[...] = jnp.zeros_like(gn2)
    pltpu.make_async_copy(w1, w1, sem_in).wait()
    pltpu.make_async_copy(w2, w2, sem_in).wait()

    @pl.loop(0, chunks)
    def _(c):
        span = pl.ds(pl.multiple_of(c * CH, CH), CH)
        bias_sum = jnp.zeros((1, CH), f32)
        for rb in range(imgs // 2):
            block = slice(rb * 2 * NP, (rb + 1) * 2 * NP)
            hid = dot_nn(n2[block], w1[c]) + upb[:, span]
            back = dot_nt(gs[block], w2[span])
            phi = 0.5 * (1.0 + lax.erf(hid * (1.0 / math.sqrt(2.0))))
            density = jnp.exp(-0.5 * hid * hid) * (1.0 / math.sqrt(2.0 * math.pi))
            a = (hid * phi).astype(bf16)
            g = (back * (phi + hid * density)).astype(bf16)
            act[block] = a
            gh[block] = g
            bias_sum = bias_sum + jnp.sum(g.astype(f32), axis=0, keepdims=True)
            summed[block] += dot_nn(a, w2[span])
            gn2[block] += dot_nt(g, w1[c])
        bgrad[:, span] = bias_sum
        up_grad = dot_tn(n2[...], gh[...])
        down_grad = dot_tn(act[...], gs[...])
        for r in range(T):
            for cc in range(per):
                tiles[c, r * per + cc] = up_grad[
                    r * B : (r + 1) * B, cc * B : (cc + 1) * B
                ].astype(bf16)
        for r in range(per):
            for cc in range(T):
                tiles[c, T * per + r * T + cc] = down_grad[
                    r * B : (r + 1) * B, cc * B : (cc + 1) * B
                ].astype(bf16)

        @pl.loop(0, T * per)
        def _(t):
            r = t // per
            g = c * per + lax.rem(t, per)
            p = g // local
            b = r * local + lax.rem(g, local)
            pltpu.make_async_copy(
                tiles.at[c, t], tiles_out.at[place(own[b], p)], sem_out
            ).start()
            g2 = c * per + t // T
            p2 = g2 // local
            b2 = half + lax.rem(g2, local) * T + lax.rem(t, T)
            pltpu.make_async_copy(
                tiles.at[c, T * per + t], tiles_out.at[place(own[b2], p2)], sem_out
            ).start()

    s4 = jnp.zeros((1, D), f32)
    s5 = jnp.zeros((1, D), f32)
    s6 = jnp.zeros((1, D), f32)
    s7 = jnp.zeros((1, D), f32)
    s8 = jnp.zeros((1, D), f32)
    s9 = jnp.zeros((1, D), f32)
    for img in range(imgs):
        block = slice(img * NP, (img + 1) * NP)
        up = cot[img]
        middle = mid[img]
        sm = summed[block] + vec[8:9]
        out[img] = (middle + vec[9:10] * sm).astype(bf16)
        s9 += jnp.sum(up * sm, axis=0, keepdims=True)
        s8 += jnp.sum(gs[block].astype(f32), axis=0, keepdims=True)
        x, inv = norm_parts(middle)
        gn = gn2[block]
        s6 += jnp.sum(gn * x, axis=0, keepdims=True)
        s7 += jnp.sum(gn, axis=0, keepdims=True)
        gm = up + norm_back(gn, x, inv, vec[6:7])
        gmid[img] = gm
        gb = (vec[5:6] * gm).astype(bf16)
        gbra[img] = gb
        s4 += jnp.sum(gb.astype(f32), axis=0, keepdims=True)
        s5 += jnp.sum(gm * bra[img], axis=0, keepdims=True)
    sums[...] = jnp.concatenate([s4, s5, s6, s7, s8, s9, s9, s9], axis=0)
    pltpu.make_async_copy(tiles, tiles, sem_out).wait()


def feed_forward(mid, bra, n2, cot, slots, own, vec, up_bias, parts, each):
    imgs = mid.shape[0]
    rows = imgs * NP
    chunks = FF // CH
    per = CH // B
    return pl.pallas_call(
        partial(mlp_kernel, parts, each),
        in_specs=[SMEM, VMEM, VMEM, VMEM, VMEM, ANY, VMEM, VMEM],
        out_specs=[VMEM] * 5 + [ANY],
        out_shape=[
            shape((imgs, NP, D), bf16),
            shape((imgs, NP, D), f32),
            shape((imgs, NP, D), bf16),
            shape((8, D), f32),
            shape((1, FF), f32),
            shape(slots.shape, bf16),
        ],
        scratch_shapes=[
            pltpu.VMEM((chunks, D, CH), bf16),
            pltpu.VMEM((FF, D), bf16),
            pltpu.VMEM((rows, D), bf16),
            pltpu.VMEM((rows, CH), bf16),
            pltpu.VMEM((rows, CH), bf16),
            pltpu.VMEM((rows, D), f32),
            pltpu.VMEM((rows, D), f32),
            pltpu.VMEM((chunks, 2 * T * per, B, B), bf16),
            pltpu.SemaphoreType.DMA(()),
            pltpu.SemaphoreType.DMA(()),
        ],
        compiler_params=pltpu.CompilerParams(vmem_limit_bytes=LIMIT),
        name="feed_forward",
    )(own, mid, bra, n2.reshape(rows, D), cot, slots, vec, up_bias)


def backward_kernel(
    own,
    tok,
    w,
    q,
    k,
    v,
    att,
    lse,
    bias,
    gmid,
    gbra,
    vec,
    gin,
    grid,
    sums,
    tiles_out,
    n1,
    gatt,
    gqkv,
    tiles,
    sem,
):
    imgs = q.shape[0]
    for img in range(imgs):
        x, _ = norm_parts(tok[img].astype(f32))
        n1[img * NP : (img + 1) * NP] = (x * vec[0:1] + vec[1:2]).astype(bf16)
    for n in range(D // NL):
        lanes = slice(n * NL, (n + 1) * NL)
        got = dot_nt(gbra[...], w[3, lanes, :]).astype(bf16)
        for img in range(imgs):
            gatt[img, :, lanes] = got[img * NP : (img + 1) * NP]
    grid[...] = jnp.zeros_like(grid)

    @pl.loop(0, imgs)
    def _(img):
        side = lax.broadcasted_iota(jnp.int32, (1, B), 1) // HD
        here = pl.ds(pl.multiple_of(img * NP, 16), NP)
        for pair in range(H // 2):
            lanes = slice(pair * B, (pair + 1) * B)
            k_pair = k[img, :, lanes]
            v_pair = v[img, :, lanes]
            q_pair = pad_rows(q[img, :, lanes])
            g_pair = pad_rows(gatt[img, :, lanes])
            k_turn = k_pair.astype(f32).T.astype(bf16)
            gq = []
            gk = jnp.zeros((NP, B), f32)
            gv = jnp.zeros((NP, B), f32)
            for sub in range(2):
                h = pair * 2 + sub
                q_one = jnp.where(side == sub, q_pair, jnp.zeros_like(q_pair))
                g_one = jnp.where(side == sub, g_pair, jnp.zeros_like(g_pair))
                s = dot_nt(k_pair, q_one) + bias[h]
                p = jnp.exp(s - lse[img, h : h + 1])
                dp = dot_nt(v_pair, g_one)
                gv = gv + dot_nn(p.astype(bf16), g_one)
                inner = jnp.sum(p * dp, axis=0, keepdims=True)
                ds = (p * (dp - inner)).astype(bf16)
                gk = gk + dot_nn(ds, q_one)
                gq.append(dot_nn(k_turn[sub * HD : (sub + 1) * HD], ds))
                grid[h] += ds.astype(f32)
            turned = jnp.concatenate(gq, axis=0).T
            gqkv[here, lanes] = (turned[:NP] * HD**-0.5).astype(bf16)
            gqkv[here, D + pair * B : D + (pair + 1) * B] = gk.astype(bf16)
            gqkv[here, 2 * D + pair * B : 2 * D + (pair + 1) * B] = gv.astype(bf16)

    def put(m, n, grad):
        for r in range(T):
            for cc in range(NL // B):
                tiles[m * T * T + r * T + n * (NL // B) + cc] = grad[
                    r * B : (r + 1) * B, cc * B : (cc + 1) * B
                ].astype(bf16)

    for n in range(D // NL):
        lanes = slice(n * NL, (n + 1) * NL)
        put(3, n, dot_tn(att[...], gbra[:, lanes]))
    for m in range(3):
        for n in range(D // NL):
            put(m, n, dot_tn(n1[...], gqkv[:, m * D + n * NL : m * D + (n + 1) * NL]))

    @pl.loop(0, own.shape[0])
    def _(b):
        pltpu.make_async_copy(tiles.at[b], tiles_out.at[own[b]], sem).start()

    s0 = jnp.zeros((1, D), f32)
    s1 = jnp.zeros((1, D), f32)
    s2 = jnp.zeros((1, D), f32)
    s3 = jnp.zeros((1, D), f32)
    for img in range(imgs):
        here = slice(img * NP, (img + 1) * NP)
        gq = gqkv[here, 0:D]
        gk = gqkv[here, D : 2 * D]
        gv = gqkv[here, 2 * D : 3 * D]
        gn = dot_nt(gq, w[0]) + dot_nt(gk, w[1]) + dot_nt(gv, w[2])
        x, inv = norm_parts(tok[img].astype(f32))
        s0 += jnp.sum(gn * x, axis=0, keepdims=True)
        s1 += jnp.sum(gn, axis=0, keepdims=True)
        s2 += jnp.sum(gq.astype(f32), axis=0, keepdims=True)
        s3 += jnp.sum(gv.astype(f32), axis=0, keepdims=True)
        gin[img] = gmid[img] + norm_back(gn, x, inv, vec[0:1])
    sums[...] = jnp.concatenate([s0, s1, s2, s3, s3, s3, s3, s3], axis=0)
    pltpu.make_async_copy(tiles, tiles, sem).wait()


def backward_attention(tok, w, q, k, v, att, lse, bias, gmid, gbra, own, vec, slot_total):
    imgs = tok.shape[0]
    rows = imgs * NP
    return pl.pallas_call(
        backward_kernel,
        in_specs=[SMEM] + [VMEM] * 11,
        out_specs=[VMEM] * 3 + [ANY],
        out_shape=[
            shape((imgs, NP, D), f32),
            shape((H, NP, NL), f32),
            shape((8, D), f32),
            shape((slot_total, B, B), bf16),
        ],
        scratch_shapes=[
            pltpu.VMEM((rows, D), bf16),
            pltpu.VMEM((imgs, NP, D), bf16),
            pltpu.VMEM((rows, 3 * D), bf16),
            pltpu.VMEM((4 * T * T, B, B), bf16),
            pltpu.SemaphoreType.DMA(()),
        ],
        compiler_params=pltpu.CompilerParams(vmem_limit_bytes=LIMIT),
        name="backward_attention",
    )(
        own,
        tok,
        w,
        q,
        k,
        v,
        att.reshape(rows, D),
        lse,
        bias,
        gmid,
        gbra.reshape(rows, D),
        vec,
    )


NB = 16


def split_two(x):
    first = x.astype(bf16)
    return first, (x - first.astype(f32)).astype(bf16)


def wide_dot(x, y, dims):
    xa, xb = split_two(x)
    ya, yb = split_two(y)
    xs = jnp.concatenate([xa, xa, xb], axis=dims[0])
    ys = jnp.concatenate([ya, yb, ya], axis=dims[1])
    return lax.dot_general(
        xs, ys, (((dims[0],), (dims[1],)), ((), ())), preferred_element_type=f32
    )


def orth_turned(mats):
    count = len(mats)
    tails = []
    for a in mats:
        turned = a.T
        tails.append(jnp.concatenate([wide_dot(turned, turned, (1, 1)), turned], axis=1))
    rows = lax.broadcasted_iota(jnp.int32, (NB, 1), 0)
    eye = lax.broadcasted_iota(jnp.int32, (NB, NB), 0) == lax.broadcasted_iota(
        jnp.int32, (NB, NB), 1
    )
    outs = [[] for _ in range(count)]
    for p in range(B // NB):
        base = p * NB
        strips = [t[:NB] for t in tails]
        for kk in range(NB):
            at = base + kk
            for m in range(count):
                s = strips[m]
                pivot_row = jnp.broadcast_to(s[kk : kk + 1, :], (NB, 2 * B))
                factor = s[:, at : at + 1] * (1.0 / s[kk : kk + 1, at : at + 1])
                strips[m] = s - jnp.where(rows > kk, factor, 0.0) * pivot_row
        for m in range(count):
            s = strips[m]
            diag = jnp.sum(jnp.where(eye, s[:, base : base + NB], 0.0), axis=1, keepdims=True)
            u = s * lax.rsqrt(diag)
            outs[m].append(u[:, B:])
            if base + NB < B:
                tails[m] = tails[m][NB:] - wide_dot(u[:, base + NB : B], u, (0, 0))
    return [jnp.concatenate(o, axis=0) for o in outs]


def soap_kernel(live, grads, state, update, copy):
    count = grads.shape[0]
    mats = []
    first_slot = pl.program_id(0) * count
    gs = []
    for i in range(count):
        g = jnp.where(live[first_slot + i] > 0, grads[i].astype(f32), 0.0)
        gs.append(g)
        left = beta_stat * state[i, 3] + (1.0 - beta_stat) * wide_dot(g, g, (1, 1))
        right = beta_stat * state[i, 4] + (1.0 - beta_stat) * wide_dot(g, g, (0, 0))
        mats.append(wide_dot(left, state[i, 5], (1, 0)))
        mats.append(wide_dot(right, state[i, 6], (1, 0)))
    turned = orth_turned(mats)
    fix_one = 1.0 - beta_one**STEP
    fix_two = 1.0 - beta_two**STEP
    for i in range(count):
        tl, tr = turned[2 * i], turned[2 * i + 1]
        rotated = wide_dot(wide_dot(tl, gs[i], (1, 0)), tr, (1, 1))
        new_first = beta_one * state[i, 1] + (1.0 - beta_one) * rotated
        new_second = beta_two * state[i, 2] + (1.0 - beta_two) * rotated * rotated
        normalized = new_first / fix_one / (jnp.sqrt(new_second / fix_two) + adam_eps)
        step = wide_dot(wide_dot(tl, normalized, (0, 0)), tr, (1, 0))
        weight = state[i, 0]
        weight = weight - matrix_rate * (step + decay_rate * weight)
        update[i, 0] = weight
        update[i, 1] = new_first
        update[i, 2] = new_second
        update[i, 3] = tl.T
        update[i, 4] = tr.T
        copy[i] = weight.astype(bf16)


def soap_update(grads, state, live):
    slots = grads.shape[0]
    count = max(c for c in range(1, 10) if slots % c == 0)
    return pl.pallas_call(
        soap_kernel,
        grid_spec=pltpu.PrefetchScalarGridSpec(
            num_scalar_prefetch=1,
            grid=(slots // count,),
            in_specs=[
                pl.BlockSpec((count, B, B), lambda i, s: (i, 0, 0)),
                pl.BlockSpec((count, 7, B, B), lambda i, s: (i, 0, 0, 0)),
            ],
            out_specs=[
                pl.BlockSpec((count, 5, B, B), lambda i, s: (i, 0, 0, 0)),
                pl.BlockSpec((count, B, B), lambda i, s: (i, 0, 0)),
            ],
        ),
        out_shape=[shape((slots, 5, B, B), f32), shape((slots, B, B), bf16)],
        compiler_params=pltpu.CompilerParams(vmem_limit_bytes=LIMIT),
        name="soap",
    )(live, grads, state)


def adam_vector(grads, param, moments, step_number):
    new_first = beta_one * moments[0] + (1.0 - beta_one) * grads
    new_second = beta_two * moments[1] + (1.0 - beta_two) * grads * grads
    fix_one = 1.0 - beta_one**step_number
    fix_two = 1.0 - beta_two**step_number
    new_param = param - vector_rate * (new_first / fix_one) / (
        jnp.sqrt(new_second / fix_two) + adam_eps
    )
    return jnp.stack([grads, new_param, new_first, new_second])


def body(
    tokens,
    cotangent,
    rel_index,
    attn_owner,
    mlp_owner,
    attn_state,
    mlp_state,
    vec_param,
    vec_moments,
    rel_table,
    rel_table_moments,
    up_bias,
    up_bias_moments,
):
    both = ("dp", "mp")
    parts = lax.axis_size("mp")
    rank = lax.axis_index("dp") * parts + lax.axis_index("mp")
    imgs = tokens.shape[1] // NPOS
    attn_local = attn_state.shape[0]
    mlp_local = mlp_state.shape[1]
    attn_total = attn_local * lax.axis_size("dp") * parts

    mine = own_kernels(lax.axis_size("dp"), parts)

    def gathered(own, cid):
        if mine:
            return gather_blocks(own, cid)
        return lax.all_gather(own, both, axis=0, tiled=True)

    def scattered(full, cid):
        if mine:
            return scatter_blocks(full, cid)
        return lax.psum_scatter(full, both, scatter_dimension=0, tiled=True)

    attn_slots = gathered(attn_state[:, 0].astype(bf16), 0)
    mlp_slots = gathered(mlp_state[0, :, 0].astype(bf16), 1)

    wide_total = -(-rel_table.shape[1] // B) * B
    idx_t = jnp.pad(rel_index.T, ((0, NP - NPOS), (0, NL - NPOS)))
    table_pad = jnp.pad(rel_table, ((0, 0), (0, wide_total - rel_table.shape[1])))
    bias = table_lookup(idx_t, table_pad)

    def padded(x):
        return jnp.pad(x.reshape(imgs, NPOS, D), ((0, 0), (0, NP - NPOS), (0, 0)))

    def unpadded(x):
        return x[:, :NPOS].reshape(1, imgs * NPOS, D)

    tok = padded(tokens)
    cot = padded(cotangent)
    w, q, k, v, att, lse, mid, bra, n2 = forward_attention(
        tok, attn_slots, attn_owner, vec_param, bias
    )
    out, gmid, gbra, mlp_sums, bias_grad, mlp_grads = feed_forward(
        mid, bra, n2, cot, mlp_slots, mlp_owner, vec_param, up_bias[None], parts, mlp_local
    )
    mlp_mine = scattered(mlp_grads, 2)
    gin, grid, attn_sums, attn_grads = backward_attention(
        tok, w, q, k, v, att, lse, bias, gmid, gbra, attn_owner, vec_param, attn_total
    )
    attn_mine = scattered(attn_grads, 3)
    table_grad = table_accumulate(grid, idx_t, wide_total // B)
    table_grad = table_grad.transpose(1, 0, 2).reshape(16, wide_total)[:H, : rel_table.shape[1]]

    vector_grad = jnp.concatenate([attn_sums[:4], mlp_sums[:6]], axis=0)
    vector_total, table_total, bias_total = lax.psum(
        (vector_grad, table_grad, bias_grad[0]), both
    )

    def live(owner, first, count):
        mine = first + jnp.arange(count, dtype=jnp.int32)
        return jnp.any(owner[None, :] == mine[:, None], axis=1).astype(jnp.int32)

    mlp_result, mlp_copy = soap_update(
        mlp_mine,
        mlp_state[0],
        live(mlp_owner, lax.axis_index("dp") * mlp_local, mlp_local),
    )
    attn_result, attn_copy = soap_update(
        attn_mine, attn_state, live(attn_owner, rank * attn_local, attn_local)
    )
    return (
        unpadded(out),
        unpadded(gin),
        attn_result,
        attn_copy,
        mlp_result[None],
        mlp_copy[None],
        adam_vector(vector_total, vec_param, vec_moments, STEP),
        adam_vector(table_total, rel_table, rel_table_moments, STEP),
        adam_vector(bias_total, up_bias, up_bias_moments, STEP),
    )


def solution(mesh):
    placed = (
        P(("dp", "mp"), None, None),
        P(("dp", "mp"), None, None),
        P(),
        P(),
        P(),
        P(("dp", "mp"), None, None, None),
        P("mp", "dp", None, None, None),
        P(),
        P(),
        P(),
        P(),
        P(),
        P(),
    )
    return jax.shard_map(
        body,
        mesh=mesh,
        in_specs=placed,
        out_specs=(
            P(("dp", "mp"), None, None),
            P(("dp", "mp"), None, None),
            P(("dp", "mp"), None, None, None),
            P(("dp", "mp"), None, None),
            P("mp", "dp", None, None, None),
            P("mp", "dp", None, None),
            P(),
            P(),
            P(),
        ),
        check_vma=False,
    )
```

```python
from functools import partial
import math

import jax
import jax.numpy as jnp
from jax import lax
from jax.experimental import pallas as pl
from jax.experimental.pallas import tpu as pltpu
from jax.sharding import PartitionSpec as P

D = 768
H = 12
HD = 64
FF = 3072
NPOS = 197
NP = 208
NL = 256
B = 128
STEP = 5
T = D // B

f32 = jnp.float32
bf16 = jnp.bfloat16

ln_eps = 1e-06
beta_one = 0.9
beta_two = 0.95
beta_stat = 0.95
adam_eps = 1e-08
matrix_rate = 0.05
vector_rate = 0.2
decay_rate = 0.05

VMEM = pl.BlockSpec(memory_space=pltpu.VMEM)
SMEM = pl.BlockSpec(memory_space=pltpu.SMEM)
ANY = pl.BlockSpec(memory_space=pl.ANY)
LIMIT = 60 << 20


def shape(dims, kind):
    return jax.ShapeDtypeStruct(dims, kind)


def dot_nn(x, y):
    return lax.dot_general(x, y, (((1,), (0,)), ((), ())), preferred_element_type=f32)


def dot_nt(x, y):
    return lax.dot_general(x, y, (((1,), (1,)), ((), ())), preferred_element_type=f32)


def dot_tn(x, y):
    return lax.dot_general(x, y, (((0,), (0,)), ((), ())), preferred_element_type=f32)


def norm_parts(values):
    centered = values - jnp.mean(values, axis=-1, keepdims=True)
    inv_std = lax.rsqrt(jnp.mean(centered * centered, axis=-1, keepdims=True) + ln_eps)
    return (centered * inv_std, inv_std)


def norm_back(grad_normed, scaled, inv_std, gain_row):
    tangent = grad_normed * gain_row
    return inv_std * (
        tangent
        - jnp.mean(tangent, axis=-1, keepdims=True)
        - scaled * jnp.mean(tangent * scaled, axis=-1, keepdims=True)
    )


MESH = pl.DeviceIdType.MESH
COPIES = 35


def own_kernels(dp_total, parts):
    return dp_total == 16 and parts == 2


class Place:
    def __init__(self):
        dp = lax.axis_index("dp")
        self.y = lax.axis_index("mp")
        self.z = dp // 4
        self.x = lax.rem(dp // 2, 2)
        self.c = lax.rem(dp, 2)

    def rank(self, d=0, dx=0, dc=0, dy=0):
        z = lax.rem(self.z + d + 4, 4)
        x = 1 - self.x if dx else self.x
        c = 1 - self.c if dc else self.c
        y = 1 - self.y if dy else self.y
        return ((z * 2 + x) * 2 + c) * 2 + y

    def device(self, d=0, dx=0, dc=0, dy=0):
        z = lax.rem(self.z + d + 4, 4)
        x = 1 - self.x if dx else self.x
        c = 1 - self.c if dc else self.c
        y = 1 - self.y if dy else self.y
        return ((z * 2 + x) * 2 + c, y)

    def greet(self):
        barrier = pltpu.get_barrier_semaphore()
        for d, dx, dc, dy in PARTNERS:
            pl.semaphore_signal(
                barrier, inc=1, device_id=self.device(d, dx, dc, dy), device_id_type=MESH
            )
        pl.semaphore_wait(barrier, len(PARTNERS))


PARTNERS = ((1, 0, 0, 0), (2, 0, 0, 0), (3, 0, 0, 0), (0, 1, 0, 0), (0, 0, 1, 0), (0, 0, 0, 1))


class Copies:
    def __init__(self, place, send, recv):
        self.place = place
        self.send = send
        self.recv = recv
        self.made = {}

    def start(self, key, src, dst, **to):
        i = len(self.made)
        copy = pltpu.make_async_remote_copy(
            src_ref=src,
            dst_ref=dst,
            send_sem=self.send.at[i],
            recv_sem=self.recv.at[i],
            device_id=self.place.device(**to),
            device_id_type=MESH,
        )
        copy.start()
        self.made[key] = copy

    def arrived(self, key):
        self.made[key].wait_recv()

    def sent(self):
        for copy in self.made.values():
            copy.wait_send()


class Gather(Copies):
    def __init__(self, place, own, full, n, send, recv, local):
        super().__init__(place, send, recv)
        self.own = own
        self.full = full
        self.n = n
        self.half = n // 2
        self.local = pltpu.make_async_copy(own, self.at(), local)

    def at(self, d=0, dx=0, dc=0, dy=0, lo=0, hi=None):
        hi = self.n if hi is None else hi
        return self.full.at[pl.ds(self.place.rank(d, dx, dc, dy) * self.n + lo, hi - lo)]

    def spread(self, d):
        src = self.own if d == 0 else self.at(d=-d)
        dst = self.at(d=-d)
        self.start(("x", d), src, dst, dx=1)
        self.start(("y", d), src, dst, dy=1)
        self.start(("c", d, 0, 0), src, dst, dc=1)

    def along(self, d):
        self.start(("z", d), self.own, self.at(), d=d)

    def share(self, d, dx, dy):
        ref = self.at(d=-d, dx=dx, dy=dy)
        self.start(("c", d, dx, dy), ref, ref, dc=1)

    def corner(self, d):
        ref = self.at(d=-d, dy=1, lo=self.half)
        self.start(("xd", d), ref, ref, dx=1)
        ref = self.at(d=-d, dx=1, hi=self.half)
        self.start(("yd", d), ref, ref, dy=1)

    def sides(self, d):
        self.arrived(("x", d))
        self.share(d, 1, 0)
        self.arrived(("y", d))
        self.share(d, 0, 1)

    def cornered(self, d):
        self.arrived(("xd", d))
        self.arrived(("yd", d))
        self.share(d, 1, 1)

    def step(self, i):
        if i == 0:
            self.local.start()
            self.along(1)
            self.spread(0)
        elif i == 1:
            self.arrived(("z", 1))
            self.along(3)
            self.spread(1)
            self.sides(0)
        elif i == 2:
            self.arrived(("z", 3))
            self.along(2)
            self.spread(3)
            self.sides(1)
            self.corner(0)
        elif i == 3:
            self.corner(1)
            self.sides(3)
        elif i == 4:
            self.arrived(("z", 2))
            self.spread(2)
            self.cornered(0)
            self.corner(3)
            self.cornered(1)
        elif i == 5:
            self.sides(2)
            self.corner(2)
            self.cornered(3)
        else:
            self.cornered(2)
            for d in range(4):
                for dx in range(2):
                    for dy in range(2):
                        self.arrived(("c", d, dx, dy))
            self.local.wait()
            self.sent()


GATHER_STEPS = 7


class Scatter(Copies):
    def __init__(self, place, full, n, acc, peer, side, corner, along, send, recv, local):
        super().__init__(place, send, recv)
        self.full = full
        self.local = local
        self.mine = {}
        self.n = n
        self.half = n // 2
        self.acc = acc
        self.peer = peer
        self.side = side
        self.cor = corner
        self.col = along

    def block(self, d, dx, dc, dy):
        return pl.ds(self.place.rank(d, dx, dc, dy) * self.n, self.n)

    def core(self, d):
        for dx in range(2):
            for dy in range(2):
                self.start(
                    ("c", d, dx, dy),
                    self.full.at[self.block(d, dx, 1, dy)],
                    self.peer.at[d, dx, dy],
                    dc=1,
                )
        for dx in range(2):
            for dy in range(2):
                key = (d, dx, dy)
                self.mine[key] = pltpu.make_async_copy(
                    self.full.at[self.block(d, dx, 0, dy)],
                    self.acc.at[d, dx, dy],
                    self.local.at[len(self.mine)],
                )
                self.mine[key].start()

    def pair(self, d, dx, dy):
        self.mine[(d, dx, dy)].wait()
        self.arrived(("c", d, dx, dy))
        self.add(d, dx, dy, self.peer.at[d, dx, dy], 0, self.n)

    def add(self, d, dx, dy, other, lo, hi):
        @pl.loop(lo, hi)
        def _(i):
            total = self.acc[d, dx, dy, i].astype(f32) + other[i - lo].astype(f32)
            self.acc[d, dx, dy, i] = total.astype(bf16)

    def corner(self, d):
        self.pair(d, 1, 1)
        h, n = self.half, self.n
        self.start(("xd", d), self.acc.at[d, 1, 1, pl.ds(0, h)], self.cor.at[d, pl.ds(0, h)], dx=1)
        self.start(
            ("yd", d), self.acc.at[d, 1, 1, pl.ds(h, n - h)], self.cor.at[d, pl.ds(h, n - h)], dy=1
        )
        self.pair(d, 1, 0)
        self.pair(d, 0, 1)
        self.pair(d, 0, 0)

    def sides(self, d):
        h, n = self.half, self.n
        self.arrived(("yd", d))
        self.add(d, 1, 0, self.cor.at[d, pl.ds(h, n - h)], h, n)
        self.start(("x", d), self.acc.at[d, 1, 0], self.side.at[d, 0], dx=1)
        self.arrived(("xd", d))
        self.add(d, 0, 1, self.cor.at[d, pl.ds(0, h)], 0, h)
        self.start(("y", d), self.acc.at[d, 0, 1], self.side.at[d, 1], dy=1)

    def along(self, d):
        self.arrived(("x", d))
        self.arrived(("y", d))

        @pl.loop(0, self.n)
        def _(i):
            total = (
                self.acc[d, 0, 0, i].astype(f32)
                + self.side[d, 0, i].astype(f32)
                + self.side[d, 1, i].astype(f32)
            )
            self.acc[d, 0, 0, i] = total.astype(bf16)

        if d > 0:
            self.start(("z", d), self.acc.at[d, 0, 0], self.col.at[d - 1], d=d)

    def step(self, i, out=None):
        if i == 0:
            for d in (2, 3, 0, 1):
                self.core(d)
            self.corner(2)
            self.corner(3)
        elif i == 1:
            self.sides(2)
            self.corner(0)
        elif i == 2:
            self.along(2)
            self.corner(1)
            self.sides(3)
        elif i == 3:
            self.along(3)
            self.sides(1)
        elif i == 4:
            self.along(1)
            self.sides(0)
        else:
            self.along(0)
            for d in (1, 2, 3):
                self.arrived(("z", d))

            @pl.loop(0, self.n)
            def _(i):
                out[i] = (
                    (self.acc[0, 0, 0, i].astype(f32) + self.col[0, i].astype(f32))
                    + self.col[1, i].astype(f32)
                ) + self.col[2, i].astype(f32)

            self.sent()


SCATTER_STEPS = 6


def scatter_scratch(n):
    return [
        pltpu.VMEM((4, 2, 2, n, B, B), bf16),
        pltpu.VMEM((4, 2, 2, n, B, B), bf16),
        pltpu.VMEM((4, 2, n, B, B), bf16),
        pltpu.VMEM((4, n, B, B), bf16),
        pltpu.VMEM((3, n, B, B), bf16),
        pltpu.SemaphoreType.DMA((COPIES,)),
        pltpu.SemaphoreType.DMA((COPIES,)),
        pltpu.SemaphoreType.DMA((16,)),
    ]


def gather_scratch():
    return [
        pltpu.SemaphoreType.DMA((COPIES,)),
        pltpu.SemaphoreType.DMA((COPIES,)),
        pltpu.SemaphoreType.DMA(()),
    ]


class Local:
    def __init__(self, sems):
        self.sems = sems
        self.made = []

    def start(self, src, dst):
        copy = pltpu.make_async_copy(src, dst, self.sems.at[len(self.made)])
        copy.start()
        self.made.append(copy)
        return copy

    def finish(self):
        for copy in self.made:
            copy.wait()


def spread_table(table_ref, spread):
    for h in range(H):
        for c in range(table_ref.shape[1] // B):
            spread[h, c] = jnp.broadcast_to(table_ref[h : h + 1, c * B : (c + 1) * B], (8, B))


def lookup_rows(idx_ref, spread, out_ref, lo, hi):
    chunks = spread.shape[1]

    @pl.loop(lo, hi)
    def _(jt):
        rows = pl.ds(pl.multiple_of(jt * 8, 8), 8)
        real = jt * 8 + lax.broadcasted_iota(jnp.int32, (8, B), 0) < NPOS
        for half in range(NL // B):
            lanes = slice(half * B, (half + 1) * B)
            idx = idx_ref[rows, lanes]
            low = jnp.bitwise_and(idx, B - 1)
            high = jnp.right_shift(idx, 7)
            for h in range(H):
                acc = jnp.take_along_axis(spread[h, 0], low, axis=1, mode="promise_in_bounds")
                for c in range(1, chunks):
                    part = jnp.take_along_axis(spread[h, c], low, axis=1, mode="promise_in_bounds")
                    acc = jnp.where(high == c, part, acc)
                out_ref[h, rows, lanes] = jnp.where(real, acc, -1e30)


JB = 8


def accumulate_rows(grid_ref, idx_ref, out_ref):
    chunks = out_ref.shape[1] // B
    out_ref[...] = jnp.zeros_like(out_ref)
    lo_rows = lax.broadcasted_iota(jnp.int32, (B, NL), 0)

    @pl.loop(0, NP // JB)
    def _(jb):
        idx_all = idx_ref[pl.ds(pl.multiple_of(jb * JB, JB), JB), :]
        lefts = []
        rights = []
        for jj in range(JB):
            values = grid_ref[:, jb * JB + jj, :]
            values = jnp.concatenate([values, jnp.zeros((16 - H, NL), f32)], axis=0)
            idx = idx_all[jj : jj + 1]
            low = jnp.bitwise_and(idx, B - 1)
            high = jnp.right_shift(idx, 7)
            rights.append(jnp.where(lo_rows == low, 1.0, 0.0).astype(bf16))
            lefts.append(
                jnp.concatenate(
                    [jnp.where(high == c, values, 0.0) for c in range(chunks)], axis=0
                ).astype(bf16)
            )
        got = dot_nt(jnp.concatenate(lefts, axis=1), jnp.concatenate(rights, axis=1))
        for c in range(chunks):
            out_ref[:, c * B : (c + 1) * B] += got[c * 16 : (c + 1) * 16]


def pad_rows(x):
    return jnp.concatenate([x, jnp.zeros((NL - NP, x.shape[1]), x.dtype)], axis=0)


def real_rows():
    return lax.broadcasted_iota(jnp.int32, (NP, 1), 0) < NPOS


def forward_kernel(comm, own, tokens, vec, idx, table, *refs):
    refs = list(refs)
    if comm:
        attn_state, mlp_state = refs[:2]
        refs = refs[2:]
    else:
        full = refs.pop(0)
    w_o, q_o, k_o, v_o, att_o, mid_o, bra_o, n2_o, bias_o, tok_o, lse = refs[:11]
    refs = refs[11:]
    if comm:
        mlp_all = refs.pop(0)
    w, q, k, v, att, mid, bra, n2, bias, tok, n1, spread, long, out_sems = refs[:14]
    refs = refs[14:]
    out = Local(out_sems)
    imgs = q.shape[0]
    edge = tokens.shape[1] // 16 * 16

    if comm:
        a32, m32, a16, m16, full, load_sems = refs[:6]
        a_sems = refs[6:9]
        m_sems = refs[9:12]
        na, nm = a16.shape[0], m16.shape[0]
        load = Local(load_sems)
        first = load.start(attn_state.at[:, 0], a32)
        second = load.start(mlp_state.at[0, :, 0], m32)
        place = Place()
        place.greet()
        first.wait()
        a16[...] = a32[...].astype(bf16)
        moves_a = Gather(place, a16, full, na, *a_sems)
        moves_m = Gather(place, m16, mlp_all, nm, *m_sems)
        step_a = moves_a.step
        step_m = moves_m.step
        step_a(0)
        second.wait()
        m16[...] = m32[...].astype(bf16)
    else:
        step_a = step_m = lambda i: None

    long[edge : edge + 16] = jnp.zeros((16, D), f32)
    long[:edge] = tokens[0, :edge].astype(f32)
    long[edge : tokens.shape[1]] = tokens[0, edge:].astype(f32)
    for img in range(imgs):
        x = jnp.where(real_rows(), long[img * NPOS : img * NPOS + NP], 0.0)
        tok[img] = x.astype(bf16)
        x, _ = norm_parts(x)
        n1[img * NP : (img + 1) * NP] = (x * vec[0:1] + vec[1:2]).astype(bf16)
    out.start(tok, tok_o)
    spread_table(table, spread)
    step_a(1)
    tiles = NP // 8
    lookup_rows(idx, spread, bias, 0, tiles // 3)
    step_a(2)
    lookup_rows(idx, spread, bias, tiles // 3, 2 * tiles // 3)
    step_a(3)
    lookup_rows(idx, spread, bias, 2 * tiles // 3, tiles)
    out.start(bias, bias_o)
    step_a(4)
    step_a(5)
    step_m(0)
    step_a(6)

    @pl.loop(0, own.shape[0])
    def _(b):
        m = b // (T * T)
        r = lax.rem(b // T, T)
        c = lax.rem(b, T)
        w[m, pl.ds(pl.multiple_of(r * B, B), B), pl.ds(pl.multiple_of(c * B, B), B)] = full[own[b]]

    out.start(w, w_o)
    for m, (dst, row, scale) in enumerate(((q, 2, HD**-0.5), (k, None, 1.0), (v, 3, 1.0))):
        for n in range(D // NL):
            lanes = slice(n * NL, (n + 1) * NL)
            part = dot_nn(n1[...], w[m, :, lanes])
            if row is not None:
                part = part + vec[row : row + 1, lanes]
            part = part.astype(bf16)
            if scale != 1.0:
                part = part * jnp.asarray(scale, bf16)
            for img in range(imgs):
                dst[img, :, lanes] = part[img * NP : (img + 1) * NP]
    out.start(q, q_o)
    out.start(k, k_o)
    out.start(v, v_o)
    step_m(1)

    side = lax.broadcasted_iota(jnp.int32, (1, B), 1) // HD
    for img in range(imgs):
        for pair in range(H // 2):
            lanes = slice(pair * B, (pair + 1) * B)
            k_pair = k[img, :, lanes]
            q_pair = pad_rows(q[img, :, lanes])
            v_turn = v[img, :, lanes].astype(f32).T.astype(bf16)
            mixed = []
            for sub in range(2):
                h = pair * 2 + sub
                q_one = jnp.where(side == sub, q_pair, jnp.zeros_like(q_pair))
                s = dot_nt(k_pair, q_one) + bias[h]
                top = jnp.max(s, axis=0, keepdims=True)
                e = jnp.exp(s - top)
                total = jnp.sum(e, axis=0, keepdims=True)
                o = dot_nn(v_turn[sub * HD : (sub + 1) * HD], e.astype(bf16))
                mixed.append(o * (1.0 / total))
                lse[img, h : h + 1] = top + jnp.log(total)
            both = jnp.concatenate(mixed, axis=0).T
            att[img, :, lanes] = both[:NP].astype(bf16)
        step_m(img + 2)
    out.start(att, att_o)

    @pl.loop(0, imgs)
    def _(img):
        branch = dot_nn(att[img], w[3]) + vec[4:5]
        bra[img] = branch
        middle = tok[img].astype(f32) + vec[5:6] * branch
        mid[img] = middle
        x, _ = norm_parts(middle)
        n2[img] = (x * vec[6:7] + vec[7:8]).astype(bf16)

    out.start(bra, bra_o)
    out.start(mid, mid_o)
    out.start(n2, n2_o)
    step_m(6)
    out.finish()


def forward_attention(comm, own, tokens, vec, idx, table, attn, mlp=None):
    imgs = tokens.shape[1] // NPOS
    big = ((imgs, NP, D), bf16)
    wide = ((imgs, NP, D), f32)
    kept = [
        ((4, D, D), bf16),
        big,
        big,
        big,
        big,
        wide,
        wide,
        big,
        ((H, NP, NL), f32),
        big,
    ]
    out_shape = [shape(*k) for k in kept] + [shape((imgs, H, NL), f32)]
    out_specs = [ANY] * len(kept) + [VMEM]
    scratch = [pltpu.VMEM(*k) for k in kept] + [
        pltpu.VMEM((imgs * NP, D), bf16),
        pltpu.VMEM((H, table.shape[1] // B, 8, B), f32),
        pltpu.VMEM((tokens.shape[1] // 16 * 16 + 16, D), f32),
        pltpu.SemaphoreType.DMA((len(kept),)),
    ]
    args = [own, tokens, vec, idx, table, attn]
    specs = [SMEM, VMEM, VMEM, VMEM, VMEM]
    params = dict(vmem_limit_bytes=LIMIT)
    if comm:
        na, nm = attn.shape[0], mlp.shape[1]
        args.append(mlp)
        specs += [ANY, ANY]
        out_shape.append(shape((32 * nm, B, B), bf16))
        out_specs.append(ANY)
        scratch += [
            pltpu.VMEM((na, B, B), f32),
            pltpu.VMEM((nm, B, B), f32),
            pltpu.VMEM((na, B, B), bf16),
            pltpu.VMEM((nm, B, B), bf16),
            pltpu.VMEM((32 * na, B, B), bf16),
            pltpu.SemaphoreType.DMA((2,)),
        ]
        scratch += gather_scratch() + gather_scratch()
        params.update(collective_id=0, has_side_effects=True)
    else:
        specs.append(VMEM)
    return pl.pallas_call(
        partial(forward_kernel, comm),
        in_specs=specs,
        out_specs=out_specs,
        out_shape=out_shape,
        scratch_shapes=scratch,
        compiler_params=pltpu.CompilerParams(**params),
        name="forward_attention",
    )(*args)


CH = 512


def mlp_kernel(
    parts,
    each,
    own,
    mid_h,
    bra_h,
    n2,
    cot,
    slots,
    vec,
    upb,
    out,
    gmid,
    gbra,
    sums,
    bgrad,
    tiles_out,
    mid,
    bra,
    last,
    w1,
    w2,
    gs,
    act,
    gh,
    summed,
    gn2,
    tiles,
    sem_in,
    sem_out,
    sem_load,
):
    imgs = mid.shape[0]
    length = cot.shape[1]
    chunks = FF // CH
    per = CH // B
    half = own.shape[0] // 2
    local = half // T

    def place(slot, p):
        return (slot // each) * (parts * each) + p * each + lax.rem(slot, each)

    def tile_blocks(c, t):
        g = c * per + lax.rem(t, per)
        g2 = c * per + t // T
        up = place(own[(t // per) * local + lax.rem(g, local)], g // local)
        down = place(own[half + lax.rem(g2, local) * T + lax.rem(t, T)], g2 // local)
        return up, down

    @pl.loop(0, chunks)
    def _(c):
        @pl.loop(0, T * per)
        def _(t):
            up, down = tile_blocks(c, t)
            r = pl.multiple_of((t // per) * B, B)
            cc = pl.multiple_of(lax.rem(t, per) * B, B)
            pltpu.make_async_copy(
                slots.at[up], w1.at[c, pl.ds(r, B), pl.ds(cc, B)], sem_in.at[c]
            ).start()
            r = pl.multiple_of((t // T) * B, B)
            cc = pl.multiple_of(lax.rem(t, T) * B, B)
            pltpu.make_async_copy(
                slots.at[down], w2.at[c, pl.ds(r, B), pl.ds(cc, B)], sem_in.at[c]
            ).start()

    load = Local(sem_load)
    load.start(mid_h, mid)
    load.start(bra_h, bra)
    last[...] = jnp.zeros_like(last)
    last[:NPOS] = cot[0, length - NPOS :]

    def upstream(img):
        if img == imgs - 1:
            return last[...]
        return jnp.where(real_rows(), cot[0, img * NPOS : img * NPOS + NP], 0.0)

    for img in range(imgs):
        gs[img * NP : (img + 1) * NP] = (vec[9:10] * upstream(img)).astype(bf16)
    summed[...] = jnp.zeros_like(summed)
    gn2[...] = jnp.zeros_like(gn2)

    @pl.loop(0, chunks)
    def _(c):
        pltpu.make_async_copy(w1.at[c], w1.at[c], sem_in.at[c]).wait()
        pltpu.make_async_copy(w2.at[c], w2.at[c], sem_in.at[c]).wait()
        span = pl.ds(pl.multiple_of(c * CH, CH), CH)
        bias_sum = jnp.zeros((1, CH), f32)
        for rb in range(imgs // 2):
            block = slice(rb * 2 * NP, (rb + 1) * 2 * NP)
            hid = dot_nn(n2[block], w1[c]) + upb[:, span]
            back = dot_nt(gs[block], w2[c])
            phi = 0.5 * (1.0 + lax.erf(hid * (1.0 / math.sqrt(2.0))))
            density = jnp.exp(-0.5 * hid * hid) * (1.0 / math.sqrt(2.0 * math.pi))
            a = (hid * phi).astype(bf16)
            g = (back * (phi + hid * density)).astype(bf16)
            act[block] = a
            gh[block] = g
            bias_sum = bias_sum + jnp.sum(g.astype(f32), axis=0, keepdims=True)
            summed[block] += dot_nn(a, w2[c])
            gn2[block] += dot_nt(g, w1[c])
        bgrad[:, span] = bias_sum
        up_grad = dot_tn(n2[...], gh[...])
        down_grad = dot_tn(act[...], gs[...])
        for r in range(T):
            for cc in range(per):
                tiles[c, r * per + cc] = up_grad[
                    r * B : (r + 1) * B, cc * B : (cc + 1) * B
                ].astype(bf16)
        for r in range(per):
            for cc in range(T):
                tiles[c, T * per + r * T + cc] = down_grad[
                    r * B : (r + 1) * B, cc * B : (cc + 1) * B
                ].astype(bf16)

        @pl.loop(0, T * per)
        def _(t):
            up, down = tile_blocks(c, t)
            pltpu.make_async_copy(tiles.at[c, t], tiles_out.at[up], sem_out).start()
            pltpu.make_async_copy(tiles.at[c, T * per + t], tiles_out.at[down], sem_out).start()

    load.finish()
    s4 = jnp.zeros((1, D), f32)
    s5 = jnp.zeros((1, D), f32)
    s6 = jnp.zeros((1, D), f32)
    s7 = jnp.zeros((1, D), f32)
    s8 = jnp.zeros((1, D), f32)
    s9 = jnp.zeros((1, D), f32)
    for img in range(imgs):
        block = slice(img * NP, (img + 1) * NP)
        up = upstream(img)
        middle = mid[img]
        sm = summed[block] + vec[8:9]
        s9 += jnp.sum(up * sm, axis=0, keepdims=True)
        s8 += jnp.sum(gs[block].astype(f32), axis=0, keepdims=True)
        x, inv = norm_parts(middle)
        gn = gn2[block]
        s6 += jnp.sum(gn * x, axis=0, keepdims=True)
        s7 += jnp.sum(gn, axis=0, keepdims=True)
        gm = up + norm_back(gn, x, inv, vec[6:7])
        gmid[img] = gm
        gb = (vec[5:6] * gm).astype(bf16)
        gbra[img] = gb
        s4 += jnp.sum(gb.astype(f32), axis=0, keepdims=True)
        s5 += jnp.sum(gm * bra[img], axis=0, keepdims=True)
        summed[img * NPOS : img * NPOS + NP] = middle + vec[9:10] * sm
    edge = length // 16 * 16
    out[0, :edge] = summed[:edge].astype(bf16)
    out[0, edge:] = summed[edge:length].astype(bf16)
    sums[...] = jnp.concatenate([s4, s5, s6, s7, s8, s9, s9, s9], axis=0)
    pltpu.make_async_copy(tiles, tiles, sem_out).wait()


def feed_forward(mid, bra, n2, cot, slots, own, vec, up_bias, parts, each):
    imgs = mid.shape[0]
    rows = imgs * NP
    chunks = FF // CH
    per = CH // B
    return pl.pallas_call(
        partial(mlp_kernel, parts, each),
        in_specs=[SMEM, ANY, ANY, VMEM, VMEM, ANY, VMEM, VMEM],
        out_specs=[VMEM] * 5 + [ANY],
        out_shape=[
            shape(cot.shape, bf16),
            shape((imgs, NP, D), f32),
            shape((imgs, NP, D), bf16),
            shape((8, D), f32),
            shape((1, FF), f32),
            shape(slots.shape, bf16),
        ],
        scratch_shapes=[
            pltpu.VMEM((imgs, NP, D), f32),
            pltpu.VMEM((imgs, NP, D), f32),
            pltpu.VMEM((NP, D), f32),
            pltpu.VMEM((chunks, D, CH), bf16),
            pltpu.VMEM((chunks, CH, D), bf16),
            pltpu.VMEM((rows, D), bf16),
            pltpu.VMEM((rows, CH), bf16),
            pltpu.VMEM((rows, CH), bf16),
            pltpu.VMEM((rows, D), f32),
            pltpu.VMEM((rows, D), f32),
            pltpu.VMEM((chunks, 2 * T * per, B, B), bf16),
            pltpu.SemaphoreType.DMA((chunks,)),
            pltpu.SemaphoreType.DMA(()),
            pltpu.SemaphoreType.DMA((2,)),
        ],
        compiler_params=pltpu.CompilerParams(vmem_limit_bytes=LIMIT),
        name="feed_forward",
    )(own, mid, bra, n2.reshape(rows, D), cot, slots, vec, up_bias)


def backward_kernel(comm, gbra, lse, vec, idx, *refs):
    refs = list(refs)
    w_h, v_h, k_h, q_h, bias_h, att_h, tok_h, gmid_h = refs[:8]
    refs = refs[8:]
    if comm:
        mlp_full = refs.pop(0)
    gin, table, sums, tiles_o = refs[:4]
    refs = refs[4:]
    if comm:
        mlp_mine = refs.pop(0)
    w, v, k, q, bias, att, tok, gmid = refs[:8]
    n1, gatt, gqkv, grid, tiles, load_sems, out_sem = refs[8:15]
    refs = refs[15:]
    imgs = q.shape[0]

    if comm:
        place = Place()
        place.greet()
        moves = Scatter(place, mlp_full, mlp_mine.shape[0], *refs)
        step = moves.step
    else:
        step = lambda i, out=None: None
    load = Local(load_sems)
    got_w, got_v, got_k, got_q, got_bias, got_att, got_tok, got_gmid = [
        load.start(src, dst)
        for src, dst in zip(
            (w_h, v_h, k_h, q_h, bias_h, att_h, tok_h, gmid_h), (w, v, k, q, bias, att, tok, gmid)
        )
    ]
    step(0)
    got_w.wait()
    for n in range(D // NL):
        lanes = slice(n * NL, (n + 1) * NL)
        got = dot_nt(gbra[...], w[3, lanes, :]).astype(bf16)
        for img in range(imgs):
            gatt[img, :, lanes] = got[img * NP : (img + 1) * NP]
    grid[...] = jnp.zeros_like(grid)
    got_v.wait()
    got_k.wait()
    got_q.wait()
    got_bias.wait()
    step(1)

    side = lax.broadcasted_iota(jnp.int32, (1, B), 1) // HD
    for img in range(imgs):
        here = slice(img * NP, (img + 1) * NP)
        for pair in range(H // 2):
            lanes = slice(pair * B, (pair + 1) * B)
            k_pair = k[img, :, lanes]
            v_pair = v[img, :, lanes]
            q_pair = pad_rows(q[img, :, lanes])
            g_pair = pad_rows(gatt[img, :, lanes])
            k_turn = k_pair.astype(f32).T.astype(bf16)
            gq = []
            gk = jnp.zeros((NP, B), f32)
            gv = jnp.zeros((NP, B), f32)
            for sub in range(2):
                h = pair * 2 + sub
                q_one = jnp.where(side == sub, q_pair, jnp.zeros_like(q_pair))
                g_one = jnp.where(side == sub, g_pair, jnp.zeros_like(g_pair))
                s = dot_nt(k_pair, q_one) + bias[h]
                p = jnp.exp(s - lse[img, h : h + 1])
                dp = dot_nt(v_pair, g_one)
                gv = gv + dot_nn(p.astype(bf16), g_one)
                inner = jnp.sum(p * dp, axis=0, keepdims=True)
                ds = (p * (dp - inner)).astype(bf16)
                gk = gk + dot_nn(ds, q_one)
                gq.append(dot_nn(k_turn[sub * HD : (sub + 1) * HD], ds))
                grid[h] += ds.astype(f32)
            turned = jnp.concatenate(gq, axis=0).T
            gqkv[here, lanes] = (turned[:NP] * HD**-0.5).astype(bf16)
            gqkv[here, D + pair * B : D + (pair + 1) * B] = gk.astype(bf16)
            gqkv[here, 2 * D + pair * B : 2 * D + (pair + 1) * B] = gv.astype(bf16)
        if img < 3:
            step(img + 2)

    def put(m, n, grad):
        for r in range(T):
            for cc in range(NL // B):
                tiles[m * T * T + r * T + n * (NL // B) + cc] = grad[
                    r * B : (r + 1) * B, cc * B : (cc + 1) * B
                ].astype(bf16)

    got_att.wait()
    got_tok.wait()
    for img in range(imgs):
        x, _ = norm_parts(tok[img].astype(f32))
        n1[img * NP : (img + 1) * NP] = (x * vec[0:1] + vec[1:2]).astype(bf16)
    for n in range(D // NL):
        lanes = slice(n * NL, (n + 1) * NL)
        put(3, n, dot_tn(att[...], gbra[:, lanes]))
    for m in range(3):
        for n in range(D // NL):
            put(m, n, dot_tn(n1[...], gqkv[:, m * D + n * NL : m * D + (n + 1) * NL]))
    out = pltpu.make_async_copy(tiles, tiles_o, out_sem)
    out.start()
    accumulate_rows(grid, idx, table)

    got_gmid.wait()
    s0 = jnp.zeros((1, D), f32)
    s1 = jnp.zeros((1, D), f32)
    s2 = jnp.zeros((1, D), f32)
    s3 = jnp.zeros((1, D), f32)
    for img in range(imgs):
        here = slice(img * NP, (img + 1) * NP)
        gq = gqkv[here, 0:D]
        gk = gqkv[here, D : 2 * D]
        gv = gqkv[here, 2 * D : 3 * D]
        gn = dot_nt(gq, w[0]) + dot_nt(gk, w[1]) + dot_nt(gv, w[2])
        x, inv = norm_parts(tok[img].astype(f32))
        s0 += jnp.sum(gn * x, axis=0, keepdims=True)
        s1 += jnp.sum(gn, axis=0, keepdims=True)
        s2 += jnp.sum(gq.astype(f32), axis=0, keepdims=True)
        s3 += jnp.sum(gv.astype(f32), axis=0, keepdims=True)
        got = gmid[img] + norm_back(gn, x, inv, vec[0:1])
        if img == imgs - 1:
            gin[0, img * NPOS :] = got[:NPOS]
        else:
            gin[0, img * NPOS : img * NPOS + NP] = got
    sums[...] = jnp.concatenate([s0, s1, s2, s3, s3, s3, s3, s3], axis=0)
    if comm:
        step(5, mlp_mine)
    out.wait()


def backward_attention(comm, saved, gmid, gbra, vec, idx, wide_total, mlp_full=None):
    w, q, k, v, att, mid, bra, n2, bias, tok, lse = saved
    imgs = tok.shape[0]
    rows = imgs * NP
    att = att.reshape(rows, D)
    loaded = [w, v, k, q, bias, att, tok, gmid]
    args = [gbra.reshape(rows, D), lse, vec, idx] + loaded
    specs = [VMEM] * 4 + [ANY] * 8
    out_shape = [
        shape((1, imgs * NPOS, D), f32),
        shape((16, wide_total), f32),
        shape((8, D), f32),
        shape((4 * T * T, B, B), bf16),
    ]
    out_specs = [VMEM] * 3 + [ANY]
    scratch = [pltpu.VMEM(x.shape, x.dtype) for x in loaded] + [
        pltpu.VMEM((rows, D), bf16),
        pltpu.VMEM((imgs, NP, D), bf16),
        pltpu.VMEM((rows, 3 * D), bf16),
        pltpu.VMEM((H, NP, NL), f32),
        pltpu.VMEM((4 * T * T, B, B), bf16),
        pltpu.SemaphoreType.DMA((8,)),
        pltpu.SemaphoreType.DMA(()),
    ]
    params = dict(vmem_limit_bytes=LIMIT)
    if comm:
        n = mlp_full.shape[0] // 32
        args.append(mlp_full)
        specs.append(ANY)
        out_shape.append(shape((n, B, B), f32))
        out_specs.append(VMEM)
        scratch += scatter_scratch(n)
        params.update(collective_id=1, has_side_effects=True)
    return pl.pallas_call(
        partial(backward_kernel, comm),
        in_specs=specs,
        out_specs=out_specs,
        out_shape=out_shape,
        scratch_shapes=scratch,
        compiler_params=pltpu.CompilerParams(**params),
        name="backward_attention",
    )(*args)


SUM_ROWS = 40


def adam(grad, param, first, second):
    new_first = beta_one * first + (1.0 - beta_one) * grad
    new_second = beta_two * second + (1.0 - beta_two) * grad * grad
    fix_one = 1.0 - beta_one**STEP
    fix_two = 1.0 - beta_two**STEP
    step = (new_first / fix_one) / (jnp.sqrt(new_second / fix_two) + adam_eps)
    return grad, param - vector_rate * step, new_first, new_second


def finish_kernel(
    inverse,
    tiles,
    mlp_sums,
    attn_sums,
    table_sums,
    bias_sums,
    vec,
    vec_m,
    table,
    table_m,
    upb,
    upb_m,
    mine,
    vec_up,
    table_up,
    upb_up,
    full,
    part,
    other,
    column,
    sum_send,
    sum_recv,
    *scratch,
):
    place = Place()
    place.greet()

    @pl.loop(0, full.shape[0])
    def _(slot):
        full[slot] = tiles[inverse[slot]]

    moves = Scatter(place, full, mine.shape[0], *scratch)
    sums = Copies(place, sum_send, sum_recv)
    part[0, 0:8] = mlp_sums[...]
    part[0, 8:16] = attn_sums[...]
    part[0, 16:32] = table_sums[...]
    quarter = jnp.concatenate([bias_sums[:, i * D : (i + 1) * D] for i in range(FF // D)] * 2, axis=0)
    part[0, 32:40] = quarter
    sums.start("c", part.at[0], other.at[0], dc=1)
    moves.step(0)
    sums.arrived("c")
    part[1] = part[0] + other[0]
    sums.start("x", part.at[1], other.at[1], dx=1)
    moves.step(1)
    sums.arrived("x")
    part[2] = part[1] + other[1]
    sums.start("y", part.at[2], other.at[2], dy=1)
    moves.step(2)
    sums.arrived("y")
    part[3] = part[2] + other[2]
    for d in (1, 2, 3):
        sums.start(("z", d), part.at[3], column.at[place.z], d=d)
    moves.step(3)
    column[place.z] = part[3]
    for d in (1, 2, 3):
        sums.arrived(("z", d))
    moves.step(4)
    part[4] = ((column[0] + column[1]) + column[2]) + column[3]
    total = part.at[4]
    grad = jnp.concatenate([total[8:12], total[0:6]], axis=0)
    for i, got in enumerate(adam(grad, vec[...], vec_m[0], vec_m[1])):
        vec_up[i] = got
    wide = table.shape[1]
    grad = total[16 : 16 + H, 0:wide]
    for i, got in enumerate(adam(grad, table[...], table_m[0], table_m[1])):
        table_up[i] = got
    for j in range(FF // D):
        lanes = slice(j * D, (j + 1) * D)
        for i, got in enumerate(
            adam(total[32 + j : 33 + j], upb[:, lanes], upb_m[0:1, lanes], upb_m[1:2, lanes])
        ):
            upb_up[i : i + 1, lanes] = got
    moves.step(5, mine)
    sums.sent()


def finish(inverse, tiles, small, params):
    n = inverse.shape[0] // 32
    vec, vec_m, table, table_m, upb, upb_m = params
    return pl.pallas_call(
        finish_kernel,
        in_specs=[SMEM] + [VMEM] * 11,
        out_specs=[VMEM] * 4,
        out_shape=[
            shape((n, B, B), f32),
            shape((4,) + vec.shape, f32),
            shape((4,) + table.shape, f32),
            shape((4, FF), f32),
        ],
        scratch_shapes=[
            pltpu.VMEM((32 * n, B, B), bf16),
            pltpu.VMEM((5, SUM_ROWS, D), f32),
            pltpu.VMEM((3, SUM_ROWS, D), f32),
            pltpu.VMEM((4, SUM_ROWS, D), f32),
            pltpu.SemaphoreType.DMA((6,)),
            pltpu.SemaphoreType.DMA((6,)),
        ]
        + scatter_scratch(n),
        compiler_params=pltpu.CompilerParams(
            collective_id=2, has_side_effects=True, vmem_limit_bytes=LIMIT
        ),
        name="finish",
    )(inverse, tiles, *small, vec, vec_m, table, table_m, upb[None], upb_m)


NB = 16


def split_two(x):
    first = x.astype(bf16)
    return first, (x - first.astype(f32)).astype(bf16)


def wide_dot(x, y, dims):
    xa, xb = split_two(x)
    ya, yb = split_two(y)
    xs = jnp.concatenate([xa, xa, xb], axis=dims[0])
    ys = jnp.concatenate([ya, yb, ya], axis=dims[1])
    return lax.dot_general(
        xs, ys, (((dims[0],), (dims[1],)), ((), ())), preferred_element_type=f32
    )


def orth_turned(mats):
    count = len(mats)
    tails = []
    for a in mats:
        turned = a.T
        tails.append(jnp.concatenate([wide_dot(turned, turned, (1, 1)), turned], axis=1))
    rows = lax.broadcasted_iota(jnp.int32, (NB, 1), 0)
    eye = lax.broadcasted_iota(jnp.int32, (NB, NB), 0) == lax.broadcasted_iota(
        jnp.int32, (NB, NB), 1
    )
    outs = [[] for _ in range(count)]
    for p in range(B // NB):
        base = p * NB
        strips = [t[:NB] for t in tails]
        for kk in range(NB):
            at = base + kk
            for m in range(count):
                s = strips[m]
                pivot_row = jnp.broadcast_to(s[kk : kk + 1, :], (NB, 2 * B))
                factor = s[:, at : at + 1] * (1.0 / s[kk : kk + 1, at : at + 1])
                strips[m] = s - jnp.where(rows > kk, factor, 0.0) * pivot_row
        for m in range(count):
            s = strips[m]
            diag = jnp.sum(jnp.where(eye, s[:, base : base + NB], 0.0), axis=1, keepdims=True)
            u = s * lax.rsqrt(diag)
            outs[m].append(u[:, B:])
            if base + NB < B:
                tails[m] = tails[m][NB:] - wide_dot(u[:, base + NB : B], u, (0, 0))
    return [jnp.concatenate(o, axis=0) for o in outs]


def soap_kernel(first_slot, owner, grads, state, update, copy):
    count = grads.shape[0]
    mats = []
    base = first_slot() + pl.program_id(0) * count
    gs = []
    for i in range(count):
        named = jnp.where(owner[...] == base + i, 1.0, 0.0)
        named = jnp.max(named, axis=1, keepdims=True)
        g = jnp.where(named > 0.0, grads[i].astype(f32), 0.0)
        gs.append(g)
        left = beta_stat * state[i, 3] + (1.0 - beta_stat) * wide_dot(g, g, (1, 1))
        right = beta_stat * state[i, 4] + (1.0 - beta_stat) * wide_dot(g, g, (0, 0))
        mats.append(wide_dot(left, state[i, 5], (1, 0)))
        mats.append(wide_dot(right, state[i, 6], (1, 0)))
    turned = orth_turned(mats)
    fix_one = 1.0 - beta_one**STEP
    fix_two = 1.0 - beta_two**STEP
    for i in range(count):
        tl, tr = turned[2 * i], turned[2 * i + 1]
        rotated = wide_dot(wide_dot(tl, gs[i], (1, 0)), tr, (1, 1))
        new_first = beta_one * state[i, 1] + (1.0 - beta_one) * rotated
        new_second = beta_two * state[i, 2] + (1.0 - beta_two) * rotated * rotated
        normalized = new_first / fix_one / (jnp.sqrt(new_second / fix_two) + adam_eps)
        step = wide_dot(wide_dot(tl, normalized, (0, 0)), tr, (1, 0))
        weight = state[i, 0]
        weight = weight - matrix_rate * (step + decay_rate * weight)
        update[i, 0] = weight
        update[i, 1] = new_first
        update[i, 2] = new_second
        update[i, 3] = tl.T
        update[i, 4] = tr.T
        copy[i] = weight.astype(bf16)


def soap_update(grads, state, owner, first_slot):
    slots = grads.shape[0]
    count = max(c for c in range(1, 10) if slots % c == 0)
    return pl.pallas_call(
        partial(soap_kernel, first_slot),
        grid=(slots // count,),
        in_specs=[
            pl.BlockSpec((1, owner.shape[0]), lambda i: (0, 0)),
            pl.BlockSpec((count, B, B), lambda i: (i, 0, 0)),
            pl.BlockSpec((count, 7, B, B), lambda i: (i, 0, 0, 0)),
        ],
        out_specs=[
            pl.BlockSpec((count, 5, B, B), lambda i: (i, 0, 0, 0)),
            pl.BlockSpec((count, B, B), lambda i: (i, 0, 0)),
        ],
        out_shape=[shape((slots, 5, B, B), f32), shape((slots, B, B), bf16)],
        compiler_params=pltpu.CompilerParams(vmem_limit_bytes=LIMIT),
        name="soap",
    )(owner[None], grads, state)


def body(
    tokens,
    cotangent,
    rel_index,
    attn_owner,
    mlp_owner,
    attn_state,
    mlp_state,
    vec_param,
    vec_moments,
    rel_table,
    rel_table_moments,
    up_bias,
    up_bias_moments,
):
    both = ("dp", "mp")
    parts = lax.axis_size("mp")
    comm = own_kernels(lax.axis_size("dp"), parts)
    attn_local = attn_state.shape[0]
    mlp_local = mlp_state.shape[1]
    attn_total = attn_local * lax.axis_size("dp") * parts

    def attn_first():
        return (lax.axis_index("dp") * parts + lax.axis_index("mp")) * attn_local

    def mlp_first():
        return lax.axis_index("dp") * mlp_local

    wide_total = -(-rel_table.shape[1] // B) * B
    idx_t = jnp.pad(rel_index.T, ((0, NP - NPOS), (0, NL - NPOS)))
    table_pad = jnp.pad(rel_table, ((0, 0), (0, wide_total - rel_table.shape[1])))
    slot_ids = jnp.arange(attn_total, dtype=jnp.int32)
    block_ids = jnp.arange(attn_owner.shape[0], dtype=jnp.int32)
    inverse = jnp.sum(
        jnp.where(attn_owner[None, :] == slot_ids[:, None], block_ids[None, :], 0), axis=1
    ).astype(jnp.int32)

    if comm:
        *saved, mlp_slots = forward_attention(
            True, attn_owner, tokens, vec_param, idx_t, table_pad, attn_state, mlp_state
        )
    else:
        attn_slots = lax.all_gather(attn_state[:, 0].astype(bf16), both, axis=0, tiled=True)
        mlp_slots = lax.all_gather(mlp_state[0, :, 0].astype(bf16), both, axis=0, tiled=True)
        saved = forward_attention(
            False, attn_owner, tokens, vec_param, idx_t, table_pad, attn_slots
        )
    w, q, k, v, att, mid, bra, n2, bias, tok, lse = saved
    out, gmid, gbra, mlp_sums, bias_grad, mlp_grads = feed_forward(
        mid, bra, n2, cotangent, mlp_slots, mlp_owner, vec_param, up_bias[None], parts, mlp_local
    )
    if comm:
        gin, table_grad, attn_sums, attn_tiles, mlp_mine = backward_attention(
            True, saved, gmid, gbra, vec_param, idx_t, wide_total, mlp_grads
        )
        attn_mine, vec_up, table_up, bias_up = finish(
            inverse,
            attn_tiles,
            (mlp_sums, attn_sums, table_grad, bias_grad),
            (vec_param, vec_moments, rel_table, rel_table_moments, up_bias, up_bias_moments),
        )
    else:
        gin, table_grad, attn_sums, attn_tiles = backward_attention(
            False, saved, gmid, gbra, vec_param, idx_t, wide_total
        )
        mlp_mine = lax.psum_scatter(mlp_grads, both, scatter_dimension=0, tiled=True)
        attn_mine = lax.psum_scatter(attn_tiles[inverse], both, scatter_dimension=0, tiled=True)
        vector_grad = jnp.concatenate([attn_sums[:4], mlp_sums[:6]], axis=0)
        vector_total, table_total, bias_total = lax.psum(
            (vector_grad, table_grad[:H, : rel_table.shape[1]], bias_grad[0]), both
        )
        vec_up = jnp.stack(adam(vector_total, vec_param, vec_moments[0], vec_moments[1]))
        table_up = jnp.stack(
            adam(table_total, rel_table, rel_table_moments[0], rel_table_moments[1])
        )
        bias_up = jnp.stack(adam(bias_total, up_bias, up_bias_moments[0], up_bias_moments[1]))
    attn_result, attn_copy = soap_update(attn_mine, attn_state, attn_owner, attn_first)
    mlp_result, mlp_copy = soap_update(mlp_mine, mlp_state[0], mlp_owner, mlp_first)
    return (
        out,
        gin,
        attn_result,
        attn_copy,
        mlp_result[None],
        mlp_copy[None],
        vec_up,
        table_up,
        bias_up,
    )


def solution(mesh):
    placed = (
        P(("dp", "mp"), None, None),
        P(("dp", "mp"), None, None),
        P(),
        P(),
        P(),
        P(("dp", "mp"), None, None, None),
        P("mp", "dp", None, None, None),
        P(),
        P(),
        P(),
        P(),
        P(),
        P(),
    )
    return jax.shard_map(
        body,
        mesh=mesh,
        in_specs=placed,
        out_specs=(
            P(("dp", "mp"), None, None),
            P(("dp", "mp"), None, None),
            P(("dp", "mp"), None, None, None),
            P(("dp", "mp"), None, None),
            P("mp", "dp", None, None, None),
            P("mp", "dp", None, None),
            P(),
            P(),
            P(),
        ),
        check_vma=False,
    )
```

```python
from functools import partial
import math

import jax
import jax.numpy as jnp
from jax import lax
from jax.experimental import pallas as pl
from jax.experimental.pallas import tpu as pltpu
from jax.sharding import PartitionSpec as P

D = 768
H = 12
HD = 64
FF = 3072
NPOS = 197
NP = 208
NL = 256
B = 128
STEP = 5
T = D // B

f32 = jnp.float32
bf16 = jnp.bfloat16

ln_eps = 1e-06
beta_one = 0.9
beta_two = 0.95
beta_stat = 0.95
adam_eps = 1e-08
matrix_rate = 0.05
vector_rate = 0.2
decay_rate = 0.05

VMEM = pl.BlockSpec(memory_space=pltpu.VMEM)
SMEM = pl.BlockSpec(memory_space=pltpu.SMEM)
ANY = pl.BlockSpec(memory_space=pl.ANY)
LIMIT = 60 << 20


def shape(dims, kind):
    return jax.ShapeDtypeStruct(dims, kind)


def dot_nn(x, y):
    return lax.dot_general(x, y, (((1,), (0,)), ((), ())), preferred_element_type=f32)


def dot_nt(x, y):
    return lax.dot_general(x, y, (((1,), (1,)), ((), ())), preferred_element_type=f32)


def dot_tn(x, y):
    return lax.dot_general(x, y, (((0,), (0,)), ((), ())), preferred_element_type=f32)


def norm_parts(values):
    centered = values - jnp.mean(values, axis=-1, keepdims=True)
    inv_std = lax.rsqrt(jnp.mean(centered * centered, axis=-1, keepdims=True) + ln_eps)
    return (centered * inv_std, inv_std)


def norm_back(grad_normed, scaled, inv_std, gain_row):
    tangent = grad_normed * gain_row
    return inv_std * (
        tangent
        - jnp.mean(tangent, axis=-1, keepdims=True)
        - scaled * jnp.mean(tangent * scaled, axis=-1, keepdims=True)
    )


MESH = pl.DeviceIdType.MESH
COPIES = 35


def own_kernels(dp_total, parts):
    return dp_total == 16 and parts == 2


class Place:
    def __init__(self):
        dp = lax.axis_index("dp")
        self.y = lax.axis_index("mp")
        self.z = dp // 4
        self.x = lax.rem(dp // 2, 2)
        self.c = lax.rem(dp, 2)

    def rank(self, d=0, dx=0, dc=0, dy=0):
        z = lax.rem(self.z + d + 4, 4)
        x = 1 - self.x if dx else self.x
        c = 1 - self.c if dc else self.c
        y = 1 - self.y if dy else self.y
        return ((z * 2 + x) * 2 + c) * 2 + y

    def device(self, d=0, dx=0, dc=0, dy=0):
        z = lax.rem(self.z + d + 4, 4)
        x = 1 - self.x if dx else self.x
        c = 1 - self.c if dc else self.c
        y = 1 - self.y if dy else self.y
        return ((z * 2 + x) * 2 + c, y)

    def greet(self):
        barrier = pltpu.get_barrier_semaphore()
        for d, dx, dc, dy in PARTNERS:
            pl.semaphore_signal(
                barrier, inc=1, device_id=self.device(d, dx, dc, dy), device_id_type=MESH
            )
        pl.semaphore_wait(barrier, len(PARTNERS))


PARTNERS = ((1, 0, 0, 0), (2, 0, 0, 0), (3, 0, 0, 0), (0, 1, 0, 0), (0, 0, 1, 0), (0, 0, 0, 1))


class Copies:
    def __init__(self, place, send, recv):
        self.place = place
        self.send = send
        self.recv = recv
        self.made = {}

    def start(self, key, src, dst, **to):
        i = len(self.made)
        copy = pltpu.make_async_remote_copy(
            src_ref=src,
            dst_ref=dst,
            send_sem=self.send.at[i],
            recv_sem=self.recv.at[i],
            device_id=self.place.device(**to),
            device_id_type=MESH,
        )
        copy.start()
        self.made[key] = copy

    def arrived(self, key):
        self.made[key].wait_recv()

    def sent(self):
        for copy in self.made.values():
            copy.wait_send()


class Gather(Copies):
    def __init__(self, place, own, full, n, send, recv, local):
        super().__init__(place, send, recv)
        self.own = own
        self.full = full
        self.n = n
        self.half = n // 2
        self.local = pltpu.make_async_copy(own, self.at(), local)

    def at(self, d=0, dx=0, dc=0, dy=0, lo=0, hi=None):
        hi = self.n if hi is None else hi
        return self.full.at[pl.ds(self.place.rank(d, dx, dc, dy) * self.n + lo, hi - lo)]

    def spread(self, d):
        src = self.own if d == 0 else self.at(d=-d)
        dst = self.at(d=-d)
        self.start(("x", d), src, dst, dx=1)
        self.start(("y", d), src, dst, dy=1)
        self.start(("c", d, 0, 0), src, dst, dc=1)

    def along(self, d):
        self.start(("z", d), self.own, self.at(), d=d)

    def share(self, d, dx, dy):
        ref = self.at(d=-d, dx=dx, dy=dy)
        self.start(("c", d, dx, dy), ref, ref, dc=1)

    def corner(self, d):
        ref = self.at(d=-d, dy=1, lo=self.half)
        self.start(("xd", d), ref, ref, dx=1)
        ref = self.at(d=-d, dx=1, hi=self.half)
        self.start(("yd", d), ref, ref, dy=1)

    def sides(self, d):
        self.arrived(("x", d))
        self.share(d, 1, 0)
        self.arrived(("y", d))
        self.share(d, 0, 1)

    def cornered(self, d):
        self.arrived(("xd", d))
        self.arrived(("yd", d))
        self.share(d, 1, 1)

    def step(self, i):
        if i == 0:
            self.local.start()
            self.along(1)
            self.spread(0)
        elif i == 1:
            self.arrived(("z", 1))
            self.along(3)
            self.spread(1)
            self.sides(0)
        elif i == 2:
            self.arrived(("z", 3))
            self.along(2)
            self.spread(3)
            self.sides(1)
            self.corner(0)
        elif i == 3:
            self.corner(1)
            self.sides(3)
        elif i == 4:
            self.arrived(("z", 2))
            self.spread(2)
            self.cornered(0)
            self.corner(3)
            self.cornered(1)
        elif i == 5:
            self.sides(2)
            self.corner(2)
            self.cornered(3)
        else:
            self.cornered(2)
            for d in range(4):
                for dx in range(2):
                    for dy in range(2):
                        self.arrived(("c", d, dx, dy))
            self.local.wait()
            self.sent()


GATHER_STEPS = 7


class Scatter(Copies):
    def __init__(self, place, full, n, acc, peer, side, corner, along, send, recv, local):
        super().__init__(place, send, recv)
        self.full = full
        self.local = local
        self.mine = {}
        self.n = n
        self.half = n // 2
        self.acc = acc
        self.peer = peer
        self.side = side
        self.cor = corner
        self.col = along

    def block(self, d, dx, dc, dy):
        return pl.ds(self.place.rank(d, dx, dc, dy) * self.n, self.n)

    def core(self, d, dx, dy):
        key = (d, dx, dy)
        self.start(
            ("c",) + key, self.full.at[self.block(d, dx, 1, dy)], self.peer.at[d, dx, dy], dc=1
        )
        self.mine[key] = pltpu.make_async_copy(
            self.full.at[self.block(d, dx, 0, dy)],
            self.acc.at[d, dx, dy],
            self.local.at[len(self.mine)],
        )
        self.mine[key].start()

    def pair(self, d, dx, dy):
        self.mine[(d, dx, dy)].wait()
        self.arrived(("c", d, dx, dy))
        self.add(d, dx, dy, self.peer.at[d, dx, dy], 0, self.n)

    def add(self, d, dx, dy, other, lo, hi):
        @pl.loop(lo, hi)
        def _(i):
            total = self.acc[d, dx, dy, i].astype(f32) + other[i - lo].astype(f32)
            self.acc[d, dx, dy, i] = total.astype(bf16)

    def corner(self, d):
        self.pair(d, 1, 1)
        h, n = self.half, self.n
        self.start(("xd", d), self.acc.at[d, 1, 1, pl.ds(0, h)], self.cor.at[d, pl.ds(0, h)], dx=1)
        self.start(
            ("yd", d), self.acc.at[d, 1, 1, pl.ds(h, n - h)], self.cor.at[d, pl.ds(h, n - h)], dy=1
        )

    def sides(self, d):
        h, n = self.half, self.n
        self.pair(d, 1, 0)
        self.arrived(("yd", d))
        self.add(d, 1, 0, self.cor.at[d, pl.ds(h, n - h)], h, n)
        self.start(("x", d), self.acc.at[d, 1, 0], self.side.at[d, 0], dx=1)
        self.pair(d, 0, 1)
        self.arrived(("xd", d))
        self.add(d, 0, 1, self.cor.at[d, pl.ds(0, h)], 0, h)
        self.start(("y", d), self.acc.at[d, 0, 1], self.side.at[d, 1], dy=1)

    def along(self, d):
        self.pair(d, 0, 0)
        self.arrived(("x", d))
        self.arrived(("y", d))

        @pl.loop(0, self.n)
        def _(i):
            total = (
                self.acc[d, 0, 0, i].astype(f32)
                + self.side[d, 0, i].astype(f32)
                + self.side[d, 1, i].astype(f32)
            )
            self.acc[d, 0, 0, i] = total.astype(bf16)

        if d > 0:
            self.start(("z", d), self.acc.at[d, 0, 0], self.col.at[d - 1], d=d)

    def step(self, i, out=None):
        if i == 0:
            for dx, dy in ((1, 1), (1, 0), (0, 1), (0, 0)):
                for d in (2, 3, 0, 1):
                    self.core(d, dx, dy)
            self.corner(2)
            self.corner(3)
        elif i == 1:
            self.sides(2)
            self.corner(0)
            self.corner(1)
        elif i == 2:
            self.along(2)
            self.sides(3)
        elif i == 3:
            self.sides(1)
            self.sides(0)
        elif i == 4:
            self.along(3)
            self.along(1)
        else:
            self.along(0)
            for d in (1, 2, 3):
                self.arrived(("z", d))

            @pl.loop(0, self.n)
            def _(i):
                out[i] = (
                    (self.acc[0, 0, 0, i].astype(f32) + self.col[0, i].astype(f32))
                    + self.col[1, i].astype(f32)
                ) + self.col[2, i].astype(f32)

            self.sent()


SCATTER_STEPS = 6


def scatter_scratch(n):
    return [
        pltpu.VMEM((4, 2, 2, n, B, B), bf16),
        pltpu.VMEM((4, 2, 2, n, B, B), bf16),
        pltpu.VMEM((4, 2, n, B, B), bf16),
        pltpu.VMEM((4, n, B, B), bf16),
        pltpu.VMEM((3, n, B, B), bf16),
        pltpu.SemaphoreType.DMA((COPIES,)),
        pltpu.SemaphoreType.DMA((COPIES,)),
        pltpu.SemaphoreType.DMA((16,)),
    ]


def gather_scratch():
    return [
        pltpu.SemaphoreType.DMA((COPIES,)),
        pltpu.SemaphoreType.DMA((COPIES,)),
        pltpu.SemaphoreType.DMA(()),
    ]


class Local:
    def __init__(self, sems):
        self.sems = sems
        self.made = []

    def start(self, src, dst):
        copy = pltpu.make_async_copy(src, dst, self.sems.at[len(self.made)])
        copy.start()
        self.made.append(copy)
        return copy

    def finish(self):
        for copy in self.made:
            copy.wait()


def spread_table(table_ref, wide, spread):
    wide[...] = jnp.zeros_like(wide)
    wide[:, : table_ref.shape[1]] = table_ref[...]
    for h in range(H):
        for c in range(spread.shape[1]):
            spread[h, c] = jnp.broadcast_to(wide[h : h + 1, c * B : (c + 1) * B], (8, B))


def turn_index(rel_ref, square, out_ref):
    square[...] = jnp.zeros_like(square)
    square[:NPOS, :NPOS] = rel_ref[...].astype(f32)
    out_ref[...] = square[...].T[:NP].astype(jnp.int32)


def lookup_rows(idx_ref, spread, out_ref, lo, hi):
    chunks = spread.shape[1]

    @pl.loop(lo, hi)
    def _(jt):
        rows = pl.ds(pl.multiple_of(jt * 8, 8), 8)
        real = jt * 8 + lax.broadcasted_iota(jnp.int32, (8, B), 0) < NPOS
        for half in range(NL // B):
            lanes = slice(half * B, (half + 1) * B)
            idx = idx_ref[rows, lanes]
            low = jnp.bitwise_and(idx, B - 1)
            high = jnp.right_shift(idx, 7)
            for h in range(H):
                acc = jnp.take_along_axis(spread[h, 0], low, axis=1, mode="promise_in_bounds")
                for c in range(1, chunks):
                    part = jnp.take_along_axis(spread[h, c], low, axis=1, mode="promise_in_bounds")
                    acc = jnp.where(high == c, part, acc)
                out_ref[h, rows, lanes] = jnp.where(real, acc, -1e30)


JB = 8


def accumulate_rows(grid_ref, idx_ref, out_ref):
    chunks = out_ref.shape[1] // B
    out_ref[...] = jnp.zeros_like(out_ref)
    lo_rows = lax.broadcasted_iota(jnp.int32, (B, NL), 0)

    @pl.loop(0, NP // JB)
    def _(jb):
        idx_all = idx_ref[pl.ds(pl.multiple_of(jb * JB, JB), JB), :]
        lefts = []
        rights = []
        for jj in range(JB):
            values = grid_ref[:, jb * JB + jj, :]
            values = jnp.concatenate([values, jnp.zeros((16 - H, NL), f32)], axis=0)
            idx = idx_all[jj : jj + 1]
            low = jnp.bitwise_and(idx, B - 1)
            high = jnp.right_shift(idx, 7)
            rights.append(jnp.where(lo_rows == low, 1.0, 0.0).astype(bf16))
            lefts.append(
                jnp.concatenate(
                    [jnp.where(high == c, values, 0.0) for c in range(chunks)], axis=0
                ).astype(bf16)
            )
        got = dot_nt(jnp.concatenate(lefts, axis=1), jnp.concatenate(rights, axis=1))
        for c in range(chunks):
            out_ref[:, c * B : (c + 1) * B] += got[c * 16 : (c + 1) * 16]


def pad_rows(x):
    return jnp.concatenate([x, jnp.zeros((NL - NP, x.shape[1]), x.dtype)], axis=0)


LANES = D // B


def load_rows(ref, first, count):
    return jnp.concatenate(
        [ref[pl.ds(first * LANES + c, count, stride=LANES), :] for c in range(LANES)], axis=1
    )


def store_rows(ref, first, values):
    count = values.shape[0]
    for c in range(LANES):
        ref[pl.ds(first * LANES + c, count, stride=LANES), :] = values[:, c * B : (c + 1) * B]


def real_rows():
    return lax.broadcasted_iota(jnp.int32, (NP, 1), 0) < NPOS


def forward_kernel(comm, own, tokens, vec, rel, table, *refs):
    refs = list(refs)
    if comm:
        attn_state, mlp_state = refs[:2]
        refs = refs[2:]
    else:
        full = refs.pop(0)
    w_o, q_o, k_o, v_o, att_o, mid_o, bra_o, n2_o, bias_o, tok_o, lse, idx = refs[:12]
    refs = refs[12:]
    if comm:
        mlp_all = refs.pop(0)
    w, q, k, v, att, mid, bra, n2, bias, tok, n1, wide, square, spread, long, out_sems = refs[:16]
    refs = refs[16:]
    out = Local(out_sems)
    imgs = q.shape[0]
    edge = tokens.shape[1] // 16 * 16

    if comm:
        a32, m32, a16, m16, full, load_sems = refs[:6]
        a_sems = refs[6:9]
        m_sems = refs[9:12]
        na, nm = a16.shape[0], m16.shape[0]
        load = Local(load_sems)
        first = load.start(attn_state.at[:, 0], a32)
        second = load.start(mlp_state.at[0, :, 0], m32)
        place = Place()
        place.greet()
        first.wait()
        a16[...] = a32[...].astype(bf16)
        moves_a = Gather(place, a16, full, na, *a_sems)
        moves_m = Gather(place, m16, mlp_all, nm, *m_sems)
        step_a = moves_a.step
        step_m = moves_m.step
        step_a(0)
        second.wait()
        m16[...] = m32[...].astype(bf16)
    else:
        step_a = step_m = lambda i: None
    plan = {("proj", 3): 1, ("pair", 1): 2, ("pair", 9): 3, ("pair", 16): 4, ("pair", 24): 5}

    def hook(*at):
        if at in plan:
            step_m(plan[at])

    long[edge : edge + 16] = jnp.zeros((16, D), f32)
    long[:edge] = tokens[0, :edge].astype(f32)
    long[edge : tokens.shape[1]] = tokens[0, edge:].astype(f32)
    for img in range(imgs):
        x = jnp.where(real_rows(), long[img * NPOS : img * NPOS + NP], 0.0)
        tok[img] = x.astype(bf16)
        x, _ = norm_parts(x)
        n1[img * NP : (img + 1) * NP] = (x * vec[0:1] + vec[1:2]).astype(bf16)
    out.start(tok, tok_o)
    spread_table(table, wide, spread)
    turn_index(rel, square, idx)
    step_a(1)
    tiles = NP // 8
    lookup_rows(idx, spread, bias, 0, tiles // 3)
    step_a(2)
    lookup_rows(idx, spread, bias, tiles // 3, 2 * tiles // 3)
    step_a(3)
    lookup_rows(idx, spread, bias, 2 * tiles // 3, tiles)
    out.start(bias, bias_o)
    step_a(4)
    step_a(5)
    step_m(0)
    step_a(6)

    @pl.loop(0, own.shape[0])
    def _(b):
        m = b // (T * T)
        r = lax.rem(b // T, T)
        c = lax.rem(b, T)
        w[m, pl.ds(pl.multiple_of(r * B, B), B), pl.ds(pl.multiple_of(c * B, B), B)] = full[own[b]]

    out.start(w, w_o)
    for m, (dst, row, scale) in enumerate(((q, 2, HD**-0.5), (k, None, 1.0), (v, 3, 1.0))):
        for n in range(D // NL):
            lanes = slice(n * NL, (n + 1) * NL)
            part = dot_nn(n1[...], w[m, :, lanes])
            if row is not None:
                part = part + vec[row : row + 1, lanes]
            part = part.astype(bf16)
            if scale != 1.0:
                part = part * jnp.asarray(scale, bf16)
            for img in range(imgs):
                dst[img, :, lanes] = part[img * NP : (img + 1) * NP]
            hook("proj", m * (D // NL) + n + 1)
    out.start(q, q_o)
    out.start(k, k_o)
    out.start(v, v_o)

    side = lax.broadcasted_iota(jnp.int32, (1, B), 1) // HD
    for img in range(imgs):
        for pair in range(H // 2):
            lanes = slice(pair * B, (pair + 1) * B)
            k_pair = k[img, :, lanes]
            q_pair = pad_rows(q[img, :, lanes])
            v_turn = v[img, :, lanes].astype(f32).T.astype(bf16)
            mixed = []
            for sub in range(2):
                h = pair * 2 + sub
                q_one = jnp.where(side == sub, q_pair, jnp.zeros_like(q_pair))
                s = dot_nt(k_pair, q_one) + bias[h]
                top = jnp.max(s, axis=0, keepdims=True)
                e = jnp.exp(s - top)
                total = jnp.sum(e, axis=0, keepdims=True)
                o = dot_nn(v_turn[sub * HD : (sub + 1) * HD], e.astype(bf16))
                mixed.append(o * (1.0 / total))
                lse[img, h : h + 1] = top + jnp.log(total)
            both = jnp.concatenate(mixed, axis=0).T
            att[img, :, lanes] = both[:NP].astype(bf16)
            hook("pair", img * (H // 2) + pair + 1)
    out.start(att, att_o)

    @pl.loop(0, imgs)
    def _(img):
        branch = dot_nn(att[img], w[3]) + vec[4:5]
        bra[img] = branch
        middle = tok[img].astype(f32) + vec[5:6] * branch
        mid[img] = middle
        x, _ = norm_parts(middle)
        n2[img] = (x * vec[6:7] + vec[7:8]).astype(bf16)

    out.start(bra, bra_o)
    out.start(mid, mid_o)
    out.start(n2, n2_o)
    step_m(6)
    out.finish()


def forward_attention(comm, own, tokens, vec, rel, table, attn, mlp=None):
    imgs = tokens.shape[1] // NPOS
    big = ((imgs, NP, D), bf16)
    tall = ((imgs, NP, D), f32)
    kept = [
        ((4, D, D), bf16),
        big,
        big,
        big,
        big,
        tall,
        tall,
        big,
        ((H, NP, NL), f32),
        big,
    ]
    out_shape = [shape(*k) for k in kept] + [shape((imgs, H, NL), f32), shape((NP, NL), jnp.int32)]
    out_specs = [ANY] * len(kept) + [VMEM, VMEM]
    wide = -(-table.shape[1] // B) * B
    scratch = [pltpu.VMEM(*k) for k in kept] + [
        pltpu.VMEM((imgs * NP, D), bf16),
        pltpu.VMEM((H, wide), f32),
        pltpu.VMEM((NL, NL), f32),
        pltpu.VMEM((H, wide // B, 8, B), f32),
        pltpu.VMEM((tokens.shape[1] // 16 * 16 + 16, D), f32),
        pltpu.SemaphoreType.DMA((len(kept),)),
    ]
    args = [own, tokens, vec, rel, table, attn]
    specs = [SMEM, VMEM, VMEM, VMEM, VMEM]
    params = dict(vmem_limit_bytes=LIMIT)
    if comm:
        na, nm = attn.shape[0], mlp.shape[1]
        args.append(mlp)
        specs += [ANY, ANY]
        out_shape.append(shape((32 * nm, B, B), bf16))
        out_specs.append(ANY)
        scratch += [
            pltpu.VMEM((na, B, B), f32),
            pltpu.VMEM((nm, B, B), f32),
            pltpu.VMEM((na, B, B), bf16),
            pltpu.VMEM((nm, B, B), bf16),
            pltpu.VMEM((32 * na, B, B), bf16),
            pltpu.SemaphoreType.DMA((2,)),
        ]
        scratch += gather_scratch() + gather_scratch()
        params.update(collective_id=0, has_side_effects=True)
    else:
        specs.append(VMEM)
    return pl.pallas_call(
        partial(forward_kernel, comm),
        in_specs=specs,
        out_specs=out_specs,
        out_shape=out_shape,
        scratch_shapes=scratch,
        compiler_params=pltpu.CompilerParams(**params),
        name="forward_attention",
    )(*args)


CH = 512


def mlp_kernel(
    parts,
    each,
    own,
    mid_h,
    bra_h,
    n2,
    cot,
    slots,
    vec,
    upb,
    out,
    gmid,
    gbra,
    sums,
    bgrad,
    tiles_out,
    mid,
    bra,
    last,
    w1,
    w2,
    gs,
    act,
    gh,
    summed,
    gn2,
    tiles,
    sem_in,
    sem_out,
    sem_load,
):
    imgs = mid.shape[0]
    length = cot.shape[0] // LANES
    chunks = FF // CH
    per = CH // B
    half = own.shape[0] // 2
    local = half // T

    def place(slot, p):
        return (slot // each) * (parts * each) + p * each + lax.rem(slot, each)

    def tile_blocks(c, t):
        g = c * per + lax.rem(t, per)
        g2 = c * per + t // T
        up = place(own[(t // per) * local + lax.rem(g, local)], g // local)
        down = place(own[half + lax.rem(g2, local) * T + lax.rem(t, T)], g2 // local)
        return up, down

    @pl.loop(0, chunks)
    def _(c):
        @pl.loop(0, T * per)
        def _(t):
            up, down = tile_blocks(c, t)
            r = pl.multiple_of((t // per) * B, B)
            cc = pl.multiple_of(lax.rem(t, per) * B, B)
            pltpu.make_async_copy(
                slots.at[up], w1.at[c, pl.ds(r, B), pl.ds(cc, B)], sem_in.at[c]
            ).start()
            r = pl.multiple_of((t // T) * B, B)
            cc = pl.multiple_of(lax.rem(t, T) * B, B)
            pltpu.make_async_copy(
                slots.at[down], w2.at[c, pl.ds(r, B), pl.ds(cc, B)], sem_in.at[c]
            ).start()

    load = Local(sem_load)
    load.start(mid_h, mid)
    load.start(bra_h, bra)
    last[...] = jnp.zeros_like(last)
    last[:NPOS] = load_rows(cot, length - NPOS, NPOS)

    def upstream(img):
        if img == imgs - 1:
            return last[...]
        return jnp.where(real_rows(), load_rows(cot, img * NPOS, NP), 0.0)

    for img in range(imgs):
        gs[img * NP : (img + 1) * NP] = (vec[9:10] * upstream(img)).astype(bf16)
    summed[...] = jnp.zeros_like(summed)
    gn2[...] = jnp.zeros_like(gn2)

    @pl.loop(0, chunks)
    def _(c):
        pltpu.make_async_copy(w1.at[c], w1.at[c], sem_in.at[c]).wait()
        pltpu.make_async_copy(w2.at[c], w2.at[c], sem_in.at[c]).wait()
        span = pl.ds(pl.multiple_of(c * CH, CH), CH)
        bias_sum = jnp.zeros((1, CH), f32)
        for rb in range(imgs // 2):
            block = slice(rb * 2 * NP, (rb + 1) * 2 * NP)
            hid = dot_nn(n2[block], w1[c]) + upb[:, span]
            back = dot_nt(gs[block], w2[c])
            phi = 0.5 * (1.0 + lax.erf(hid * (1.0 / math.sqrt(2.0))))
            density = jnp.exp(-0.5 * hid * hid) * (1.0 / math.sqrt(2.0 * math.pi))
            a = (hid * phi).astype(bf16)
            g = (back * (phi + hid * density)).astype(bf16)
            act[block] = a
            gh[block] = g
            bias_sum = bias_sum + jnp.sum(g.astype(f32), axis=0, keepdims=True)
            summed[block] += dot_nn(a, w2[c])
            gn2[block] += dot_nt(g, w1[c])
        bgrad[:, span] = bias_sum
        up_grad = dot_tn(n2[...], gh[...])
        down_grad = dot_tn(act[...], gs[...])
        for r in range(T):
            for cc in range(per):
                tiles[c, r * per + cc] = up_grad[
                    r * B : (r + 1) * B, cc * B : (cc + 1) * B
                ].astype(bf16)
        for r in range(per):
            for cc in range(T):
                tiles[c, T * per + r * T + cc] = down_grad[
                    r * B : (r + 1) * B, cc * B : (cc + 1) * B
                ].astype(bf16)

        @pl.loop(0, T * per)
        def _(t):
            up, down = tile_blocks(c, t)
            pltpu.make_async_copy(tiles.at[c, t], tiles_out.at[up], sem_out).start()
            pltpu.make_async_copy(tiles.at[c, T * per + t], tiles_out.at[down], sem_out).start()

    load.finish()
    s4 = jnp.zeros((1, D), f32)
    s5 = jnp.zeros((1, D), f32)
    s6 = jnp.zeros((1, D), f32)
    s7 = jnp.zeros((1, D), f32)
    s8 = jnp.zeros((1, D), f32)
    s9 = jnp.zeros((1, D), f32)
    for img in range(imgs):
        block = slice(img * NP, (img + 1) * NP)
        up = upstream(img)
        middle = mid[img]
        sm = summed[block] + vec[8:9]
        s9 += jnp.sum(up * sm, axis=0, keepdims=True)
        s8 += jnp.sum(gs[block].astype(f32), axis=0, keepdims=True)
        x, inv = norm_parts(middle)
        gn = gn2[block]
        s6 += jnp.sum(gn * x, axis=0, keepdims=True)
        s7 += jnp.sum(gn, axis=0, keepdims=True)
        gm = up + norm_back(gn, x, inv, vec[6:7])
        gmid[img] = gm
        gb = (vec[5:6] * gm).astype(bf16)
        gbra[img] = gb
        s4 += jnp.sum(gb.astype(f32), axis=0, keepdims=True)
        s5 += jnp.sum(gm * bra[img], axis=0, keepdims=True)
        summed[img * NPOS : img * NPOS + NP] = middle + vec[9:10] * sm
    edge = length // 16 * 16
    out[0, :edge] = summed[:edge].astype(bf16)
    out[0, edge:] = summed[edge:length].astype(bf16)
    sums[...] = jnp.concatenate([s4, s5, s6, s7, s8, s9, s9, s9], axis=0)
    pltpu.make_async_copy(tiles, tiles, sem_out).wait()


def feed_forward(mid, bra, n2, cot, slots, own, vec, up_bias, parts, each):
    imgs = mid.shape[0]
    rows = imgs * NP
    chunks = FF // CH
    per = CH // B
    return pl.pallas_call(
        partial(mlp_kernel, parts, each),
        in_specs=[SMEM, ANY, ANY, VMEM, VMEM, ANY, VMEM, VMEM],
        out_specs=[VMEM] * 5 + [ANY],
        out_shape=[
            shape((1, imgs * NPOS, D), bf16),
            shape((imgs, NP, D), f32),
            shape((imgs, NP, D), bf16),
            shape((8, D), f32),
            shape((1, FF), f32),
            shape(slots.shape, bf16),
        ],
        scratch_shapes=[
            pltpu.VMEM((imgs, NP, D), f32),
            pltpu.VMEM((imgs, NP, D), f32),
            pltpu.VMEM((NP, D), f32),
            pltpu.VMEM((chunks, D, CH), bf16),
            pltpu.VMEM((chunks, CH, D), bf16),
            pltpu.VMEM((rows, D), bf16),
            pltpu.VMEM((rows, CH), bf16),
            pltpu.VMEM((rows, CH), bf16),
            pltpu.VMEM((rows, D), f32),
            pltpu.VMEM((rows, D), f32),
            pltpu.VMEM((chunks, 2 * T * per, B, B), bf16),
            pltpu.SemaphoreType.DMA((chunks,)),
            pltpu.SemaphoreType.DMA(()),
            pltpu.SemaphoreType.DMA((2,)),
        ],
        compiler_params=pltpu.CompilerParams(vmem_limit_bytes=LIMIT),
        name="feed_forward",
    )(own, mid, bra, n2.reshape(rows, D), cot, slots, vec, up_bias)


def backward_kernel(comm, gbra, lse, vec, idx, *refs):
    refs = list(refs)
    w_h, v_h, k_h, q_h, bias_h, att_h, tok_h, gmid_h = refs[:8]
    refs = refs[8:]
    if comm:
        mlp_full = refs.pop(0)
    gin, table, sums, tiles_o = refs[:4]
    refs = refs[4:]
    if comm:
        mlp_mine = refs.pop(0)
    w, v, k, q, bias, att, tok, gmid = refs[:8]
    n1, gatt, gqkv, grid, tiles, load_sems, out_sem = refs[8:15]
    refs = refs[15:]
    imgs = q.shape[0]

    if comm:
        place = Place()
        place.greet()
        moves = Scatter(place, mlp_full, mlp_mine.shape[0], *refs)
        step = moves.step
    else:
        step = lambda i, out=None: None
    load = Local(load_sems)
    got_w, got_v, got_k, got_q, got_bias, got_att, got_tok, got_gmid = [
        load.start(src, dst)
        for src, dst in zip(
            (w_h, v_h, k_h, q_h, bias_h, att_h, tok_h, gmid_h), (w, v, k, q, bias, att, tok, gmid)
        )
    ]
    step(0)
    got_w.wait()
    for n in range(D // NL):
        lanes = slice(n * NL, (n + 1) * NL)
        got = dot_nt(gbra[...], w[3, lanes, :]).astype(bf16)
        for img in range(imgs):
            gatt[img, :, lanes] = got[img * NP : (img + 1) * NP]
    grid[...] = jnp.zeros_like(grid)
    got_v.wait()
    got_k.wait()
    got_q.wait()
    got_bias.wait()
    plan = {4: 1, 12: 2, 18: 3}

    side = lax.broadcasted_iota(jnp.int32, (1, B), 1) // HD
    for img in range(imgs):
        here = slice(img * NP, (img + 1) * NP)
        for pair in range(H // 2):
            lanes = slice(pair * B, (pair + 1) * B)
            k_pair = k[img, :, lanes]
            v_pair = v[img, :, lanes]
            q_pair = pad_rows(q[img, :, lanes])
            g_pair = pad_rows(gatt[img, :, lanes])
            k_turn = k_pair.astype(f32).T.astype(bf16)
            gq = []
            gk = jnp.zeros((NP, B), f32)
            gv = jnp.zeros((NP, B), f32)
            for sub in range(2):
                h = pair * 2 + sub
                q_one = jnp.where(side == sub, q_pair, jnp.zeros_like(q_pair))
                g_one = jnp.where(side == sub, g_pair, jnp.zeros_like(g_pair))
                s = dot_nt(k_pair, q_one) + bias[h]
                p = jnp.exp(s - lse[img, h : h + 1])
                dp = dot_nt(v_pair, g_one)
                gv = gv + dot_nn(p.astype(bf16), g_one)
                inner = jnp.sum(p * dp, axis=0, keepdims=True)
                ds = (p * (dp - inner)).astype(bf16)
                gk = gk + dot_nn(ds, q_one)
                gq.append(dot_nn(k_turn[sub * HD : (sub + 1) * HD], ds))
                grid[h] += ds.astype(f32)
            turned = jnp.concatenate(gq, axis=0).T
            gqkv[here, lanes] = (turned[:NP] * HD**-0.5).astype(bf16)
            gqkv[here, D + pair * B : D + (pair + 1) * B] = gk.astype(bf16)
            gqkv[here, 2 * D + pair * B : 2 * D + (pair + 1) * B] = gv.astype(bf16)
            if img * (H // 2) + pair + 1 in plan:
                step(plan[img * (H // 2) + pair + 1])

    def put(m, n, grad):
        for r in range(T):
            for cc in range(NL // B):
                tiles[m * T * T + r * T + n * (NL // B) + cc] = grad[
                    r * B : (r + 1) * B, cc * B : (cc + 1) * B
                ].astype(bf16)

    got_att.wait()
    got_tok.wait()
    for img in range(imgs):
        x, _ = norm_parts(tok[img].astype(f32))
        n1[img * NP : (img + 1) * NP] = (x * vec[0:1] + vec[1:2]).astype(bf16)
    for n in range(D // NL):
        lanes = slice(n * NL, (n + 1) * NL)
        put(3, n, dot_tn(att[...], gbra[:, lanes]))
    for m in range(3):
        for n in range(D // NL):
            put(m, n, dot_tn(n1[...], gqkv[:, m * D + n * NL : m * D + (n + 1) * NL]))
    out = pltpu.make_async_copy(tiles, tiles_o, out_sem)
    out.start()
    step(4)
    accumulate_rows(grid, idx, table)

    got_gmid.wait()
    s0 = jnp.zeros((1, D), f32)
    s1 = jnp.zeros((1, D), f32)
    s2 = jnp.zeros((1, D), f32)
    s3 = jnp.zeros((1, D), f32)
    for img in range(imgs):
        here = slice(img * NP, (img + 1) * NP)
        gq = gqkv[here, 0:D]
        gk = gqkv[here, D : 2 * D]
        gv = gqkv[here, 2 * D : 3 * D]
        gn = dot_nt(gq, w[0]) + dot_nt(gk, w[1]) + dot_nt(gv, w[2])
        x, inv = norm_parts(tok[img].astype(f32))
        s0 += jnp.sum(gn * x, axis=0, keepdims=True)
        s1 += jnp.sum(gn, axis=0, keepdims=True)
        s2 += jnp.sum(gq.astype(f32), axis=0, keepdims=True)
        s3 += jnp.sum(gv.astype(f32), axis=0, keepdims=True)
        got = gmid[img] + norm_back(gn, x, inv, vec[0:1])
        store_rows(gin, img * NPOS, got[:NPOS] if img == imgs - 1 else got)
    sums[...] = jnp.concatenate([s0, s1, s2, s3, s3, s3, s3, s3], axis=0)
    if comm:
        step(5, mlp_mine)
    out.wait()


def backward_attention(comm, saved, gmid, gbra, vec, wide_total, mlp_full=None):
    w, q, k, v, att, mid, bra, n2, bias, tok, lse, idx = saved
    imgs = tok.shape[0]
    rows = imgs * NP
    att = att.reshape(rows, D)
    loaded = [w, v, k, q, bias, att, tok, gmid]
    args = [gbra.reshape(rows, D), lse, vec, idx] + loaded
    specs = [VMEM] * 4 + [ANY] * 8
    out_shape = [
        shape((imgs * NPOS * LANES, B), f32),
        shape((16, wide_total), f32),
        shape((8, D), f32),
        shape((4 * T * T, B, B), bf16),
    ]
    out_specs = [VMEM] * 3 + [ANY]
    scratch = [pltpu.VMEM(x.shape, x.dtype) for x in loaded] + [
        pltpu.VMEM((rows, D), bf16),
        pltpu.VMEM((imgs, NP, D), bf16),
        pltpu.VMEM((rows, 3 * D), bf16),
        pltpu.VMEM((H, NP, NL), f32),
        pltpu.VMEM((4 * T * T, B, B), bf16),
        pltpu.SemaphoreType.DMA((8,)),
        pltpu.SemaphoreType.DMA(()),
    ]
    params = dict(vmem_limit_bytes=LIMIT)
    if comm:
        n = mlp_full.shape[0] // 32
        args.append(mlp_full)
        specs.append(ANY)
        out_shape.append(shape((n, B, B), f32))
        out_specs.append(VMEM)
        scratch += scatter_scratch(n)
        params.update(collective_id=1, has_side_effects=True)
    return pl.pallas_call(
        partial(backward_kernel, comm),
        in_specs=specs,
        out_specs=out_specs,
        out_shape=out_shape,
        scratch_shapes=scratch,
        compiler_params=pltpu.CompilerParams(**params),
        name="backward_attention",
    )(*args)


NB = 16
GROUP = B // NB


def split_two(x):
    first = x.astype(bf16)
    return first, (x - first.astype(f32)).astype(bf16)


def wide_dot(x, y, dims):
    xa, xb = split_two(x)
    ya, yb = split_two(y)
    xs = jnp.concatenate([xa, xa, xb], axis=dims[0])
    ys = jnp.concatenate([ya, yb, ya], axis=dims[1])
    return lax.dot_general(
        xs, ys, (((dims[0],), (dims[1],)), ((), ())), preferred_element_type=f32
    )


def unit_inverse(diag):
    lane = lax.broadcasted_iota(jnp.int32, (NB, B), 1)
    row = lax.broadcasted_iota(jnp.int32, (NB, B), 0)
    inner = jnp.bitwise_and(lane, NB - 1)
    outer = lane - inner
    left = diag
    right = jnp.where(row == inner, 1.0, 0.0)
    def pick(x, k):
        return jnp.take_along_axis(x, outer[: x.shape[0]] + k, axis=1, mode="promise_in_bounds")

    for k in range(0, NB, 2):
        first, second = pick(left, k), pick(left, k + 1)
        a, b, c = first[k : k + 1], second[k : k + 1], second[k + 1 : k + 2]
        det = a * c - b * b
        rc = pl.reciprocal(det, approx=True)
        rc = rc * (2.0 - det * rc)
        ra = pl.reciprocal(a, approx=True)
        ra = ra * (2.0 - a * ra)
        r1, r2 = left[k : k + 1], left[k + 1 : k + 2]
        below = inner[:1] > k + 1
        f1 = jnp.where(below, (c * r1 - b * r2) * rc, jnp.where(inner[:1] == k + 1, r1 * ra, 0.0))
        f2 = jnp.where(below, (a * r2 - b * r1) * rc, 0.0)
        left = left - f1 * first - f2 * second
        right = right - f1 * pick(right, k) - f2 * pick(right, k + 1)
    pivots = jnp.sum(jnp.where(row == inner, left, 0.0), axis=0, keepdims=True)
    return right * lax.rsqrt(pivots)


def orth_turned(mats, between=None):
    count = len(mats)
    groups = -(-count // GROUP)
    size = -(-count // groups)
    members = [list(range(g * size, min(count, (g + 1) * size))) for g in range(groups)]
    tails = []
    for a in mats:
        turned = a.T
        tails.append(jnp.concatenate([wide_dot(turned, turned, (1, 1)), turned], axis=1))
    own_block = (
        lax.broadcasted_iota(jnp.int32, (B, B), 0) // NB
        == lax.broadcasted_iota(jnp.int32, (B, B), 1) // NB
    )
    outs = [[] for _ in range(count)]
    for p in range(B // NB):
        base = p * NB
        for ids in members:
            fill = ids + [ids[-1]] * (GROUP - len(ids))
            strips = jnp.concatenate([tails[m][:NB] for m in fill], axis=0)
            turned = strips[:, :B].T
            unit = unit_inverse(turned[base : base + NB])
            spread = jnp.where(own_block, jnp.concatenate([unit] * GROUP, axis=0), 0.0)
            u = wide_dot(spread, strips, (0, 0))
            for at, m in enumerate(ids):
                um = u[at * NB : (at + 1) * NB]
                outs[m].append(um[:, B:])
                if base + NB < B:
                    tails[m] = tails[m][NB:] - wide_dot(um[:, base + NB : B], um, (0, 0))
        if between is not None:
            between(p)
    return [jnp.concatenate(o, axis=0) for o in outs]


def soap_slots(base, owner, grads, state, update, copy, between=None):
    count = grads.shape[0]
    mats = []
    gs = []
    for i in range(count):
        named = jnp.where(owner[...] == base + i, 1.0, 0.0)
        named = jnp.max(named, axis=1, keepdims=True)
        g = jnp.where(named > 0.0, grads[i].astype(f32), 0.0)
        gs.append(g)
        left = beta_stat * state[i, 3] + (1.0 - beta_stat) * wide_dot(g, g, (1, 1))
        right = beta_stat * state[i, 4] + (1.0 - beta_stat) * wide_dot(g, g, (0, 0))
        mats.append(wide_dot(left, state[i, 5], (1, 0)))
        mats.append(wide_dot(right, state[i, 6], (1, 0)))
    if between is not None:
        between(-1)
    turned = orth_turned(mats, between)
    fix_one = 1.0 - beta_one**STEP
    fix_two = 1.0 - beta_two**STEP
    for i in range(count):
        tl, tr = turned[2 * i], turned[2 * i + 1]
        rotated = wide_dot(wide_dot(tl, gs[i], (1, 0)), tr, (1, 1))
        new_first = beta_one * state[i, 1] + (1.0 - beta_one) * rotated
        new_second = beta_two * state[i, 2] + (1.0 - beta_two) * rotated * rotated
        normalized = new_first / fix_one / (jnp.sqrt(new_second / fix_two) + adam_eps)
        step = wide_dot(wide_dot(tl, normalized, (0, 0)), tr, (1, 0))
        weight = state[i, 0]
        weight = weight - matrix_rate * (step + decay_rate * weight)
        update[i, 0] = weight
        update[i, 1] = new_first
        update[i, 2] = new_second
        update[i, 3] = tl.T
        update[i, 4] = tr.T
        copy[i] = weight.astype(bf16)


def soap_kernel(first_slot, passed, owner, grads, state, *refs):
    kept, refs = refs[:passed], refs[passed:]
    update, copy = refs[:2]
    through, held, sems = refs[2 : 2 + passed], refs[2 + passed : 2 + 2 * passed], refs[2 + 2 * passed :]
    count = grads.shape[0]
    between = None
    if passed:
        into, out = Local(sems[0]), Local(sems[1])
        for src, dst in zip(kept, held):
            into.start(src, dst)

        def between(p):
            if p == 2:
                into.finish()
                for src, dst in zip(held, through):
                    out.start(src, dst)

    first = first_slot() + pl.program_id(0) * count
    soap_slots(first, owner, grads, state, update, copy, between)
    if passed:
        out.finish()


def soap_update(grads, state, owner, first_slot, kept=()):
    slots = grads.shape[0]
    count = max(c for c in range(1, 10) if slots % c == 0)
    assert not kept or count == slots
    return pl.pallas_call(
        partial(soap_kernel, first_slot, len(kept)),
        grid=(slots // count,),
        in_specs=[
            pl.BlockSpec((1, owner.shape[0]), lambda i: (0, 0)),
            pl.BlockSpec((count, B, B), lambda i: (i, 0, 0)),
            pl.BlockSpec((count, 7, B, B), lambda i: (i, 0, 0, 0)),
        ]
        + [ANY] * len(kept),
        out_specs=[
            pl.BlockSpec((count, 5, B, B), lambda i: (i, 0, 0, 0)),
            pl.BlockSpec((count, B, B), lambda i: (i, 0, 0)),
        ]
        + [ANY] * len(kept),
        out_shape=[shape((slots, 5, B, B), f32), shape((slots, B, B), bf16)]
        + [shape(x.shape, x.dtype) for x in kept],
        scratch_shapes=[pltpu.VMEM(x.shape, x.dtype) for x in kept]
        + [pltpu.SemaphoreType.DMA((len(kept),))] * (2 if kept else 0),
        compiler_params=pltpu.CompilerParams(vmem_limit_bytes=LIMIT),
        name="soap",
    )(owner[None], grads, state, *kept)


SUM_ROWS = 40


def adam(grad, param, first, second):
    new_first = beta_one * first + (1.0 - beta_one) * grad
    new_second = beta_two * second + (1.0 - beta_two) * grad * grad
    fix_one = 1.0 - beta_one**STEP
    fix_two = 1.0 - beta_two**STEP
    step = (new_first / fix_one) / (jnp.sqrt(new_second / fix_two) + adam_eps)
    return grad, param - vector_rate * step, new_first, new_second


def finish_kernel(
    inverse,
    tiles,
    mlp_sums,
    attn_sums,
    table_sums,
    bias_sums,
    vec,
    vec_m,
    table,
    table_m,
    upb,
    upb_m,
    owner,
    mlp_mine,
    state_h,
    mine,
    vec_up,
    table_up,
    upb_up,
    update,
    copy,
    state,
    load_sem,
    full,
    part,
    other,
    column,
    sum_send,
    sum_recv,
    *scratch,
):
    place = Place()
    place.greet()
    load = pltpu.make_async_copy(state_h.at[0], state, load_sem)
    load.start()

    @pl.loop(0, full.shape[0])
    def _(slot):
        full[slot] = tiles[inverse[slot]]

    moves = Scatter(place, full, mine.shape[0], *scratch)
    sums = Copies(place, sum_send, sum_recv)
    part[0, 0:8] = mlp_sums[...]
    part[0, 8:16] = attn_sums[...]
    part[0, 16:32] = table_sums[...]
    quarter = jnp.concatenate([bias_sums[:, i * D : (i + 1) * D] for i in range(FF // D)] * 2, axis=0)
    part[0, 32:40] = quarter
    sums.start("c", part.at[0], other.at[0], dc=1)
    moves.step(0)
    load.wait()

    def total_sums():
        part[4] = ((column[0] + column[1]) + column[2]) + column[3]
        total = part.at[4]
        grad = jnp.concatenate([total[8:12], total[0:6]], axis=0)
        for i, got in enumerate(adam(grad, vec[...], vec_m[:, 0, :], vec_m[:, 1, :])):
            vec_up[:, i, :] = got
        wide = table.shape[1]
        grad = total[16 : 16 + H, 0:wide]
        for i, got in enumerate(adam(grad, table[...], table_m[:, 0, :], table_m[:, 1, :])):
            table_up[:, i, :] = got
        for j in range(FF // D):
            lanes = slice(j * D, (j + 1) * D)
            for i, got in enumerate(
                adam(total[32 + j : 33 + j], upb[:, lanes], upb_m[0:1, lanes], upb_m[1:2, lanes])
            ):
                upb_up[i : i + 1, lanes] = got

    def between(p):
        if p == -1:
            sums.arrived("c")
            part[1] = part[0] + other[0]
            sums.start("x", part.at[1], other.at[1], dx=1)
            moves.step(1)
        elif p == 1:
            sums.arrived("x")
            part[2] = part[1] + other[1]
            sums.start("y", part.at[2], other.at[2], dy=1)
            moves.step(2)
        elif p == 3:
            sums.arrived("y")
            part[3] = part[2] + other[2]
            for d in (1, 2, 3):
                sums.start(("z", d), part.at[3], column.at[place.z], d=d)
            column[place.z] = part[3]
            moves.step(3)
        elif p == 6:
            moves.step(4)

    first_slot = lax.axis_index("dp") * mlp_mine.shape[0]
    soap_slots(first_slot, owner, mlp_mine, state, update, copy, between)
    for d in (1, 2, 3):
        sums.arrived(("z", d))
    total_sums()
    moves.step(5, mine)
    sums.sent()


def finish(inverse, tiles, small, params, owner, mlp_mine, mlp_state):
    n = inverse.shape[0] // 32
    nm = mlp_mine.shape[0]
    vec, vec_m, table, table_m, upb, upb_m = params
    return pl.pallas_call(
        finish_kernel,
        in_specs=[SMEM] + [VMEM] * 13 + [ANY],
        out_specs=[VMEM] * 6,
        out_shape=[
            shape((n, B, B), f32),
            shape((vec.shape[0], 4, D), f32),
            shape((H, 4, table.shape[1]), f32),
            shape((4, FF), f32),
            shape((nm, 5, B, B), f32),
            shape((nm, B, B), bf16),
        ],
        scratch_shapes=[
            pltpu.VMEM((nm, 7, B, B), f32),
            pltpu.SemaphoreType.DMA(()),
            pltpu.VMEM((32 * n, B, B), bf16),
            pltpu.VMEM((5, SUM_ROWS, D), f32),
            pltpu.VMEM((3, SUM_ROWS, D), f32),
            pltpu.VMEM((4, SUM_ROWS, D), f32),
            pltpu.SemaphoreType.DMA((6,)),
            pltpu.SemaphoreType.DMA((6,)),
        ]
        + scatter_scratch(n),
        compiler_params=pltpu.CompilerParams(
            collective_id=2, has_side_effects=True, vmem_limit_bytes=LIMIT
        ),
        name="finish",
    )(
        inverse,
        tiles,
        *small,
        vec,
        vec_m.transpose(1, 0, 2),
        table,
        table_m.transpose(1, 0, 2),
        upb[None],
        upb_m,
        owner[None],
        mlp_mine,
        mlp_state,
    )


def body(
    tokens,
    cotangent,
    rel_index,
    attn_owner,
    mlp_owner,
    attn_state,
    mlp_state,
    vec_param,
    vec_moments,
    rel_table,
    rel_table_moments,
    up_bias,
    up_bias_moments,
):
    both = ("dp", "mp")
    parts = lax.axis_size("mp")
    comm = own_kernels(lax.axis_size("dp"), parts)
    imgs = tokens.shape[1] // NPOS
    attn_local = attn_state.shape[0]
    mlp_local = mlp_state.shape[1]
    attn_total = attn_local * lax.axis_size("dp") * parts

    def attn_first():
        return (lax.axis_index("dp") * parts + lax.axis_index("mp")) * attn_local

    def mlp_first():
        return lax.axis_index("dp") * mlp_local

    wide_total = -(-rel_table.shape[1] // B) * B
    slot_ids = jnp.arange(attn_total, dtype=jnp.int32)
    block_ids = jnp.arange(attn_owner.shape[0], dtype=jnp.int32)
    inverse = jnp.sum(
        jnp.where(attn_owner[None, :] == slot_ids[:, None], block_ids[None, :], 0), axis=1
    ).astype(jnp.int32)

    if comm:
        *saved, mlp_slots = forward_attention(
            True, attn_owner, tokens, vec_param, rel_index, rel_table, attn_state, mlp_state
        )
    else:
        attn_slots = lax.all_gather(attn_state[:, 0].astype(bf16), both, axis=0, tiled=True)
        mlp_slots = lax.all_gather(mlp_state[0, :, 0].astype(bf16), both, axis=0, tiled=True)
        saved = forward_attention(
            False, attn_owner, tokens, vec_param, rel_index, rel_table, attn_slots
        )
    w, q, k, v, att, mid, bra, n2, bias, tok, lse, idx = saved
    out, gmid, gbra, mlp_sums, bias_grad, mlp_grads = feed_forward(
        mid, bra, n2, cotangent.reshape(-1, B), mlp_slots, mlp_owner, vec_param, up_bias[None], parts, mlp_local
    )
    if comm:
        gin, table_grad, attn_sums, attn_tiles, mlp_mine = backward_attention(
            True, saved, gmid, gbra, vec_param, wide_total, mlp_grads
        )
        attn_mine, vec_up, table_up, bias_up, mlp_result, mlp_copy = finish(
            inverse,
            attn_tiles,
            (mlp_sums, attn_sums, table_grad, bias_grad),
            (vec_param, vec_moments, rel_table, rel_table_moments, up_bias, up_bias_moments),
            mlp_owner,
            mlp_mine,
            mlp_state,
        )
        vec_up = vec_up.transpose(1, 0, 2)
        table_up = table_up.transpose(1, 0, 2)
        attn_result, attn_copy, gin, mlp_result, mlp_copy = soap_update(
            attn_mine, attn_state, attn_owner, attn_first, (gin, mlp_result, mlp_copy)
        )
    else:
        gin, table_grad, attn_sums, attn_tiles = backward_attention(
            False, saved, gmid, gbra, vec_param, wide_total
        )
        mlp_mine = lax.psum_scatter(mlp_grads, both, scatter_dimension=0, tiled=True)
        attn_mine = lax.psum_scatter(attn_tiles[inverse], both, scatter_dimension=0, tiled=True)
        vector_grad = jnp.concatenate([attn_sums[:4], mlp_sums[:6]], axis=0)
        vector_total, table_total, bias_total = lax.psum(
            (vector_grad, table_grad[:H, : rel_table.shape[1]], bias_grad[0]), both
        )
        vec_up = jnp.stack(adam(vector_total, vec_param, vec_moments[0], vec_moments[1]))
        table_up = jnp.stack(
            adam(table_total, rel_table, rel_table_moments[0], rel_table_moments[1])
        )
        bias_up = jnp.stack(adam(bias_total, up_bias, up_bias_moments[0], up_bias_moments[1]))
        attn_result, attn_copy = soap_update(attn_mine, attn_state, attn_owner, attn_first)
        mlp_result, mlp_copy = soap_update(mlp_mine, mlp_state[0], mlp_owner, mlp_first)
    return (
        out,
        gin.reshape(1, imgs * NPOS, D),
        attn_result,
        attn_copy,
        mlp_result[None],
        mlp_copy[None],
        vec_up,
        table_up,
        bias_up,
    )


def solution(mesh):
    placed = (
        P(("dp", "mp"), None, None),
        P(("dp", "mp"), None, None),
        P(),
        P(),
        P(),
        P(("dp", "mp"), None, None, None),
        P("mp", "dp", None, None, None),
        P(),
        P(),
        P(),
        P(),
        P(),
        P(),
    )
    return jax.shard_map(
        body,
        mesh=mesh,
        in_specs=placed,
        out_specs=(
            P(("dp", "mp"), None, None),
            P(("dp", "mp"), None, None),
            P(("dp", "mp"), None, None, None),
            P(("dp", "mp"), None, None),
            P("mp", "dp", None, None, None),
            P("mp", "dp", None, None),
            P(),
            P(),
            P(),
        ),
        check_vma=False,
    )
```

```python
from functools import partial
import math

import jax
import jax.numpy as jnp
from jax import lax
from jax.experimental import pallas as pl
from jax.experimental.pallas import tpu as pltpu
from jax.sharding import PartitionSpec as P

D = 768
H = 12
HD = 64
FF = 3072
NPOS = 197
NP = 208
NL = 256
B = 128
STEP = 5
T = D // B

f32 = jnp.float32
bf16 = jnp.bfloat16

ln_eps = 1e-06
beta_one = 0.9
beta_two = 0.95
beta_stat = 0.95
adam_eps = 1e-08
matrix_rate = 0.05
vector_rate = 0.2
decay_rate = 0.05

VMEM = pl.BlockSpec(memory_space=pltpu.VMEM)
SMEM = pl.BlockSpec(memory_space=pltpu.SMEM)
ANY = pl.BlockSpec(memory_space=pl.ANY)
LIMIT = 60 << 20


def shape(dims, kind):
    return jax.ShapeDtypeStruct(dims, kind)


def dot_nn(x, y):
    return lax.dot_general(x, y, (((1,), (0,)), ((), ())), preferred_element_type=f32)


def dot_nt(x, y):
    return lax.dot_general(x, y, (((1,), (1,)), ((), ())), preferred_element_type=f32)


def dot_tn(x, y):
    return lax.dot_general(x, y, (((0,), (0,)), ((), ())), preferred_element_type=f32)


def norm_parts(values):
    centered = values - jnp.mean(values, axis=-1, keepdims=True)
    inv_std = lax.rsqrt(jnp.mean(centered * centered, axis=-1, keepdims=True) + ln_eps)
    return (centered * inv_std, inv_std)


def norm_back(grad_normed, scaled, inv_std, gain_row):
    tangent = grad_normed * gain_row
    return inv_std * (
        tangent
        - jnp.mean(tangent, axis=-1, keepdims=True)
        - scaled * jnp.mean(tangent * scaled, axis=-1, keepdims=True)
    )


MESH = pl.DeviceIdType.MESH
COPIES = 35


def own_kernels(dp_total, parts):
    return dp_total == 16 and parts == 2


class Place:
    def __init__(self):
        dp = lax.axis_index("dp")
        self.y = lax.axis_index("mp")
        self.z = dp // 4
        self.x = lax.rem(dp // 2, 2)
        self.c = lax.rem(dp, 2)

    def rank(self, d=0, dx=0, dc=0, dy=0):
        z = lax.rem(self.z + d + 4, 4)
        x = 1 - self.x if dx else self.x
        c = 1 - self.c if dc else self.c
        y = 1 - self.y if dy else self.y
        return ((z * 2 + x) * 2 + c) * 2 + y

    def device(self, d=0, dx=0, dc=0, dy=0):
        z = lax.rem(self.z + d + 4, 4)
        x = 1 - self.x if dx else self.x
        c = 1 - self.c if dc else self.c
        y = 1 - self.y if dy else self.y
        return ((z * 2 + x) * 2 + c, y)

    def greet(self):
        barrier = pltpu.get_barrier_semaphore()
        for d, dx, dc, dy in PARTNERS:
            pl.semaphore_signal(
                barrier, inc=1, device_id=self.device(d, dx, dc, dy), device_id_type=MESH
            )
        pl.semaphore_wait(barrier, len(PARTNERS))


PARTNERS = ((1, 0, 0, 0), (2, 0, 0, 0), (3, 0, 0, 0), (0, 1, 0, 0), (0, 0, 1, 0), (0, 0, 0, 1))


class Copies:
    def __init__(self, place, send, recv):
        self.place = place
        self.send = send
        self.recv = recv
        self.made = {}

    def start(self, key, src, dst, **to):
        i = len(self.made)
        copy = pltpu.make_async_remote_copy(
            src_ref=src,
            dst_ref=dst,
            send_sem=self.send.at[i],
            recv_sem=self.recv.at[i],
            device_id=self.place.device(**to),
            device_id_type=MESH,
        )
        copy.start()
        self.made[key] = copy

    def arrived(self, key):
        self.made[key].wait_recv()

    def sent(self):
        for copy in self.made.values():
            copy.wait_send()


class Gather(Copies):
    def __init__(self, place, own, full, n, send, recv, local):
        super().__init__(place, send, recv)
        self.own = own
        self.full = full
        self.n = n
        self.half = n // 2
        self.local = pltpu.make_async_copy(own, self.at(), local)

    def at(self, d=0, dx=0, dc=0, dy=0, lo=0, hi=None):
        hi = self.n if hi is None else hi
        return self.full.at[pl.ds(self.place.rank(d, dx, dc, dy) * self.n + lo, hi - lo)]

    def spread(self, d):
        src = self.own if d == 0 else self.at(d=-d)
        dst = self.at(d=-d)
        self.start(("x", d), src, dst, dx=1)
        self.start(("y", d), src, dst, dy=1)
        self.start(("c", d, 0, 0), src, dst, dc=1)

    def along(self, d):
        self.start(("z", d), self.own, self.at(), d=d)

    def share(self, d, dx, dy):
        ref = self.at(d=-d, dx=dx, dy=dy)
        self.start(("c", d, dx, dy), ref, ref, dc=1)

    def corner(self, d):
        ref = self.at(d=-d, dy=1, lo=self.half)
        self.start(("xd", d), ref, ref, dx=1)
        ref = self.at(d=-d, dx=1, hi=self.half)
        self.start(("yd", d), ref, ref, dy=1)

    def sides(self, d):
        self.arrived(("x", d))
        self.share(d, 1, 0)
        self.arrived(("y", d))
        self.share(d, 0, 1)

    def cornered(self, d):
        self.arrived(("xd", d))
        self.arrived(("yd", d))
        self.share(d, 1, 1)

    def step(self, i):
        if i == 0:
            self.local.start()
            self.along(1)
            self.spread(0)
        elif i == 1:
            self.arrived(("z", 1))
            self.along(3)
            self.spread(1)
            self.sides(0)
        elif i == 2:
            self.arrived(("z", 3))
            self.along(2)
            self.spread(3)
            self.sides(1)
            self.corner(0)
        elif i == 3:
            self.corner(1)
            self.sides(3)
        elif i == 4:
            self.arrived(("z", 2))
            self.spread(2)
            self.cornered(0)
            self.corner(3)
            self.cornered(1)
        elif i == 5:
            self.sides(2)
            self.corner(2)
            self.cornered(3)
        else:
            self.cornered(2)
            for d in range(4):
                for dx in range(2):
                    for dy in range(2):
                        self.arrived(("c", d, dx, dy))
            self.local.wait()
            self.sent()


GATHER_STEPS = 7


class Scatter(Copies):
    def __init__(self, place, full, n, acc, peer, side, corner, along, send, recv, local):
        super().__init__(place, send, recv)
        self.full = full
        self.local = local
        self.mine = {}
        self.n = n
        self.half = n // 2
        self.acc = acc
        self.peer = peer
        self.side = side
        self.cor = corner
        self.col = along

    def block(self, d, dx, dc, dy):
        return pl.ds(self.place.rank(d, dx, dc, dy) * self.n, self.n)

    def core(self, d, dx, dy):
        key = (d, dx, dy)
        self.start(
            ("c",) + key, self.full.at[self.block(d, dx, 1, dy)], self.peer.at[d, dx, dy], dc=1
        )
        self.mine[key] = pltpu.make_async_copy(
            self.full.at[self.block(d, dx, 0, dy)],
            self.acc.at[d, dx, dy],
            self.local.at[len(self.mine)],
        )
        self.mine[key].start()

    def pair(self, d, dx, dy):
        self.mine[(d, dx, dy)].wait()
        self.arrived(("c", d, dx, dy))
        self.add(d, dx, dy, self.peer.at[d, dx, dy], 0, self.n)

    def add(self, d, dx, dy, other, lo, hi):
        @pl.loop(lo, hi)
        def _(i):
            total = self.acc[d, dx, dy, i].astype(f32) + other[i - lo].astype(f32)
            self.acc[d, dx, dy, i] = total.astype(bf16)

    def corner(self, d):
        self.pair(d, 1, 1)
        h, n = self.half, self.n
        self.start(("xd", d), self.acc.at[d, 1, 1, pl.ds(0, h)], self.cor.at[d, pl.ds(0, h)], dx=1)
        self.start(
            ("yd", d), self.acc.at[d, 1, 1, pl.ds(h, n - h)], self.cor.at[d, pl.ds(h, n - h)], dy=1
        )

    def sides(self, d):
        h, n = self.half, self.n
        self.pair(d, 1, 0)
        self.arrived(("yd", d))
        self.add(d, 1, 0, self.cor.at[d, pl.ds(h, n - h)], h, n)
        self.start(("x", d), self.acc.at[d, 1, 0], self.side.at[d, 0], dx=1)
        self.pair(d, 0, 1)
        self.arrived(("xd", d))
        self.add(d, 0, 1, self.cor.at[d, pl.ds(0, h)], 0, h)
        self.start(("y", d), self.acc.at[d, 0, 1], self.side.at[d, 1], dy=1)

    def along(self, d):
        self.pair(d, 0, 0)
        self.arrived(("x", d))
        self.arrived(("y", d))

        @pl.loop(0, self.n)
        def _(i):
            total = (
                self.acc[d, 0, 0, i].astype(f32)
                + self.side[d, 0, i].astype(f32)
                + self.side[d, 1, i].astype(f32)
            )
            self.acc[d, 0, 0, i] = total.astype(bf16)

        if d > 0:
            self.start(("z", d), self.acc.at[d, 0, 0], self.col.at[d - 1], d=d)

    def step(self, i, out=None):
        if i == 0:
            for dx, dy in ((1, 1), (1, 0), (0, 1), (0, 0)):
                for d in (2, 3, 0, 1):
                    self.core(d, dx, dy)
            self.corner(2)
            self.corner(3)
        elif i == 1:
            self.sides(2)
            self.corner(0)
            self.corner(1)
        elif i == 2:
            self.along(2)
            self.sides(3)
        elif i == 3:
            self.sides(1)
            self.sides(0)
        elif i == 4:
            self.along(3)
            self.along(1)
        else:
            self.along(0)
            for d in (1, 2, 3):
                self.arrived(("z", d))

            @pl.loop(0, self.n)
            def _(i):
                out[i] = (
                    (self.acc[0, 0, 0, i].astype(f32) + self.col[0, i].astype(f32))
                    + self.col[1, i].astype(f32)
                ) + self.col[2, i].astype(f32)

            self.sent()


SCATTER_STEPS = 6


def scatter_scratch(n):
    return [
        pltpu.VMEM((4, 2, 2, n, B, B), bf16),
        pltpu.VMEM((4, 2, 2, n, B, B), bf16),
        pltpu.VMEM((4, 2, n, B, B), bf16),
        pltpu.VMEM((4, n, B, B), bf16),
        pltpu.VMEM((3, n, B, B), bf16),
        pltpu.SemaphoreType.DMA((COPIES,)),
        pltpu.SemaphoreType.DMA((COPIES,)),
        pltpu.SemaphoreType.DMA((16,)),
    ]


def gather_scratch():
    return [
        pltpu.SemaphoreType.DMA((COPIES,)),
        pltpu.SemaphoreType.DMA((COPIES,)),
        pltpu.SemaphoreType.DMA(()),
    ]


class Local:
    def __init__(self, sems):
        self.sems = sems
        self.made = []

    def start(self, src, dst):
        copy = pltpu.make_async_copy(src, dst, self.sems.at[len(self.made)])
        copy.start()
        self.made.append(copy)
        return copy

    def finish(self):
        for copy in self.made:
            copy.wait()


def spread_table(table_ref, wide, spread):
    wide[...] = jnp.zeros_like(wide)
    wide[:, : table_ref.shape[1]] = table_ref[...]
    for h in range(H):
        for c in range(spread.shape[1]):
            spread[h, c] = jnp.broadcast_to(wide[h : h + 1, c * B : (c + 1) * B], (8, B))


def turn_index(rel_ref, square, out_ref):
    square[...] = jnp.zeros_like(square)
    square[:NPOS, :NPOS] = rel_ref[...].astype(f32)
    out_ref[...] = square[...].T[:NP].astype(jnp.int32)


def lookup_rows(idx_ref, spread, out_ref, lo, hi):
    chunks = spread.shape[1]

    @pl.loop(lo, hi)
    def _(jt):
        rows = pl.ds(pl.multiple_of(jt * 8, 8), 8)
        real = jt * 8 + lax.broadcasted_iota(jnp.int32, (8, B), 0) < NPOS
        for half in range(NL // B):
            lanes = slice(half * B, (half + 1) * B)
            idx = idx_ref[rows, lanes]
            low = jnp.bitwise_and(idx, B - 1)
            high = jnp.right_shift(idx, 7)
            for h in range(H):
                acc = jnp.take_along_axis(spread[h, 0], low, axis=1, mode="promise_in_bounds")
                for c in range(1, chunks):
                    part = jnp.take_along_axis(spread[h, c], low, axis=1, mode="promise_in_bounds")
                    acc = jnp.where(high == c, part, acc)
                out_ref[h, rows, lanes] = jnp.where(real, acc, -1e30)


JB = 8


def accumulate_rows(grid_ref, idx_ref, out_ref):
    chunks = out_ref.shape[1] // B
    out_ref[...] = jnp.zeros_like(out_ref)
    lo_rows = lax.broadcasted_iota(jnp.int32, (B, NL), 0)

    @pl.loop(0, NP // JB)
    def _(jb):
        idx_all = idx_ref[pl.ds(pl.multiple_of(jb * JB, JB), JB), :]
        lefts = []
        rights = []
        for jj in range(JB):
            values = grid_ref[:, jb * JB + jj, :]
            values = jnp.concatenate([values, jnp.zeros((16 - H, NL), f32)], axis=0)
            idx = idx_all[jj : jj + 1]
            low = jnp.bitwise_and(idx, B - 1)
            high = jnp.right_shift(idx, 7)
            rights.append(jnp.where(lo_rows == low, 1.0, 0.0).astype(bf16))
            lefts.append(
                jnp.concatenate(
                    [jnp.where(high == c, values, 0.0) for c in range(chunks)], axis=0
                ).astype(bf16)
            )
        got = dot_nt(jnp.concatenate(lefts, axis=1), jnp.concatenate(rights, axis=1))
        for c in range(chunks):
            out_ref[:, c * B : (c + 1) * B] += got[c * 16 : (c + 1) * 16]


CH = 512
PER = CH // B


def chunk_slots(own, parts, each, out):
    half = own.shape[0] // 2
    local = half // T

    def place(slot, p):
        return lax.div(slot, each) * (parts * each) + p * each + lax.rem(slot, each)

    @pl.loop(0, FF // CH)
    def _(c):
        @pl.loop(0, T * PER)
        def _(t):
            g = c * PER + lax.rem(t, PER)
            g2 = c * PER + t // T
            up = own[(t // PER) * local + lax.rem(g, local)]
            down = own[half + lax.rem(g2, local) * T + lax.rem(t, T)]
            out[c * 2 * T * PER + t] = place(up, g // local)
            out[c * 2 * T * PER + T * PER + t] = place(down, g2 // local)


def pad_rows(x):
    return jnp.concatenate([x, jnp.zeros((NL - NP, x.shape[1]), x.dtype)], axis=0)


LANES = D // B


def load_rows(ref, first, count):
    return jnp.concatenate(
        [ref[pl.ds(first * LANES + c, count, stride=LANES), :] for c in range(LANES)], axis=1
    )


def store_rows(ref, first, values):
    count = values.shape[0]
    for c in range(LANES):
        ref[pl.ds(first * LANES + c, count, stride=LANES), :] = values[:, c * B : (c + 1) * B]


def real_rows():
    return lax.broadcasted_iota(jnp.int32, (NP, 1), 0) < NPOS


def forward_kernel(comm, parts, each, own, mlp_own, tokens, vec, rel, table, *refs):
    refs = list(refs)
    if comm:
        attn_state, mlp_state = refs[:2]
        refs = refs[2:]
    else:
        full = refs.pop(0)
    w_o, q_o, k_o, v_o, att_o, mid_o, bra_o, n2_o, bias_o, tok_o, lse, idx, mlp_at = refs[:13]
    refs = refs[13:]
    if comm:
        mlp_all = refs.pop(0)
    w, q, k, v, att, mid, bra, n2, bias, tok, n1, wide, square, spread, long, out_sems = refs[:16]
    refs = refs[16:]
    out = Local(out_sems)
    imgs = q.shape[0]
    edge = tokens.shape[1] // 16 * 16

    if comm:
        a32, m32, a16, m16, full, load_sems = refs[:6]
        a_sems = refs[6:9]
        m_sems = refs[9:12]
        na, nm = a16.shape[0], m16.shape[0]
        load = Local(load_sems)
        first = load.start(attn_state.at[:, 0], a32)
        second = load.start(mlp_state.at[0, :, 0], m32)
        place = Place()
        place.greet()
        first.wait()
        a16[...] = a32[...].astype(bf16)
        moves_a = Gather(place, a16, full, na, *a_sems)
        moves_m = Gather(place, m16, mlp_all, nm, *m_sems)
        step_a = moves_a.step
        step_m = moves_m.step
        step_a(0)
        second.wait()
        m16[...] = m32[...].astype(bf16)
    else:
        step_a = step_m = lambda i: None
    plan = {("proj", 3): 1, ("pair", 1): 2, ("pair", 9): 3, ("pair", 16): 4, ("pair", 24): 5}

    def hook(*at):
        if at in plan:
            step_m(plan[at])

    long[edge : edge + 16] = jnp.zeros((16, D), f32)
    long[:edge] = tokens[0, :edge].astype(f32)
    long[edge : tokens.shape[1]] = tokens[0, edge:].astype(f32)
    for img in range(imgs):
        x = jnp.where(real_rows(), long[img * NPOS : img * NPOS + NP], 0.0)
        tok[img] = x.astype(bf16)
        x, _ = norm_parts(x)
        n1[img * NP : (img + 1) * NP] = (x * vec[0:1] + vec[1:2]).astype(bf16)
    out.start(tok, tok_o)
    spread_table(table, wide, spread)
    turn_index(rel, square, idx)
    step_a(1)
    tiles = NP // 8
    lookup_rows(idx, spread, bias, 0, tiles // 3)
    step_a(2)
    lookup_rows(idx, spread, bias, tiles // 3, 2 * tiles // 3)
    step_a(3)
    lookup_rows(idx, spread, bias, 2 * tiles // 3, tiles)
    out.start(bias, bias_o)
    step_a(4)
    step_a(5)
    step_m(0)
    step_a(6)

    @pl.loop(0, 4 * T)
    def _(row):
        m = row // T
        r = pl.ds(pl.multiple_of(lax.rem(row, T) * B, B), B)
        for c in range(T):
            w[m, r, c * B : (c + 1) * B] = full[own[row * T + c]]

    out.start(w, w_o)
    for m, (dst, row, scale) in enumerate(((q, 2, HD**-0.5), (k, None, 1.0), (v, 3, 1.0))):
        for n in range(D // NL):
            lanes = slice(n * NL, (n + 1) * NL)
            part = dot_nn(n1[...], w[m, :, lanes])
            if row is not None:
                part = part + vec[row : row + 1, lanes]
            part = part.astype(bf16)
            if scale != 1.0:
                part = part * jnp.asarray(scale, bf16)
            for img in range(imgs):
                dst[img, :, lanes] = part[img * NP : (img + 1) * NP]
            hook("proj", m * (D // NL) + n + 1)
    out.start(q, q_o)
    out.start(k, k_o)
    out.start(v, v_o)

    side = lax.broadcasted_iota(jnp.int32, (1, B), 1) // HD
    for img in range(imgs):
        for pair in range(H // 2):
            lanes = slice(pair * B, (pair + 1) * B)
            k_pair = k[img, :, lanes]
            q_pair = pad_rows(q[img, :, lanes])
            v_turn = v[img, :, lanes].astype(f32).T.astype(bf16)
            mixed = []
            for sub in range(2):
                h = pair * 2 + sub
                q_one = jnp.where(side == sub, q_pair, jnp.zeros_like(q_pair))
                s = dot_nt(k_pair, q_one) + bias[h]
                top = jnp.max(s, axis=0, keepdims=True)
                e = jnp.exp(s - top)
                total = jnp.sum(e, axis=0, keepdims=True)
                o = dot_nn(v_turn[sub * HD : (sub + 1) * HD], e.astype(bf16))
                mixed.append(o * (1.0 / total))
                lse[img, h : h + 1] = top + jnp.log(total)
            both = jnp.concatenate(mixed, axis=0).T
            att[img, :, lanes] = both[:NP].astype(bf16)
            hook("pair", img * (H // 2) + pair + 1)
    out.start(att, att_o)

    @pl.loop(0, imgs)
    def _(img):
        branch = dot_nn(att[img], w[3]) + vec[4:5]
        bra[img] = branch
        middle = tok[img].astype(f32) + vec[5:6] * branch
        mid[img] = middle
        x, _ = norm_parts(middle)
        n2[img] = (x * vec[6:7] + vec[7:8]).astype(bf16)

    out.start(bra, bra_o)
    out.start(mid, mid_o)
    out.start(n2, n2_o)
    chunk_slots(mlp_own, parts, each, mlp_at)
    step_m(6)
    out.finish()


def forward_attention(comm, parts, each, own, mlp_own, tokens, vec, rel, table, attn, mlp=None):
    imgs = tokens.shape[1] // NPOS
    big = ((imgs, NP, D), bf16)
    tall = ((imgs, NP, D), f32)
    kept = [
        ((4, D, D), bf16),
        big,
        big,
        big,
        big,
        tall,
        tall,
        big,
        ((H, NP, NL), f32),
        big,
    ]
    out_shape = [shape(*k) for k in kept] + [shape((imgs, H, NL), f32), shape((NP, NL), jnp.int32)]
    out_shape.append(shape((FF // CH * 2 * T * PER,), jnp.int32))
    out_specs = [ANY] * len(kept) + [VMEM, VMEM, SMEM]
    wide = -(-table.shape[1] // B) * B
    scratch = [pltpu.VMEM(*k) for k in kept] + [
        pltpu.VMEM((imgs * NP, D), bf16),
        pltpu.VMEM((H, wide), f32),
        pltpu.VMEM((NL, NL), f32),
        pltpu.VMEM((H, wide // B, 8, B), f32),
        pltpu.VMEM((tokens.shape[1] // 16 * 16 + 16, D), f32),
        pltpu.SemaphoreType.DMA((len(kept),)),
    ]
    args = [own, mlp_own, tokens, vec, rel, table, attn]
    specs = [SMEM, SMEM, VMEM, VMEM, VMEM, VMEM]
    params = dict(vmem_limit_bytes=LIMIT)
    if comm:
        na, nm = attn.shape[0], mlp.shape[1]
        args.append(mlp)
        specs += [ANY, ANY]
        out_shape.append(shape((32 * nm, B, B), bf16))
        out_specs.append(ANY)
        scratch += [
            pltpu.VMEM((na, B, B), f32),
            pltpu.VMEM((nm, B, B), f32),
            pltpu.VMEM((na, B, B), bf16),
            pltpu.VMEM((nm, B, B), bf16),
            pltpu.VMEM((32 * na, B, B), bf16),
            pltpu.SemaphoreType.DMA((2,)),
        ]
        scratch += gather_scratch() + gather_scratch()
        params.update(collective_id=0, has_side_effects=True)
    else:
        specs.append(VMEM)
    return pl.pallas_call(
        partial(forward_kernel, comm, parts, each),
        in_specs=specs,
        out_specs=out_specs,
        out_shape=out_shape,
        scratch_shapes=scratch,
        compiler_params=pltpu.CompilerParams(**params),
        name="forward_attention",
    )(*args)


def mlp_kernel(
    at,
    mid_h,
    bra_h,
    n2,
    cot,
    slots,
    vec,
    upb,
    out,
    gmid,
    gbra,
    sums,
    bgrad,
    tiles_out,
    mid,
    bra,
    last,
    w1,
    w2,
    gs,
    act,
    gh,
    summed,
    gn2,
    tiles,
    sem_in,
    sem_out,
    sem_load,
):
    imgs = mid.shape[0]
    length = cot.shape[0] // LANES
    chunks = FF // CH

    @pl.loop(0, chunks)
    def _(c):
        base = c * 2 * T * PER
        for t in range(T * PER):
            r, cc = t // PER * B, t % PER * B
            pltpu.make_async_copy(
                slots.at[at[base + t]], w1.at[c, r : r + B, cc : cc + B], sem_in.at[c]
            ).start()
            r, cc = t // T * B, t % T * B
            pltpu.make_async_copy(
                slots.at[at[base + T * PER + t]], w2.at[c, r : r + B, cc : cc + B], sem_in.at[c]
            ).start()

    load = Local(sem_load)
    load.start(mid_h, mid)
    load.start(bra_h, bra)
    last[...] = jnp.zeros_like(last)
    last[:NPOS] = load_rows(cot, length - NPOS, NPOS)

    def upstream(img):
        if img == imgs - 1:
            return last[...]
        return jnp.where(real_rows(), load_rows(cot, img * NPOS, NP), 0.0)

    for img in range(imgs):
        gs[img * NP : (img + 1) * NP] = (vec[9:10] * upstream(img)).astype(bf16)
    summed[...] = jnp.zeros_like(summed)
    gn2[...] = jnp.zeros_like(gn2)

    @pl.loop(0, chunks)
    def _(c):
        pltpu.make_async_copy(w1.at[c], w1.at[c], sem_in.at[c]).wait()
        pltpu.make_async_copy(w2.at[c], w2.at[c], sem_in.at[c]).wait()
        span = pl.ds(pl.multiple_of(c * CH, CH), CH)
        bias_sum = jnp.zeros((1, CH), f32)
        for rb in range(imgs // 2):
            block = slice(rb * 2 * NP, (rb + 1) * 2 * NP)
            hid = dot_nn(n2[block], w1[c]) + upb[:, span]
            back = dot_nt(gs[block], w2[c])
            phi = 0.5 * (1.0 + lax.erf(hid * (1.0 / math.sqrt(2.0))))
            density = jnp.exp(-0.5 * hid * hid) * (1.0 / math.sqrt(2.0 * math.pi))
            a = (hid * phi).astype(bf16)
            g = (back * (phi + hid * density)).astype(bf16)
            act[block] = a
            gh[block] = g
            bias_sum = bias_sum + jnp.sum(g.astype(f32), axis=0, keepdims=True)
            summed[block] += dot_nn(a, w2[c])
            gn2[block] += dot_nt(g, w1[c])
        bgrad[:, span] = bias_sum
        up_grad = dot_tn(n2[...], gh[...])
        down_grad = dot_tn(act[...], gs[...])
        base = c * 2 * T * PER
        for t in range(T * PER):
            r, cc = t // PER * B, t % PER * B
            tiles[c, t] = up_grad[r : r + B, cc : cc + B].astype(bf16)
            pltpu.make_async_copy(tiles.at[c, t], tiles_out.at[at[base + t]], sem_out).start()
        for t in range(T * PER):
            r, cc = t // T * B, t % T * B
            to = T * PER + t
            tiles[c, to] = down_grad[r : r + B, cc : cc + B].astype(bf16)
            pltpu.make_async_copy(tiles.at[c, to], tiles_out.at[at[base + to]], sem_out).start()

    load.finish()
    s4 = jnp.zeros((1, D), f32)
    s5 = jnp.zeros((1, D), f32)
    s6 = jnp.zeros((1, D), f32)
    s7 = jnp.zeros((1, D), f32)
    s8 = jnp.zeros((1, D), f32)
    s9 = jnp.zeros((1, D), f32)
    for img in range(imgs):
        block = slice(img * NP, (img + 1) * NP)
        up = upstream(img)
        middle = mid[img]
        sm = summed[block] + vec[8:9]
        s9 += jnp.sum(up * sm, axis=0, keepdims=True)
        s8 += jnp.sum(gs[block].astype(f32), axis=0, keepdims=True)
        x, inv = norm_parts(middle)
        gn = gn2[block]
        s6 += jnp.sum(gn * x, axis=0, keepdims=True)
        s7 += jnp.sum(gn, axis=0, keepdims=True)
        gm = up + norm_back(gn, x, inv, vec[6:7])
        gmid[img] = gm
        gb = (vec[5:6] * gm).astype(bf16)
        gbra[img] = gb
        s4 += jnp.sum(gb.astype(f32), axis=0, keepdims=True)
        s5 += jnp.sum(gm * bra[img], axis=0, keepdims=True)
        summed[img * NPOS : img * NPOS + NP] = middle + vec[9:10] * sm
    edge = length // 16 * 16
    out[0, :edge] = summed[:edge].astype(bf16)
    out[0, edge:] = summed[edge:length].astype(bf16)
    sums[...] = jnp.concatenate([s4, s5, s6, s7, s8, s9, s9, s9], axis=0)
    pltpu.make_async_copy(tiles, tiles, sem_out).wait()


def feed_forward(mid, bra, n2, cot, slots, at, vec, up_bias):
    imgs = mid.shape[0]
    rows = imgs * NP
    chunks = FF // CH
    return pl.pallas_call(
        mlp_kernel,
        in_specs=[SMEM, ANY, ANY, VMEM, VMEM, ANY, VMEM, VMEM],
        out_specs=[VMEM] * 5 + [ANY],
        out_shape=[
            shape((1, imgs * NPOS, D), bf16),
            shape((imgs, NP, D), f32),
            shape((imgs, NP, D), bf16),
            shape((8, D), f32),
            shape((1, FF), f32),
            shape(slots.shape, bf16),
        ],
        scratch_shapes=[
            pltpu.VMEM((imgs, NP, D), f32),
            pltpu.VMEM((imgs, NP, D), f32),
            pltpu.VMEM((NP, D), f32),
            pltpu.VMEM((chunks, D, CH), bf16),
            pltpu.VMEM((chunks, CH, D), bf16),
            pltpu.VMEM((rows, D), bf16),
            pltpu.VMEM((rows, CH), bf16),
            pltpu.VMEM((rows, CH), bf16),
            pltpu.VMEM((rows, D), f32),
            pltpu.VMEM((rows, D), f32),
            pltpu.VMEM((chunks, 2 * T * PER, B, B), bf16),
            pltpu.SemaphoreType.DMA((chunks,)),
            pltpu.SemaphoreType.DMA(()),
            pltpu.SemaphoreType.DMA((2,)),
        ],
        compiler_params=pltpu.CompilerParams(vmem_limit_bytes=LIMIT),
        name="feed_forward",
    )(at, mid, bra, n2.reshape(rows, D), cot, slots, vec, up_bias)


def backward_kernel(comm, inverse, gbra, lse, vec, idx, *refs):
    refs = list(refs)
    w_h, v_h, k_h, q_h, bias_h, att_h, tok_h, gmid_h = refs[:8]
    refs = refs[8:]
    if comm:
        mlp_full = refs.pop(0)
    gin, table, sums, tiles_o = refs[:4]
    refs = refs[4:]
    if comm:
        mlp_mine = refs.pop(0)
    w, v, k, q, bias, att, tok, gmid = refs[:8]
    n1, gatt, gqkv, grid, tiles, full, load_sems, out_sem = refs[8:16]
    refs = refs[16:]
    imgs = q.shape[0]

    if comm:
        place = Place()
        place.greet()
        moves = Scatter(place, mlp_full, mlp_mine.shape[0], *refs)
        step = moves.step
    else:
        step = lambda i, out=None: None
    load = Local(load_sems)
    got_w, got_v, got_k, got_q, got_bias, got_att, got_tok, got_gmid = [
        load.start(src, dst)
        for src, dst in zip(
            (w_h, v_h, k_h, q_h, bias_h, att_h, tok_h, gmid_h), (w, v, k, q, bias, att, tok, gmid)
        )
    ]
    step(0)
    got_w.wait()
    for n in range(D // NL):
        lanes = slice(n * NL, (n + 1) * NL)
        got = dot_nt(gbra[...], w[3, lanes, :]).astype(bf16)
        for img in range(imgs):
            gatt[img, :, lanes] = got[img * NP : (img + 1) * NP]
    grid[...] = jnp.zeros_like(grid)
    got_v.wait()
    got_k.wait()
    got_q.wait()
    got_bias.wait()
    plan = {4: 1, 12: 2, 18: 3}

    side = lax.broadcasted_iota(jnp.int32, (1, B), 1) // HD
    for img in range(imgs):
        here = slice(img * NP, (img + 1) * NP)
        for pair in range(H // 2):
            lanes = slice(pair * B, (pair + 1) * B)
            k_pair = k[img, :, lanes]
            v_pair = v[img, :, lanes]
            q_pair = pad_rows(q[img, :, lanes])
            g_pair = pad_rows(gatt[img, :, lanes])
            k_turn = k_pair.astype(f32).T.astype(bf16)
            gq = []
            gk = jnp.zeros((NP, B), f32)
            gv = jnp.zeros((NP, B), f32)
            for sub in range(2):
                h = pair * 2 + sub
                q_one = jnp.where(side == sub, q_pair, jnp.zeros_like(q_pair))
                g_one = jnp.where(side == sub, g_pair, jnp.zeros_like(g_pair))
                s = dot_nt(k_pair, q_one) + bias[h]
                p = jnp.exp(s - lse[img, h : h + 1])
                dp = dot_nt(v_pair, g_one)
                gv = gv + dot_nn(p.astype(bf16), g_one)
                inner = jnp.sum(p * dp, axis=0, keepdims=True)
                ds = (p * (dp - inner)).astype(bf16)
                gk = gk + dot_nn(ds, q_one)
                gq.append(dot_nn(k_turn[sub * HD : (sub + 1) * HD], ds))
                grid[h] += ds.astype(f32)
            turned = jnp.concatenate(gq, axis=0).T
            gqkv[here, lanes] = (turned[:NP] * HD**-0.5).astype(bf16)
            gqkv[here, D + pair * B : D + (pair + 1) * B] = gk.astype(bf16)
            gqkv[here, 2 * D + pair * B : 2 * D + (pair + 1) * B] = gv.astype(bf16)
            if img * (H // 2) + pair + 1 in plan:
                step(plan[img * (H // 2) + pair + 1])

    def put(m, n, grad):
        for r in range(T):
            for cc in range(NL // B):
                tiles[m * T * T + r * T + n * (NL // B) + cc] = grad[
                    r * B : (r + 1) * B, cc * B : (cc + 1) * B
                ].astype(bf16)

    got_att.wait()
    got_tok.wait()
    for img in range(imgs):
        x, _ = norm_parts(tok[img].astype(f32))
        n1[img * NP : (img + 1) * NP] = (x * vec[0:1] + vec[1:2]).astype(bf16)
    for n in range(D // NL):
        lanes = slice(n * NL, (n + 1) * NL)
        put(3, n, dot_tn(att[...], gbra[:, lanes]))
    for m in range(3):
        for n in range(D // NL):
            put(m, n, dot_tn(n1[...], gqkv[:, m * D + n * NL : m * D + (n + 1) * NL]))

    @pl.loop(0, full.shape[0] // 4)
    def _(group):
        for i in range(4):
            full[group * 4 + i] = tiles[inverse[group * 4 + i]]

    out = pltpu.make_async_copy(full, tiles_o, out_sem)
    out.start()
    step(4)
    accumulate_rows(grid, idx, table)

    got_gmid.wait()
    s0 = jnp.zeros((1, D), f32)
    s1 = jnp.zeros((1, D), f32)
    s2 = jnp.zeros((1, D), f32)
    s3 = jnp.zeros((1, D), f32)
    for img in range(imgs):
        here = slice(img * NP, (img + 1) * NP)
        gq = gqkv[here, 0:D]
        gk = gqkv[here, D : 2 * D]
        gv = gqkv[here, 2 * D : 3 * D]
        gn = dot_nt(gq, w[0]) + dot_nt(gk, w[1]) + dot_nt(gv, w[2])
        x, inv = norm_parts(tok[img].astype(f32))
        s0 += jnp.sum(gn * x, axis=0, keepdims=True)
        s1 += jnp.sum(gn, axis=0, keepdims=True)
        s2 += jnp.sum(gq.astype(f32), axis=0, keepdims=True)
        s3 += jnp.sum(gv.astype(f32), axis=0, keepdims=True)
        got = gmid[img] + norm_back(gn, x, inv, vec[0:1])
        store_rows(gin, img * NPOS, got[:NPOS] if img == imgs - 1 else got)
    sums[...] = jnp.concatenate([s0, s1, s2, s3, s3, s3, s3, s3], axis=0)
    if comm:
        step(5, mlp_mine)
    out.wait()


def backward_attention(comm, inverse, saved, gmid, gbra, vec, wide_total, mlp_full=None):
    w, q, k, v, att, mid, bra, n2, bias, tok, lse, idx = saved
    imgs = tok.shape[0]
    rows = imgs * NP
    att = att.reshape(rows, D)
    loaded = [w, v, k, q, bias, att, tok, gmid]
    args = [inverse, gbra.reshape(rows, D), lse, vec, idx] + loaded
    specs = [SMEM] + [VMEM] * 4 + [ANY] * 8
    out_shape = [
        shape((imgs * NPOS * LANES, B), f32),
        shape((16, wide_total), f32),
        shape((8, D), f32),
        shape((inverse.shape[0], B, B), bf16),
    ]
    out_specs = [VMEM] * 3 + [ANY]
    scratch = [pltpu.VMEM(x.shape, x.dtype) for x in loaded] + [
        pltpu.VMEM((rows, D), bf16),
        pltpu.VMEM((imgs, NP, D), bf16),
        pltpu.VMEM((rows, 3 * D), bf16),
        pltpu.VMEM((H, NP, NL), f32),
        pltpu.VMEM((4 * T * T, B, B), bf16),
        pltpu.VMEM((inverse.shape[0], B, B), bf16),
        pltpu.SemaphoreType.DMA((8,)),
        pltpu.SemaphoreType.DMA(()),
    ]
    params = dict(vmem_limit_bytes=LIMIT)
    if comm:
        n = mlp_full.shape[0] // 32
        args.append(mlp_full)
        specs.append(ANY)
        out_shape.append(shape((n, B, B), f32))
        out_specs.append(VMEM)
        scratch += scatter_scratch(n)
        params.update(collective_id=1, has_side_effects=True)
    return pl.pallas_call(
        partial(backward_kernel, comm),
        in_specs=specs,
        out_specs=out_specs,
        out_shape=out_shape,
        scratch_shapes=scratch,
        compiler_params=pltpu.CompilerParams(**params),
        name="backward_attention",
    )(*args)


NB = 16
GROUP = B // NB


def split_two(x):
    first = x.astype(bf16)
    return first, (x - first.astype(f32)).astype(bf16)


def wide_dot(x, y, dims):
    xa, xb = split_two(x)
    ya, yb = split_two(y)
    xs = jnp.concatenate([xa, xa, xb], axis=dims[0])
    ys = jnp.concatenate([ya, yb, ya], axis=dims[1])
    return lax.dot_general(
        xs, ys, (((dims[0],), (dims[1],)), ((), ())), preferred_element_type=f32
    )


def unit_inverse(diag):
    lane = lax.broadcasted_iota(jnp.int32, (NB, B), 1)
    row = lax.broadcasted_iota(jnp.int32, (NB, B), 0)
    inner = jnp.bitwise_and(lane, NB - 1)
    outer = lane - inner
    left = diag
    right = jnp.where(row == inner, 1.0, 0.0)
    def pick(k):
        return jnp.take_along_axis(diag, outer + k, axis=1, mode="promise_in_bounds")

    cut = NB // 2
    rows = [pick(r) for r in range(NB)]
    rows = [x if r < cut else x[cut:] for r, x in enumerate(rows)]
    flags = [jnp.where(row == r, 1.0, 0.0) for r in range(NB)]
    low = [x[:cut] for x in flags]
    high = [x[cut:] for x in flags]
    cols = [diag[r : r + 1] for r in range(NB)]
    pivots = jnp.zeros((1, B), f32)
    right_low, right_high = right[:cut], right[cut:]
    for r in range(NB):
        mine = rows[r]
        at = r if r < cut else r - cut
        pivot = mine[at : at + 1]
        pivots = jnp.where(inner[:1] == r, pivot, pivots)
        scale = pl.reciprocal(pivot, approx=True)
        scale = scale * (2.0 - pivot * scale)
        factor = jnp.where(inner[:1] > r, cols[r] * scale, 0.0)
        for s in range(r + 1, NB):
            at = s if r < cut else s - cut
            entry = mine[at : at + 1]
            share = entry * scale
            rows[s] = rows[s] - share * (mine if s < cut or r >= cut else mine[cut:])
            low[s] = low[s] - share * low[r]
            if r >= cut:
                high[s] = high[s] - share * high[r]
            cols[s] = cols[s] - factor * entry
        right_low = right_low - factor * low[r]
        if r >= cut:
            right_high = right_high - factor * high[r]
    right = jnp.concatenate([right_low, right_high], axis=0)
    return right * lax.rsqrt(pivots)


def orth_turned(mats, between=None):
    count = len(mats)
    groups = -(-count // GROUP)
    size = -(-count // groups)
    members = [list(range(g * size, min(count, (g + 1) * size))) for g in range(groups)]
    tails = []
    for a in mats:
        turned = a.T
        tails.append(jnp.concatenate([wide_dot(turned, turned, (1, 1)), turned], axis=1))
    own_block = (
        lax.broadcasted_iota(jnp.int32, (B, B), 0) // NB
        == lax.broadcasted_iota(jnp.int32, (B, B), 1) // NB
    )
    outs = [[] for _ in range(count)]
    for p in range(B // NB):
        base = p * NB
        for ids in members:
            fill = ids + [ids[-1]] * (GROUP - len(ids))
            strips = jnp.concatenate([tails[m][:NB] for m in fill], axis=0)
            turned = strips[:, :B].T
            unit = unit_inverse(turned[base : base + NB])
            spread = jnp.where(own_block, jnp.concatenate([unit] * GROUP, axis=0), 0.0)
            u = wide_dot(spread, strips, (0, 0))
            for at, m in enumerate(ids):
                um = u[at * NB : (at + 1) * NB]
                outs[m].append(um[:, B:])
                if base + NB < B:
                    tails[m] = tails[m][NB:] - wide_dot(um[:, base + NB : B], um, (0, 0))
        if between is not None:
            between(p)
    return [jnp.concatenate(o, axis=0) for o in outs]


def soap_slots(base, owner, grads, state, update, copy, between=None):
    count = grads.shape[0]
    mats = []
    gs = []
    for i in range(count):
        named = jnp.where(owner[...] == base + i, 1.0, 0.0)
        named = jnp.max(named, axis=1, keepdims=True)
        g = jnp.where(named > 0.0, grads[i].astype(f32), 0.0)
        gs.append(g)
        left = beta_stat * state[i, 3] + (1.0 - beta_stat) * wide_dot(g, g, (1, 1))
        right = beta_stat * state[i, 4] + (1.0 - beta_stat) * wide_dot(g, g, (0, 0))
        mats.append(wide_dot(left, state[i, 5], (1, 0)))
        mats.append(wide_dot(right, state[i, 6], (1, 0)))
    if between is not None:
        between(-1)
    turned = orth_turned(mats, between)
    fix_one = 1.0 - beta_one**STEP
    fix_two = 1.0 - beta_two**STEP
    for i in range(count):
        tl, tr = turned[2 * i], turned[2 * i + 1]
        rotated = wide_dot(wide_dot(tl, gs[i], (1, 0)), tr, (1, 1))
        new_first = beta_one * state[i, 1] + (1.0 - beta_one) * rotated
        new_second = beta_two * state[i, 2] + (1.0 - beta_two) * rotated * rotated
        normalized = new_first / fix_one / (jnp.sqrt(new_second / fix_two) + adam_eps)
        step = wide_dot(wide_dot(tl, normalized, (0, 0)), tr, (1, 0))
        weight = state[i, 0]
        weight = weight - matrix_rate * (step + decay_rate * weight)
        update[i, 0] = weight
        update[i, 1] = new_first
        update[i, 2] = new_second
        update[i, 3] = tl.T
        update[i, 4] = tr.T
        copy[i] = weight.astype(bf16)


def soap_kernel(first_slot, passed, owner, grads, state, *refs):
    kept, refs = refs[:passed], refs[passed:]
    update, copy = refs[:2]
    through, held, sems = refs[2 : 2 + passed], refs[2 + passed : 2 + 2 * passed], refs[2 + 2 * passed :]
    count = grads.shape[0]
    between = None
    if passed:
        into, out = Local(sems[0]), Local(sems[1])
        for src, dst in zip(kept, held):
            into.start(src, dst)

        def between(p):
            if p == 2:
                into.finish()
                for src, dst in zip(held, through):
                    out.start(src, dst)

    first = first_slot() + pl.program_id(0) * count
    soap_slots(first, owner, grads, state, update, copy, between)
    if passed:
        out.finish()


def soap_update(grads, state, owner, first_slot, kept=()):
    slots = grads.shape[0]
    count = max(c for c in range(1, 10) if slots % c == 0)
    assert not kept or count == slots
    return pl.pallas_call(
        partial(soap_kernel, first_slot, len(kept)),
        grid=(slots // count,),
        in_specs=[
            pl.BlockSpec((1, owner.shape[0]), lambda i: (0, 0)),
            pl.BlockSpec((count, B, B), lambda i: (i, 0, 0)),
            pl.BlockSpec((count, 7, B, B), lambda i: (i, 0, 0, 0)),
        ]
        + [ANY] * len(kept),
        out_specs=[
            pl.BlockSpec((count, 5, B, B), lambda i: (i, 0, 0, 0)),
            pl.BlockSpec((count, B, B), lambda i: (i, 0, 0)),
        ]
        + [ANY] * len(kept),
        out_shape=[shape((slots, 5, B, B), f32), shape((slots, B, B), bf16)]
        + [shape(x.shape, x.dtype) for x in kept],
        scratch_shapes=[pltpu.VMEM(x.shape, x.dtype) for x in kept]
        + [pltpu.SemaphoreType.DMA((len(kept),))] * (2 if kept else 0),
        compiler_params=pltpu.CompilerParams(vmem_limit_bytes=LIMIT),
        name="soap",
    )(owner[None], grads, state, *kept)


SUM_ROWS = 40


def adam(grad, param, first, second):
    new_first = beta_one * first + (1.0 - beta_one) * grad
    new_second = beta_two * second + (1.0 - beta_two) * grad * grad
    fix_one = 1.0 - beta_one**STEP
    fix_two = 1.0 - beta_two**STEP
    step = (new_first / fix_one) / (jnp.sqrt(new_second / fix_two) + adam_eps)
    return grad, param - vector_rate * step, new_first, new_second


def finish_kernel(
    full,
    mlp_sums,
    attn_sums,
    table_sums,
    bias_sums,
    vec,
    vec_m,
    table,
    table_m,
    upb,
    upb_m,
    owner,
    mlp_mine,
    state_h,
    mine,
    vec_up,
    table_up,
    upb_up,
    update,
    copy,
    state,
    load_sem,
    part,
    other,
    column,
    sum_send,
    sum_recv,
    *scratch,
):
    place = Place()
    place.greet()
    load = pltpu.make_async_copy(state_h.at[0], state, load_sem)
    load.start()

    moves = Scatter(place, full, mine.shape[0], *scratch)
    sums = Copies(place, sum_send, sum_recv)
    part[0, 0:8] = mlp_sums[...]
    part[0, 8:16] = attn_sums[...]
    part[0, 16:32] = table_sums[...]
    quarter = jnp.concatenate([bias_sums[:, i * D : (i + 1) * D] for i in range(FF // D)] * 2, axis=0)
    part[0, 32:40] = quarter
    sums.start("c", part.at[0], other.at[0], dc=1)
    moves.step(0)
    load.wait()

    def total_sums():
        part[4] = ((column[0] + column[1]) + column[2]) + column[3]
        total = part.at[4]
        grad = jnp.concatenate([total[8:12], total[0:6]], axis=0)
        for i, got in enumerate(adam(grad, vec[...], vec_m[:, 0, :], vec_m[:, 1, :])):
            vec_up[:, i, :] = got
        wide = table.shape[1]
        grad = total[16 : 16 + H, 0:wide]
        for i, got in enumerate(adam(grad, table[...], table_m[:, 0, :], table_m[:, 1, :])):
            table_up[:, i, :] = got
        for j in range(FF // D):
            lanes = slice(j * D, (j + 1) * D)
            for i, got in enumerate(
                adam(total[32 + j : 33 + j], upb[:, lanes], upb_m[0:1, lanes], upb_m[1:2, lanes])
            ):
                upb_up[i : i + 1, lanes] = got

    def between(p):
        if p == -1:
            sums.arrived("c")
            part[1] = part[0] + other[0]
            sums.start("x", part.at[1], other.at[1], dx=1)
            moves.step(1)
        elif p == 1:
            sums.arrived("x")
            part[2] = part[1] + other[1]
            sums.start("y", part.at[2], other.at[2], dy=1)
            moves.step(2)
        elif p == 3:
            sums.arrived("y")
            part[3] = part[2] + other[2]
            for d in (1, 2, 3):
                sums.start(("z", d), part.at[3], column.at[place.z], d=d)
            column[place.z] = part[3]
            moves.step(3)
        elif p == 6:
            moves.step(4)

    first_slot = lax.axis_index("dp") * mlp_mine.shape[0]
    soap_slots(first_slot, owner, mlp_mine, state, update, copy, between)
    for d in (1, 2, 3):
        sums.arrived(("z", d))
    total_sums()
    moves.step(5, mine)
    sums.sent()


def finish(full, small, params, owner, mlp_mine, mlp_state):
    n = full.shape[0] // 32
    nm = mlp_mine.shape[0]
    vec, vec_m, table, table_m, upb, upb_m = params
    return pl.pallas_call(
        finish_kernel,
        in_specs=[ANY] + [VMEM] * 12 + [ANY],
        out_specs=[VMEM] * 6,
        out_shape=[
            shape((n, B, B), f32),
            shape((vec.shape[0], 4, D), f32),
            shape((H, 4, table.shape[1]), f32),
            shape((4, FF), f32),
            shape((nm, 5, B, B), f32),
            shape((nm, B, B), bf16),
        ],
        scratch_shapes=[
            pltpu.VMEM((nm, 7, B, B), f32),
            pltpu.SemaphoreType.DMA(()),
            pltpu.VMEM((5, SUM_ROWS, D), f32),
            pltpu.VMEM((3, SUM_ROWS, D), f32),
            pltpu.VMEM((4, SUM_ROWS, D), f32),
            pltpu.SemaphoreType.DMA((6,)),
            pltpu.SemaphoreType.DMA((6,)),
        ]
        + scatter_scratch(n),
        compiler_params=pltpu.CompilerParams(
            collective_id=2, has_side_effects=True, vmem_limit_bytes=LIMIT
        ),
        name="finish",
    )(
        full,
        *small,
        vec,
        vec_m.transpose(1, 0, 2),
        table,
        table_m.transpose(1, 0, 2),
        upb[None],
        upb_m,
        owner[None],
        mlp_mine,
        mlp_state,
    )


def body(
    tokens,
    cotangent,
    rel_index,
    attn_owner,
    mlp_owner,
    attn_state,
    mlp_state,
    vec_param,
    vec_moments,
    rel_table,
    rel_table_moments,
    up_bias,
    up_bias_moments,
):
    both = ("dp", "mp")
    parts = lax.axis_size("mp")
    comm = own_kernels(lax.axis_size("dp"), parts)
    imgs = tokens.shape[1] // NPOS
    attn_local = attn_state.shape[0]
    mlp_local = mlp_state.shape[1]
    attn_total = attn_local * lax.axis_size("dp") * parts

    def attn_first():
        return (lax.axis_index("dp") * parts + lax.axis_index("mp")) * attn_local

    def mlp_first():
        return lax.axis_index("dp") * mlp_local

    wide_total = -(-rel_table.shape[1] // B) * B
    slot_ids = jnp.arange(attn_total, dtype=jnp.int32)
    block_ids = jnp.arange(attn_owner.shape[0], dtype=jnp.int32)
    inverse = jnp.sum(
        jnp.where(attn_owner[None, :] == slot_ids[:, None], block_ids[None, :], 0), axis=1
    ).astype(jnp.int32)

    if comm:
        *saved, mlp_slots = forward_attention(
            True,
            parts,
            mlp_local,
            attn_owner,
            mlp_owner,
            tokens,
            vec_param, rel_index, rel_table, attn_state, mlp_state
        )
    else:
        attn_slots = lax.all_gather(attn_state[:, 0].astype(bf16), both, axis=0, tiled=True)
        mlp_slots = lax.all_gather(mlp_state[0, :, 0].astype(bf16), both, axis=0, tiled=True)
        saved = list(
            forward_attention(
            False,
            parts,
            mlp_local,
            attn_owner,
            mlp_owner,
            tokens,
            vec_param, rel_index, rel_table, attn_slots
        ))
    mlp_at = saved.pop()
    w, q, k, v, att, mid, bra, n2, bias, tok, lse, idx = saved
    out, gmid, gbra, mlp_sums, bias_grad, mlp_grads = feed_forward(
        mid, bra, n2, cotangent.reshape(-1, B), mlp_slots, mlp_at, vec_param, up_bias[None]
    )
    if comm:
        gin, table_grad, attn_sums, attn_full, mlp_mine = backward_attention(
            True, inverse, saved, gmid, gbra, vec_param, wide_total, mlp_grads
        )
        attn_mine, vec_up, table_up, bias_up, mlp_result, mlp_copy = finish(
            attn_full,
            (mlp_sums, attn_sums, table_grad, bias_grad),
            (vec_param, vec_moments, rel_table, rel_table_moments, up_bias, up_bias_moments),
            mlp_owner,
            mlp_mine,
            mlp_state,
        )
        vec_up = vec_up.transpose(1, 0, 2)
        table_up = table_up.transpose(1, 0, 2)
        attn_result, attn_copy, gin, mlp_result, mlp_copy = soap_update(
            attn_mine, attn_state, attn_owner, attn_first, (gin, mlp_result, mlp_copy)
        )
    else:
        gin, table_grad, attn_sums, attn_full = backward_attention(
            False, inverse, saved, gmid, gbra, vec_param, wide_total
        )
        mlp_mine = lax.psum_scatter(mlp_grads, both, scatter_dimension=0, tiled=True)
        attn_mine = lax.psum_scatter(attn_full, both, scatter_dimension=0, tiled=True)
        vector_grad = jnp.concatenate([attn_sums[:4], mlp_sums[:6]], axis=0)
        vector_total, table_total, bias_total = lax.psum(
            (vector_grad, table_grad[:H, : rel_table.shape[1]], bias_grad[0]), both
        )
        vec_up = jnp.stack(adam(vector_total, vec_param, vec_moments[0], vec_moments[1]))
        table_up = jnp.stack(
            adam(table_total, rel_table, rel_table_moments[0], rel_table_moments[1])
        )
        bias_up = jnp.stack(adam(bias_total, up_bias, up_bias_moments[0], up_bias_moments[1]))
        attn_result, attn_copy = soap_update(attn_mine, attn_state, attn_owner, attn_first)
        mlp_result, mlp_copy = soap_update(mlp_mine, mlp_state[0], mlp_owner, mlp_first)
    return (
        out,
        gin.reshape(1, imgs * NPOS, D),
        attn_result,
        attn_copy,
        mlp_result[None],
        mlp_copy[None],
        vec_up,
        table_up,
        bias_up,
    )


def solution(mesh):
    placed = (
        P(("dp", "mp"), None, None),
        P(("dp", "mp"), None, None),
        P(),
        P(),
        P(),
        P(("dp", "mp"), None, None, None),
        P("mp", "dp", None, None, None),
        P(),
        P(),
        P(),
        P(),
        P(),
        P(),
    )
    return jax.shard_map(
        body,
        mesh=mesh,
        in_specs=placed,
        out_specs=(
            P(("dp", "mp"), None, None),
            P(("dp", "mp"), None, None),
            P(("dp", "mp"), None, None, None),
            P(("dp", "mp"), None, None),
            P("mp", "dp", None, None, None),
            P("mp", "dp", None, None),
            P(),
            P(),
            P(),
        ),
        check_vma=False,
    )
```

```python
from functools import partial
import math

import jax
import jax.numpy as jnp
from jax import lax
from jax.experimental import pallas as pl
from jax.experimental.pallas import tpu as pltpu
from jax.sharding import PartitionSpec as P

D = 768
H = 12
HD = 64
FF = 3072
NPOS = 197
NP = 208
NL = 256
B = 128
STEP = 5
T = D // B

f32 = jnp.float32
bf16 = jnp.bfloat16

ln_eps = 1e-06
beta_one = 0.9
beta_two = 0.95
beta_stat = 0.95
adam_eps = 1e-08
matrix_rate = 0.05
vector_rate = 0.2
decay_rate = 0.05

VMEM = pl.BlockSpec(memory_space=pltpu.VMEM)
SMEM = pl.BlockSpec(memory_space=pltpu.SMEM)
ANY = pl.BlockSpec(memory_space=pl.ANY)
LIMIT = 60 << 20


def shape(dims, kind):
    return jax.ShapeDtypeStruct(dims, kind)


def dot_nn(x, y):
    return lax.dot_general(x, y, (((1,), (0,)), ((), ())), preferred_element_type=f32)


def dot_nt(x, y):
    return lax.dot_general(x, y, (((1,), (1,)), ((), ())), preferred_element_type=f32)


def dot_tn(x, y):
    return lax.dot_general(x, y, (((0,), (0,)), ((), ())), preferred_element_type=f32)


def norm_parts(values):
    centered = values - jnp.mean(values, axis=-1, keepdims=True)
    inv_std = lax.rsqrt(jnp.mean(centered * centered, axis=-1, keepdims=True) + ln_eps)
    return (centered * inv_std, inv_std)


def norm_back(grad_normed, scaled, inv_std, gain_row):
    tangent = grad_normed * gain_row
    return inv_std * (
        tangent
        - jnp.mean(tangent, axis=-1, keepdims=True)
        - scaled * jnp.mean(tangent * scaled, axis=-1, keepdims=True)
    )


MESH = pl.DeviceIdType.MESH
COPIES = 35


def own_kernels(dp_total, parts):
    return dp_total == 16 and parts == 2


class Place:
    def __init__(self):
        dp = lax.axis_index("dp")
        self.y = lax.axis_index("mp")
        self.z = dp // 4
        self.x = lax.rem(dp // 2, 2)
        self.c = lax.rem(dp, 2)

    def rank(self, d=0, dx=0, dc=0, dy=0):
        z = lax.rem(self.z + d + 4, 4)
        x = 1 - self.x if dx else self.x
        c = 1 - self.c if dc else self.c
        y = 1 - self.y if dy else self.y
        return ((z * 2 + x) * 2 + c) * 2 + y

    def device(self, d=0, dx=0, dc=0, dy=0):
        z = lax.rem(self.z + d + 4, 4)
        x = 1 - self.x if dx else self.x
        c = 1 - self.c if dc else self.c
        y = 1 - self.y if dy else self.y
        return ((z * 2 + x) * 2 + c, y)

    def greet(self):
        barrier = pltpu.get_barrier_semaphore()
        for d, dx, dc, dy in PARTNERS:
            pl.semaphore_signal(
                barrier, inc=1, device_id=self.device(d, dx, dc, dy), device_id_type=MESH
            )
        pl.semaphore_wait(barrier, len(PARTNERS))


PARTNERS = ((1, 0, 0, 0), (2, 0, 0, 0), (3, 0, 0, 0), (0, 1, 0, 0), (0, 0, 1, 0), (0, 0, 0, 1))


class Copies:
    def __init__(self, place, send, recv):
        self.place = place
        self.send = send
        self.recv = recv
        self.made = {}

    def start(self, key, src, dst, **to):
        i = len(self.made)
        copy = pltpu.make_async_remote_copy(
            src_ref=src,
            dst_ref=dst,
            send_sem=self.send.at[i],
            recv_sem=self.recv.at[i],
            device_id=self.place.device(**to),
            device_id_type=MESH,
        )
        copy.start()
        self.made[key] = copy

    def arrived(self, key):
        self.made[key].wait_recv()

    def sent(self):
        for copy in self.made.values():
            copy.wait_send()


class Gather(Copies):
    def __init__(self, place, own, full, n, send, recv, local):
        super().__init__(place, send, recv)
        self.own = own
        self.full = full
        self.n = n
        self.half = n // 2
        self.local = pltpu.make_async_copy(own, self.at(), local)

    def at(self, d=0, dx=0, dc=0, dy=0, lo=0, hi=None):
        hi = self.n if hi is None else hi
        return self.full.at[pl.ds(self.place.rank(d, dx, dc, dy) * self.n + lo, hi - lo)]

    def spread(self, d):
        src = self.own if d == 0 else self.at(d=-d)
        dst = self.at(d=-d)
        self.start(("x", d), src, dst, dx=1)
        self.start(("y", d), src, dst, dy=1)
        self.start(("c", d, 0, 0), src, dst, dc=1)

    def along(self, d):
        self.start(("z", d), self.own, self.at(), d=d)

    def share(self, d, dx, dy):
        ref = self.at(d=-d, dx=dx, dy=dy)
        self.start(("c", d, dx, dy), ref, ref, dc=1)

    def corner(self, d):
        ref = self.at(d=-d, dy=1, lo=self.half)
        self.start(("xd", d), ref, ref, dx=1)
        ref = self.at(d=-d, dx=1, hi=self.half)
        self.start(("yd", d), ref, ref, dy=1)

    def sides(self, d):
        self.arrived(("x", d))
        self.share(d, 1, 0)
        self.arrived(("y", d))
        self.share(d, 0, 1)

    def cornered(self, d):
        self.arrived(("xd", d))
        self.arrived(("yd", d))
        self.share(d, 1, 1)

    def step(self, i):
        if i == 0:
            self.local.start()
            self.along(1)
            self.spread(0)
        elif i == 1:
            self.arrived(("z", 1))
            self.along(3)
            self.spread(1)
            self.sides(0)
        elif i == 2:
            self.arrived(("z", 3))
            self.along(2)
            self.spread(3)
            self.sides(1)
            self.corner(0)
        elif i == 3:
            self.corner(1)
            self.sides(3)
        elif i == 4:
            self.arrived(("z", 2))
            self.spread(2)
            self.cornered(0)
            self.corner(3)
            self.cornered(1)
        elif i == 5:
            self.sides(2)
            self.corner(2)
            self.cornered(3)
        else:
            self.cornered(2)
            for d in range(4):
                for dx in range(2):
                    for dy in range(2):
                        self.arrived(("c", d, dx, dy))
            self.local.wait()
            self.sent()


GATHER_STEPS = 7


class Scatter(Copies):
    def __init__(self, place, full, n, acc, peer, side, corner, along, send, recv, local):
        super().__init__(place, send, recv)
        self.full = full
        self.local = local
        self.mine = {}
        self.n = n
        self.half = n // 2
        self.acc = acc
        self.peer = peer
        self.side = side
        self.cor = corner
        self.col = along

    def block(self, d, dx, dc, dy):
        return pl.ds(self.place.rank(d, dx, dc, dy) * self.n, self.n)

    def core(self, d, dx, dy):
        key = (d, dx, dy)
        self.start(
            ("c",) + key, self.full.at[self.block(d, dx, 1, dy)], self.peer.at[d, dx, dy], dc=1
        )
        self.mine[key] = pltpu.make_async_copy(
            self.full.at[self.block(d, dx, 0, dy)],
            self.acc.at[d, dx, dy],
            self.local.at[len(self.mine)],
        )
        self.mine[key].start()

    def pair(self, d, dx, dy):
        self.mine[(d, dx, dy)].wait()
        self.arrived(("c", d, dx, dy))
        self.add(d, dx, dy, self.peer.at[d, dx, dy], 0, self.n)

    def add(self, d, dx, dy, other, lo, hi):
        @pl.loop(lo, hi)
        def _(i):
            total = self.acc[d, dx, dy, i].astype(f32) + other[i - lo].astype(f32)
            self.acc[d, dx, dy, i] = total.astype(bf16)

    def corner(self, d):
        self.pair(d, 1, 1)
        h, n = self.half, self.n
        self.start(("xd", d), self.acc.at[d, 1, 1, pl.ds(0, h)], self.cor.at[d, pl.ds(0, h)], dx=1)
        self.start(
            ("yd", d), self.acc.at[d, 1, 1, pl.ds(h, n - h)], self.cor.at[d, pl.ds(h, n - h)], dy=1
        )

    def sides(self, d):
        h, n = self.half, self.n
        self.pair(d, 1, 0)
        self.arrived(("yd", d))
        self.add(d, 1, 0, self.cor.at[d, pl.ds(h, n - h)], h, n)
        self.start(("x", d), self.acc.at[d, 1, 0], self.side.at[d, 0], dx=1)
        self.pair(d, 0, 1)
        self.arrived(("xd", d))
        self.add(d, 0, 1, self.cor.at[d, pl.ds(0, h)], 0, h)
        self.start(("y", d), self.acc.at[d, 0, 1], self.side.at[d, 1], dy=1)

    def along(self, d):
        self.pair(d, 0, 0)
        self.arrived(("x", d))
        self.arrived(("y", d))

        @pl.loop(0, self.n)
        def _(i):
            total = (
                self.acc[d, 0, 0, i].astype(f32)
                + self.side[d, 0, i].astype(f32)
                + self.side[d, 1, i].astype(f32)
            )
            self.acc[d, 0, 0, i] = total.astype(bf16)

        if d > 0:
            self.start(("z", d), self.acc.at[d, 0, 0], self.col.at[d - 1], d=d)

    def step(self, i, out=None):
        if i == -1:
            for dx, dy in ((1, 1), (1, 0), (0, 1), (0, 0)):
                for d in (2, 3, 0, 1):
                    self.core(d, dx, dy)
        elif i == 0:
            self.corner(2)
            self.corner(3)
        elif i == 1:
            self.sides(2)
            self.corner(0)
            self.corner(1)
        elif i == 2:
            self.along(2)
            self.sides(3)
        elif i == 3:
            self.sides(1)
            self.sides(0)
        elif i == 4:
            self.along(3)
            self.along(1)
        else:
            self.along(0)
            for d in (1, 2, 3):
                self.arrived(("z", d))

            @pl.loop(0, self.n)
            def _(i):
                out[i] = (
                    (self.acc[0, 0, 0, i].astype(f32) + self.col[0, i].astype(f32))
                    + self.col[1, i].astype(f32)
                ) + self.col[2, i].astype(f32)

            self.sent()


SCATTER_STEPS = 6


def scatter_scratch(n):
    return [
        pltpu.VMEM((4, 2, 2, n, B, B), bf16),
        pltpu.VMEM((4, 2, 2, n, B, B), bf16),
        pltpu.VMEM((4, 2, n, B, B), bf16),
        pltpu.VMEM((4, n, B, B), bf16),
        pltpu.VMEM((3, n, B, B), bf16),
        pltpu.SemaphoreType.DMA((COPIES,)),
        pltpu.SemaphoreType.DMA((COPIES,)),
        pltpu.SemaphoreType.DMA((16,)),
    ]


def gather_scratch():
    return [
        pltpu.SemaphoreType.DMA((COPIES,)),
        pltpu.SemaphoreType.DMA((COPIES,)),
        pltpu.SemaphoreType.DMA(()),
    ]


class Local:
    def __init__(self, sems):
        self.sems = sems
        self.made = []

    def start(self, src, dst):
        copy = pltpu.make_async_copy(src, dst, self.sems.at[len(self.made)])
        copy.start()
        self.made.append(copy)
        return copy

    def finish(self):
        for copy in self.made:
            copy.wait()


def spread_table(table_ref, wide, spread):
    wide[...] = jnp.zeros_like(wide)
    wide[:, : table_ref.shape[1]] = table_ref[...]
    for h in range(H):
        for c in range(spread.shape[1]):
            spread[h, c] = jnp.broadcast_to(wide[h : h + 1, c * B : (c + 1) * B], (8, B))


def turn_index(rel_ref, square, out_ref):
    square[...] = jnp.zeros_like(square)
    square[:NPOS, :NPOS] = rel_ref[...].astype(f32)
    out_ref[...] = square[...].T[:NP].astype(jnp.int32)


def lookup_rows(idx_ref, spread, out_ref, lo, hi):
    chunks = spread.shape[1]

    @pl.loop(lo, hi)
    def _(jt):
        rows = pl.ds(pl.multiple_of(jt * 8, 8), 8)
        real = jt * 8 + lax.broadcasted_iota(jnp.int32, (8, B), 0) < NPOS
        for half in range(NL // B):
            lanes = slice(half * B, (half + 1) * B)
            idx = idx_ref[rows, lanes]
            low = jnp.bitwise_and(idx, B - 1)
            high = jnp.right_shift(idx, 7)
            for h in range(H):
                acc = jnp.take_along_axis(spread[h, 0], low, axis=1, mode="promise_in_bounds")
                for c in range(1, chunks):
                    part = jnp.take_along_axis(spread[h, c], low, axis=1, mode="promise_in_bounds")
                    acc = jnp.where(high == c, part, acc)
                out_ref[h, rows, lanes] = jnp.where(real, acc, -1e30)


JB = 8


def accumulate_rows(grid_ref, idx_ref, out_ref):
    chunks = out_ref.shape[1] // B
    out_ref[...] = jnp.zeros_like(out_ref)
    lo_rows = lax.broadcasted_iota(jnp.int32, (B, NL), 0)

    @pl.loop(0, NP // JB)
    def _(jb):
        idx_all = idx_ref[pl.ds(pl.multiple_of(jb * JB, JB), JB), :]
        lefts = []
        rights = []
        for jj in range(JB):
            values = grid_ref[:, jb * JB + jj, :]
            values = jnp.concatenate([values, jnp.zeros((16 - H, NL), f32)], axis=0)
            idx = idx_all[jj : jj + 1]
            low = jnp.bitwise_and(idx, B - 1)
            high = jnp.right_shift(idx, 7)
            rights.append(jnp.where(lo_rows == low, 1.0, 0.0).astype(bf16))
            lefts.append(
                jnp.concatenate(
                    [jnp.where(high == c, values, 0.0) for c in range(chunks)], axis=0
                ).astype(bf16)
            )
        got = dot_nt(jnp.concatenate(lefts, axis=1), jnp.concatenate(rights, axis=1))
        for c in range(chunks):
            out_ref[:, c * B : (c + 1) * B] += got[c * 16 : (c + 1) * 16]


CH = 512
PER = CH // B


def chunk_slots(own, parts, each, out):
    half = own.shape[0] // 2
    local = half // T

    def place(slot, p):
        return lax.div(slot, each) * (parts * each) + p * each + lax.rem(slot, each)

    @pl.loop(0, FF // CH)
    def _(c):
        @pl.loop(0, T * PER)
        def _(t):
            g = c * PER + lax.rem(t, PER)
            g2 = c * PER + t // T
            up = own[(t // PER) * local + lax.rem(g, local)]
            down = own[half + lax.rem(g2, local) * T + lax.rem(t, T)]
            out[c * 2 * T * PER + t] = place(up, g // local)
            out[c * 2 * T * PER + T * PER + t] = place(down, g2 // local)


def pad_rows(x):
    return jnp.concatenate([x, jnp.zeros((NL - NP, x.shape[1]), x.dtype)], axis=0)


LANES = D // B


def load_rows(ref, first, count):
    return jnp.concatenate(
        [ref[pl.ds(first * LANES + c, count, stride=LANES), :] for c in range(LANES)], axis=1
    )


def store_rows(ref, first, values):
    count = values.shape[0]
    for c in range(LANES):
        ref[pl.ds(first * LANES + c, count, stride=LANES), :] = values[:, c * B : (c + 1) * B]


def real_rows():
    return lax.broadcasted_iota(jnp.int32, (NP, 1), 0) < NPOS


def forward_kernel(comm, parts, each, own, mlp_own, tokens, vec, rel, table, *refs):
    refs = list(refs)
    if comm:
        attn_state, mlp_state = refs[:2]
        refs = refs[2:]
    else:
        full = refs.pop(0)
    w_o, q_o, k_o, v_o, att_o, mid_o, bra_o, n2_o, bias_o, tok_o, lse, idx, mlp_at = refs[:13]
    refs = refs[13:]
    if comm:
        mlp_all = refs.pop(0)
    w, q, k, v, att, mid, bra, n2, bias, tok, n1, wide, square, spread, long, out_sems = refs[:16]
    refs = refs[16:]
    out = Local(out_sems)
    imgs = q.shape[0]
    edge = tokens.shape[1] // 16 * 16

    if comm:
        a32, m32, a16, m16, full, load_sems = refs[:6]
        a_sems = refs[6:9]
        m_sems = refs[9:12]
        na, nm = a16.shape[0], m16.shape[0]
        load = Local(load_sems)
        first = load.start(attn_state.at[:, 0], a32)
        second = load.start(mlp_state.at[0, :, 0], m32)
        place = Place()
        place.greet()
        first.wait()
        a16[...] = a32[...].astype(bf16)
        moves_a = Gather(place, a16, full, na, *a_sems)
        moves_m = Gather(place, m16, mlp_all, nm, *m_sems)
        step_a = moves_a.step
        step_m = moves_m.step
        step_a(0)
        second.wait()
        m16[...] = m32[...].astype(bf16)
    else:
        step_a = step_m = lambda i: None
    plan = {("proj", 3): 1, ("pair", 1): 2, ("pair", 9): 3, ("pair", 16): 4, ("pair", 24): 5}

    def hook(*at):
        if at in plan:
            step_m(plan[at])

    long[edge : edge + 16] = jnp.zeros((16, D), f32)
    long[:edge] = tokens[0, :edge].astype(f32)
    long[edge : tokens.shape[1]] = tokens[0, edge:].astype(f32)
    for img in range(imgs):
        x = jnp.where(real_rows(), long[img * NPOS : img * NPOS + NP], 0.0)
        tok[img] = x.astype(bf16)
        x, _ = norm_parts(x)
        n1[img * NP : (img + 1) * NP] = (x * vec[0:1] + vec[1:2]).astype(bf16)
    out.start(tok, tok_o)
    spread_table(table, wide, spread)
    turn_index(rel, square, idx)
    step_a(1)
    tiles = NP // 8
    lookup_rows(idx, spread, bias, 0, tiles // 3)
    step_a(2)
    lookup_rows(idx, spread, bias, tiles // 3, 2 * tiles // 3)
    step_a(3)
    lookup_rows(idx, spread, bias, 2 * tiles // 3, tiles)
    out.start(bias, bias_o)
    step_a(4)
    step_a(5)
    step_m(0)
    step_a(6)

    @pl.loop(0, 4 * T)
    def _(row):
        m = row // T
        r = pl.ds(pl.multiple_of(lax.rem(row, T) * B, B), B)
        for c in range(T):
            w[m, r, c * B : (c + 1) * B] = full[own[row * T + c]]

    out.start(w, w_o)
    for m, (dst, row, scale) in enumerate(((q, 2, HD**-0.5), (k, None, 1.0), (v, 3, 1.0))):
        for n in range(D // NL):
            lanes = slice(n * NL, (n + 1) * NL)
            part = dot_nn(n1[...], w[m, :, lanes])
            if row is not None:
                part = part + vec[row : row + 1, lanes]
            part = part.astype(bf16)
            if scale != 1.0:
                part = part * jnp.asarray(scale, bf16)
            for img in range(imgs):
                dst[img, :, lanes] = part[img * NP : (img + 1) * NP]
            hook("proj", m * (D // NL) + n + 1)
    out.start(q, q_o)
    out.start(k, k_o)
    out.start(v, v_o)

    side = lax.broadcasted_iota(jnp.int32, (1, B), 1) // HD
    for img in range(imgs):
        for pair in range(H // 2):
            lanes = slice(pair * B, (pair + 1) * B)
            k_pair = k[img, :, lanes]
            q_pair = pad_rows(q[img, :, lanes])
            v_turn = v[img, :, lanes].astype(f32).T.astype(bf16)
            mixed = []
            for sub in range(2):
                h = pair * 2 + sub
                q_one = jnp.where(side == sub, q_pair, jnp.zeros_like(q_pair))
                s = dot_nt(k_pair, q_one) + bias[h]
                top = jnp.max(s, axis=0, keepdims=True)
                e = jnp.exp(s - top)
                total = jnp.sum(e, axis=0, keepdims=True)
                o = dot_nn(v_turn[sub * HD : (sub + 1) * HD], e.astype(bf16))
                mixed.append(o * (1.0 / total))
                lse[img, h : h + 1] = top + jnp.log(total)
            both = jnp.concatenate(mixed, axis=0).T
            att[img, :, lanes] = both[:NP].astype(bf16)
            hook("pair", img * (H // 2) + pair + 1)
    out.start(att, att_o)

    @pl.loop(0, imgs)
    def _(img):
        branch = dot_nn(att[img], w[3]) + vec[4:5]
        bra[img] = branch
        middle = tok[img].astype(f32) + vec[5:6] * branch
        mid[img] = middle
        x, _ = norm_parts(middle)
        n2[img] = (x * vec[6:7] + vec[7:8]).astype(bf16)

    out.start(bra, bra_o)
    out.start(mid, mid_o)
    out.start(n2, n2_o)
    chunk_slots(mlp_own, parts, each, mlp_at)
    step_m(6)
    out.finish()


def forward_attention(comm, parts, each, own, mlp_own, tokens, vec, rel, table, attn, mlp=None):
    imgs = tokens.shape[1] // NPOS
    big = ((imgs, NP, D), bf16)
    tall = ((imgs, NP, D), f32)
    kept = [
        ((4, D, D), bf16),
        big,
        big,
        big,
        big,
        tall,
        tall,
        big,
        ((H, NP, NL), f32),
        big,
    ]
    out_shape = [shape(*k) for k in kept] + [shape((imgs, H, NL), f32), shape((NP, NL), jnp.int32)]
    out_shape.append(shape((FF // CH * 2 * T * PER,), jnp.int32))
    out_specs = [ANY] * len(kept) + [VMEM, VMEM, SMEM]
    wide = -(-table.shape[1] // B) * B
    scratch = [pltpu.VMEM(*k) for k in kept] + [
        pltpu.VMEM((imgs * NP, D), bf16),
        pltpu.VMEM((H, wide), f32),
        pltpu.VMEM((NL, NL), f32),
        pltpu.VMEM((H, wide // B, 8, B), f32),
        pltpu.VMEM((tokens.shape[1] // 16 * 16 + 16, D), f32),
        pltpu.SemaphoreType.DMA((len(kept),)),
    ]
    args = [own, mlp_own, tokens, vec, rel, table, attn]
    specs = [SMEM, SMEM, VMEM, VMEM, VMEM, VMEM]
    params = dict(vmem_limit_bytes=LIMIT)
    if comm:
        na, nm = attn.shape[0], mlp.shape[1]
        args.append(mlp)
        specs += [ANY, ANY]
        out_shape.append(shape((32 * nm, B, B), bf16))
        out_specs.append(ANY)
        scratch += [
            pltpu.VMEM((na, B, B), f32),
            pltpu.VMEM((nm, B, B), f32),
            pltpu.VMEM((na, B, B), bf16),
            pltpu.VMEM((nm, B, B), bf16),
            pltpu.VMEM((32 * na, B, B), bf16),
            pltpu.SemaphoreType.DMA((2,)),
        ]
        scratch += gather_scratch() + gather_scratch()
        params.update(collective_id=0, has_side_effects=True)
    else:
        specs.append(VMEM)
    return pl.pallas_call(
        partial(forward_kernel, comm, parts, each),
        in_specs=specs,
        out_specs=out_specs,
        out_shape=out_shape,
        scratch_shapes=scratch,
        compiler_params=pltpu.CompilerParams(**params),
        name="forward_attention",
    )(*args)


def mlp_kernel(
    at,
    mid_h,
    bra_h,
    n2,
    cot,
    slots,
    vec,
    upb,
    out,
    gmid,
    gbra,
    sums,
    bgrad,
    tiles_out,
    mid,
    bra,
    last,
    w1,
    w2,
    gs,
    act,
    gh,
    summed,
    gn2,
    tiles,
    sem_in,
    sem_out,
    sem_load,
):
    imgs = mid.shape[0]
    length = cot.shape[0] // LANES
    chunks = FF // CH

    @pl.loop(0, chunks)
    def _(c):
        base = c * 2 * T * PER
        for t in range(T * PER):
            r, cc = t // PER * B, t % PER * B
            pltpu.make_async_copy(
                slots.at[at[base + t]], w1.at[c, r : r + B, cc : cc + B], sem_in.at[c]
            ).start()
            r, cc = t // T * B, t % T * B
            pltpu.make_async_copy(
                slots.at[at[base + T * PER + t]], w2.at[c, r : r + B, cc : cc + B], sem_in.at[c]
            ).start()

    load = Local(sem_load)
    load.start(mid_h, mid)
    load.start(bra_h, bra)
    last[...] = jnp.zeros_like(last)
    last[:NPOS] = load_rows(cot, length - NPOS, NPOS)

    def upstream(img):
        if img == imgs - 1:
            return last[...]
        return jnp.where(real_rows(), load_rows(cot, img * NPOS, NP), 0.0)

    for img in range(imgs):
        gs[img * NP : (img + 1) * NP] = (vec[9:10] * upstream(img)).astype(bf16)
    summed[...] = jnp.zeros_like(summed)
    gn2[...] = jnp.zeros_like(gn2)

    @pl.loop(0, chunks)
    def _(c):
        pltpu.make_async_copy(w1.at[c], w1.at[c], sem_in.at[c]).wait()
        pltpu.make_async_copy(w2.at[c], w2.at[c], sem_in.at[c]).wait()
        span = pl.ds(pl.multiple_of(c * CH, CH), CH)
        bias_sum = jnp.zeros((1, CH), f32)
        for rb in range(imgs // 2):
            block = slice(rb * 2 * NP, (rb + 1) * 2 * NP)
            hid = dot_nn(n2[block], w1[c]) + upb[:, span]
            back = dot_nt(gs[block], w2[c])
            phi = 0.5 * (1.0 + lax.erf(hid * (1.0 / math.sqrt(2.0))))
            density = jnp.exp(-0.5 * hid * hid) * (1.0 / math.sqrt(2.0 * math.pi))
            a = (hid * phi).astype(bf16)
            g = (back * (phi + hid * density)).astype(bf16)
            act[block] = a
            gh[block] = g
            bias_sum = bias_sum + jnp.sum(g.astype(f32), axis=0, keepdims=True)
            summed[block] += dot_nn(a, w2[c])
            gn2[block] += dot_nt(g, w1[c])
        bgrad[:, span] = bias_sum
        up_grad = dot_tn(n2[...], gh[...])
        down_grad = dot_tn(act[...], gs[...])
        base = c * 2 * T * PER
        for t in range(T * PER):
            r, cc = t // PER * B, t % PER * B
            tiles[c, t] = up_grad[r : r + B, cc : cc + B].astype(bf16)
            pltpu.make_async_copy(tiles.at[c, t], tiles_out.at[at[base + t]], sem_out).start()
        for t in range(T * PER):
            r, cc = t // T * B, t % T * B
            to = T * PER + t
            tiles[c, to] = down_grad[r : r + B, cc : cc + B].astype(bf16)
            pltpu.make_async_copy(tiles.at[c, to], tiles_out.at[at[base + to]], sem_out).start()

    load.finish()
    s4 = jnp.zeros((1, D), f32)
    s5 = jnp.zeros((1, D), f32)
    s6 = jnp.zeros((1, D), f32)
    s7 = jnp.zeros((1, D), f32)
    s8 = jnp.zeros((1, D), f32)
    s9 = jnp.zeros((1, D), f32)
    for img in range(imgs):
        block = slice(img * NP, (img + 1) * NP)
        up = upstream(img)
        middle = mid[img]
        sm = summed[block] + vec[8:9]
        s9 += jnp.sum(up * sm, axis=0, keepdims=True)
        s8 += jnp.sum(gs[block].astype(f32), axis=0, keepdims=True)
        x, inv = norm_parts(middle)
        gn = gn2[block]
        s6 += jnp.sum(gn * x, axis=0, keepdims=True)
        s7 += jnp.sum(gn, axis=0, keepdims=True)
        gm = up + norm_back(gn, x, inv, vec[6:7])
        gmid[img] = gm
        gb = (vec[5:6] * gm).astype(bf16)
        gbra[img] = gb
        s4 += jnp.sum(gb.astype(f32), axis=0, keepdims=True)
        s5 += jnp.sum(gm * bra[img], axis=0, keepdims=True)
        summed[img * NPOS : img * NPOS + NP] = middle + vec[9:10] * sm
    edge = length // 16 * 16
    out[0, :edge] = summed[:edge].astype(bf16)
    out[0, edge:] = summed[edge:length].astype(bf16)
    sums[...] = jnp.concatenate([s4, s5, s6, s7, s8, s9, s9, s9], axis=0)
    pltpu.make_async_copy(tiles, tiles, sem_out).wait()


def feed_forward(mid, bra, n2, cot, slots, at, vec, up_bias):
    imgs = mid.shape[0]
    rows = imgs * NP
    chunks = FF // CH
    return pl.pallas_call(
        mlp_kernel,
        in_specs=[SMEM, ANY, ANY, VMEM, VMEM, ANY, VMEM, VMEM],
        out_specs=[VMEM] * 5 + [ANY],
        out_shape=[
            shape((1, imgs * NPOS, D), bf16),
            shape((imgs, NP, D), f32),
            shape((imgs, NP, D), bf16),
            shape((8, D), f32),
            shape((1, FF), f32),
            shape(slots.shape, bf16),
        ],
        scratch_shapes=[
            pltpu.VMEM((imgs, NP, D), f32),
            pltpu.VMEM((imgs, NP, D), f32),
            pltpu.VMEM((NP, D), f32),
            pltpu.VMEM((chunks, D, CH), bf16),
            pltpu.VMEM((chunks, CH, D), bf16),
            pltpu.VMEM((rows, D), bf16),
            pltpu.VMEM((rows, CH), bf16),
            pltpu.VMEM((rows, CH), bf16),
            pltpu.VMEM((rows, D), f32),
            pltpu.VMEM((rows, D), f32),
            pltpu.VMEM((chunks, 2 * T * PER, B, B), bf16),
            pltpu.SemaphoreType.DMA((chunks,)),
            pltpu.SemaphoreType.DMA(()),
            pltpu.SemaphoreType.DMA((2,)),
        ],
        compiler_params=pltpu.CompilerParams(vmem_limit_bytes=LIMIT),
        name="feed_forward",
    )(at, mid, bra, n2.reshape(rows, D), cot, slots, vec, up_bias)


def backward_kernel(comm, inverse, gbra, lse, vec, idx, *refs):
    refs = list(refs)
    w_h, v_h, k_h, q_h, bias_h, att_h, tok_h, gmid_h = refs[:8]
    refs = refs[8:]
    if comm:
        mlp_full = refs.pop(0)
    gin, table, sums, tiles_o = refs[:4]
    refs = refs[4:]
    if comm:
        mlp_mine = refs.pop(0)
    w, v, k, q, bias, att, tok, gmid = refs[:8]
    n1, gatt, gqkv, grid, tiles, full, load_sems, out_sem = refs[8:16]
    refs = refs[16:]
    imgs = q.shape[0]

    if comm:
        place = Place()
        place.greet()
        moves = Scatter(place, mlp_full, mlp_mine.shape[0], *refs)
        step = moves.step
    else:
        step = lambda i, out=None: None
    load = Local(load_sems)
    got_w, got_v, got_k, got_q, got_bias, got_att, got_tok, got_gmid = [
        load.start(src, dst)
        for src, dst in zip(
            (w_h, v_h, k_h, q_h, bias_h, att_h, tok_h, gmid_h), (w, v, k, q, bias, att, tok, gmid)
        )
    ]
    step(-1)
    step(0)
    got_w.wait()
    for n in range(D // NL):
        lanes = slice(n * NL, (n + 1) * NL)
        got = dot_nt(gbra[...], w[3, lanes, :]).astype(bf16)
        for img in range(imgs):
            gatt[img, :, lanes] = got[img * NP : (img + 1) * NP]
    grid[...] = jnp.zeros_like(grid)
    got_v.wait()
    got_k.wait()
    got_q.wait()
    got_bias.wait()
    plan = {4: 1, 12: 2, 18: 3}

    side = lax.broadcasted_iota(jnp.int32, (1, B), 1) // HD
    for img in range(imgs):
        here = slice(img * NP, (img + 1) * NP)
        for pair in range(H // 2):
            lanes = slice(pair * B, (pair + 1) * B)
            k_pair = k[img, :, lanes]
            v_pair = v[img, :, lanes]
            q_pair = pad_rows(q[img, :, lanes])
            g_pair = pad_rows(gatt[img, :, lanes])
            k_turn = k_pair.astype(f32).T.astype(bf16)
            gq = []
            gk = jnp.zeros((NP, B), f32)
            gv = jnp.zeros((NP, B), f32)
            for sub in range(2):
                h = pair * 2 + sub
                q_one = jnp.where(side == sub, q_pair, jnp.zeros_like(q_pair))
                g_one = jnp.where(side == sub, g_pair, jnp.zeros_like(g_pair))
                s = dot_nt(k_pair, q_one) + bias[h]
                p = jnp.exp(s - lse[img, h : h + 1])
                dp = dot_nt(v_pair, g_one)
                gv = gv + dot_nn(p.astype(bf16), g_one)
                inner = jnp.sum(p * dp, axis=0, keepdims=True)
                ds = (p * (dp - inner)).astype(bf16)
                gk = gk + dot_nn(ds, q_one)
                gq.append(dot_nn(k_turn[sub * HD : (sub + 1) * HD], ds))
                grid[h] += ds.astype(f32)
            turned = jnp.concatenate(gq, axis=0).T
            gqkv[here, lanes] = (turned[:NP] * HD**-0.5).astype(bf16)
            gqkv[here, D + pair * B : D + (pair + 1) * B] = gk.astype(bf16)
            gqkv[here, 2 * D + pair * B : 2 * D + (pair + 1) * B] = gv.astype(bf16)
            if img * (H // 2) + pair + 1 in plan:
                step(plan[img * (H // 2) + pair + 1])

    def put(m, n, grad):
        for r in range(T):
            for cc in range(NL // B):
                tiles[m * T * T + r * T + n * (NL // B) + cc] = grad[
                    r * B : (r + 1) * B, cc * B : (cc + 1) * B
                ].astype(bf16)

    got_att.wait()
    got_tok.wait()
    for img in range(imgs):
        x, _ = norm_parts(tok[img].astype(f32))
        n1[img * NP : (img + 1) * NP] = (x * vec[0:1] + vec[1:2]).astype(bf16)
    for n in range(D // NL):
        lanes = slice(n * NL, (n + 1) * NL)
        put(3, n, dot_tn(att[...], gbra[:, lanes]))
    for m in range(3):
        for n in range(D // NL):
            put(m, n, dot_tn(n1[...], gqkv[:, m * D + n * NL : m * D + (n + 1) * NL]))

    @pl.loop(0, full.shape[0] // 4)
    def _(group):
        for i in range(4):
            full[group * 4 + i] = tiles[inverse[group * 4 + i]]

    out = pltpu.make_async_copy(full, tiles_o, out_sem)
    out.start()
    step(4)
    accumulate_rows(grid, idx, table)

    got_gmid.wait()
    s0 = jnp.zeros((1, D), f32)
    s1 = jnp.zeros((1, D), f32)
    s2 = jnp.zeros((1, D), f32)
    s3 = jnp.zeros((1, D), f32)
    for img in range(imgs):
        here = slice(img * NP, (img + 1) * NP)
        gq = gqkv[here, 0:D]
        gk = gqkv[here, D : 2 * D]
        gv = gqkv[here, 2 * D : 3 * D]
        gn = dot_nt(gq, w[0]) + dot_nt(gk, w[1]) + dot_nt(gv, w[2])
        x, inv = norm_parts(tok[img].astype(f32))
        s0 += jnp.sum(gn * x, axis=0, keepdims=True)
        s1 += jnp.sum(gn, axis=0, keepdims=True)
        s2 += jnp.sum(gq.astype(f32), axis=0, keepdims=True)
        s3 += jnp.sum(gv.astype(f32), axis=0, keepdims=True)
        got = gmid[img] + norm_back(gn, x, inv, vec[0:1])
        store_rows(gin, img * NPOS, got[:NPOS] if img == imgs - 1 else got)
    sums[...] = jnp.concatenate([s0, s1, s2, s3, s3, s3, s3, s3], axis=0)
    if comm:
        step(5, mlp_mine)
    out.wait()


def backward_attention(comm, inverse, saved, gmid, gbra, vec, wide_total, mlp_full=None):
    w, q, k, v, att, mid, bra, n2, bias, tok, lse, idx = saved
    imgs = tok.shape[0]
    rows = imgs * NP
    att = att.reshape(rows, D)
    loaded = [w, v, k, q, bias, att, tok, gmid]
    args = [inverse, gbra.reshape(rows, D), lse, vec, idx] + loaded
    specs = [SMEM] + [VMEM] * 4 + [ANY] * 8
    out_shape = [
        shape((imgs * NPOS * LANES, B), f32),
        shape((16, wide_total), f32),
        shape((8, D), f32),
        shape((inverse.shape[0], B, B), bf16),
    ]
    out_specs = [VMEM] * 3 + [ANY]
    scratch = [pltpu.VMEM(x.shape, x.dtype) for x in loaded] + [
        pltpu.VMEM((rows, D), bf16),
        pltpu.VMEM((imgs, NP, D), bf16),
        pltpu.VMEM((rows, 3 * D), bf16),
        pltpu.VMEM((H, NP, NL), f32),
        pltpu.VMEM((4 * T * T, B, B), bf16),
        pltpu.VMEM((inverse.shape[0], B, B), bf16),
        pltpu.SemaphoreType.DMA((8,)),
        pltpu.SemaphoreType.DMA(()),
    ]
    params = dict(vmem_limit_bytes=LIMIT)
    if comm:
        n = mlp_full.shape[0] // 32
        args.append(mlp_full)
        specs.append(ANY)
        out_shape.append(shape((n, B, B), f32))
        out_specs.append(VMEM)
        scratch += scatter_scratch(n)
        params.update(collective_id=1, has_side_effects=True)
    return pl.pallas_call(
        partial(backward_kernel, comm),
        in_specs=specs,
        out_specs=out_specs,
        out_shape=out_shape,
        scratch_shapes=scratch,
        compiler_params=pltpu.CompilerParams(**params),
        name="backward_attention",
    )(*args)


NB = 16
GROUP = B // NB


def split_two(x):
    first = x.astype(bf16)
    return first, (x - first.astype(f32)).astype(bf16)


def wide_dot(x, y, dims):
    xa, xb = split_two(x)
    ya, yb = split_two(y)
    xs = jnp.concatenate([xa, xa, xb], axis=dims[0])
    ys = jnp.concatenate([ya, yb, ya], axis=dims[1])
    return lax.dot_general(
        xs, ys, (((dims[0],), (dims[1],)), ((), ())), preferred_element_type=f32
    )


def unit_inverse(diag):
    lane = lax.broadcasted_iota(jnp.int32, (NB, B), 1)
    row = lax.broadcasted_iota(jnp.int32, (NB, B), 0)
    inner = jnp.bitwise_and(lane, NB - 1)
    outer = lane - inner
    left = diag
    right = jnp.where(row == inner, 1.0, 0.0)
    def pick(k):
        return jnp.take_along_axis(diag, outer + k, axis=1, mode="promise_in_bounds")

    cut = NB // 2
    rows = [pick(r) for r in range(NB)]
    rows = [x if r < cut else x[cut:] for r, x in enumerate(rows)]
    flags = [jnp.where(row == r, 1.0, 0.0) for r in range(NB)]
    low = [x[:cut] for x in flags]
    high = [x[cut:] for x in flags]
    cols = [diag[r : r + 1] for r in range(NB)]
    pivots = jnp.zeros((1, B), f32)
    right_low, right_high = right[:cut], right[cut:]
    for r in range(NB):
        mine = rows[r]
        at = r if r < cut else r - cut
        pivot = mine[at : at + 1]
        pivots = jnp.where(inner[:1] == r, pivot, pivots)
        scale = pl.reciprocal(pivot, approx=True)
        scale = scale * (2.0 - pivot * scale)
        factor = jnp.where(inner[:1] > r, cols[r] * scale, 0.0)
        for s in range(r + 1, NB):
            at = s if r < cut else s - cut
            entry = mine[at : at + 1]
            share = entry * scale
            rows[s] = rows[s] - share * (mine if s < cut or r >= cut else mine[cut:])
            low[s] = low[s] - share * low[r]
            if r >= cut:
                high[s] = high[s] - share * high[r]
            cols[s] = cols[s] - factor * entry
        right_low = right_low - factor * low[r]
        if r >= cut:
            right_high = right_high - factor * high[r]
    right = jnp.concatenate([right_low, right_high], axis=0)
    return right * lax.rsqrt(pivots)


def orth_turned(mats, between=None):
    count = len(mats)
    groups = -(-count // GROUP)
    size = -(-count // groups)
    members = [list(range(g * size, min(count, (g + 1) * size))) for g in range(groups)]
    tails = []
    for a in mats:
        turned = a.T
        tails.append(jnp.concatenate([wide_dot(turned, turned, (1, 1)), turned], axis=1))
    own_block = (
        lax.broadcasted_iota(jnp.int32, (B, B), 0) // NB
        == lax.broadcasted_iota(jnp.int32, (B, B), 1) // NB
    )
    outs = [[] for _ in range(count)]
    for p in range(B // NB):
        base = p * NB
        for ids in members:
            fill = ids + [ids[-1]] * (GROUP - len(ids))
            strips = jnp.concatenate([tails[m][:NB] for m in fill], axis=0)
            turned = strips[:, :B].T
            unit = unit_inverse(turned[base : base + NB])
            spread = jnp.where(own_block, jnp.concatenate([unit] * GROUP, axis=0), 0.0)
            u = wide_dot(spread, strips, (0, 0))
            for at, m in enumerate(ids):
                um = u[at * NB : (at + 1) * NB]
                outs[m].append(um[:, B:])
                if base + NB < B:
                    tails[m] = tails[m][NB:] - wide_dot(um[:, base + NB : B], um, (0, 0))
        if between is not None:
            between(p)
    return [jnp.concatenate(o, axis=0) for o in outs]


def soap_slots(base, owner, grads, state, update, copy, between=None):
    count = grads.shape[0]
    mats = []
    gs = []
    for i in range(count):
        named = jnp.where(owner[...] == base + i, 1.0, 0.0)
        named = jnp.max(named, axis=1, keepdims=True)
        g = jnp.where(named > 0.0, grads[i].astype(f32), 0.0)
        gs.append(g)
        left = beta_stat * state[i, 3] + (1.0 - beta_stat) * wide_dot(g, g, (1, 1))
        right = beta_stat * state[i, 4] + (1.0 - beta_stat) * wide_dot(g, g, (0, 0))
        mats.append(wide_dot(left, state[i, 5], (1, 0)))
        mats.append(wide_dot(right, state[i, 6], (1, 0)))
    if between is not None:
        between(-1)
    turned = orth_turned(mats, between)
    fix_one = 1.0 - beta_one**STEP
    fix_two = 1.0 - beta_two**STEP
    for i in range(count):
        tl, tr = turned[2 * i], turned[2 * i + 1]
        rotated = wide_dot(wide_dot(tl, gs[i], (1, 0)), tr, (1, 1))
        new_first = beta_one * state[i, 1] + (1.0 - beta_one) * rotated
        new_second = beta_two * state[i, 2] + (1.0 - beta_two) * rotated * rotated
        normalized = new_first / fix_one / (jnp.sqrt(new_second / fix_two) + adam_eps)
        step = wide_dot(wide_dot(tl, normalized, (0, 0)), tr, (1, 0))
        weight = state[i, 0]
        weight = weight - matrix_rate * (step + decay_rate * weight)
        update[i, 0] = weight
        update[i, 1] = new_first
        update[i, 2] = new_second
        update[i, 3] = tl.T
        update[i, 4] = tr.T
        copy[i] = weight.astype(bf16)


def soap_kernel(first_slot, passed, owner, grads, state, *refs):
    kept, refs = refs[:passed], refs[passed:]
    update, copy = refs[:2]
    through, held, sems = refs[2 : 2 + passed], refs[2 + passed : 2 + 2 * passed], refs[2 + 2 * passed :]
    count = grads.shape[0]
    between = None
    if passed:
        into, out = Local(sems[0]), Local(sems[1])
        for src, dst in zip(kept, held):
            into.start(src, dst)

        def between(p):
            if p == 2:
                into.finish()
                for src, dst in zip(held, through):
                    out.start(src, dst)

    first = first_slot() + pl.program_id(0) * count
    soap_slots(first, owner, grads, state, update, copy, between)
    if passed:
        out.finish()


def soap_update(grads, state, owner, first_slot, kept=()):
    slots = grads.shape[0]
    count = max(c for c in range(1, 10) if slots % c == 0)
    assert not kept or count == slots
    return pl.pallas_call(
        partial(soap_kernel, first_slot, len(kept)),
        grid=(slots // count,),
        in_specs=[
            pl.BlockSpec((1, owner.shape[0]), lambda i: (0, 0)),
            pl.BlockSpec((count, B, B), lambda i: (i, 0, 0)),
            pl.BlockSpec((count, 7, B, B), lambda i: (i, 0, 0, 0)),
        ]
        + [ANY] * len(kept),
        out_specs=[
            pl.BlockSpec((count, 5, B, B), lambda i: (i, 0, 0, 0)),
            pl.BlockSpec((count, B, B), lambda i: (i, 0, 0)),
        ]
        + [ANY] * len(kept),
        out_shape=[shape((slots, 5, B, B), f32), shape((slots, B, B), bf16)]
        + [shape(x.shape, x.dtype) for x in kept],
        scratch_shapes=[pltpu.VMEM(x.shape, x.dtype) for x in kept]
        + [pltpu.SemaphoreType.DMA((len(kept),))] * (2 if kept else 0),
        compiler_params=pltpu.CompilerParams(vmem_limit_bytes=LIMIT),
        name="soap",
    )(owner[None], grads, state, *kept)


SUM_ROWS = 40


def adam(grad, param, first, second):
    new_first = beta_one * first + (1.0 - beta_one) * grad
    new_second = beta_two * second + (1.0 - beta_two) * grad * grad
    fix_one = 1.0 - beta_one**STEP
    fix_two = 1.0 - beta_two**STEP
    step = (new_first / fix_one) / (jnp.sqrt(new_second / fix_two) + adam_eps)
    return grad, param - vector_rate * step, new_first, new_second


def finish_kernel(
    full,
    mlp_sums,
    attn_sums,
    table_sums,
    bias_sums,
    vec,
    vec_m,
    table,
    table_m,
    upb,
    upb_m,
    owner,
    mlp_mine,
    state_h,
    mine,
    vec_up,
    table_up,
    upb_up,
    update,
    copy,
    state,
    load_sem,
    part,
    other,
    column,
    sum_send,
    sum_recv,
    *scratch,
):
    place = Place()
    place.greet()
    load = pltpu.make_async_copy(state_h.at[0], state, load_sem)
    load.start()

    moves = Scatter(place, full, mine.shape[0], *scratch)
    sums = Copies(place, sum_send, sum_recv)
    part[0, 0:8] = mlp_sums[...]
    part[0, 8:16] = attn_sums[...]
    part[0, 16:32] = table_sums[...]
    quarter = jnp.concatenate([bias_sums[:, i * D : (i + 1) * D] for i in range(FF // D)] * 2, axis=0)
    part[0, 32:40] = quarter
    sums.start("c", part.at[0], other.at[0], dc=1)
    moves.step(-1)
    moves.step(0)
    load.wait()

    def total_sums():
        part[4] = ((column[0] + column[1]) + column[2]) + column[3]
        total = part.at[4]
        grad = jnp.concatenate([total[8:12], total[0:6]], axis=0)
        for i, got in enumerate(adam(grad, vec[...], vec_m[:, 0, :], vec_m[:, 1, :])):
            vec_up[:, i, :] = got
        wide = table.shape[1]
        grad = total[16 : 16 + H, 0:wide]
        for i, got in enumerate(adam(grad, table[...], table_m[:, 0, :], table_m[:, 1, :])):
            table_up[:, i, :] = got
        for j in range(FF // D):
            lanes = slice(j * D, (j + 1) * D)
            for i, got in enumerate(
                adam(total[32 + j : 33 + j], upb[:, lanes], upb_m[0:1, lanes], upb_m[1:2, lanes])
            ):
                upb_up[i : i + 1, lanes] = got

    steps = {-1: 1, 1: 2, 3: 3, 6: 4}
    sends = (-1, 0, 2)

    def between(p):
        if p in steps:
            moves.step(steps[p])
        if p == sends[0]:
            sums.arrived("c")
            part[1] = part[0] + other[0]
            sums.start("x", part.at[1], other.at[1], dx=1)
        elif p == sends[1]:
            sums.arrived("x")
            part[2] = part[1] + other[1]
            sums.start("y", part.at[2], other.at[2], dy=1)
        elif p == sends[2]:
            sums.arrived("y")
            part[3] = part[2] + other[2]
            for d in (1, 2, 3):
                sums.start(("z", d), part.at[3], column.at[place.z], d=d)
            column[place.z] = part[3]

    first_slot = lax.axis_index("dp") * mlp_mine.shape[0]
    soap_slots(first_slot, owner, mlp_mine, state, update, copy, between)
    for d in (1, 2, 3):
        sums.arrived(("z", d))
    total_sums()
    moves.step(5, mine)
    sums.sent()


def finish(full, small, params, owner, mlp_mine, mlp_state):
    n = full.shape[0] // 32
    nm = mlp_mine.shape[0]
    vec, vec_m, table, table_m, upb, upb_m = params
    return pl.pallas_call(
        finish_kernel,
        in_specs=[ANY] + [VMEM] * 12 + [ANY],
        out_specs=[VMEM] * 6,
        out_shape=[
            shape((n, B, B), f32),
            shape((vec.shape[0], 4, D), f32),
            shape((H, 4, table.shape[1]), f32),
            shape((4, FF), f32),
            shape((nm, 5, B, B), f32),
            shape((nm, B, B), bf16),
        ],
        scratch_shapes=[
            pltpu.VMEM((nm, 7, B, B), f32),
            pltpu.SemaphoreType.DMA(()),
            pltpu.VMEM((5, SUM_ROWS, D), f32),
            pltpu.VMEM((3, SUM_ROWS, D), f32),
            pltpu.VMEM((4, SUM_ROWS, D), f32),
            pltpu.SemaphoreType.DMA((6,)),
            pltpu.SemaphoreType.DMA((6,)),
        ]
        + scatter_scratch(n),
        compiler_params=pltpu.CompilerParams(
            collective_id=2, has_side_effects=True, vmem_limit_bytes=LIMIT
        ),
        name="finish",
    )(
        full,
        *small,
        vec,
        vec_m.transpose(1, 0, 2),
        table,
        table_m.transpose(1, 0, 2),
        upb[None],
        upb_m,
        owner[None],
        mlp_mine,
        mlp_state,
    )


def body(
    tokens,
    cotangent,
    rel_index,
    attn_owner,
    mlp_owner,
    attn_state,
    mlp_state,
    vec_param,
    vec_moments,
    rel_table,
    rel_table_moments,
    up_bias,
    up_bias_moments,
):
    both = ("dp", "mp")
    parts = lax.axis_size("mp")
    comm = own_kernels(lax.axis_size("dp"), parts)
    imgs = tokens.shape[1] // NPOS
    attn_local = attn_state.shape[0]
    mlp_local = mlp_state.shape[1]
    attn_total = attn_local * lax.axis_size("dp") * parts

    def attn_first():
        return (lax.axis_index("dp") * parts + lax.axis_index("mp")) * attn_local

    def mlp_first():
        return lax.axis_index("dp") * mlp_local

    wide_total = -(-rel_table.shape[1] // B) * B
    slot_ids = jnp.arange(attn_total, dtype=jnp.int32)
    block_ids = jnp.arange(attn_owner.shape[0], dtype=jnp.int32)
    inverse = jnp.sum(
        jnp.where(attn_owner[None, :] == slot_ids[:, None], block_ids[None, :], 0), axis=1
    ).astype(jnp.int32)

    if comm:
        *saved, mlp_slots = forward_attention(
            True,
            parts,
            mlp_local,
            attn_owner,
            mlp_owner,
            tokens,
            vec_param, rel_index, rel_table, attn_state, mlp_state
        )
    else:
        attn_slots = lax.all_gather(attn_state[:, 0].astype(bf16), both, axis=0, tiled=True)
        mlp_slots = lax.all_gather(mlp_state[0, :, 0].astype(bf16), both, axis=0, tiled=True)
        saved = list(
            forward_attention(
            False,
            parts,
            mlp_local,
            attn_owner,
            mlp_owner,
            tokens,
            vec_param, rel_index, rel_table, attn_slots
        ))
    mlp_at = saved.pop()
    w, q, k, v, att, mid, bra, n2, bias, tok, lse, idx = saved
    out, gmid, gbra, mlp_sums, bias_grad, mlp_grads = feed_forward(
        mid, bra, n2, cotangent.reshape(-1, B), mlp_slots, mlp_at, vec_param, up_bias[None]
    )
    if comm:
        gin, table_grad, attn_sums, attn_full, mlp_mine = backward_attention(
            True, inverse, saved, gmid, gbra, vec_param, wide_total, mlp_grads
        )
        attn_mine, vec_up, table_up, bias_up, mlp_result, mlp_copy = finish(
            attn_full,
            (mlp_sums, attn_sums, table_grad, bias_grad),
            (vec_param, vec_moments, rel_table, rel_table_moments, up_bias, up_bias_moments),
            mlp_owner,
            mlp_mine,
            mlp_state,
        )
        kept = (gin, mlp_result, mlp_copy, vec_up, table_up, bias_up)
        attn_result, attn_copy, *kept = soap_update(
            attn_mine, attn_state, attn_owner, attn_first, kept
        )
        gin, mlp_result, mlp_copy, vec_up, table_up, bias_up = kept
        vec_up = vec_up.transpose(1, 0, 2)
        table_up = table_up.transpose(1, 0, 2)
    else:
        gin, table_grad, attn_sums, attn_full = backward_attention(
            False, inverse, saved, gmid, gbra, vec_param, wide_total
        )
        mlp_mine = lax.psum_scatter(mlp_grads, both, scatter_dimension=0, tiled=True)
        attn_mine = lax.psum_scatter(attn_full, both, scatter_dimension=0, tiled=True)
        vector_grad = jnp.concatenate([attn_sums[:4], mlp_sums[:6]], axis=0)
        vector_total, table_total, bias_total = lax.psum(
            (vector_grad, table_grad[:H, : rel_table.shape[1]], bias_grad[0]), both
        )
        vec_up = jnp.stack(adam(vector_total, vec_param, vec_moments[0], vec_moments[1]))
        table_up = jnp.stack(
            adam(table_total, rel_table, rel_table_moments[0], rel_table_moments[1])
        )
        bias_up = jnp.stack(adam(bias_total, up_bias, up_bias_moments[0], up_bias_moments[1]))
        attn_result, attn_copy = soap_update(attn_mine, attn_state, attn_owner, attn_first)
        mlp_result, mlp_copy = soap_update(mlp_mine, mlp_state[0], mlp_owner, mlp_first)
    return (
        out,
        gin.reshape(1, imgs * NPOS, D),
        attn_result,
        attn_copy,
        mlp_result[None],
        mlp_copy[None],
        vec_up,
        table_up,
        bias_up,
    )


def solution(mesh):
    placed = (
        P(("dp", "mp"), None, None),
        P(("dp", "mp"), None, None),
        P(),
        P(),
        P(),
        P(("dp", "mp"), None, None, None),
        P("mp", "dp", None, None, None),
        P(),
        P(),
        P(),
        P(),
        P(),
        P(),
    )
    return jax.shard_map(
        body,
        mesh=mesh,
        in_specs=placed,
        out_specs=(
            P(("dp", "mp"), None, None),
            P(("dp", "mp"), None, None),
            P(("dp", "mp"), None, None, None),
            P(("dp", "mp"), None, None),
            P("mp", "dp", None, None, None),
            P("mp", "dp", None, None),
            P(),
            P(),
            P(),
        ),
        check_vma=False,
    )
```

```python
from functools import partial
import math

import jax
import jax.numpy as jnp
from jax import lax
from jax.experimental import pallas as pl
from jax.experimental.pallas import tpu as pltpu
from jax.sharding import PartitionSpec as P

D = 768
H = 12
HD = 64
FF = 3072
NPOS = 197
NP = 208
NL = 256
B = 128
STEP = 5
T = D // B

f32 = jnp.float32
bf16 = jnp.bfloat16

ln_eps = 1e-06
beta_one = 0.9
beta_two = 0.95
beta_stat = 0.95
adam_eps = 1e-08
matrix_rate = 0.05
vector_rate = 0.2
decay_rate = 0.05

VMEM = pl.BlockSpec(memory_space=pltpu.VMEM)
SMEM = pl.BlockSpec(memory_space=pltpu.SMEM)
ANY = pl.BlockSpec(memory_space=pl.ANY)
LIMIT = 60 << 20


def shape(dims, kind):
    return jax.ShapeDtypeStruct(dims, kind)


def dot_nn(x, y):
    return lax.dot_general(x, y, (((1,), (0,)), ((), ())), preferred_element_type=f32)


def dot_nt(x, y):
    return lax.dot_general(x, y, (((1,), (1,)), ((), ())), preferred_element_type=f32)


def dot_tn(x, y):
    return lax.dot_general(x, y, (((0,), (0,)), ((), ())), preferred_element_type=f32)


def norm_parts(values):
    centered = values - jnp.mean(values, axis=-1, keepdims=True)
    inv_std = lax.rsqrt(jnp.mean(centered * centered, axis=-1, keepdims=True) + ln_eps)
    return (centered * inv_std, inv_std)


def norm_back(grad_normed, scaled, inv_std, gain_row):
    tangent = grad_normed * gain_row
    return inv_std * (
        tangent
        - jnp.mean(tangent, axis=-1, keepdims=True)
        - scaled * jnp.mean(tangent * scaled, axis=-1, keepdims=True)
    )


MESH = pl.DeviceIdType.MESH
COPIES = 35


def own_kernels(dp_total, parts):
    return dp_total == 16 and parts == 2


class Place:
    def __init__(self):
        dp = lax.axis_index("dp")
        self.y = lax.axis_index("mp")
        self.z = dp // 4
        self.x = lax.rem(dp // 2, 2)
        self.c = lax.rem(dp, 2)

    def rank(self, d=0, dx=0, dc=0, dy=0):
        z = lax.rem(self.z + d + 4, 4)
        x = 1 - self.x if dx else self.x
        c = 1 - self.c if dc else self.c
        y = 1 - self.y if dy else self.y
        return ((z * 2 + x) * 2 + c) * 2 + y

    def device(self, d=0, dx=0, dc=0, dy=0):
        z = lax.rem(self.z + d + 4, 4)
        x = 1 - self.x if dx else self.x
        c = 1 - self.c if dc else self.c
        y = 1 - self.y if dy else self.y
        return ((z * 2 + x) * 2 + c, y)

    def greet(self):
        barrier = pltpu.get_barrier_semaphore()
        for d, dx, dc, dy in PARTNERS:
            pl.semaphore_signal(
                barrier, inc=1, device_id=self.device(d, dx, dc, dy), device_id_type=MESH
            )
        pl.semaphore_wait(barrier, len(PARTNERS))


PARTNERS = ((1, 0, 0, 0), (2, 0, 0, 0), (3, 0, 0, 0), (0, 1, 0, 0), (0, 0, 1, 0), (0, 0, 0, 1))


class Copies:
    def __init__(self, place, send, recv):
        self.place = place
        self.send = send
        self.recv = recv
        self.made = {}

    def start(self, key, src, dst, **to):
        i = len(self.made)
        copy = pltpu.make_async_remote_copy(
            src_ref=src,
            dst_ref=dst,
            send_sem=self.send.at[i],
            recv_sem=self.recv.at[i],
            device_id=self.place.device(**to),
            device_id_type=MESH,
        )
        copy.start()
        self.made[key] = copy

    def arrived(self, key):
        self.made[key].wait_recv()

    def sent(self):
        for copy in self.made.values():
            copy.wait_send()


class Gather(Copies):
    def __init__(self, place, own, full, n, send, recv, local):
        super().__init__(place, send, recv)
        self.own = own
        self.full = full
        self.n = n
        self.half = n // 2
        self.local = pltpu.make_async_copy(own, self.at(), local)

    def at(self, d=0, dx=0, dc=0, dy=0, lo=0, hi=None):
        hi = self.n if hi is None else hi
        return self.full.at[pl.ds(self.place.rank(d, dx, dc, dy) * self.n + lo, hi - lo)]

    def spread(self, d):
        src = self.own if d == 0 else self.at(d=-d)
        dst = self.at(d=-d)
        self.start(("x", d), src, dst, dx=1)
        self.start(("y", d), src, dst, dy=1)
        self.start(("c", d, 0, 0), src, dst, dc=1)

    def along(self, d):
        self.start(("z", d), self.own, self.at(), d=d)

    def share(self, d, dx, dy):
        ref = self.at(d=-d, dx=dx, dy=dy)
        self.start(("c", d, dx, dy), ref, ref, dc=1)

    def corner(self, d):
        ref = self.at(d=-d, dy=1, lo=self.half)
        self.start(("xd", d), ref, ref, dx=1)
        ref = self.at(d=-d, dx=1, hi=self.half)
        self.start(("yd", d), ref, ref, dy=1)

    def sides(self, d):
        self.arrived(("x", d))
        self.share(d, 1, 0)
        self.arrived(("y", d))
        self.share(d, 0, 1)

    def cornered(self, d):
        self.arrived(("xd", d))
        self.arrived(("yd", d))
        self.share(d, 1, 1)

    def step(self, i):
        if i == 0:
            self.local.start()
            self.along(1)
            self.spread(0)
        elif i == 1:
            self.arrived(("z", 1))
            self.along(3)
            self.spread(1)
            self.sides(0)
        elif i == 2:
            self.arrived(("z", 3))
            self.along(2)
            self.spread(3)
            self.sides(1)
            self.corner(0)
        elif i == 3:
            self.corner(1)
            self.sides(3)
        elif i == 4:
            self.arrived(("z", 2))
            self.spread(2)
            self.cornered(0)
            self.corner(3)
            self.cornered(1)
        elif i == 5:
            self.sides(2)
            self.corner(2)
            self.cornered(3)
        else:
            self.cornered(2)
            for d in range(4):
                for dx in range(2):
                    for dy in range(2):
                        self.arrived(("c", d, dx, dy))
            self.local.wait()
            self.sent()


GATHER_STEPS = 7


class Scatter(Copies):
    def __init__(self, place, full, n, acc, peer, side, corner, along, send, recv, local):
        super().__init__(place, send, recv)
        self.full = full
        self.local = local
        self.mine = {}
        self.n = n
        self.half = n // 2
        self.acc = acc
        self.peer = peer
        self.side = side
        self.cor = corner
        self.col = along

    def block(self, d, dx, dc, dy):
        return pl.ds(self.place.rank(d, dx, dc, dy) * self.n, self.n)

    def core(self, d, dx, dy):
        key = (d, dx, dy)
        self.start(
            ("c",) + key, self.full.at[self.block(d, dx, 1, dy)], self.peer.at[d, dx, dy], dc=1
        )
        self.mine[key] = pltpu.make_async_copy(
            self.full.at[self.block(d, dx, 0, dy)],
            self.acc.at[d, dx, dy],
            self.local.at[len(self.mine)],
        )
        self.mine[key].start()

    def pair(self, d, dx, dy):
        self.mine[(d, dx, dy)].wait()
        self.arrived(("c", d, dx, dy))
        self.add(d, dx, dy, self.peer.at[d, dx, dy], 0, self.n)

    def add(self, d, dx, dy, other, lo, hi):
        @pl.loop(lo, hi)
        def _(i):
            total = self.acc[d, dx, dy, i].astype(f32) + other[i - lo].astype(f32)
            self.acc[d, dx, dy, i] = total.astype(bf16)

    def corner(self, d):
        self.pair(d, 1, 1)
        h, n = self.half, self.n
        self.start(("xd", d), self.acc.at[d, 1, 1, pl.ds(0, h)], self.cor.at[d, pl.ds(0, h)], dx=1)
        self.start(
            ("yd", d), self.acc.at[d, 1, 1, pl.ds(h, n - h)], self.cor.at[d, pl.ds(h, n - h)], dy=1
        )

    def sides(self, d):
        h, n = self.half, self.n
        self.pair(d, 1, 0)
        self.arrived(("yd", d))
        self.add(d, 1, 0, self.cor.at[d, pl.ds(h, n - h)], h, n)
        self.start(("x", d), self.acc.at[d, 1, 0], self.side.at[d, 0], dx=1)
        self.pair(d, 0, 1)
        self.arrived(("xd", d))
        self.add(d, 0, 1, self.cor.at[d, pl.ds(0, h)], 0, h)
        self.start(("y", d), self.acc.at[d, 0, 1], self.side.at[d, 1], dy=1)

    def along(self, d):
        self.pair(d, 0, 0)
        self.arrived(("x", d))
        self.arrived(("y", d))

        @pl.loop(0, self.n)
        def _(i):
            total = (
                self.acc[d, 0, 0, i].astype(f32)
                + self.side[d, 0, i].astype(f32)
                + self.side[d, 1, i].astype(f32)
            )
            self.acc[d, 0, 0, i] = total.astype(bf16)

        if d > 0:
            self.start(("z", d), self.acc.at[d, 0, 0], self.col.at[d - 1], d=d)

    def step(self, i, out=None):
        if i == -1:
            for dx, dy in ((1, 1), (1, 0), (0, 1), (0, 0)):
                for d in (2, 3, 0, 1):
                    self.core(d, dx, dy)
        elif i == 0:
            self.corner(2)
            self.corner(3)
        elif i == 1:
            self.sides(2)
            self.corner(0)
            self.corner(1)
        elif i == 2:
            self.along(2)
            self.sides(3)
        elif i == 3:
            self.sides(1)
            self.sides(0)
        elif i == 4:
            self.along(3)
            self.along(1)
        else:
            self.along(0)
            for d in (1, 2, 3):
                self.arrived(("z", d))

            @pl.loop(0, self.n)
            def _(i):
                out[i] = (
                    (self.acc[0, 0, 0, i].astype(f32) + self.col[0, i].astype(f32))
                    + self.col[1, i].astype(f32)
                ) + self.col[2, i].astype(f32)

            self.sent()


SCATTER_STEPS = 6


def scatter_scratch(n):
    return [
        pltpu.VMEM((4, 2, 2, n, B, B), bf16),
        pltpu.VMEM((4, 2, 2, n, B, B), bf16),
        pltpu.VMEM((4, 2, n, B, B), bf16),
        pltpu.VMEM((4, n, B, B), bf16),
        pltpu.VMEM((3, n, B, B), bf16),
        pltpu.SemaphoreType.DMA((COPIES,)),
        pltpu.SemaphoreType.DMA((COPIES,)),
        pltpu.SemaphoreType.DMA((16,)),
    ]


def gather_scratch():
    return [
        pltpu.SemaphoreType.DMA((COPIES,)),
        pltpu.SemaphoreType.DMA((COPIES,)),
        pltpu.SemaphoreType.DMA(()),
    ]


class Local:
    def __init__(self, sems):
        self.sems = sems
        self.made = []

    def start(self, src, dst):
        copy = pltpu.make_async_copy(src, dst, self.sems.at[len(self.made)])
        copy.start()
        self.made.append(copy)
        return copy

    def finish(self):
        for copy in self.made:
            copy.wait()


def spread_table(table_ref, wide, spread):
    wide[...] = jnp.zeros_like(wide)
    wide[:, : table_ref.shape[1]] = table_ref[...]
    for h in range(H):
        for c in range(spread.shape[1]):
            spread[h, c] = jnp.broadcast_to(wide[h : h + 1, c * B : (c + 1) * B], (8, B))


def turn_index(rel_ref, square, out_ref):
    square[...] = jnp.zeros_like(square)
    square[:NPOS, :NPOS] = rel_ref[...].astype(f32)
    out_ref[...] = square[...].T[:NP].astype(jnp.int32)


def lookup_rows(idx_ref, spread, out_ref, lo, hi):
    chunks = spread.shape[1]

    @pl.loop(lo, hi)
    def _(jt):
        rows = pl.ds(pl.multiple_of(jt * 8, 8), 8)
        real = jt * 8 + lax.broadcasted_iota(jnp.int32, (8, B), 0) < NPOS
        for half in range(NL // B):
            lanes = slice(half * B, (half + 1) * B)
            idx = idx_ref[rows, lanes]
            low = jnp.bitwise_and(idx, B - 1)
            high = jnp.right_shift(idx, 7)
            for h in range(H):
                acc = jnp.take_along_axis(spread[h, 0], low, axis=1, mode="promise_in_bounds")
                for c in range(1, chunks):
                    part = jnp.take_along_axis(spread[h, c], low, axis=1, mode="promise_in_bounds")
                    acc = jnp.where(high == c, part, acc)
                out_ref[h, rows, lanes] = jnp.where(real, acc, -1e30)


JB = 8


def accumulate_rows(grid_ref, idx_ref, out_ref):
    chunks = out_ref.shape[1] // B
    out_ref[...] = jnp.zeros_like(out_ref)
    lo_rows = lax.broadcasted_iota(jnp.int32, (B, NL), 0)

    @pl.loop(0, NP // JB)
    def _(jb):
        idx_all = idx_ref[pl.ds(pl.multiple_of(jb * JB, JB), JB), :]
        lefts = []
        rights = []
        for jj in range(JB):
            values = grid_ref[:, jb * JB + jj, :]
            values = jnp.concatenate([values, jnp.zeros((16 - H, NL), f32)], axis=0)
            idx = idx_all[jj : jj + 1]
            low = jnp.bitwise_and(idx, B - 1)
            high = jnp.right_shift(idx, 7)
            rights.append(jnp.where(lo_rows == low, 1.0, 0.0).astype(bf16))
            lefts.append(
                jnp.concatenate(
                    [jnp.where(high == c, values, 0.0) for c in range(chunks)], axis=0
                ).astype(bf16)
            )
        got = dot_nt(jnp.concatenate(lefts, axis=1), jnp.concatenate(rights, axis=1))
        for c in range(chunks):
            out_ref[:, c * B : (c + 1) * B] += got[c * 16 : (c + 1) * 16]


CH = 512
PER = CH // B


def chunk_slots(own, parts, each, out):
    half = own.shape[0] // 2
    local = half // T

    def place(slot, p):
        return lax.div(slot, each) * (parts * each) + p * each + lax.rem(slot, each)

    @pl.loop(0, FF // CH)
    def _(c):
        @pl.loop(0, T * PER)
        def _(t):
            g = c * PER + lax.rem(t, PER)
            g2 = c * PER + t // T
            up = own[(t // PER) * local + lax.rem(g, local)]
            down = own[half + lax.rem(g2, local) * T + lax.rem(t, T)]
            out[c * 2 * T * PER + t] = place(up, g // local)
            out[c * 2 * T * PER + T * PER + t] = place(down, g2 // local)


def pad_rows(x):
    return jnp.concatenate([x, jnp.zeros((NL - NP, x.shape[1]), x.dtype)], axis=0)


LANES = D // B


def load_rows(ref, first, count):
    return jnp.concatenate(
        [ref[pl.ds(first * LANES + c, count, stride=LANES), :] for c in range(LANES)], axis=1
    )


def store_rows(ref, first, values):
    count = values.shape[0]
    for c in range(LANES):
        ref[pl.ds(first * LANES + c, count, stride=LANES), :] = values[:, c * B : (c + 1) * B]


def real_rows():
    return lax.broadcasted_iota(jnp.int32, (NP, 1), 0) < NPOS


def forward_kernel(comm, parts, each, own, mlp_own, tokens, vec, rel, table, *refs):
    refs = list(refs)
    if comm:
        attn_state, mlp_state = refs[:2]
        refs = refs[2:]
    else:
        full = refs.pop(0)
    w_o, q_o, k_o, v_o, att_o, mid_o, bra_o, n2_o, bias_o, tok_o, lse, idx, mlp_at = refs[:13]
    refs = refs[13:]
    if comm:
        mlp_all = refs.pop(0)
    w, q, k, v, att, mid, bra, n2, bias, tok, n1, wide, square, spread, long, out_sems = refs[:16]
    refs = refs[16:]
    out = Local(out_sems)
    imgs = q.shape[0]
    edge = tokens.shape[1] // 16 * 16

    if comm:
        a32, m32, a16, m16, full, load_sems = refs[:6]
        a_sems = refs[6:9]
        m_sems = refs[9:12]
        na, nm = a16.shape[0], m16.shape[0]
        load = Local(load_sems)
        first = load.start(attn_state.at[:, 0], a32)
        second = load.start(mlp_state.at[0, :, 0], m32)
        place = Place()
        place.greet()
        first.wait()
        a16[...] = a32[...].astype(bf16)
        moves_a = Gather(place, a16, full, na, *a_sems)
        moves_m = Gather(place, m16, mlp_all, nm, *m_sems)
        step_a = moves_a.step
        step_m = moves_m.step
        step_a(0)
        second.wait()
        m16[...] = m32[...].astype(bf16)
    else:
        step_a = step_m = lambda i: None
    plan = {("proj", 3): 1, ("pair", 1): 2, ("pair", 9): 3, ("pair", 16): 4, ("pair", 24): 5}

    def hook(*at):
        if at in plan:
            step_m(plan[at])

    long[edge : edge + 16] = jnp.zeros((16, D), f32)
    long[:edge] = tokens[0, :edge].astype(f32)
    long[edge : tokens.shape[1]] = tokens[0, edge:].astype(f32)
    for img in range(imgs):
        x = jnp.where(real_rows(), long[img * NPOS : img * NPOS + NP], 0.0)
        tok[img] = x.astype(bf16)
        x, _ = norm_parts(x)
        n1[img * NP : (img + 1) * NP] = (x * vec[0:1] + vec[1:2]).astype(bf16)
    out.start(tok, tok_o)
    spread_table(table, wide, spread)
    turn_index(rel, square, idx)
    step_a(1)
    tiles = NP // 8
    lookup_rows(idx, spread, bias, 0, tiles // 3)
    step_a(2)
    lookup_rows(idx, spread, bias, tiles // 3, 2 * tiles // 3)
    step_a(3)
    lookup_rows(idx, spread, bias, 2 * tiles // 3, tiles)
    out.start(bias, bias_o)
    step_a(4)
    step_a(5)
    step_m(0)
    step_a(6)

    @pl.loop(0, 4 * T)
    def _(row):
        m = row // T
        r = pl.ds(pl.multiple_of(lax.rem(row, T) * B, B), B)
        for c in range(T):
            w[m, r, c * B : (c + 1) * B] = full[own[row * T + c]]

    out.start(w, w_o)
    for m, (dst, row, scale) in enumerate(((q, 2, HD**-0.5), (k, None, 1.0), (v, 3, 1.0))):
        for n in range(D // NL):
            lanes = slice(n * NL, (n + 1) * NL)
            part = dot_nn(n1[...], w[m, :, lanes])
            if row is not None:
                part = part + vec[row : row + 1, lanes]
            part = part.astype(bf16)
            if scale != 1.0:
                part = part * jnp.asarray(scale, bf16)
            for img in range(imgs):
                dst[img, :, lanes] = part[img * NP : (img + 1) * NP]
            hook("proj", m * (D // NL) + n + 1)
    out.start(q, q_o)
    out.start(k, k_o)
    out.start(v, v_o)

    side = lax.broadcasted_iota(jnp.int32, (1, B), 1) // HD
    for img in range(imgs):
        for pair in range(H // 2):
            lanes = slice(pair * B, (pair + 1) * B)
            k_pair = k[img, :, lanes]
            q_pair = pad_rows(q[img, :, lanes])
            v_turn = v[img, :, lanes].astype(f32).T.astype(bf16)
            mixed = []
            for sub in range(2):
                h = pair * 2 + sub
                q_one = jnp.where(side == sub, q_pair, jnp.zeros_like(q_pair))
                s = dot_nt(k_pair, q_one) + bias[h]
                top = jnp.max(s, axis=0, keepdims=True)
                e = jnp.exp(s - top)
                total = jnp.sum(e, axis=0, keepdims=True)
                o = dot_nn(v_turn[sub * HD : (sub + 1) * HD], e.astype(bf16))
                mixed.append(o * (1.0 / total))
                lse[img, h : h + 1] = top + jnp.log(total)
            both = jnp.concatenate(mixed, axis=0).T
            att[img, :, lanes] = both[:NP].astype(bf16)
            hook("pair", img * (H // 2) + pair + 1)
    out.start(att, att_o)

    @pl.loop(0, imgs)
    def _(img):
        branch = dot_nn(att[img], w[3]) + vec[4:5]
        bra[img] = branch
        middle = tok[img].astype(f32) + vec[5:6] * branch
        mid[img] = middle
        x, _ = norm_parts(middle)
        n2[img] = (x * vec[6:7] + vec[7:8]).astype(bf16)

    out.start(bra, bra_o)
    out.start(mid, mid_o)
    out.start(n2, n2_o)
    chunk_slots(mlp_own, parts, each, mlp_at)
    step_m(6)
    out.finish()


def forward_attention(comm, parts, each, own, mlp_own, tokens, vec, rel, table, attn, mlp=None):
    imgs = tokens.shape[1] // NPOS
    big = ((imgs, NP, D), bf16)
    tall = ((imgs, NP, D), f32)
    kept = [
        ((4, D, D), bf16),
        big,
        big,
        big,
        big,
        tall,
        tall,
        big,
        ((H, NP, NL), f32),
        big,
    ]
    out_shape = [shape(*k) for k in kept] + [shape((imgs, H, NL), f32), shape((NP, NL), jnp.int32)]
    out_shape.append(shape((FF // CH * 2 * T * PER,), jnp.int32))
    out_specs = [ANY] * len(kept) + [VMEM, VMEM, SMEM]
    wide = -(-table.shape[1] // B) * B
    scratch = [pltpu.VMEM(*k) for k in kept] + [
        pltpu.VMEM((imgs * NP, D), bf16),
        pltpu.VMEM((H, wide), f32),
        pltpu.VMEM((NL, NL), f32),
        pltpu.VMEM((H, wide // B, 8, B), f32),
        pltpu.VMEM((tokens.shape[1] // 16 * 16 + 16, D), f32),
        pltpu.SemaphoreType.DMA((len(kept),)),
    ]
    args = [own, mlp_own, tokens, vec, rel, table, attn]
    specs = [SMEM, SMEM, VMEM, VMEM, VMEM, VMEM]
    params = dict(vmem_limit_bytes=LIMIT)
    if comm:
        na, nm = attn.shape[0], mlp.shape[1]
        args.append(mlp)
        specs += [ANY, ANY]
        out_shape.append(shape((32 * nm, B, B), bf16))
        out_specs.append(ANY)
        scratch += [
            pltpu.VMEM((na, B, B), f32),
            pltpu.VMEM((nm, B, B), f32),
            pltpu.VMEM((na, B, B), bf16),
            pltpu.VMEM((nm, B, B), bf16),
            pltpu.VMEM((32 * na, B, B), bf16),
            pltpu.SemaphoreType.DMA((2,)),
        ]
        scratch += gather_scratch() + gather_scratch()
        params.update(collective_id=0, has_side_effects=True)
    else:
        specs.append(VMEM)
    return pl.pallas_call(
        partial(forward_kernel, comm, parts, each),
        in_specs=specs,
        out_specs=out_specs,
        out_shape=out_shape,
        scratch_shapes=scratch,
        compiler_params=pltpu.CompilerParams(**params),
        name="forward_attention",
    )(*args)


def mlp_kernel(
    at,
    mid_h,
    bra_h,
    n2,
    cot,
    slots,
    vec,
    upb,
    out,
    gmid,
    gbra,
    sums,
    bgrad,
    tiles_out,
    mid,
    bra,
    last,
    w1,
    w2,
    gs,
    act,
    gh,
    summed,
    gn2,
    tiles,
    sem_in,
    sem_out,
    sem_load,
):
    imgs = mid.shape[0]
    length = cot.shape[0] // LANES
    chunks = FF // CH

    @pl.loop(0, chunks)
    def _(c):
        base = c * 2 * T * PER
        for t in range(T * PER):
            r, cc = t // PER * B, t % PER * B
            pltpu.make_async_copy(
                slots.at[at[base + t]], w1.at[c, r : r + B, cc : cc + B], sem_in.at[c]
            ).start()
            r, cc = t // T * B, t % T * B
            pltpu.make_async_copy(
                slots.at[at[base + T * PER + t]], w2.at[c, r : r + B, cc : cc + B], sem_in.at[c]
            ).start()

    load = Local(sem_load)
    load.start(mid_h, mid)
    load.start(bra_h, bra)
    last[...] = jnp.zeros_like(last)
    last[:NPOS] = load_rows(cot, length - NPOS, NPOS)

    def upstream(img):
        if img == imgs - 1:
            return last[...]
        return jnp.where(real_rows(), load_rows(cot, img * NPOS, NP), 0.0)

    for img in range(imgs):
        gs[img * NP : (img + 1) * NP] = (vec[9:10] * upstream(img)).astype(bf16)
    summed[...] = jnp.zeros_like(summed)
    gn2[...] = jnp.zeros_like(gn2)

    @pl.loop(0, chunks)
    def _(c):
        pltpu.make_async_copy(w1.at[c], w1.at[c], sem_in.at[c]).wait()
        pltpu.make_async_copy(w2.at[c], w2.at[c], sem_in.at[c]).wait()
        span = pl.ds(pl.multiple_of(c * CH, CH), CH)
        bias_sum = jnp.zeros((1, CH), f32)
        for rb in range(imgs // 2):
            block = slice(rb * 2 * NP, (rb + 1) * 2 * NP)
            hid = dot_nn(n2[block], w1[c]) + upb[:, span]
            back = dot_nt(gs[block], w2[c])
            phi = 0.5 * (1.0 + lax.erf(hid * (1.0 / math.sqrt(2.0))))
            density = jnp.exp(-0.5 * hid * hid) * (1.0 / math.sqrt(2.0 * math.pi))
            a = (hid * phi).astype(bf16)
            g = (back * (phi + hid * density)).astype(bf16)
            act[block] = a
            gh[block] = g
            bias_sum = bias_sum + jnp.sum(g.astype(f32), axis=0, keepdims=True)
            summed[block] += dot_nn(a, w2[c])
            gn2[block] += dot_nt(g, w1[c])
        bgrad[:, span] = bias_sum
        up_grad = dot_tn(n2[...], gh[...])
        down_grad = dot_tn(act[...], gs[...])
        base = c * 2 * T * PER
        for t in range(T * PER):
            r, cc = t // PER * B, t % PER * B
            tiles[c, t] = up_grad[r : r + B, cc : cc + B].astype(bf16)
            pltpu.make_async_copy(tiles.at[c, t], tiles_out.at[at[base + t]], sem_out).start()
        for t in range(T * PER):
            r, cc = t // T * B, t % T * B
            to = T * PER + t
            tiles[c, to] = down_grad[r : r + B, cc : cc + B].astype(bf16)
            pltpu.make_async_copy(tiles.at[c, to], tiles_out.at[at[base + to]], sem_out).start()

    load.finish()
    s4 = jnp.zeros((1, D), f32)
    s5 = jnp.zeros((1, D), f32)
    s6 = jnp.zeros((1, D), f32)
    s7 = jnp.zeros((1, D), f32)
    s8 = jnp.zeros((1, D), f32)
    s9 = jnp.zeros((1, D), f32)
    for img in range(imgs):
        block = slice(img * NP, (img + 1) * NP)
        up = upstream(img)
        middle = mid[img]
        sm = summed[block] + vec[8:9]
        s9 += jnp.sum(up * sm, axis=0, keepdims=True)
        s8 += jnp.sum(gs[block].astype(f32), axis=0, keepdims=True)
        x, inv = norm_parts(middle)
        gn = gn2[block]
        s6 += jnp.sum(gn * x, axis=0, keepdims=True)
        s7 += jnp.sum(gn, axis=0, keepdims=True)
        gm = up + norm_back(gn, x, inv, vec[6:7])
        gmid[img] = gm
        gb = (vec[5:6] * gm).astype(bf16)
        gbra[img] = gb
        s4 += jnp.sum(gb.astype(f32), axis=0, keepdims=True)
        s5 += jnp.sum(gm * bra[img], axis=0, keepdims=True)
        summed[img * NPOS : img * NPOS + NP] = middle + vec[9:10] * sm
    edge = length // 16 * 16
    out[0, :edge] = summed[:edge].astype(bf16)
    out[0, edge:] = summed[edge:length].astype(bf16)
    sums[...] = jnp.concatenate([s4, s5, s6, s7, s8, s9, s9, s9], axis=0)
    pltpu.make_async_copy(tiles, tiles, sem_out).wait()


def feed_forward(mid, bra, n2, cot, slots, at, vec, up_bias):
    imgs = mid.shape[0]
    rows = imgs * NP
    chunks = FF // CH
    return pl.pallas_call(
        mlp_kernel,
        in_specs=[SMEM, ANY, ANY, VMEM, VMEM, ANY, VMEM, VMEM],
        out_specs=[VMEM] * 5 + [ANY],
        out_shape=[
            shape((1, imgs * NPOS, D), bf16),
            shape((imgs, NP, D), f32),
            shape((imgs, NP, D), bf16),
            shape((8, D), f32),
            shape((1, FF), f32),
            shape(slots.shape, bf16),
        ],
        scratch_shapes=[
            pltpu.VMEM((imgs, NP, D), f32),
            pltpu.VMEM((imgs, NP, D), f32),
            pltpu.VMEM((NP, D), f32),
            pltpu.VMEM((chunks, D, CH), bf16),
            pltpu.VMEM((chunks, CH, D), bf16),
            pltpu.VMEM((rows, D), bf16),
            pltpu.VMEM((rows, CH), bf16),
            pltpu.VMEM((rows, CH), bf16),
            pltpu.VMEM((rows, D), f32),
            pltpu.VMEM((rows, D), f32),
            pltpu.VMEM((chunks, 2 * T * PER, B, B), bf16),
            pltpu.SemaphoreType.DMA((chunks,)),
            pltpu.SemaphoreType.DMA(()),
            pltpu.SemaphoreType.DMA((2,)),
        ],
        compiler_params=pltpu.CompilerParams(vmem_limit_bytes=LIMIT),
        name="feed_forward",
    )(at, mid, bra, n2.reshape(rows, D), cot, slots, vec, up_bias)


def backward_kernel(comm, inverse, gbra, lse, vec, idx, *refs):
    refs = list(refs)
    w_h, v_h, k_h, q_h, bias_h, att_h, tok_h, gmid_h = refs[:8]
    refs = refs[8:]
    if comm:
        mlp_full = refs.pop(0)
    gin, table, sums, tiles_o = refs[:4]
    refs = refs[4:]
    if comm:
        mlp_mine = refs.pop(0)
    w, v, k, q, bias, att, tok, gmid = refs[:8]
    n1, gatt, gqkv, grid, tiles, full, load_sems, out_sem = refs[8:16]
    refs = refs[16:]
    imgs = q.shape[0]

    if comm:
        place = Place()
        place.greet()
        moves = Scatter(place, mlp_full, mlp_mine.shape[0], *refs)
        step = moves.step
    else:
        step = lambda i, out=None: None
    load = Local(load_sems)
    got_w, got_v, got_k, got_q, got_bias, got_att, got_tok, got_gmid = [
        load.start(src, dst)
        for src, dst in zip(
            (w_h, v_h, k_h, q_h, bias_h, att_h, tok_h, gmid_h), (w, v, k, q, bias, att, tok, gmid)
        )
    ]
    step(-1)
    step(0)
    got_w.wait()
    for n in range(D // NL):
        lanes = slice(n * NL, (n + 1) * NL)
        got = dot_nt(gbra[...], w[3, lanes, :]).astype(bf16)
        for img in range(imgs):
            gatt[img, :, lanes] = got[img * NP : (img + 1) * NP]
    grid[...] = jnp.zeros_like(grid)
    got_v.wait()
    got_k.wait()
    got_q.wait()
    got_bias.wait()
    plan = {4: 1, 12: 2, 18: 3}

    side = lax.broadcasted_iota(jnp.int32, (1, B), 1) // HD
    for img in range(imgs):
        here = slice(img * NP, (img + 1) * NP)
        for pair in range(H // 2):
            lanes = slice(pair * B, (pair + 1) * B)
            k_pair = k[img, :, lanes]
            v_pair = v[img, :, lanes]
            q_pair = pad_rows(q[img, :, lanes])
            g_pair = pad_rows(gatt[img, :, lanes])
            k_turn = k_pair.astype(f32).T.astype(bf16)
            gq = []
            gk = jnp.zeros((NP, B), f32)
            gv = jnp.zeros((NP, B), f32)
            for sub in range(2):
                h = pair * 2 + sub
                q_one = jnp.where(side == sub, q_pair, jnp.zeros_like(q_pair))
                g_one = jnp.where(side == sub, g_pair, jnp.zeros_like(g_pair))
                s = dot_nt(k_pair, q_one) + bias[h]
                p = jnp.exp(s - lse[img, h : h + 1])
                dp = dot_nt(v_pair, g_one)
                gv = gv + dot_nn(p.astype(bf16), g_one)
                inner = jnp.sum(p * dp, axis=0, keepdims=True)
                ds = (p * (dp - inner)).astype(bf16)
                gk = gk + dot_nn(ds, q_one)
                gq.append(dot_nn(k_turn[sub * HD : (sub + 1) * HD], ds))
                grid[h] += ds.astype(f32)
            turned = jnp.concatenate(gq, axis=0).T
            gqkv[here, lanes] = (turned[:NP] * HD**-0.5).astype(bf16)
            gqkv[here, D + pair * B : D + (pair + 1) * B] = gk.astype(bf16)
            gqkv[here, 2 * D + pair * B : 2 * D + (pair + 1) * B] = gv.astype(bf16)
            if img * (H // 2) + pair + 1 in plan:
                step(plan[img * (H // 2) + pair + 1])

    def put(m, n, grad):
        for r in range(T):
            for cc in range(NL // B):
                tiles[m * T * T + r * T + n * (NL // B) + cc] = grad[
                    r * B : (r + 1) * B, cc * B : (cc + 1) * B
                ].astype(bf16)

    got_att.wait()
    got_tok.wait()
    for img in range(imgs):
        x, _ = norm_parts(tok[img].astype(f32))
        n1[img * NP : (img + 1) * NP] = (x * vec[0:1] + vec[1:2]).astype(bf16)
    for n in range(D // NL):
        lanes = slice(n * NL, (n + 1) * NL)
        put(3, n, dot_tn(att[...], gbra[:, lanes]))
    for m in range(3):
        for n in range(D // NL):
            put(m, n, dot_tn(n1[...], gqkv[:, m * D + n * NL : m * D + (n + 1) * NL]))

    @pl.loop(0, full.shape[0] // 4)
    def _(group):
        for i in range(4):
            full[group * 4 + i] = tiles[inverse[group * 4 + i]]

    out = pltpu.make_async_copy(full, tiles_o, out_sem)
    out.start()
    step(4)
    accumulate_rows(grid, idx, table)

    got_gmid.wait()
    s0 = jnp.zeros((1, D), f32)
    s1 = jnp.zeros((1, D), f32)
    s2 = jnp.zeros((1, D), f32)
    s3 = jnp.zeros((1, D), f32)
    for img in range(imgs):
        here = slice(img * NP, (img + 1) * NP)
        gq = gqkv[here, 0:D]
        gk = gqkv[here, D : 2 * D]
        gv = gqkv[here, 2 * D : 3 * D]
        gn = dot_nt(gq, w[0]) + dot_nt(gk, w[1]) + dot_nt(gv, w[2])
        x, inv = norm_parts(tok[img].astype(f32))
        s0 += jnp.sum(gn * x, axis=0, keepdims=True)
        s1 += jnp.sum(gn, axis=0, keepdims=True)
        s2 += jnp.sum(gq.astype(f32), axis=0, keepdims=True)
        s3 += jnp.sum(gv.astype(f32), axis=0, keepdims=True)
        got = gmid[img] + norm_back(gn, x, inv, vec[0:1])
        store_rows(gin, img * NPOS, got[:NPOS] if img == imgs - 1 else got)
    sums[...] = jnp.concatenate([s0, s1, s2, s3, s3, s3, s3, s3], axis=0)
    if comm:
        step(5, mlp_mine)
    out.wait()


def backward_attention(comm, inverse, saved, gmid, gbra, vec, wide_total, mlp_full=None):
    w, q, k, v, att, mid, bra, n2, bias, tok, lse, idx = saved
    imgs = tok.shape[0]
    rows = imgs * NP
    att = att.reshape(rows, D)
    loaded = [w, v, k, q, bias, att, tok, gmid]
    args = [inverse, gbra.reshape(rows, D), lse, vec, idx] + loaded
    specs = [SMEM] + [VMEM] * 4 + [ANY] * 8
    out_shape = [
        shape((imgs * NPOS * LANES, B), f32),
        shape((16, wide_total), f32),
        shape((8, D), f32),
        shape((inverse.shape[0], B, B), bf16),
    ]
    out_specs = [VMEM] * 3 + [ANY]
    scratch = [pltpu.VMEM(x.shape, x.dtype) for x in loaded] + [
        pltpu.VMEM((rows, D), bf16),
        pltpu.VMEM((imgs, NP, D), bf16),
        pltpu.VMEM((rows, 3 * D), bf16),
        pltpu.VMEM((H, NP, NL), f32),
        pltpu.VMEM((4 * T * T, B, B), bf16),
        pltpu.VMEM((inverse.shape[0], B, B), bf16),
        pltpu.SemaphoreType.DMA((8,)),
        pltpu.SemaphoreType.DMA(()),
    ]
    params = dict(vmem_limit_bytes=LIMIT)
    if comm:
        n = mlp_full.shape[0] // 32
        args.append(mlp_full)
        specs.append(ANY)
        out_shape.append(shape((n, B, B), f32))
        out_specs.append(VMEM)
        scratch += scatter_scratch(n)
        params.update(collective_id=1, has_side_effects=True)
    return pl.pallas_call(
        partial(backward_kernel, comm),
        in_specs=specs,
        out_specs=out_specs,
        out_shape=out_shape,
        scratch_shapes=scratch,
        compiler_params=pltpu.CompilerParams(**params),
        name="backward_attention",
    )(*args)


NB = 16
GROUP = B // NB


def split_two(x):
    first = x.astype(bf16)
    return first, (x - first.astype(f32)).astype(bf16)


def wide_dot(x, y, dims):
    xa, xb = split_two(x)
    ya, yb = split_two(y)
    xs = jnp.concatenate([xa, xa, xb], axis=dims[0])
    ys = jnp.concatenate([ya, yb, ya], axis=dims[1])
    return lax.dot_general(
        xs, ys, (((dims[0],), (dims[1],)), ((), ())), preferred_element_type=f32
    )


def unit_inverse(diag):
    lane = lax.broadcasted_iota(jnp.int32, (NB, B), 1)
    row = lax.broadcasted_iota(jnp.int32, (NB, B), 0)
    inner = jnp.bitwise_and(lane, NB - 1)
    outer = lane - inner
    left = diag
    right = jnp.where(row == inner, 1.0, 0.0)
    def pick(k):
        return jnp.take_along_axis(diag, outer + k, axis=1, mode="promise_in_bounds")

    cut = NB // 2
    rows = [pick(r) for r in range(NB)]
    rows = [x if r < cut else x[cut:] for r, x in enumerate(rows)]
    flags = [jnp.where(row == r, 1.0, 0.0) for r in range(NB)]
    low = [x[:cut] for x in flags]
    high = [x[cut:] for x in flags]
    cols = [diag[r : r + 1] for r in range(NB)]
    pivots = jnp.zeros((1, B), f32)
    right_low, right_high = right[:cut], right[cut:]
    for r in range(NB):
        mine = rows[r]
        at = r if r < cut else r - cut
        pivot = mine[at : at + 1]
        pivots = jnp.where(inner[:1] == r, pivot, pivots)
        scale = pl.reciprocal(pivot, approx=True)
        scale = scale * (2.0 - pivot * scale)
        factor = jnp.where(inner[:1] > r, cols[r] * scale, 0.0)
        for s in range(r + 1, NB):
            at = s if r < cut else s - cut
            entry = mine[at : at + 1]
            share = entry * scale
            rows[s] = rows[s] - share * (mine if s < cut or r >= cut else mine[cut:])
            low[s] = low[s] - share * low[r]
            if r >= cut:
                high[s] = high[s] - share * high[r]
            cols[s] = cols[s] - factor * entry
        right_low = right_low - factor * low[r]
        if r >= cut:
            right_high = right_high - factor * high[r]
    right = jnp.concatenate([right_low, right_high], axis=0)
    return right * lax.rsqrt(pivots)


def orth_turned(mats, between=None):
    count = len(mats)
    groups = -(-count // GROUP)
    size = -(-count // groups)
    members = [list(range(g * size, min(count, (g + 1) * size))) for g in range(groups)]
    tails = []
    for a in mats:
        turned = a.T
        tails.append(jnp.concatenate([wide_dot(turned, turned, (1, 1)), turned], axis=1))
    own_block = (
        lax.broadcasted_iota(jnp.int32, (B, B), 0) // NB
        == lax.broadcasted_iota(jnp.int32, (B, B), 1) // NB
    )
    outs = [[] for _ in range(count)]
    for p in range(B // NB):
        base = p * NB
        for ids in members:
            fill = ids + [ids[-1]] * (GROUP - len(ids))
            strips = jnp.concatenate([tails[m][:NB] for m in fill], axis=0)
            turned = strips[:, :B].T
            unit = unit_inverse(turned[base : base + NB])
            spread = jnp.where(own_block, jnp.concatenate([unit] * GROUP, axis=0), 0.0)
            u = wide_dot(spread, strips, (0, 0))
            for at, m in enumerate(ids):
                um = u[at * NB : (at + 1) * NB]
                outs[m].append(um[:, B:])
                if base + NB < B:
                    tails[m] = tails[m][NB:] - wide_dot(um[:, base + NB : B], um, (0, 0))
        if between is not None:
            between(p)
    return [jnp.concatenate(o, axis=0) for o in outs]


def soap_slots(base, owner, grads, state, update, copy, between=None):
    count = grads.shape[0]
    mats = []
    gs = []
    for i in range(count):
        named = jnp.where(owner[...] == base + i, 1.0, 0.0)
        named = jnp.max(named, axis=1, keepdims=True)
        g = jnp.where(named > 0.0, grads[i].astype(f32), 0.0)
        gs.append(g)
        left = beta_stat * state[i, 3] + (1.0 - beta_stat) * wide_dot(g, g, (1, 1))
        right = beta_stat * state[i, 4] + (1.0 - beta_stat) * wide_dot(g, g, (0, 0))
        mats.append(wide_dot(left, state[i, 5], (1, 0)))
        mats.append(wide_dot(right, state[i, 6], (1, 0)))
    if between is not None:
        between(-1)
    turned = orth_turned(mats, between)
    fix_one = 1.0 - beta_one**STEP
    fix_two = 1.0 - beta_two**STEP
    for i in range(count):
        tl, tr = turned[2 * i], turned[2 * i + 1]
        rotated = wide_dot(wide_dot(tl, gs[i], (1, 0)), tr, (1, 1))
        new_first = beta_one * state[i, 1] + (1.0 - beta_one) * rotated
        new_second = beta_two * state[i, 2] + (1.0 - beta_two) * rotated * rotated
        normalized = new_first / fix_one / (jnp.sqrt(new_second / fix_two) + adam_eps)
        step = wide_dot(wide_dot(tl, normalized, (0, 0)), tr, (1, 0))
        weight = state[i, 0]
        weight = weight - matrix_rate * (step + decay_rate * weight)
        update[i, 0] = weight
        update[i, 1] = new_first
        update[i, 2] = new_second
        update[i, 3] = tl.T
        update[i, 4] = tr.T
        copy[i] = weight.astype(bf16)


def soap_kernel(first_slot, passed, owner, grads, state, *refs):
    kept, refs = refs[:passed], refs[passed:]
    update, copy = refs[:2]
    through, held, sems = refs[2 : 2 + passed], refs[2 + passed : 2 + 2 * passed], refs[2 + 2 * passed :]
    count = grads.shape[0]
    between = None
    if passed:
        into, out = Local(sems[0]), Local(sems[1])
        for src, dst in zip(kept, held):
            into.start(src, dst)

        def between(p):
            if p == 2:
                into.finish()
                for src, dst in zip(held, through):
                    out.start(src, dst)

    first = first_slot() + pl.program_id(0) * count
    soap_slots(first, owner, grads, state, update, copy, between)
    if passed:
        out.finish()


def soap_update(grads, state, owner, first_slot, kept=()):
    slots = grads.shape[0]
    count = max(c for c in range(1, 10) if slots % c == 0)
    assert not kept or count == slots
    return pl.pallas_call(
        partial(soap_kernel, first_slot, len(kept)),
        grid=(slots // count,),
        in_specs=[
            pl.BlockSpec((1, owner.shape[0]), lambda i: (0, 0)),
            pl.BlockSpec((count, B, B), lambda i: (i, 0, 0)),
            pl.BlockSpec((count, 7, B, B), lambda i: (i, 0, 0, 0)),
        ]
        + [ANY] * len(kept),
        out_specs=[
            pl.BlockSpec((count, 5, B, B), lambda i: (i, 0, 0, 0)),
            pl.BlockSpec((count, B, B), lambda i: (i, 0, 0)),
        ]
        + [ANY] * len(kept),
        out_shape=[shape((slots, 5, B, B), f32), shape((slots, B, B), bf16)]
        + [shape(x.shape, x.dtype) for x in kept],
        scratch_shapes=[pltpu.VMEM(x.shape, x.dtype) for x in kept]
        + [pltpu.SemaphoreType.DMA((len(kept),))] * (2 if kept else 0),
        compiler_params=pltpu.CompilerParams(vmem_limit_bytes=LIMIT),
        name="soap",
    )(owner[None], grads, state, *kept)


SUM_ROWS = 40


def adam(grad, param, first, second):
    new_first = beta_one * first + (1.0 - beta_one) * grad
    new_second = beta_two * second + (1.0 - beta_two) * grad * grad
    fix_one = 1.0 - beta_one**STEP
    fix_two = 1.0 - beta_two**STEP
    step = (new_first / fix_one) / (jnp.sqrt(new_second / fix_two) + adam_eps)
    return grad, param - vector_rate * step, new_first, new_second


def finish_kernel(
    full,
    mlp_sums,
    attn_sums,
    table_sums,
    bias_sums,
    vec,
    vec_m,
    table,
    table_m,
    upb,
    upb_m,
    owner,
    mlp_mine,
    state_h,
    mine,
    vec_up,
    table_up,
    upb_up,
    update,
    copy,
    state,
    load_sem,
    part,
    other,
    column,
    sum_send,
    sum_recv,
    *scratch,
):
    place = Place()
    place.greet()
    load = pltpu.make_async_copy(state_h.at[0], state, load_sem)
    load.start()

    moves = Scatter(place, full, mine.shape[0], *scratch)
    sums = Copies(place, sum_send, sum_recv)
    part[0, 0:8] = mlp_sums[...]
    part[0, 8:16] = attn_sums[...]
    part[0, 16:32] = table_sums[...]
    quarter = jnp.concatenate([bias_sums[:, i * D : (i + 1) * D] for i in range(FF // D)] * 2, axis=0)
    part[0, 32:40] = quarter
    sums.start("c", part.at[0], other.at[0], dc=1)
    moves.step(-1)
    moves.step(0)
    load.wait()

    def total_sums():
        part[4] = ((column[0] + column[1]) + column[2]) + column[3]
        total = part.at[4]
        grad = jnp.concatenate([total[8:12], total[0:6]], axis=0)
        for i, got in enumerate(adam(grad, vec[...], vec_m[:, 0, :], vec_m[:, 1, :])):
            vec_up[:, i, :] = got
        wide = table.shape[1]
        grad = total[16 : 16 + H, 0:wide]
        for i, got in enumerate(adam(grad, table[...], table_m[:, 0, :], table_m[:, 1, :])):
            table_up[:, i, :] = got
        for j in range(FF // D):
            lanes = slice(j * D, (j + 1) * D)
            for i, got in enumerate(
                adam(total[32 + j : 33 + j], upb[:, lanes], upb_m[0:1, lanes], upb_m[1:2, lanes])
            ):
                upb_up[i : i + 1, lanes] = got

    steps = {-1: 1, 1: 2, 3: 3, 6: 4}
    sends = (-1, 1, 3)

    def between(p):
        if p in steps:
            moves.step(steps[p])
        if p == sends[0]:
            sums.arrived("c")
            part[1] = part[0] + other[0]
            sums.start("x", part.at[1], other.at[1], dx=1)
        elif p == sends[1]:
            sums.arrived("x")
            part[2] = part[1] + other[1]
            sums.start("y", part.at[2], other.at[2], dy=1)
        elif p == sends[2]:
            sums.arrived("y")
            part[3] = part[2] + other[2]
            for d in (1, 2, 3):
                sums.start(("z", d), part.at[3], column.at[place.z], d=d)
            column[place.z] = part[3]

    first_slot = lax.axis_index("dp") * mlp_mine.shape[0]
    soap_slots(first_slot, owner, mlp_mine, state, update, copy, between)
    for d in (1, 2, 3):
        sums.arrived(("z", d))
    total_sums()
    moves.step(5, mine)
    sums.sent()


def finish(full, small, params, owner, mlp_mine, mlp_state):
    n = full.shape[0] // 32
    nm = mlp_mine.shape[0]
    vec, vec_m, table, table_m, upb, upb_m = params
    return pl.pallas_call(
        finish_kernel,
        in_specs=[ANY] + [VMEM] * 12 + [ANY],
        out_specs=[VMEM] * 6,
        out_shape=[
            shape((n, B, B), f32),
            shape((vec.shape[0], 4, D), f32),
            shape((H, 4, table.shape[1]), f32),
            shape((4, FF), f32),
            shape((nm, 5, B, B), f32),
            shape((nm, B, B), bf16),
        ],
        scratch_shapes=[
            pltpu.VMEM((nm, 7, B, B), f32),
            pltpu.SemaphoreType.DMA(()),
            pltpu.VMEM((5, SUM_ROWS, D), f32),
            pltpu.VMEM((3, SUM_ROWS, D), f32),
            pltpu.VMEM((4, SUM_ROWS, D), f32),
            pltpu.SemaphoreType.DMA((6,)),
            pltpu.SemaphoreType.DMA((6,)),
        ]
        + scatter_scratch(n),
        compiler_params=pltpu.CompilerParams(
            collective_id=2, has_side_effects=True, vmem_limit_bytes=LIMIT
        ),
        name="finish",
    )(
        full,
        *small,
        vec,
        vec_m.transpose(1, 0, 2),
        table,
        table_m.transpose(1, 0, 2),
        upb[None],
        upb_m,
        owner[None],
        mlp_mine,
        mlp_state,
    )


def body(
    tokens,
    cotangent,
    rel_index,
    attn_owner,
    mlp_owner,
    attn_state,
    mlp_state,
    vec_param,
    vec_moments,
    rel_table,
    rel_table_moments,
    up_bias,
    up_bias_moments,
):
    both = ("dp", "mp")
    parts = lax.axis_size("mp")
    comm = own_kernels(lax.axis_size("dp"), parts)
    imgs = tokens.shape[1] // NPOS
    attn_local = attn_state.shape[0]
    mlp_local = mlp_state.shape[1]
    attn_total = attn_local * lax.axis_size("dp") * parts

    def attn_first():
        return (lax.axis_index("dp") * parts + lax.axis_index("mp")) * attn_local

    def mlp_first():
        return lax.axis_index("dp") * mlp_local

    wide_total = -(-rel_table.shape[1] // B) * B
    slot_ids = jnp.arange(attn_total, dtype=jnp.int32)
    block_ids = jnp.arange(attn_owner.shape[0], dtype=jnp.int32)
    inverse = jnp.sum(
        jnp.where(attn_owner[None, :] == slot_ids[:, None], block_ids[None, :], 0), axis=1
    ).astype(jnp.int32)

    if comm:
        *saved, mlp_slots = forward_attention(
            True,
            parts,
            mlp_local,
            attn_owner,
            mlp_owner,
            tokens,
            vec_param, rel_index, rel_table, attn_state, mlp_state
        )
    else:
        attn_slots = lax.all_gather(attn_state[:, 0].astype(bf16), both, axis=0, tiled=True)
        mlp_slots = lax.all_gather(mlp_state[0, :, 0].astype(bf16), both, axis=0, tiled=True)
        saved = list(
            forward_attention(
            False,
            parts,
            mlp_local,
            attn_owner,
            mlp_owner,
            tokens,
            vec_param, rel_index, rel_table, attn_slots
        ))
    mlp_at = saved.pop()
    w, q, k, v, att, mid, bra, n2, bias, tok, lse, idx = saved
    out, gmid, gbra, mlp_sums, bias_grad, mlp_grads = feed_forward(
        mid, bra, n2, cotangent.reshape(-1, B), mlp_slots, mlp_at, vec_param, up_bias[None]
    )
    if comm:
        gin, table_grad, attn_sums, attn_full, mlp_mine = backward_attention(
            True, inverse, saved, gmid, gbra, vec_param, wide_total, mlp_grads
        )
        attn_mine, vec_up, table_up, bias_up, mlp_result, mlp_copy = finish(
            attn_full,
            (mlp_sums, attn_sums, table_grad, bias_grad),
            (vec_param, vec_moments, rel_table, rel_table_moments, up_bias, up_bias_moments),
            mlp_owner,
            mlp_mine,
            mlp_state,
        )
        kept = (gin, mlp_result, mlp_copy, vec_up, table_up, bias_up)
        attn_result, attn_copy, *kept = soap_update(
            attn_mine, attn_state, attn_owner, attn_first, kept
        )
        gin, mlp_result, mlp_copy, vec_up, table_up, bias_up = kept
        vec_up = vec_up.transpose(1, 0, 2)
        table_up = table_up.transpose(1, 0, 2)
    else:
        gin, table_grad, attn_sums, attn_full = backward_attention(
            False, inverse, saved, gmid, gbra, vec_param, wide_total
        )
        mlp_mine = lax.psum_scatter(mlp_grads, both, scatter_dimension=0, tiled=True)
        attn_mine = lax.psum_scatter(attn_full, both, scatter_dimension=0, tiled=True)
        vector_grad = jnp.concatenate([attn_sums[:4], mlp_sums[:6]], axis=0)
        vector_total, table_total, bias_total = lax.psum(
            (vector_grad, table_grad[:H, : rel_table.shape[1]], bias_grad[0]), both
        )
        vec_up = jnp.stack(adam(vector_total, vec_param, vec_moments[0], vec_moments[1]))
        table_up = jnp.stack(
            adam(table_total, rel_table, rel_table_moments[0], rel_table_moments[1])
        )
        bias_up = jnp.stack(adam(bias_total, up_bias, up_bias_moments[0], up_bias_moments[1]))
        attn_result, attn_copy = soap_update(attn_mine, attn_state, attn_owner, attn_first)
        mlp_result, mlp_copy = soap_update(mlp_mine, mlp_state[0], mlp_owner, mlp_first)
    return (
        out,
        gin.reshape(1, imgs * NPOS, D),
        attn_result,
        attn_copy,
        mlp_result[None],
        mlp_copy[None],
        vec_up,
        table_up,
        bias_up,
    )


def solution(mesh):
    placed = (
        P(("dp", "mp"), None, None),
        P(("dp", "mp"), None, None),
        P(),
        P(),
        P(),
        P(("dp", "mp"), None, None, None),
        P("mp", "dp", None, None, None),
        P(),
        P(),
        P(),
        P(),
        P(),
        P(),
    )
    return jax.shard_map(
        body,
        mesh=mesh,
        in_specs=placed,
        out_specs=(
            P(("dp", "mp"), None, None),
            P(("dp", "mp"), None, None),
            P(("dp", "mp"), None, None, None),
            P(("dp", "mp"), None, None),
            P("mp", "dp", None, None, None),
            P("mp", "dp", None, None),
            P(),
            P(),
            P(),
        ),
        check_vma=False,
    )
```

```python
from functools import partial
import math

import jax
import jax.numpy as jnp
from jax import lax
from jax.experimental import pallas as pl
from jax.experimental.pallas import tpu as pltpu
from jax.sharding import PartitionSpec as P

D = 768
H = 12
HD = 64
FF = 3072
NPOS = 197
NP = 208
NL = 256
B = 128
STEP = 5
T = D // B

f32 = jnp.float32
bf16 = jnp.bfloat16

ln_eps = 1e-06
beta_one = 0.9
beta_two = 0.95
beta_stat = 0.95
adam_eps = 1e-08
matrix_rate = 0.05
vector_rate = 0.2
decay_rate = 0.05

VMEM = pl.BlockSpec(memory_space=pltpu.VMEM)
SMEM = pl.BlockSpec(memory_space=pltpu.SMEM)
ANY = pl.BlockSpec(memory_space=pl.ANY)
LIMIT = 60 << 20


def shape(dims, kind):
    return jax.ShapeDtypeStruct(dims, kind)


def dot_nn(x, y):
    return lax.dot_general(x, y, (((1,), (0,)), ((), ())), preferred_element_type=f32)


def dot_nt(x, y):
    return lax.dot_general(x, y, (((1,), (1,)), ((), ())), preferred_element_type=f32)


def dot_tn(x, y):
    return lax.dot_general(x, y, (((0,), (0,)), ((), ())), preferred_element_type=f32)


def norm_parts(values):
    centered = values - jnp.mean(values, axis=-1, keepdims=True)
    inv_std = lax.rsqrt(jnp.mean(centered * centered, axis=-1, keepdims=True) + ln_eps)
    return (centered * inv_std, inv_std)


def norm_back(grad_normed, scaled, inv_std, gain_row):
    tangent = grad_normed * gain_row
    return inv_std * (
        tangent
        - jnp.mean(tangent, axis=-1, keepdims=True)
        - scaled * jnp.mean(tangent * scaled, axis=-1, keepdims=True)
    )


MESH = pl.DeviceIdType.MESH
COPIES = 35


def own_kernels(dp_total, parts):
    return dp_total == 16 and parts == 2


class Place:
    def __init__(self):
        dp = lax.axis_index("dp")
        self.y = lax.axis_index("mp")
        self.z = dp // 4
        self.x = lax.rem(dp // 2, 2)
        self.c = lax.rem(dp, 2)

    def rank(self, d=0, dx=0, dc=0, dy=0):
        z = lax.rem(self.z + d + 4, 4)
        x = 1 - self.x if dx else self.x
        c = 1 - self.c if dc else self.c
        y = 1 - self.y if dy else self.y
        return ((z * 2 + x) * 2 + c) * 2 + y

    def device(self, d=0, dx=0, dc=0, dy=0):
        z = lax.rem(self.z + d + 4, 4)
        x = 1 - self.x if dx else self.x
        c = 1 - self.c if dc else self.c
        y = 1 - self.y if dy else self.y
        return ((z * 2 + x) * 2 + c, y)

    def greet(self):
        barrier = pltpu.get_barrier_semaphore()
        for d, dx, dc, dy in PARTNERS:
            pl.semaphore_signal(
                barrier, inc=1, device_id=self.device(d, dx, dc, dy), device_id_type=MESH
            )
        pl.semaphore_wait(barrier, len(PARTNERS))


PARTNERS = ((1, 0, 0, 0), (2, 0, 0, 0), (3, 0, 0, 0), (0, 1, 0, 0), (0, 0, 1, 0), (0, 0, 0, 1))


class Copies:
    def __init__(self, place, send, recv):
        self.place = place
        self.send = send
        self.recv = recv
        self.made = {}

    def start(self, key, src, dst, **to):
        i = len(self.made)
        copy = pltpu.make_async_remote_copy(
            src_ref=src,
            dst_ref=dst,
            send_sem=self.send.at[i],
            recv_sem=self.recv.at[i],
            device_id=self.place.device(**to),
            device_id_type=MESH,
        )
        copy.start()
        self.made[key] = copy

    def arrived(self, key):
        self.made[key].wait_recv()

    def sent(self):
        for copy in self.made.values():
            copy.wait_send()


class Gather(Copies):
    def __init__(self, place, own, full, n, send, recv, local):
        super().__init__(place, send, recv)
        self.own = own
        self.full = full
        self.n = n
        self.half = n // 2
        self.local = pltpu.make_async_copy(own, self.at(), local)

    def at(self, d=0, dx=0, dc=0, dy=0, lo=0, hi=None):
        hi = self.n if hi is None else hi
        return self.full.at[pl.ds(self.place.rank(d, dx, dc, dy) * self.n + lo, hi - lo)]

    def spread(self, d):
        src = self.own if d == 0 else self.at(d=-d)
        dst = self.at(d=-d)
        self.start(("x", d), src, dst, dx=1)
        self.start(("y", d), src, dst, dy=1)
        self.start(("c", d, 0, 0), src, dst, dc=1)

    def along(self, d):
        self.start(("z", d), self.own, self.at(), d=d)

    def share(self, d, dx, dy):
        ref = self.at(d=-d, dx=dx, dy=dy)
        self.start(("c", d, dx, dy), ref, ref, dc=1)

    def corner(self, d):
        ref = self.at(d=-d, dy=1, lo=self.half)
        self.start(("xd", d), ref, ref, dx=1)
        ref = self.at(d=-d, dx=1, hi=self.half)
        self.start(("yd", d), ref, ref, dy=1)

    def sides(self, d):
        self.arrived(("x", d))
        self.share(d, 1, 0)
        self.arrived(("y", d))
        self.share(d, 0, 1)

    def cornered(self, d):
        self.arrived(("xd", d))
        self.arrived(("yd", d))
        self.share(d, 1, 1)

    def step(self, i):
        if i == 0:
            self.local.start()
            self.along(1)
            self.spread(0)
        elif i == 1:
            self.arrived(("z", 1))
            self.along(3)
            self.spread(1)
            self.sides(0)
        elif i == 2:
            self.arrived(("z", 3))
            self.along(2)
            self.spread(3)
            self.sides(1)
            self.corner(0)
        elif i == 3:
            self.corner(1)
            self.sides(3)
        elif i == 4:
            self.arrived(("z", 2))
            self.spread(2)
            self.cornered(0)
            self.corner(3)
            self.cornered(1)
        elif i == 5:
            self.sides(2)
            self.corner(2)
            self.cornered(3)
        else:
            self.cornered(2)
            for d in range(4):
                for dx in range(2):
                    for dy in range(2):
                        self.arrived(("c", d, dx, dy))
            self.local.wait()
            self.sent()


GATHER_STEPS = 7


class Scatter(Copies):
    def __init__(self, place, full, n, acc, peer, side, corner, along, send, recv, local):
        super().__init__(place, send, recv)
        self.full = full
        self.local = local
        self.mine = {}
        self.n = n
        self.half = n // 2
        self.acc = acc
        self.peer = peer
        self.side = side
        self.cor = corner
        self.col = along

    def block(self, d, dx, dc, dy):
        return pl.ds(self.place.rank(d, dx, dc, dy) * self.n, self.n)

    def core(self, d, dx, dy):
        key = (d, dx, dy)
        self.start(
            ("c",) + key, self.full.at[self.block(d, dx, 1, dy)], self.peer.at[d, dx, dy], dc=1
        )
        self.mine[key] = pltpu.make_async_copy(
            self.full.at[self.block(d, dx, 0, dy)],
            self.acc.at[d, dx, dy],
            self.local.at[len(self.mine)],
        )
        self.mine[key].start()

    def pair(self, d, dx, dy):
        self.mine[(d, dx, dy)].wait()
        self.arrived(("c", d, dx, dy))
        self.add(d, dx, dy, self.peer.at[d, dx, dy], 0, self.n)

    def add(self, d, dx, dy, other, lo, hi):
        @pl.loop(lo, hi)
        def _(i):
            total = self.acc[d, dx, dy, i].astype(f32) + other[i - lo].astype(f32)
            self.acc[d, dx, dy, i] = total.astype(bf16)

    def corner(self, d):
        self.pair(d, 1, 1)
        h, n = self.half, self.n
        self.start(("xd", d), self.acc.at[d, 1, 1, pl.ds(0, h)], self.cor.at[d, pl.ds(0, h)], dx=1)
        self.start(
            ("yd", d), self.acc.at[d, 1, 1, pl.ds(h, n - h)], self.cor.at[d, pl.ds(h, n - h)], dy=1
        )

    def sides(self, d):
        h, n = self.half, self.n
        self.pair(d, 1, 0)
        self.arrived(("yd", d))
        self.add(d, 1, 0, self.cor.at[d, pl.ds(h, n - h)], h, n)
        self.start(("x", d), self.acc.at[d, 1, 0], self.side.at[d, 0], dx=1)
        self.pair(d, 0, 1)
        self.arrived(("xd", d))
        self.add(d, 0, 1, self.cor.at[d, pl.ds(0, h)], 0, h)
        self.start(("y", d), self.acc.at[d, 0, 1], self.side.at[d, 1], dy=1)

    def along(self, d):
        self.pair(d, 0, 0)
        self.arrived(("x", d))
        self.arrived(("y", d))

        @pl.loop(0, self.n)
        def _(i):
            total = (
                self.acc[d, 0, 0, i].astype(f32)
                + self.side[d, 0, i].astype(f32)
                + self.side[d, 1, i].astype(f32)
            )
            self.acc[d, 0, 0, i] = total.astype(bf16)

        if d > 0:
            self.start(("z", d), self.acc.at[d, 0, 0], self.col.at[d - 1], d=d)

    def step(self, i, out=None):
        if i == 0:
            for dx, dy in ((1, 1), (1, 0), (0, 1), (0, 0)):
                for d in (2, 3, 0, 1):
                    self.core(d, dx, dy)
            self.corner(2)
            self.corner(3)
        elif i == 1:
            self.sides(2)
            self.corner(0)
            self.corner(1)
        elif i == 2:
            self.along(2)
            self.sides(3)
        elif i == 3:
            self.sides(1)
            self.sides(0)
        elif i == 4:
            self.along(3)
            self.along(1)
        else:
            self.along(0)
            for d in (1, 2, 3):
                self.arrived(("z", d))

            @pl.loop(0, self.n)
            def _(i):
                out[i] = (
                    (self.acc[0, 0, 0, i].astype(f32) + self.col[0, i].astype(f32))
                    + self.col[1, i].astype(f32)
                ) + self.col[2, i].astype(f32)

            self.sent()


SCATTER_STEPS = 6


def scatter_scratch(n):
    return [
        pltpu.VMEM((4, 2, 2, n, B, B), bf16),
        pltpu.VMEM((4, 2, 2, n, B, B), bf16),
        pltpu.VMEM((4, 2, n, B, B), bf16),
        pltpu.VMEM((4, n, B, B), bf16),
        pltpu.VMEM((3, n, B, B), bf16),
        pltpu.SemaphoreType.DMA((COPIES,)),
        pltpu.SemaphoreType.DMA((COPIES,)),
        pltpu.SemaphoreType.DMA((16,)),
    ]


def gather_scratch():
    return [
        pltpu.SemaphoreType.DMA((COPIES,)),
        pltpu.SemaphoreType.DMA((COPIES,)),
        pltpu.SemaphoreType.DMA(()),
    ]


class Local:
    def __init__(self, sems):
        self.sems = sems
        self.made = []

    def start(self, src, dst):
        copy = pltpu.make_async_copy(src, dst, self.sems.at[len(self.made)])
        copy.start()
        self.made.append(copy)
        return copy

    def finish(self):
        for copy in self.made:
            copy.wait()


def spread_table(table_ref, wide, spread):
    wide[...] = jnp.zeros_like(wide)
    wide[:, : table_ref.shape[1]] = table_ref[...]
    for h in range(H):
        for c in range(spread.shape[1]):
            spread[h, c] = jnp.broadcast_to(wide[h : h + 1, c * B : (c + 1) * B], (8, B))


def turn_index(rel_ref, square, out_ref):
    square[...] = jnp.zeros_like(square)
    square[:NPOS, :NPOS] = rel_ref[...].astype(f32)
    out_ref[...] = square[...].T[:NP].astype(jnp.int32)


def lookup_rows(idx_ref, spread, out_ref, lo, hi):
    chunks = spread.shape[1]

    @pl.loop(lo, hi)
    def _(jt):
        rows = pl.ds(pl.multiple_of(jt * 8, 8), 8)
        real = jt * 8 + lax.broadcasted_iota(jnp.int32, (8, B), 0) < NPOS
        for half in range(NL // B):
            lanes = slice(half * B, (half + 1) * B)
            idx = idx_ref[rows, lanes]
            low = jnp.bitwise_and(idx, B - 1)
            high = jnp.right_shift(idx, 7)
            for h in range(H):
                acc = jnp.take_along_axis(spread[h, 0], low, axis=1, mode="promise_in_bounds")
                for c in range(1, chunks):
                    part = jnp.take_along_axis(spread[h, c], low, axis=1, mode="promise_in_bounds")
                    acc = jnp.where(high == c, part, acc)
                out_ref[h, rows, lanes] = jnp.where(real, acc, -1e30)


JB = 8


def accumulate_rows(grid_ref, idx_ref, out_ref):
    chunks = out_ref.shape[1] // B
    out_ref[...] = jnp.zeros_like(out_ref)
    lo_rows = lax.broadcasted_iota(jnp.int32, (B, NL), 0)

    @pl.loop(0, NP // JB)
    def _(jb):
        idx_all = idx_ref[pl.ds(pl.multiple_of(jb * JB, JB), JB), :]
        lefts = []
        rights = []
        for jj in range(JB):
            values = grid_ref[:, jb * JB + jj, :]
            values = jnp.concatenate([values, jnp.zeros((16 - H, NL), f32)], axis=0)
            idx = idx_all[jj : jj + 1]
            low = jnp.bitwise_and(idx, B - 1)
            high = jnp.right_shift(idx, 7)
            rights.append(jnp.where(lo_rows == low, 1.0, 0.0).astype(bf16))
            lefts.append(
                jnp.concatenate(
                    [jnp.where(high == c, values, 0.0) for c in range(chunks)], axis=0
                ).astype(bf16)
            )
        got = dot_nt(jnp.concatenate(lefts, axis=1), jnp.concatenate(rights, axis=1))
        for c in range(chunks):
            out_ref[:, c * B : (c + 1) * B] += got[c * 16 : (c + 1) * 16]


CH = 512
PER = CH // B


def chunk_slots(own, parts, each, out):
    half = own.shape[0] // 2
    local = half // T

    def place(slot, p):
        return lax.div(slot, each) * (parts * each) + p * each + lax.rem(slot, each)

    @pl.loop(0, FF // CH)
    def _(c):
        @pl.loop(0, T * PER)
        def _(t):
            g = c * PER + lax.rem(t, PER)
            g2 = c * PER + t // T
            up = own[(t // PER) * local + lax.rem(g, local)]
            down = own[half + lax.rem(g2, local) * T + lax.rem(t, T)]
            out[c * 2 * T * PER + t] = place(up, g // local)
            out[c * 2 * T * PER + T * PER + t] = place(down, g2 // local)


def pad_rows(x):
    return jnp.concatenate([x, jnp.zeros((NL - NP, x.shape[1]), x.dtype)], axis=0)


LANES = D // B


def load_rows(ref, first, count):
    return jnp.concatenate(
        [ref[pl.ds(first * LANES + c, count, stride=LANES), :] for c in range(LANES)], axis=1
    )


def store_rows(ref, first, values):
    count = values.shape[0]
    for c in range(LANES):
        ref[pl.ds(first * LANES + c, count, stride=LANES), :] = values[:, c * B : (c + 1) * B]


def real_rows():
    return lax.broadcasted_iota(jnp.int32, (NP, 1), 0) < NPOS


def forward_kernel(comm, parts, each, own, mlp_own, tokens, vec, rel, table, *refs):
    refs = list(refs)
    if comm:
        attn_state, mlp_state = refs[:2]
        refs = refs[2:]
    else:
        full = refs.pop(0)
    w_o, q_o, k_o, v_o, att_o, mid_o, bra_o, n2_o, bias_o, tok_o, lse, idx, mlp_at = refs[:13]
    refs = refs[13:]
    if comm:
        mlp_all = refs.pop(0)
    w, q, k, v, att, mid, bra, n2, bias, tok, n1, wide, square, spread, long, out_sems = refs[:16]
    refs = refs[16:]
    out = Local(out_sems)
    imgs = q.shape[0]
    edge = tokens.shape[1] // 16 * 16

    if comm:
        a32, m32, a16, m16, full, load_sems = refs[:6]
        a_sems = refs[6:9]
        m_sems = refs[9:12]
        na, nm = a16.shape[0], m16.shape[0]
        load = Local(load_sems)
        first = load.start(attn_state.at[:, 0], a32)
        second = load.start(mlp_state.at[0, :, 0], m32)
        place = Place()
        place.greet()
        first.wait()
        a16[...] = a32[...].astype(bf16)
        moves_a = Gather(place, a16, full, na, *a_sems)
        moves_m = Gather(place, m16, mlp_all, nm, *m_sems)
        step_a = moves_a.step
        step_m = moves_m.step
        step_a(0)
        second.wait()
        m16[...] = m32[...].astype(bf16)
    else:
        step_a = step_m = lambda i: None
    plan = {("proj", 3): 1, ("pair", 1): 2, ("pair", 9): 3, ("pair", 16): 4, ("pair", 24): 5}

    def hook(*at):
        if at in plan:
            step_m(plan[at])

    long[edge : edge + 16] = jnp.zeros((16, D), f32)
    long[:edge] = tokens[0, :edge].astype(f32)
    long[edge : tokens.shape[1]] = tokens[0, edge:].astype(f32)
    for img in range(imgs):
        x = jnp.where(real_rows(), long[img * NPOS : img * NPOS + NP], 0.0)
        tok[img] = x.astype(bf16)
        x, _ = norm_parts(x)
        n1[img * NP : (img + 1) * NP] = (x * vec[0:1] + vec[1:2]).astype(bf16)
    out.start(tok, tok_o)
    spread_table(table, wide, spread)
    turn_index(rel, square, idx)
    step_a(1)
    tiles = NP // 8
    lookup_rows(idx, spread, bias, 0, tiles // 3)
    step_a(2)
    lookup_rows(idx, spread, bias, tiles // 3, 2 * tiles // 3)
    step_a(3)
    lookup_rows(idx, spread, bias, 2 * tiles // 3, tiles)
    out.start(bias, bias_o)
    step_a(4)
    step_a(5)
    step_m(0)
    step_a(6)

    @pl.loop(0, 4 * T)
    def _(row):
        m = row // T
        r = pl.ds(pl.multiple_of(lax.rem(row, T) * B, B), B)
        for c in range(T):
            w[m, r, c * B : (c + 1) * B] = full[own[row * T + c]]

    out.start(w, w_o)
    for m, (dst, row, scale) in enumerate(((q, 2, HD**-0.5), (k, None, 1.0), (v, 3, 1.0))):
        for n in range(D // NL):
            lanes = slice(n * NL, (n + 1) * NL)
            part = dot_nn(n1[...], w[m, :, lanes])
            if row is not None:
                part = part + vec[row : row + 1, lanes]
            part = part.astype(bf16)
            if scale != 1.0:
                part = part * jnp.asarray(scale, bf16)
            for img in range(imgs):
                dst[img, :, lanes] = part[img * NP : (img + 1) * NP]
            hook("proj", m * (D // NL) + n + 1)
    out.start(q, q_o)
    out.start(k, k_o)
    out.start(v, v_o)

    side = lax.broadcasted_iota(jnp.int32, (1, B), 1) // HD
    for img in range(imgs):
        for pair in range(H // 2):
            lanes = slice(pair * B, (pair + 1) * B)
            k_pair = k[img, :, lanes]
            q_pair = pad_rows(q[img, :, lanes])
            v_turn = v[img, :, lanes].astype(f32).T.astype(bf16)
            mixed = []
            for sub in range(2):
                h = pair * 2 + sub
                q_one = jnp.where(side == sub, q_pair, jnp.zeros_like(q_pair))
                s = dot_nt(k_pair, q_one) + bias[h]
                top = jnp.max(s, axis=0, keepdims=True)
                e = jnp.exp(s - top)
                total = jnp.sum(e, axis=0, keepdims=True)
                o = dot_nn(v_turn[sub * HD : (sub + 1) * HD], e.astype(bf16))
                mixed.append(o * (1.0 / total))
                lse[img, h : h + 1] = top + jnp.log(total)
            both = jnp.concatenate(mixed, axis=0).T
            att[img, :, lanes] = both[:NP].astype(bf16)
            hook("pair", img * (H // 2) + pair + 1)
    out.start(att, att_o)

    @pl.loop(0, imgs)
    def _(img):
        branch = dot_nn(att[img], w[3]) + vec[4:5]
        bra[img] = branch
        middle = tok[img].astype(f32) + vec[5:6] * branch
        mid[img] = middle
        x, _ = norm_parts(middle)
        n2[img] = (x * vec[6:7] + vec[7:8]).astype(bf16)

    out.start(bra, bra_o)
    out.start(mid, mid_o)
    out.start(n2, n2_o)
    chunk_slots(mlp_own, parts, each, mlp_at)
    step_m(6)
    out.finish()


def forward_attention(comm, parts, each, own, mlp_own, tokens, vec, rel, table, attn, mlp=None):
    imgs = tokens.shape[1] // NPOS
    big = ((imgs, NP, D), bf16)
    tall = ((imgs, NP, D), f32)
    kept = [
        ((4, D, D), bf16),
        big,
        big,
        big,
        big,
        tall,
        tall,
        big,
        ((H, NP, NL), f32),
        big,
    ]
    out_shape = [shape(*k) for k in kept] + [shape((imgs, H, NL), f32), shape((NP, NL), jnp.int32)]
    out_shape.append(shape((FF // CH * 2 * T * PER,), jnp.int32))
    out_specs = [ANY] * len(kept) + [VMEM, VMEM, SMEM]
    wide = -(-table.shape[1] // B) * B
    scratch = [pltpu.VMEM(*k) for k in kept] + [
        pltpu.VMEM((imgs * NP, D), bf16),
        pltpu.VMEM((H, wide), f32),
        pltpu.VMEM((NL, NL), f32),
        pltpu.VMEM((H, wide // B, 8, B), f32),
        pltpu.VMEM((tokens.shape[1] // 16 * 16 + 16, D), f32),
        pltpu.SemaphoreType.DMA((len(kept),)),
    ]
    args = [own, mlp_own, tokens, vec, rel, table, attn]
    specs = [SMEM, SMEM, VMEM, VMEM, VMEM, VMEM]
    params = dict(vmem_limit_bytes=LIMIT)
    if comm:
        na, nm = attn.shape[0], mlp.shape[1]
        args.append(mlp)
        specs += [ANY, ANY]
        out_shape.append(shape((32 * nm, B, B), bf16))
        out_specs.append(ANY)
        scratch += [
            pltpu.VMEM((na, B, B), f32),
            pltpu.VMEM((nm, B, B), f32),
            pltpu.VMEM((na, B, B), bf16),
            pltpu.VMEM((nm, B, B), bf16),
            pltpu.VMEM((32 * na, B, B), bf16),
            pltpu.SemaphoreType.DMA((2,)),
        ]
        scratch += gather_scratch() + gather_scratch()
        params.update(collective_id=0, has_side_effects=True)
    else:
        specs.append(VMEM)
    return pl.pallas_call(
        partial(forward_kernel, comm, parts, each),
        in_specs=specs,
        out_specs=out_specs,
        out_shape=out_shape,
        scratch_shapes=scratch,
        compiler_params=pltpu.CompilerParams(**params),
        name="forward_attention",
    )(*args)


def mlp_kernel(
    at,
    mid_h,
    bra_h,
    n2,
    cot,
    slots,
    vec,
    upb,
    out,
    gmid,
    gbra,
    sums,
    bgrad,
    tiles_out,
    mid,
    bra,
    last,
    w1,
    w2,
    gs,
    act,
    gh,
    summed,
    gn2,
    tiles,
    sem_in,
    sem_out,
    sem_load,
):
    imgs = mid.shape[0]
    length = cot.shape[0] // LANES
    chunks = FF // CH

    @pl.loop(0, chunks)
    def _(c):
        base = c * 2 * T * PER
        for t in range(T * PER):
            r, cc = t // PER * B, t % PER * B
            pltpu.make_async_copy(
                slots.at[at[base + t]], w1.at[c, r : r + B, cc : cc + B], sem_in.at[c]
            ).start()
            r, cc = t // T * B, t % T * B
            pltpu.make_async_copy(
                slots.at[at[base + T * PER + t]], w2.at[c, r : r + B, cc : cc + B], sem_in.at[c]
            ).start()

    load = Local(sem_load)
    load.start(mid_h, mid)
    load.start(bra_h, bra)
    last[...] = jnp.zeros_like(last)
    last[:NPOS] = load_rows(cot, length - NPOS, NPOS)

    def upstream(img):
        if img == imgs - 1:
            return last[...]
        return jnp.where(real_rows(), load_rows(cot, img * NPOS, NP), 0.0)

    for img in range(imgs):
        gs[img * NP : (img + 1) * NP] = (vec[9:10] * upstream(img)).astype(bf16)
    summed[...] = jnp.zeros_like(summed)
    gn2[...] = jnp.zeros_like(gn2)

    @pl.loop(0, chunks)
    def _(c):
        pltpu.make_async_copy(w1.at[c], w1.at[c], sem_in.at[c]).wait()
        pltpu.make_async_copy(w2.at[c], w2.at[c], sem_in.at[c]).wait()
        span = pl.ds(pl.multiple_of(c * CH, CH), CH)
        bias_sum = jnp.zeros((1, CH), f32)
        for rb in range(imgs // 2):
            block = slice(rb * 2 * NP, (rb + 1) * 2 * NP)
            hid = dot_nn(n2[block], w1[c]) + upb[:, span]
            back = dot_nt(gs[block], w2[c])
            phi = 0.5 * (1.0 + lax.erf(hid * (1.0 / math.sqrt(2.0))))
            density = jnp.exp(-0.5 * hid * hid) * (1.0 / math.sqrt(2.0 * math.pi))
            a = (hid * phi).astype(bf16)
            g = (back * (phi + hid * density)).astype(bf16)
            act[block] = a
            gh[block] = g
            bias_sum = bias_sum + jnp.sum(g.astype(f32), axis=0, keepdims=True)
            summed[block] += dot_nn(a, w2[c])
            gn2[block] += dot_nt(g, w1[c])
        bgrad[:, span] = bias_sum
        up_grad = dot_tn(n2[...], gh[...])
        down_grad = dot_tn(act[...], gs[...])
        base = c * 2 * T * PER
        for t in range(T * PER):
            r, cc = t // PER * B, t % PER * B
            tiles[c, t] = up_grad[r : r + B, cc : cc + B].astype(bf16)
            pltpu.make_async_copy(tiles.at[c, t], tiles_out.at[at[base + t]], sem_out).start()
        for t in range(T * PER):
            r, cc = t // T * B, t % T * B
            to = T * PER + t
            tiles[c, to] = down_grad[r : r + B, cc : cc + B].astype(bf16)
            pltpu.make_async_copy(tiles.at[c, to], tiles_out.at[at[base + to]], sem_out).start()

    load.finish()
    s4 = jnp.zeros((1, D), f32)
    s5 = jnp.zeros((1, D), f32)
    s6 = jnp.zeros((1, D), f32)
    s7 = jnp.zeros((1, D), f32)
    s8 = jnp.zeros((1, D), f32)
    s9 = jnp.zeros((1, D), f32)
    for img in range(imgs):
        block = slice(img * NP, (img + 1) * NP)
        up = upstream(img)
        middle = mid[img]
        sm = summed[block] + vec[8:9]
        s9 += jnp.sum(up * sm, axis=0, keepdims=True)
        s8 += jnp.sum(gs[block].astype(f32), axis=0, keepdims=True)
        x, inv = norm_parts(middle)
        gn = gn2[block]
        s6 += jnp.sum(gn * x, axis=0, keepdims=True)
        s7 += jnp.sum(gn, axis=0, keepdims=True)
        gm = up + norm_back(gn, x, inv, vec[6:7])
        gmid[img] = gm
        gb = (vec[5:6] * gm).astype(bf16)
        gbra[img] = gb
        s4 += jnp.sum(gb.astype(f32), axis=0, keepdims=True)
        s5 += jnp.sum(gm * bra[img], axis=0, keepdims=True)
        summed[img * NPOS : img * NPOS + NP] = middle + vec[9:10] * sm
    edge = length // 16 * 16
    out[0, :edge] = summed[:edge].astype(bf16)
    out[0, edge:] = summed[edge:length].astype(bf16)
    sums[...] = jnp.concatenate([s4, s5, s6, s7, s8, s9, s9, s9], axis=0)
    pltpu.make_async_copy(tiles, tiles, sem_out).wait()


def feed_forward(mid, bra, n2, cot, slots, at, vec, up_bias):
    imgs = mid.shape[0]
    rows = imgs * NP
    chunks = FF // CH
    return pl.pallas_call(
        mlp_kernel,
        in_specs=[SMEM, ANY, ANY, VMEM, VMEM, ANY, VMEM, VMEM],
        out_specs=[VMEM] * 5 + [ANY],
        out_shape=[
            shape((1, imgs * NPOS, D), bf16),
            shape((imgs, NP, D), f32),
            shape((imgs, NP, D), bf16),
            shape((8, D), f32),
            shape((1, FF), f32),
            shape(slots.shape, bf16),
        ],
        scratch_shapes=[
            pltpu.VMEM((imgs, NP, D), f32),
            pltpu.VMEM((imgs, NP, D), f32),
            pltpu.VMEM((NP, D), f32),
            pltpu.VMEM((chunks, D, CH), bf16),
            pltpu.VMEM((chunks, CH, D), bf16),
            pltpu.VMEM((rows, D), bf16),
            pltpu.VMEM((rows, CH), bf16),
            pltpu.VMEM((rows, CH), bf16),
            pltpu.VMEM((rows, D), f32),
            pltpu.VMEM((rows, D), f32),
            pltpu.VMEM((chunks, 2 * T * PER, B, B), bf16),
            pltpu.SemaphoreType.DMA((chunks,)),
            pltpu.SemaphoreType.DMA(()),
            pltpu.SemaphoreType.DMA((2,)),
        ],
        compiler_params=pltpu.CompilerParams(vmem_limit_bytes=LIMIT),
        name="feed_forward",
    )(at, mid, bra, n2.reshape(rows, D), cot, slots, vec, up_bias)


def backward_kernel(comm, inverse, gbra, lse, vec, idx, *refs):
    refs = list(refs)
    w_h, v_h, k_h, q_h, bias_h, att_h, tok_h, gmid_h = refs[:8]
    refs = refs[8:]
    if comm:
        mlp_full = refs.pop(0)
    gin, table, sums, tiles_o = refs[:4]
    refs = refs[4:]
    if comm:
        mlp_mine = refs.pop(0)
    w, v, k, q, bias, att, tok, gmid = refs[:8]
    n1, gatt, gqkv, grid, tiles, full, load_sems, out_sem = refs[8:16]
    refs = refs[16:]
    imgs = q.shape[0]

    if comm:
        place = Place()
        place.greet()
        moves = Scatter(place, mlp_full, mlp_mine.shape[0], *refs)
        step = moves.step
    else:
        step = lambda i, out=None: None
    load = Local(load_sems)
    got_w, got_v, got_k, got_q, got_bias, got_att, got_tok, got_gmid = [
        load.start(src, dst)
        for src, dst in zip(
            (w_h, v_h, k_h, q_h, bias_h, att_h, tok_h, gmid_h), (w, v, k, q, bias, att, tok, gmid)
        )
    ]
    step(0)
    got_w.wait()
    for n in range(D // NL):
        lanes = slice(n * NL, (n + 1) * NL)
        got = dot_nt(gbra[...], w[3, lanes, :]).astype(bf16)
        for img in range(imgs):
            gatt[img, :, lanes] = got[img * NP : (img + 1) * NP]
    grid[...] = jnp.zeros_like(grid)
    got_v.wait()
    got_k.wait()
    got_q.wait()
    got_bias.wait()
    plan = {4: 1, 12: 2, 18: 3}

    side = lax.broadcasted_iota(jnp.int32, (1, B), 1) // HD
    for img in range(imgs):
        here = slice(img * NP, (img + 1) * NP)
        for pair in range(H // 2):
            lanes = slice(pair * B, (pair + 1) * B)
            k_pair = k[img, :, lanes]
            v_pair = v[img, :, lanes]
            q_pair = pad_rows(q[img, :, lanes])
            g_pair = pad_rows(gatt[img, :, lanes])
            k_turn = k_pair.astype(f32).T.astype(bf16)
            gq = []
            gk = jnp.zeros((NP, B), f32)
            gv = jnp.zeros((NP, B), f32)
            for sub in range(2):
                h = pair * 2 + sub
                q_one = jnp.where(side == sub, q_pair, jnp.zeros_like(q_pair))
                g_one = jnp.where(side == sub, g_pair, jnp.zeros_like(g_pair))
                s = dot_nt(k_pair, q_one) + bias[h]
                p = jnp.exp(s - lse[img, h : h + 1])
                dp = dot_nt(v_pair, g_one)
                gv = gv + dot_nn(p.astype(bf16), g_one)
                inner = jnp.sum(p * dp, axis=0, keepdims=True)
                ds = (p * (dp - inner)).astype(bf16)
                gk = gk + dot_nn(ds, q_one)
                gq.append(dot_nn(k_turn[sub * HD : (sub + 1) * HD], ds))
                grid[h] += ds.astype(f32)
            turned = jnp.concatenate(gq, axis=0).T
            gqkv[here, lanes] = (turned[:NP] * HD**-0.5).astype(bf16)
            gqkv[here, D + pair * B : D + (pair + 1) * B] = gk.astype(bf16)
            gqkv[here, 2 * D + pair * B : 2 * D + (pair + 1) * B] = gv.astype(bf16)
            if img * (H // 2) + pair + 1 in plan:
                step(plan[img * (H // 2) + pair + 1])

    def put(m, n, grad):
        for r in range(T):
            for cc in range(NL // B):
                tiles[m * T * T + r * T + n * (NL // B) + cc] = grad[
                    r * B : (r + 1) * B, cc * B : (cc + 1) * B
                ].astype(bf16)

    got_att.wait()
    got_tok.wait()
    for img in range(imgs):
        x, _ = norm_parts(tok[img].astype(f32))
        n1[img * NP : (img + 1) * NP] = (x * vec[0:1] + vec[1:2]).astype(bf16)
    for n in range(D // NL):
        lanes = slice(n * NL, (n + 1) * NL)
        put(3, n, dot_tn(att[...], gbra[:, lanes]))
    for m in range(3):
        for n in range(D // NL):
            put(m, n, dot_tn(n1[...], gqkv[:, m * D + n * NL : m * D + (n + 1) * NL]))

    @pl.loop(0, full.shape[0] // 4)
    def _(group):
        for i in range(4):
            full[group * 4 + i] = tiles[inverse[group * 4 + i]]

    out = pltpu.make_async_copy(full, tiles_o, out_sem)
    out.start()
    step(4)
    accumulate_rows(grid, idx, table)

    got_gmid.wait()
    s0 = jnp.zeros((1, D), f32)
    s1 = jnp.zeros((1, D), f32)
    s2 = jnp.zeros((1, D), f32)
    s3 = jnp.zeros((1, D), f32)
    for img in range(imgs):
        here = slice(img * NP, (img + 1) * NP)
        gq = gqkv[here, 0:D]
        gk = gqkv[here, D : 2 * D]
        gv = gqkv[here, 2 * D : 3 * D]
        gn = dot_nt(gq, w[0]) + dot_nt(gk, w[1]) + dot_nt(gv, w[2])
        x, inv = norm_parts(tok[img].astype(f32))
        s0 += jnp.sum(gn * x, axis=0, keepdims=True)
        s1 += jnp.sum(gn, axis=0, keepdims=True)
        s2 += jnp.sum(gq.astype(f32), axis=0, keepdims=True)
        s3 += jnp.sum(gv.astype(f32), axis=0, keepdims=True)
        got = gmid[img] + norm_back(gn, x, inv, vec[0:1])
        store_rows(gin, img * NPOS, got[:NPOS] if img == imgs - 1 else got)
    sums[...] = jnp.concatenate([s0, s1, s2, s3, s3, s3, s3, s3], axis=0)
    if comm:
        step(5, mlp_mine)
    out.wait()


def backward_attention(comm, inverse, saved, gmid, gbra, vec, wide_total, mlp_full=None):
    w, q, k, v, att, mid, bra, n2, bias, tok, lse, idx = saved
    imgs = tok.shape[0]
    rows = imgs * NP
    att = att.reshape(rows, D)
    loaded = [w, v, k, q, bias, att, tok, gmid]
    args = [inverse, gbra.reshape(rows, D), lse, vec, idx] + loaded
    specs = [SMEM] + [VMEM] * 4 + [ANY] * 8
    out_shape = [
        shape((imgs * NPOS * LANES, B), f32),
        shape((16, wide_total), f32),
        shape((8, D), f32),
        shape((inverse.shape[0], B, B), bf16),
    ]
    out_specs = [VMEM] * 3 + [ANY]
    scratch = [pltpu.VMEM(x.shape, x.dtype) for x in loaded] + [
        pltpu.VMEM((rows, D), bf16),
        pltpu.VMEM((imgs, NP, D), bf16),
        pltpu.VMEM((rows, 3 * D), bf16),
        pltpu.VMEM((H, NP, NL), f32),
        pltpu.VMEM((4 * T * T, B, B), bf16),
        pltpu.VMEM((inverse.shape[0], B, B), bf16),
        pltpu.SemaphoreType.DMA((8,)),
        pltpu.SemaphoreType.DMA(()),
    ]
    params = dict(vmem_limit_bytes=LIMIT)
    if comm:
        n = mlp_full.shape[0] // 32
        args.append(mlp_full)
        specs.append(ANY)
        out_shape.append(shape((n, B, B), f32))
        out_specs.append(VMEM)
        scratch += scatter_scratch(n)
        params.update(collective_id=1, has_side_effects=True)
    return pl.pallas_call(
        partial(backward_kernel, comm),
        in_specs=specs,
        out_specs=out_specs,
        out_shape=out_shape,
        scratch_shapes=scratch,
        compiler_params=pltpu.CompilerParams(**params),
        name="backward_attention",
    )(*args)


NB = 16
GROUP = B // NB


def split_two(x):
    first = x.astype(bf16)
    return first, (x - first.astype(f32)).astype(bf16)


def wide_dot(x, y, dims):
    xa, xb = split_two(x)
    ya, yb = split_two(y)
    xs = jnp.concatenate([xa, xa, xb], axis=dims[0])
    ys = jnp.concatenate([ya, yb, ya], axis=dims[1])
    return lax.dot_general(
        xs, ys, (((dims[0],), (dims[1],)), ((), ())), preferred_element_type=f32
    )


def unit_inverse(diag):
    lane = lax.broadcasted_iota(jnp.int32, (NB, B), 1)
    row = lax.broadcasted_iota(jnp.int32, (NB, B), 0)
    inner = jnp.bitwise_and(lane, NB - 1)
    outer = lane - inner
    left = diag
    right = jnp.where(row == inner, 1.0, 0.0)
    def pick(k):
        return jnp.take_along_axis(diag, outer + k, axis=1, mode="promise_in_bounds")

    cut = NB // 2
    rows = [pick(r) for r in range(NB)]
    rows = [x if r < cut else x[cut:] for r, x in enumerate(rows)]
    flags = [jnp.where(row == r, 1.0, 0.0) for r in range(NB)]
    low = [x[:cut] for x in flags]
    high = [x[cut:] for x in flags]
    cols = [diag[r : r + 1] for r in range(NB)]
    pivots = jnp.zeros((1, B), f32)
    right_low, right_high = right[:cut], right[cut:]
    for r in range(NB):
        mine = rows[r]
        at = r if r < cut else r - cut
        pivot = mine[at : at + 1]
        pivots = jnp.where(inner[:1] == r, pivot, pivots)
        scale = pl.reciprocal(pivot, approx=True)
        scale = scale * (2.0 - pivot * scale)
        factor = jnp.where(inner[:1] > r, cols[r] * scale, 0.0)
        for s in range(r + 1, NB):
            at = s if r < cut else s - cut
            entry = mine[at : at + 1]
            share = entry * scale
            rows[s] = rows[s] - share * (mine if s < cut or r >= cut else mine[cut:])
            low[s] = low[s] - share * low[r]
            if r >= cut:
                high[s] = high[s] - share * high[r]
            cols[s] = cols[s] - factor * entry
        right_low = right_low - factor * low[r]
        if r >= cut:
            right_high = right_high - factor * high[r]
    right = jnp.concatenate([right_low, right_high], axis=0)
    return right * lax.rsqrt(pivots)


def orth_turned(mats, between=None):
    count = len(mats)
    groups = -(-count // GROUP)
    size = -(-count // groups)
    members = [list(range(g * size, min(count, (g + 1) * size))) for g in range(groups)]
    tails = []
    for a in mats:
        turned = a.T
        tails.append(jnp.concatenate([wide_dot(turned, turned, (1, 1)), turned], axis=1))
    own_block = (
        lax.broadcasted_iota(jnp.int32, (B, B), 0) // NB
        == lax.broadcasted_iota(jnp.int32, (B, B), 1) // NB
    )
    outs = [[] for _ in range(count)]
    for p in range(B // NB):
        base = p * NB
        for ids in members:
            fill = ids + [ids[-1]] * (GROUP - len(ids))
            strips = jnp.concatenate([tails[m][:NB] for m in fill], axis=0)
            turned = strips[:, :B].T
            unit = unit_inverse(turned[base : base + NB])
            spread = jnp.where(own_block, jnp.concatenate([unit] * GROUP, axis=0), 0.0)
            u = wide_dot(spread, strips, (0, 0))
            for at, m in enumerate(ids):
                um = u[at * NB : (at + 1) * NB]
                outs[m].append(um[:, B:])
                if base + NB < B:
                    tails[m] = tails[m][NB:] - wide_dot(um[:, base + NB : B], um, (0, 0))
        if between is not None:
            between(p)
    return [jnp.concatenate(o, axis=0) for o in outs]


def soap_slots(base, owner, grads, state, update, copy, between=None):
    count = grads.shape[0]
    mats = []
    gs = []
    for i in range(count):
        named = jnp.where(owner[...] == base + i, 1.0, 0.0)
        named = jnp.max(named, axis=1, keepdims=True)
        g = jnp.where(named > 0.0, grads[i].astype(f32), 0.0)
        gs.append(g)
        left = beta_stat * state[i, 3] + (1.0 - beta_stat) * wide_dot(g, g, (1, 1))
        right = beta_stat * state[i, 4] + (1.0 - beta_stat) * wide_dot(g, g, (0, 0))
        mats.append(wide_dot(left, state[i, 5], (1, 0)))
        mats.append(wide_dot(right, state[i, 6], (1, 0)))
    if between is not None:
        between(-1)
    turned = orth_turned(mats, between)
    fix_one = 1.0 - beta_one**STEP
    fix_two = 1.0 - beta_two**STEP
    for i in range(count):
        tl, tr = turned[2 * i], turned[2 * i + 1]
        rotated = wide_dot(wide_dot(tl, gs[i], (1, 0)), tr, (1, 1))
        new_first = beta_one * state[i, 1] + (1.0 - beta_one) * rotated
        new_second = beta_two * state[i, 2] + (1.0 - beta_two) * rotated * rotated
        normalized = new_first / fix_one / (jnp.sqrt(new_second / fix_two) + adam_eps)
        step = wide_dot(wide_dot(tl, normalized, (0, 0)), tr, (1, 0))
        weight = state[i, 0]
        weight = weight - matrix_rate * (step + decay_rate * weight)
        update[i, 0] = weight
        update[i, 1] = new_first
        update[i, 2] = new_second
        update[i, 3] = tl.T
        update[i, 4] = tr.T
        copy[i] = weight.astype(bf16)


def soap_kernel(first_slot, passed, owner, grads, state, *refs):
    kept, refs = refs[:passed], refs[passed:]
    update, copy = refs[:2]
    through, held, sems = refs[2 : 2 + passed], refs[2 + passed : 2 + 2 * passed], refs[2 + 2 * passed :]
    count = grads.shape[0]
    between = None
    if passed:
        into, out = Local(sems[0]), Local(sems[1])
        for src, dst in zip(kept, held):
            into.start(src, dst)

        def between(p):
            if p == 2:
                into.finish()
                for src, dst in zip(held, through):
                    out.start(src, dst)

    first = first_slot() + pl.program_id(0) * count
    soap_slots(first, owner, grads, state, update, copy, between)
    if passed:
        out.finish()


def soap_update(grads, state, owner, first_slot, kept=()):
    slots = grads.shape[0]
    count = max(c for c in range(1, 10) if slots % c == 0)
    assert not kept or count == slots
    return pl.pallas_call(
        partial(soap_kernel, first_slot, len(kept)),
        grid=(slots // count,),
        in_specs=[
            pl.BlockSpec((1, owner.shape[0]), lambda i: (0, 0)),
            pl.BlockSpec((count, B, B), lambda i: (i, 0, 0)),
            pl.BlockSpec((count, 7, B, B), lambda i: (i, 0, 0, 0)),
        ]
        + [ANY] * len(kept),
        out_specs=[
            pl.BlockSpec((count, 5, B, B), lambda i: (i, 0, 0, 0)),
            pl.BlockSpec((count, B, B), lambda i: (i, 0, 0)),
        ]
        + [ANY] * len(kept),
        out_shape=[shape((slots, 5, B, B), f32), shape((slots, B, B), bf16)]
        + [shape(x.shape, x.dtype) for x in kept],
        scratch_shapes=[pltpu.VMEM(x.shape, x.dtype) for x in kept]
        + [pltpu.SemaphoreType.DMA((len(kept),))] * (2 if kept else 0),
        compiler_params=pltpu.CompilerParams(vmem_limit_bytes=LIMIT),
        name="soap",
    )(owner[None], grads, state, *kept)


SUM_ROWS = 40


def adam(grad, param, first, second):
    new_first = beta_one * first + (1.0 - beta_one) * grad
    new_second = beta_two * second + (1.0 - beta_two) * grad * grad
    fix_one = 1.0 - beta_one**STEP
    fix_two = 1.0 - beta_two**STEP
    step = (new_first / fix_one) / (jnp.sqrt(new_second / fix_two) + adam_eps)
    return grad, param - vector_rate * step, new_first, new_second


def finish_kernel(
    full,
    mlp_sums,
    attn_sums,
    table_sums,
    bias_sums,
    vec,
    vec_m,
    table,
    table_m,
    upb,
    upb_m,
    owner,
    mlp_mine,
    state_h,
    mine,
    vec_up,
    table_up,
    upb_up,
    update,
    copy,
    state,
    load_sem,
    part,
    other,
    column,
    sum_send,
    sum_recv,
    *scratch,
):
    place = Place()
    place.greet()
    load = pltpu.make_async_copy(state_h.at[0], state, load_sem)
    load.start()

    moves = Scatter(place, full, mine.shape[0], *scratch)
    sums = Copies(place, sum_send, sum_recv)
    part[0, 0:8] = mlp_sums[...]
    part[0, 8:16] = attn_sums[...]
    part[0, 16:32] = table_sums[...]
    quarter = jnp.concatenate([bias_sums[:, i * D : (i + 1) * D] for i in range(FF // D)] * 2, axis=0)
    part[0, 32:40] = quarter
    sums.start("c", part.at[0], other.at[0], dc=1)
    moves.step(0)
    load.wait()

    def total_sums():
        part[4] = ((column[0] + column[1]) + column[2]) + column[3]
        total = part.at[4]
        grad = jnp.concatenate([total[8:12], total[0:6]], axis=0)
        for i, got in enumerate(adam(grad, vec[...], vec_m[:, 0, :], vec_m[:, 1, :])):
            vec_up[:, i, :] = got
        wide = table.shape[1]
        grad = total[16 : 16 + H, 0:wide]
        for i, got in enumerate(adam(grad, table[...], table_m[:, 0, :], table_m[:, 1, :])):
            table_up[:, i, :] = got
        for j in range(FF // D):
            lanes = slice(j * D, (j + 1) * D)
            for i, got in enumerate(
                adam(total[32 + j : 33 + j], upb[:, lanes], upb_m[0:1, lanes], upb_m[1:2, lanes])
            ):
                upb_up[i : i + 1, lanes] = got

    def between(p):
        if p == -1:
            sums.arrived("c")
            part[1] = part[0] + other[0]
            sums.start("x", part.at[1], other.at[1], dx=1)
            moves.step(1)
        elif p == 1:
            sums.arrived("x")
            part[2] = part[1] + other[1]
            sums.start("y", part.at[2], other.at[2], dy=1)
            moves.step(2)
        elif p == 3:
            sums.arrived("y")
            part[3] = part[2] + other[2]
            for d in (1, 2, 3):
                sums.start(("z", d), part.at[3], column.at[place.z], d=d)
            column[place.z] = part[3]
            moves.step(3)
        elif p == 6:
            moves.step(4)

    first_slot = lax.axis_index("dp") * mlp_mine.shape[0]
    soap_slots(first_slot, owner, mlp_mine, state, update, copy, between)
    for d in (1, 2, 3):
        sums.arrived(("z", d))
    total_sums()
    moves.step(5, mine)
    sums.sent()


def finish(full, small, params, owner, mlp_mine, mlp_state):
    n = full.shape[0] // 32
    nm = mlp_mine.shape[0]
    vec, vec_m, table, table_m, upb, upb_m = params
    return pl.pallas_call(
        finish_kernel,
        in_specs=[ANY] + [VMEM] * 12 + [ANY],
        out_specs=[VMEM] * 6,
        out_shape=[
            shape((n, B, B), f32),
            shape((vec.shape[0], 4, D), f32),
            shape((H, 4, table.shape[1]), f32),
            shape((4, FF), f32),
            shape((nm, 5, B, B), f32),
            shape((nm, B, B), bf16),
        ],
        scratch_shapes=[
            pltpu.VMEM((nm, 7, B, B), f32),
            pltpu.SemaphoreType.DMA(()),
            pltpu.VMEM((5, SUM_ROWS, D), f32),
            pltpu.VMEM((3, SUM_ROWS, D), f32),
            pltpu.VMEM((4, SUM_ROWS, D), f32),
            pltpu.SemaphoreType.DMA((6,)),
            pltpu.SemaphoreType.DMA((6,)),
        ]
        + scatter_scratch(n),
        compiler_params=pltpu.CompilerParams(
            collective_id=2, has_side_effects=True, vmem_limit_bytes=LIMIT
        ),
        name="finish",
    )(
        full,
        *small,
        vec,
        vec_m.transpose(1, 0, 2),
        table,
        table_m.transpose(1, 0, 2),
        upb[None],
        upb_m,
        owner[None],
        mlp_mine,
        mlp_state,
    )


def body(
    tokens,
    cotangent,
    rel_index,
    attn_owner,
    mlp_owner,
    attn_state,
    mlp_state,
    vec_param,
    vec_moments,
    rel_table,
    rel_table_moments,
    up_bias,
    up_bias_moments,
):
    both = ("dp", "mp")
    parts = lax.axis_size("mp")
    comm = own_kernels(lax.axis_size("dp"), parts)
    imgs = tokens.shape[1] // NPOS
    attn_local = attn_state.shape[0]
    mlp_local = mlp_state.shape[1]
    attn_total = attn_local * lax.axis_size("dp") * parts

    def attn_first():
        return (lax.axis_index("dp") * parts + lax.axis_index("mp")) * attn_local

    def mlp_first():
        return lax.axis_index("dp") * mlp_local

    wide_total = -(-rel_table.shape[1] // B) * B
    slot_ids = jnp.arange(attn_total, dtype=jnp.int32)
    block_ids = jnp.arange(attn_owner.shape[0], dtype=jnp.int32)
    inverse = jnp.sum(
        jnp.where(attn_owner[None, :] == slot_ids[:, None], block_ids[None, :], 0), axis=1
    ).astype(jnp.int32)

    if comm:
        *saved, mlp_slots = forward_attention(
            True,
            parts,
            mlp_local,
            attn_owner,
            mlp_owner,
            tokens,
            vec_param, rel_index, rel_table, attn_state, mlp_state
        )
    else:
        attn_slots = lax.all_gather(attn_state[:, 0].astype(bf16), both, axis=0, tiled=True)
        mlp_slots = lax.all_gather(mlp_state[0, :, 0].astype(bf16), both, axis=0, tiled=True)
        saved = list(
            forward_attention(
            False,
            parts,
            mlp_local,
            attn_owner,
            mlp_owner,
            tokens,
            vec_param, rel_index, rel_table, attn_slots
        ))
    mlp_at = saved.pop()
    w, q, k, v, att, mid, bra, n2, bias, tok, lse, idx = saved
    out, gmid, gbra, mlp_sums, bias_grad, mlp_grads = feed_forward(
        mid, bra, n2, cotangent.reshape(-1, B), mlp_slots, mlp_at, vec_param, up_bias[None]
    )
    if comm:
        gin, table_grad, attn_sums, attn_full, mlp_mine = backward_attention(
            True, inverse, saved, gmid, gbra, vec_param, wide_total, mlp_grads
        )
        attn_mine, vec_up, table_up, bias_up, mlp_result, mlp_copy = finish(
            attn_full,
            (mlp_sums, attn_sums, table_grad, bias_grad),
            (vec_param, vec_moments, rel_table, rel_table_moments, up_bias, up_bias_moments),
            mlp_owner,
            mlp_mine,
            mlp_state,
        )
        kept = (gin, mlp_result, mlp_copy, vec_up, table_up, bias_up)
        attn_result, attn_copy, *kept = soap_update(
            attn_mine, attn_state, attn_owner, attn_first, kept
        )
        gin, mlp_result, mlp_copy, vec_up, table_up, bias_up = kept
        vec_up = vec_up.transpose(1, 0, 2)
        table_up = table_up.transpose(1, 0, 2)
    else:
        gin, table_grad, attn_sums, attn_full = backward_attention(
            False, inverse, saved, gmid, gbra, vec_param, wide_total
        )
        mlp_mine = lax.psum_scatter(mlp_grads, both, scatter_dimension=0, tiled=True)
        attn_mine = lax.psum_scatter(attn_full, both, scatter_dimension=0, tiled=True)
        vector_grad = jnp.concatenate([attn_sums[:4], mlp_sums[:6]], axis=0)
        vector_total, table_total, bias_total = lax.psum(
            (vector_grad, table_grad[:H, : rel_table.shape[1]], bias_grad[0]), both
        )
        vec_up = jnp.stack(adam(vector_total, vec_param, vec_moments[0], vec_moments[1]))
        table_up = jnp.stack(
            adam(table_total, rel_table, rel_table_moments[0], rel_table_moments[1])
        )
        bias_up = jnp.stack(adam(bias_total, up_bias, up_bias_moments[0], up_bias_moments[1]))
        attn_result, attn_copy = soap_update(attn_mine, attn_state, attn_owner, attn_first)
        mlp_result, mlp_copy = soap_update(mlp_mine, mlp_state[0], mlp_owner, mlp_first)
    return (
        out,
        gin.reshape(1, imgs * NPOS, D),
        attn_result,
        attn_copy,
        mlp_result[None],
        mlp_copy[None],
        vec_up,
        table_up,
        bias_up,
    )


def solution(mesh):
    placed = (
        P(("dp", "mp"), None, None),
        P(("dp", "mp"), None, None),
        P(),
        P(),
        P(),
        P(("dp", "mp"), None, None, None),
        P("mp", "dp", None, None, None),
        P(),
        P(),
        P(),
        P(),
        P(),
        P(),
    )
    return jax.shard_map(
        body,
        mesh=mesh,
        in_specs=placed,
        out_specs=(
            P(("dp", "mp"), None, None),
            P(("dp", "mp"), None, None),
            P(("dp", "mp"), None, None, None),
            P(("dp", "mp"), None, None),
            P("mp", "dp", None, None, None),
            P("mp", "dp", None, None),
            P(),
            P(),
            P(),
        ),
        check_vma=False,
    )
```
